32 devices in a mesh: dp: 8 (over y, x, core), shard: 4 (over z).
Axes of the slice: x: 2, y: 2, z: 4, core: 2. Of those that a mesh axis runs over, the one named last changes fastest.
Arguments:
- inputs: bfloat16 [16, 1024, 768], P('dp', 'shard'), may hold values from -6 to 6
- segments: int32 [16, 1024], P('dp', 'shard'), may hold values from 0 to 11, as said below
- random_key_blocks: int32 [12, 16, 3], replicated, may hold values from 0 to 15, as said below
- adapter_index_table: int32 [16, 6], P('dp'), may hold values from 0 to 7
- frozen_query_key_value_weight: bfloat16 [768, 2304], P('shard'), may hold values from -0.21875 to 0.21875
- frozen_output_weight: bfloat16 [768, 768], P('shard'), may hold values from -0.875 to 0.875
- frozen_up_weight: bfloat16 [768, 3072], P('shard'), may hold values from -0.21875 to 0.21875
- frozen_down_weight: bfloat16 [3072, 768], P('shard'), may hold values from -0.109375 to 0.109375
- attention_norm_gain: float32 [768], replicated, may hold values from 0.5 to 1.5
- feedforward_norm_gain: float32 [768], replicated, may hold values from 0.5 to 1.5
- adapter_down_from_width: bfloat16 [5, 8, 16, 768], replicated, may hold values from -0.21875 to 0.21875
- adapter_down_from_hidden: bfloat16 [8, 16, 3072], replicated, may hold values from -0.109375 to 0.109375
- adapter_up_to_width: bfloat16 [5, 8, 16, 768], replicated, may hold values from -0.75 to 0.75
- adapter_up_to_hidden: bfloat16 [8, 16, 3072], replicated, may hold values from -0.75 to 0.75
- cotangent: bfloat16 [16, 1024, 768], P('dp', 'shard'), may hold values from -6 to 6
Outputs:
- layer_out: bfloat16 [16, 1024, 768], P('dp', 'shard')
- input_grad: float32 [16, 1024, 768], P('dp', 'shard')
- grad_lora_in_d: float32 [5, 8, 16, 768], P(None, None, None, 'shard')
- grad_lora_in_f: float32 [8, 16, 3072], P(None, None, 'shard')
- grad_lora_out_d: float32 [5, 8, 16, 768], P(None, None, None, 'shard')
- grad_lora_out_f: float32 [8, 16, 3072], P(None, None, 'shard')
The draws below stay inside these ranges and needn't reach their ends.
Inputs may be any that keep to these rules, and one draw needn't show every extreme that they name: `segments`: document numbers start at 0 and never fall along a sequence; among the 2 sequences of each index of dp one holds a single document. `random_key_blocks`: for each head and query block i the three numbers differ and none is below 2 or within one of i.
All inputs are finite; a program needn't handle non-finite values.
Results may differ from the reference program's by a relative error of at most 0.02.
Values may be sent and summed in bfloat16 or wider, within the bound.
No kernel may reach another device: no remote copies, remote signals or barrier semaphores. Data moves between devices by JAX's collectives and lax.ppermute only.
A program may use at most 448 MiB of HBM per device.

```python
import jax
import jax.numpy as jnp
from jax import lax

MODEL_WIDTH = 768
H = 12
HIDDEN_UNITS = 3072
HD = 64
ADAPTER_RANK = 16
ADAPTER_COUNT = 8
BLOCK = 64
GLOBALS = 2
RANDOMS = 3
SEQ_DP = 2
LENGTH = 1024
NBLK = 16
SEQS = 16


def draw_segments(key, part):
    key = jax.random.fold_in(key, 11)
    key_counts, key_single, key_left, key_right = jax.random.split(key, 4)
    groups = SEQS // SEQ_DP
    counts = jax.random.randint(key_counts, (SEQS,), 1, 12)
    single = jax.random.randint(key_single, (groups,), 0, SEQ_DP)
    placing = jnp.arange(SEQS, dtype=jnp.int32) % SEQ_DP
    chosen = jnp.repeat(single, SEQ_DP)
    counts = jnp.where(placing == chosen, 0, jnp.where(placing == (chosen + 1) % SEQ_DP, 11, counts))
    left_factor = jax.random.randint(key_left, (SEQS, 11), 0, LENGTH - 1)
    right_factor = jax.random.randint(key_right, (SEQS, 11), 0, LENGTH - 1)
    bounds = 1 + left_factor * right_factor // (LENGTH - 1)
    active = jnp.arange(11, dtype=jnp.int32)[None, :] < counts[:, None]
    position = jnp.arange(LENGTH, dtype=jnp.int32)
    passed = active[:, None, :] & (position[None, :, None] >= bounds[:, None, :])
    return jnp.sum(passed.astype(jnp.int32), axis=-1).astype(jnp.int32)


def draw_random_key_blocks(key, part):
    key = jax.random.fold_in(key, 23)
    raw_scores = jax.random.randint(key, (H, NBLK, NBLK), 0, 1 << 20)
    blocks = jnp.arange(NBLK, dtype=jnp.int32)
    scores = raw_scores * NBLK + blocks[None, None, :]
    banned = (blocks[None, :] < GLOBALS) | (jnp.abs(blocks[None, :] - blocks[:, None]) <= 1)
    scores = jnp.where(banned[None], -1, scores)
    return lax.top_k(scores, RANDOMS)[1].astype(jnp.int32)


def place_ends(values, stream_key, smallest, top_value):
    spot = [jax.random.randint(jax.random.fold_in(stream_key, axis), (), 0, length) for axis, length in enumerate(values.shape)]
    longest = values.shape.index(max(values.shape))
    neighbour = spot[:longest] + [(spot[longest] + 1) % values.shape[longest]] + spot[longest + 1:]
    return values.at[tuple(spot)].set(smallest).at[tuple(neighbour)].set(top_value)


def levels(rng, dims, cuts, low, top_value):
    loudness, own = 1.0, jax.random.fold_in(rng, 6)
    for axis_at, parts in cuts:
        steps = jnp.exp(jax.random.uniform(jax.random.fold_in(own, axis_at), (parts,), jnp.float32, low / len(cuts), top_value / len(cuts)))
        loudness = loudness * jnp.repeat(steps, dims[axis_at] // parts).reshape([-1 if axis == axis_at else 1 for axis in range(len(dims))])
    return loudness


def bell_draw(key, dims, scale, most, cuts=(), kind=jnp.bfloat16):
    factor_of = levels(key, dims, cuts, -0.22, 0.18) if cuts else 1.0
    drawn = jax.random.normal(key, dims, jnp.float32) * scale * factor_of
    return jnp.minimum(jnp.maximum(drawn, -most), most).astype(kind)


def setup_inputs(seed: int = 0) -> dict:
    streams_of = jax.random.split(jax.random.key(seed), 16)
    inputs = bell_draw(streams_of[0], (SEQS, LENGTH, MODEL_WIDTH), 1.0, 6.0, ((0, 8), (1, 4)))
    segments = draw_segments(jax.random.fold_in(streams_of[15], 71), 0)
    random_key_blocks = draw_random_key_blocks(jax.random.fold_in(streams_of[15], 71), 0)
    adapter_index_table = place_ends(jax.random.randint(streams_of[3], (SEQS, 6), 0, ADAPTER_COUNT), jax.random.fold_in(streams_of[3], 1), 0, ADAPTER_COUNT - 1).astype(jnp.int32)
    frozen_query_key_value_weight = bell_draw(streams_of[4], (MODEL_WIDTH, 3 * MODEL_WIDTH), MODEL_WIDTH ** -0.5, 0.21875, ((0, 4),))
    frozen_output_weight = bell_draw(streams_of[5], (MODEL_WIDTH, MODEL_WIDTH), (MODEL_WIDTH // 16) ** -0.5, 0.875, ((0, 4),))
    frozen_up_weight = bell_draw(streams_of[6], (MODEL_WIDTH, HIDDEN_UNITS), MODEL_WIDTH ** -0.5, 0.21875, ((0, 4),))
    frozen_down_weight = bell_draw(streams_of[7], (HIDDEN_UNITS, MODEL_WIDTH), HIDDEN_UNITS ** -0.5, 0.109375, ((0, 4),))
    attention_norm_gain = jnp.clip(1.0 + 0.1 * jax.random.normal(streams_of[8], (MODEL_WIDTH,), jnp.float32), 0.5, 1.5)
    feedforward_norm_gain = jnp.clip(1.0 + 0.1 * jax.random.normal(streams_of[9], (MODEL_WIDTH,), jnp.float32), 0.5, 1.5)
    adapter_down_from_width = bell_draw(streams_of[10], (5, ADAPTER_COUNT, ADAPTER_RANK, MODEL_WIDTH), MODEL_WIDTH ** -0.5, 0.21875)
    adapter_down_from_hidden = bell_draw(streams_of[11], (ADAPTER_COUNT, ADAPTER_RANK, HIDDEN_UNITS), HIDDEN_UNITS ** -0.5, 0.109375)
    adapter_up_to_width = bell_draw(streams_of[12], (5, ADAPTER_COUNT, ADAPTER_RANK, MODEL_WIDTH), (4 * ADAPTER_RANK) ** -0.5, 0.75)
    adapter_up_to_hidden = bell_draw(streams_of[13], (ADAPTER_COUNT, ADAPTER_RANK, HIDDEN_UNITS), (4 * ADAPTER_RANK) ** -0.5, 0.75)
    cotangent = bell_draw(streams_of[14], (SEQS, LENGTH, MODEL_WIDTH), 1.0, 6.0, ((0, 8), (1, 4)))
    return dict(inputs=inputs, segments=segments, random_key_blocks=random_key_blocks, adapter_index_table=adapter_index_table, frozen_query_key_value_weight=frozen_query_key_value_weight, frozen_output_weight=frozen_output_weight, frozen_up_weight=frozen_up_weight, frozen_down_weight=frozen_down_weight, attention_norm_gain=attention_norm_gain, feedforward_norm_gain=feedforward_norm_gain, adapter_down_from_width=adapter_down_from_width, adapter_down_from_hidden=adapter_down_from_hidden, adapter_up_to_width=adapter_up_to_width, adapter_up_to_hidden=adapter_up_to_hidden, cotangent=cotangent)


@jax.custom_vjp
def low(v):
    return lax.optimization_barrier(v.astype(jnp.bfloat16)).astype(jnp.float32)

@jax.custom_vjp
def low_back(v):
    return v

def low_keep(v):
    return (low(v), None)

def low_pass(kept, grad):
    return (grad,)

def back_keep(v):
    return (v, None)

def back_low(kept, grad):
    return (low(grad),)
low.defvjp(low_keep, low_pass)
low_back.defvjp(back_keep, back_low)
EPSILON = 1e-06
NEGATIVE = -1e+30
highest = lax.Precision.HIGHEST

def matmul(left_side, right_side):
    return jnp.dot(left_side, right_side, precision=highest, preferred_element_type=jnp.float32)

def norm_rows(hidden, gain_vector):
    average = lax.optimization_barrier(jnp.mean(hidden, axis=-1, keepdims=True))
    centred = hidden - average
    spread = lax.optimization_barrier(jnp.mean(centred * centred, axis=-1, keepdims=True))
    return centred * lax.rsqrt(spread + EPSILON) * gain_vector

def adapter(source, table_in, table_out, chosen):
    down_rows = table_in[chosen]
    up_rows = table_out[chosen]
    rank_part = low_back(low(matmul(source, down_rows.T)))
    return matmul(rank_part, up_rows)

def attend(queries, keys_all, values_all, seg_all, allowed):
    group_rows = min(512, LENGTH)
    groups = LENGTH // group_rows
    query_heads = queries.reshape(LENGTH, H, HD).transpose(1, 0, 2)
    key_heads = keys_all.reshape(LENGTH, H, HD).transpose(1, 0, 2)
    value_heads = values_all.reshape(LENGTH, H, HD).transpose(1, 0, 2)
    query_groups = query_heads.reshape(H, groups, group_rows, HD).transpose(1, 0, 2, 3)
    seg_groups = seg_all.reshape(groups, group_rows)
    starts = jnp.arange(groups, dtype=jnp.int32) * group_rows
    key_blocks = jnp.arange(LENGTH, dtype=jnp.int32) // BLOCK
    scaling = HD ** (-0.5)

    def one_group(packet):
        query_rows, seg_rows, start_row = packet
        scores = jnp.einsum('hqd,hkd->hqk', query_rows, key_heads, precision=highest) * scaling
        scores = low_back(scores)
        row_blocks = (start_row + jnp.arange(group_rows, dtype=jnp.int32)) // BLOCK
        block_allow = allowed[:, row_blocks][:, :, key_blocks]
        permit = block_allow & (seg_rows[:, None] == seg_all[None, :])[None]
        scores = jnp.where(permit, scores, NEGATIVE)
        top_score = lax.optimization_barrier(jnp.max(scores, axis=-1, keepdims=True))
        weights = jnp.exp(scores - top_score)
        shares = low(weights / lax.optimization_barrier(jnp.sum(weights, axis=-1, keepdims=True)))
        return jnp.einsum('hqk,hkd->hqd', shares, value_heads, precision=highest)
    results = lax.map(jax.checkpoint(one_group), (query_groups, seg_groups, starts))
    return results.transpose(0, 2, 1, 3).reshape(LENGTH, H * HD)

def layer(inputs, in_d, in_f, out_d, out_f, chosen, seg_all, allowed, frozen_query_key_value_weight, frozen_output_weight, frozen_up_weight, frozen_down_weight, attention_norm_gain, feedforward_norm_gain):
    width = inputs.shape[1]
    main_part = matmul(inputs, frozen_query_key_value_weight)
    projected = []
    for table_column in range(3):
        extra = adapter(inputs, in_d[table_column], out_d[table_column], chosen[table_column])
        projected.append(low_back(low(main_part[:, table_column * width:(table_column + 1) * width] + extra)))
    mixed = low_back(low(attend(projected[0], projected[1], projected[2], seg_all, allowed)))
    branch = low_back(matmul(mixed, frozen_output_weight) + adapter(mixed, in_d[3], out_d[3], chosen[3]))
    first = norm_rows(inputs + branch, attention_norm_gain)
    first_low = low(first)
    lifted = low_back(matmul(first_low, frozen_up_weight) + adapter(first_low, in_d[4], out_f, chosen[4]))
    activated = low(jax.nn.gelu(lifted, approximate=False))
    lowered = low_back(matmul(activated, frozen_down_weight) + adapter(activated, in_f, out_d[4], chosen[5]))
    return norm_rows(first + lowered, feedforward_norm_gain)

def widen_rows(values):
    return values.astype(jnp.float32)

def reference(inputs, segments, random_key_blocks, adapter_index_table, frozen_query_key_value_weight, frozen_output_weight, frozen_up_weight, frozen_down_weight, attention_norm_gain, feedforward_norm_gain, adapter_down_from_width, adapter_down_from_hidden, adapter_up_to_width, adapter_up_to_hidden, cotangent):
    blocks = jnp.arange(NBLK, dtype=jnp.int32)
    nearby = jnp.abs(blocks[:, None] - blocks[None, :]) <= 1
    global_part = (blocks[:, None] < GLOBALS) | (blocks[None, :] < GLOBALS)
    picked = jnp.any(random_key_blocks[:, :, :, None] == blocks[None, None, None, :], axis=2)
    allowed = picked | (nearby | global_part)[None]
    frozen_qkv = widen_rows(frozen_query_key_value_weight)
    frozen_out = widen_rows(frozen_output_weight)
    frozen_up = widen_rows(frozen_up_weight)
    frozen_down = widen_rows(frozen_down_weight)
    adapter_tables = (widen_rows(adapter_down_from_width), widen_rows(adapter_down_from_hidden), widen_rows(adapter_up_to_width), widen_rows(adapter_up_to_hidden))

    def step(carry, packet):
        seq_rows, seq_segments, seq_ids, seq_grad = packet

        def forward(x_in, table_a, table_b, table_c, table_d):
            return layer(x_in, table_a, table_b, table_c, table_d, seq_ids, seq_segments, allowed, frozen_qkv, frozen_out, frozen_up, frozen_down, attention_norm_gain, feedforward_norm_gain)
        result, pullback = jax.vjp(forward, seq_rows, adapter_tables[0], adapter_tables[1], adapter_tables[2], adapter_tables[3])
        grads = pullback(seq_grad)
        carry = tuple((total + part for total, part in zip(carry, grads[1:])))
        return (carry, (result.astype(jnp.bfloat16), grads[0]))
    start_sums = tuple((jnp.zeros_like(table) for table in adapter_tables))
    totals, (results, input_grads) = lax.scan(step, start_sums, (widen_rows(inputs), segments, adapter_index_table, widen_rows(cotangent)))
    return (results, input_grads, totals[0], totals[1], totals[2], totals[3])
```

```python
import jax
import jax.numpy as jnp
from jax import lax
from jax.experimental import pallas as pl
from jax.experimental.pallas import tpu as pltpu
from jax.sharding import PartitionSpec as P

H = 12
HD = 64
BLOCK = 64
GLOBALS = 2
RANDOMS = 3


EPSILON = 1e-06
NEGATIVE = -1e30


def norm_rows(hidden, gain_vector):
    average = jnp.mean(hidden, axis=-1, keepdims=True)
    centred = hidden - average
    spread = jnp.mean(centred * centred, axis=-1, keepdims=True)
    return centred * lax.rsqrt(spread + EPSILON) * gain_vector


def gelu_exact(values):
    return jax.nn.gelu(values, approximate=False)


def dense_forward(inputs, weight):
    return jnp.einsum("sti,io->sto", inputs, weight, preferred_element_type=jnp.float32)


def dense_backward(grad_low, weight):
    return jnp.einsum("sto,io->sti", grad_low, weight, preferred_element_type=jnp.float32)


def adapt(inputs, down_rows, up_rows):
    rank_part = jnp.einsum(
        "sti,sri->str", inputs, down_rows, preferred_element_type=jnp.float32
    ).astype(jnp.bfloat16)
    return (
        rank_part,
        jnp.einsum("str,sro->sto", rank_part, up_rows, preferred_element_type=jnp.float32),
    )


def adapt_back(inputs, down_rows, up_rows, rank_part, grad_low):
    grad_up = jnp.einsum("str,sto->sro", rank_part, grad_low, preferred_element_type=jnp.float32)
    rank_grad = jnp.einsum(
        "sto,sro->str", grad_low, up_rows, preferred_element_type=jnp.float32
    ).astype(jnp.bfloat16)
    grad_down = jnp.einsum("str,sti->sri", rank_grad, inputs, preferred_element_type=jnp.float32)
    grad_inputs = jnp.einsum(
        "str,sri->sti", rank_grad, down_rows, preferred_element_type=jnp.float32
    )
    return (grad_down, grad_up, grad_inputs)


def table_sum(per_sequence, chosen, table_size):
    matches = (chosen[:, None] == jnp.arange(table_size, dtype=jnp.int32)[None, :]).astype(
        jnp.float32
    )
    return jnp.sum(matches[:, :, None, None] * per_sequence[:, None], axis=0)


def sparse_scores(query_heads, key_picked, permit, scaling):
    scores = (
        jnp.einsum(
            "shbqd,shbkd->shbqk", query_heads, key_picked, preferred_element_type=jnp.float32
        )
        * scaling
    )
    return jnp.where(permit, scores, NEGATIVE)


def global_scores(query_rows, key_rows, seg_query, seg_keys, scaling):
    scores = (
        jnp.einsum("hqd,hkd->hqk", query_rows, key_rows, preferred_element_type=jnp.float32)
        * scaling
    )
    return jnp.where((seg_query[:, None] == seg_keys[None, :])[None], scores, NEGATIVE)


def global_forward(query_rows, key_rows, value_rows, seg_query, seg_keys, scaling):
    scores = global_scores(query_rows, key_rows, seg_query, seg_keys, scaling)
    top_score = jnp.max(scores, axis=-1, keepdims=True)
    weights = jnp.exp(scores - top_score)
    totals = jnp.sum(weights, axis=-1, keepdims=True)
    shares = (weights / totals).astype(jnp.bfloat16)
    attended = jnp.einsum("hqk,hkd->hqd", shares, value_rows, preferred_element_type=jnp.float32)
    return (attended, (top_score + jnp.log(totals))[..., 0])


def global_backward(
    query_rows, key_rows, value_rows, seg_query, seg_keys, grad_rows, log_total, scaling
):
    scores = global_scores(query_rows, key_rows, seg_query, seg_keys, scaling)
    shares = jnp.exp(scores - log_total[..., None])
    share_low = shares.astype(jnp.bfloat16)
    grad_shares = jnp.einsum(
        "hqd,hkd->hqk", grad_rows, value_rows, preferred_element_type=jnp.float32
    )
    centre = jnp.sum(shares * grad_shares, axis=-1, keepdims=True)
    grad_scores = (shares * (grad_shares - centre)).astype(jnp.bfloat16)
    grad_query = (
        jnp.einsum("hqk,hkd->hqd", grad_scores, key_rows, preferred_element_type=jnp.float32)
        * scaling
    )
    grad_keys = (
        jnp.einsum("hqk,hqd->hkd", grad_scores, query_rows, preferred_element_type=jnp.float32)
        * scaling
    )
    grad_values = jnp.einsum(
        "hqk,hqd->hkd", share_low, grad_rows, preferred_element_type=jnp.float32
    )
    return (grad_query, grad_keys, grad_values, centre[..., 0])


def general_body(
    inputs,
    segments,
    random_key_blocks,
    adapter_index_table,
    frozen_query_key_value_weight,
    frozen_output_weight,
    frozen_up_weight,
    frozen_down_weight,
    attention_norm_gain,
    feedforward_norm_gain,
    adapter_down_from_width,
    adapter_down_from_hidden,
    adapter_up_to_width,
    adapter_up_to_hidden,
    cotangent,
):
    seq_count = inputs.shape[0]
    local_tokens = inputs.shape[1]
    width = inputs.shape[2]
    shard_count = lax.axis_size("shard")
    full_length = local_tokens * shard_count
    total_blocks = full_length // BLOCK
    local_blocks = local_tokens // BLOCK
    cand_count = 3 + GLOBALS + RANDOMS
    glob_rows = GLOBALS * BLOCK
    scaling = HD ** (-0.5)

    def select_adapter_table(table, table_column):
        return jnp.take(table, adapter_index_table[:, table_column], axis=0)

    adapter_tables_input = [
        select_adapter_table(adapter_down_from_width[table_column], table_column)
        for table_column in range(5)
    ] + [select_adapter_table(adapter_down_from_hidden, 5)]
    adapter_tables_output = [
        select_adapter_table(adapter_up_to_width[table_column], table_column)
        for table_column in range(4)
    ]
    adapter_tables_output = adapter_tables_output + [
        select_adapter_table(adapter_up_to_hidden, 4),
        select_adapter_table(adapter_up_to_width[4], 5),
    ]
    qkv_full, out_full = (
        lax.all_gather(frozen_query_key_value_weight, "shard", axis=0, tiled=True),
        lax.all_gather(frozen_output_weight, "shard", axis=0, tiled=True),
    )
    main_part = dense_forward(inputs, qkv_full)
    rank_parts = []
    projected = []
    for table_column in range(3):
        rank_part, extra = adapt(
            inputs, adapter_tables_input[table_column], adapter_tables_output[table_column]
        )
        rank_parts.append(rank_part)
        projected.append(
            (main_part[..., table_column * width : (table_column + 1) * width] + extra).astype(
                jnp.bfloat16
            )
        )
    seg_low = segments.astype(jnp.bfloat16)
    key_all, value_all, seg_all = (
        lax.all_gather(projected[1], "shard", axis=1, tiled=True),
        lax.all_gather(projected[2], "shard", axis=1, tiled=True),
        lax.all_gather(seg_low, "shard", axis=1, tiled=True),
    )
    shard_pos = lax.axis_index("shard")
    is_first = shard_pos == 0
    first_block = shard_pos * local_blocks
    block_ids = first_block + jnp.arange(local_blocks, dtype=jnp.int32)
    rand_local = lax.dynamic_slice_in_dim(random_key_blocks, first_block, local_blocks, axis=1)
    window_part = jnp.stack([block_ids - 1, block_ids, block_ids + 1], axis=-1)
    global_ids = jnp.broadcast_to(
        jnp.arange(GLOBALS, dtype=jnp.int32)[None, :], (local_blocks, GLOBALS)
    )
    fixed_part = jnp.concatenate([window_part, global_ids], axis=-1)
    candidates = jnp.concatenate(
        [jnp.broadcast_to(fixed_part[None], (H, local_blocks, 3 + GLOBALS)), rand_local], axis=-1
    )
    candidates = jnp.clip(candidates, 0, total_blocks - 1)
    always_true = jnp.ones((local_blocks,), dtype=bool)
    fixed_valid = jnp.stack(
        [block_ids - 1 >= GLOBALS, always_true, block_ids + 1 < total_blocks]
        + [always_true] * GLOBALS,
        axis=-1,
    )
    valid = jnp.concatenate(
        [
            jnp.broadcast_to(fixed_valid[None], (H, local_blocks, 3 + GLOBALS)),
            jnp.ones((H, local_blocks, RANDOMS), dtype=bool),
        ],
        axis=-1,
    )
    valid_keys = jnp.repeat(valid, BLOCK, axis=-1)
    query_heads = (
        projected[0].reshape(seq_count, local_blocks, BLOCK, H, HD).transpose(0, 3, 1, 2, 4)
    )
    key_source = key_all.reshape(seq_count, total_blocks, BLOCK, H, HD).transpose(0, 3, 1, 2, 4)
    value_source = value_all.reshape(seq_count, total_blocks, BLOCK, H, HD).transpose(0, 3, 1, 2, 4)
    head_index = jnp.arange(H, dtype=jnp.int32)[:, None, None]
    key_picked = key_source[:, head_index, candidates].reshape(
        seq_count, H, local_blocks, cand_count * BLOCK, HD
    )
    value_picked = value_source[:, head_index, candidates].reshape(
        seq_count, H, local_blocks, cand_count * BLOCK, HD
    )
    seg_picked = seg_all.reshape(seq_count, total_blocks, BLOCK)[:, candidates].reshape(
        seq_count, H, local_blocks, cand_count * BLOCK
    )
    seg_local = seg_low.reshape(seq_count, local_blocks, BLOCK)
    permit = valid_keys[None, :, :, None, :] & (
        seg_local[:, None, :, :, None] == seg_picked[:, :, :, None, :]
    )
    scores = sparse_scores(query_heads, key_picked, permit, scaling)
    top_score = jnp.max(scores, axis=-1, keepdims=True)
    weights = jnp.exp(scores - top_score)
    totals = jnp.sum(weights, axis=-1, keepdims=True)
    share_low = (weights / totals).astype(jnp.bfloat16)
    sparse_lse = (top_score + jnp.log(totals))[..., 0]
    sparse_out = jnp.einsum(
        "shbqk,shbkd->shbqd", share_low, value_picked, preferred_element_type=jnp.float32
    )
    key_heads = key_source.reshape(seq_count, H, full_length, HD)
    value_heads = value_source.reshape(seq_count, H, full_length, HD)
    glob_query = query_heads[:, :, :GLOBALS].reshape(seq_count, H, glob_rows, HD)
    glob_seg = seg_low[:, :glob_rows]

    def run_forward(operands):
        return lax.map(
            lambda packet: global_forward(
                packet[0], packet[1], packet[2], packet[3], packet[4], scaling
            ),
            operands,
        )

    def skip_forward(operands):
        return (
            jnp.zeros((seq_count, H, glob_rows, HD), jnp.float32),
            jnp.zeros((seq_count, H, glob_rows), jnp.float32),
        )

    global_out, global_lse = lax.cond(
        is_first, run_forward, skip_forward, (glob_query, key_heads, value_heads, glob_seg, seg_all)
    )
    glob_blocks = global_out.reshape(seq_count, H, GLOBALS, BLOCK, HD)
    head_out = jnp.concatenate(
        [jnp.where(is_first, glob_blocks, sparse_out[:, :, :GLOBALS]), sparse_out[:, :, GLOBALS:]],
        axis=2,
    )
    mixed_low = (
        head_out.transpose(0, 2, 3, 1, 4)
        .reshape(seq_count, local_tokens, width)
        .astype(jnp.bfloat16)
    )
    rank_out, extra_out = adapt(mixed_low, adapter_tables_input[3], adapter_tables_output[3])
    branch = dense_forward(mixed_low, out_full) + extra_out
    first, first_pull = jax.vjp(
        lambda hidden: norm_rows(hidden, attention_norm_gain), inputs.astype(jnp.float32) + branch
    )
    first_low = first.astype(jnp.bfloat16)
    up_full, down_full = (
        lax.all_gather(frozen_up_weight, "shard", axis=0, tiled=True),
        lax.all_gather(frozen_down_weight, "shard", axis=0, tiled=True),
    )
    rank_up, extra_up = adapt(first_low, adapter_tables_input[4], adapter_tables_output[4])
    lifted = dense_forward(first_low, up_full) + extra_up
    activated, gelu_pull = jax.vjp(gelu_exact, lifted)
    active_low = activated.astype(jnp.bfloat16)
    rank_down, extra_down = adapt(active_low, adapter_tables_input[5], adapter_tables_output[5])
    lowered = dense_forward(active_low, down_full) + extra_down
    result, final_pull = jax.vjp(
        lambda hidden: norm_rows(hidden, feedforward_norm_gain), first + lowered
    )
    layer_out = result.astype(jnp.bfloat16)
    up_back, down_back = (
        lax.all_gather(frozen_up_weight, "shard", axis=0, tiled=True),
        lax.all_gather(frozen_down_weight, "shard", axis=0, tiled=True),
    )
    grad_adapt_in = [None] * 6
    grad_adapt_out = [None] * 6
    (grad_sum,) = final_pull(cotangent.astype(jnp.float32))
    grad_lowered = grad_sum.astype(jnp.bfloat16)
    grad_adapt_in[5], grad_adapt_out[5], extra_grad = adapt_back(
        active_low, adapter_tables_input[5], adapter_tables_output[5], rank_down, grad_lowered
    )
    grad_active = dense_backward(grad_lowered, down_back) + extra_grad
    (grad_lifted,) = gelu_pull(grad_active)
    grad_lift_low = grad_lifted.astype(jnp.bfloat16)
    grad_adapt_in[4], grad_adapt_out[4], extra_grad = adapt_back(
        first_low, adapter_tables_input[4], adapter_tables_output[4], rank_up, grad_lift_low
    )
    grad_first = grad_sum + dense_backward(grad_lift_low, up_back) + extra_grad
    (grad_branch,) = first_pull(grad_first)
    grad_branch_low = grad_branch.astype(jnp.bfloat16)
    qkv_back, out_back = (
        lax.all_gather(frozen_query_key_value_weight, "shard", axis=0, tiled=True),
        lax.all_gather(frozen_output_weight, "shard", axis=0, tiled=True),
    )
    grad_adapt_in[3], grad_adapt_out[3], extra_grad = adapt_back(
        mixed_low, adapter_tables_input[3], adapter_tables_output[3], rank_out, grad_branch_low
    )
    grad_mixed = (dense_backward(grad_branch_low, out_back) + extra_grad).astype(jnp.bfloat16)
    grad_heads = grad_mixed.reshape(seq_count, local_blocks, BLOCK, H, HD).transpose(0, 3, 1, 2, 4)
    row_keep = (block_ids >= GLOBALS)[None, None, :, None, None]
    grad_sparse = jnp.where(row_keep, grad_heads, jnp.zeros_like(grad_heads))
    scores = sparse_scores(query_heads, key_picked, permit, scaling)
    shares = jnp.exp(scores - sparse_lse[..., None])
    share_low = shares.astype(jnp.bfloat16)
    grad_shares = jnp.einsum(
        "shbqd,shbkd->shbqk", grad_sparse, value_picked, preferred_element_type=jnp.float32
    )
    centre = jnp.sum(shares * grad_shares, axis=-1, keepdims=True)
    grad_scores = (shares * (grad_shares - centre)).astype(jnp.bfloat16)
    grad_query = (
        jnp.einsum(
            "shbqk,shbkd->shbqd", grad_scores, key_picked, preferred_element_type=jnp.float32
        )
        * scaling
    )
    glob_grad = grad_heads[:, :, :GLOBALS].reshape(seq_count, H, glob_rows, HD)

    def run_backward(operands):
        return lax.map(
            lambda packet: global_backward(
                packet[0], packet[1], packet[2], packet[3], packet[4], packet[5], packet[6], scaling
            ),
            operands,
        )

    def skip_backward(operands):
        return (
            jnp.zeros((seq_count, H, glob_rows, HD), jnp.float32),
            jnp.zeros((seq_count, H, full_length, HD), jnp.float32),
            jnp.zeros((seq_count, H, full_length, HD), jnp.float32),
            jnp.zeros((seq_count, H, glob_rows), jnp.float32),
        )

    glob_dq, glob_dk, glob_dv, glob_centre = lax.cond(
        is_first,
        run_backward,
        skip_backward,
        (glob_query, key_heads, value_heads, glob_seg, seg_all, glob_grad, global_lse),
    )
    grad_query = grad_query.at[:, :, :GLOBALS].add(
        glob_dq.reshape(seq_count, H, GLOBALS, BLOCK, HD)
    )
    grad_key_picked = (
        jnp.einsum(
            "shbqk,shbqd->shbkd", grad_scores, query_heads, preferred_element_type=jnp.float32
        )
        * scaling
    )
    grad_value_picked = jnp.einsum(
        "shbqk,shbqd->shbkd", share_low, grad_sparse, preferred_element_type=jnp.float32
    )
    block_shape = (seq_count, H, local_blocks, cand_count, BLOCK, HD)
    key_grad_blocks = (
        jnp.zeros((seq_count, H, total_blocks, BLOCK, HD), jnp.float32)
        .at[:, head_index, candidates]
        .add(grad_key_picked.reshape(block_shape))
    )
    value_grad_blocks = (
        jnp.zeros((seq_count, H, total_blocks, BLOCK, HD), jnp.float32)
        .at[:, head_index, candidates]
        .add(grad_value_picked.reshape(block_shape))
    )
    key_grad_full = (
        (key_grad_blocks.reshape(seq_count, H, full_length, HD) + glob_dk)
        .transpose(0, 2, 1, 3)
        .reshape(seq_count, full_length, width)
    )
    value_grad_full = (
        (value_grad_blocks.reshape(seq_count, H, full_length, HD) + glob_dv)
        .transpose(0, 2, 1, 3)
        .reshape(seq_count, full_length, width)
    )
    key_grad, value_grad = (
        lax.psum_scatter(
            key_grad_full.astype(jnp.bfloat16), "shard", scatter_dimension=1, tiled=True
        ).astype(jnp.float32),
        lax.psum_scatter(
            value_grad_full.astype(jnp.bfloat16), "shard", scatter_dimension=1, tiled=True
        ).astype(jnp.float32),
    )
    query_grad = grad_query.transpose(0, 2, 3, 1, 4).reshape(seq_count, local_tokens, width)
    grad_proj = [
        query_grad.astype(jnp.bfloat16),
        key_grad.astype(jnp.bfloat16),
        value_grad.astype(jnp.bfloat16),
    ]
    input_grad = grad_branch + dense_backward(jnp.concatenate(grad_proj, axis=-1), qkv_back)
    for table_column in range(3):
        grad_adapt_in[table_column], grad_adapt_out[table_column], extra_grad = adapt_back(
            inputs,
            adapter_tables_input[table_column],
            adapter_tables_output[table_column],
            rank_parts[table_column],
            grad_proj[table_column],
        )
        input_grad = input_grad + extra_grad
    adapter_table_count = adapter_down_from_width.shape[1]
    grad_in_d = jnp.stack(
        [
            table_sum(
                grad_adapt_in[table_column],
                adapter_index_table[:, table_column],
                adapter_table_count,
            )
            for table_column in range(5)
        ],
        axis=0,
    )
    grad_in_f = table_sum(grad_adapt_in[5], adapter_index_table[:, 5], adapter_table_count)
    out_list = [
        table_sum(
            grad_adapt_out[table_column], adapter_index_table[:, table_column], adapter_table_count
        )
        for table_column in range(4)
    ]
    grad_out_d = jnp.stack(
        out_list + [table_sum(grad_adapt_out[5], adapter_index_table[:, 5], adapter_table_count)],
        axis=0,
    )
    grad_out_f = table_sum(grad_adapt_out[4], adapter_index_table[:, 4], adapter_table_count)
    owned = (
        lax.psum_scatter(
            grad_in_d.astype(jnp.bfloat16), "shard", scatter_dimension=3, tiled=True
        ).astype(jnp.float32),
        lax.psum_scatter(
            grad_in_f.astype(jnp.bfloat16), "shard", scatter_dimension=2, tiled=True
        ).astype(jnp.float32),
        lax.psum_scatter(
            grad_out_d.astype(jnp.bfloat16), "shard", scatter_dimension=3, tiled=True
        ).astype(jnp.float32),
        lax.psum_scatter(
            grad_out_f.astype(jnp.bfloat16), "shard", scatter_dimension=2, tiled=True
        ).astype(jnp.float32),
    )
    summed = (
        lax.psum(owned[0].astype(jnp.bfloat16), "dp").astype(jnp.float32),
        lax.psum(owned[1].astype(jnp.bfloat16), "dp").astype(jnp.float32),
        lax.psum(owned[2].astype(jnp.bfloat16), "dp").astype(jnp.float32),
        lax.psum(owned[3].astype(jnp.bfloat16), "dp").astype(jnp.float32),
    )
    return (layer_out, input_grad, summed[0], summed[1], summed[2], summed[3])


BF = jnp.bfloat16
F32 = jnp.float32
NT = (((1,), (1,)), ((), ()))
TN = (((0,), (0,)), ((), ()))
BIG = 1e30
RANK = 16
ANY = pl.ANY
VMEM = pltpu.VMEM
VMEM_LIMIT = 56 * 1024 * 1024


def mm(left, right):
    return jnp.dot(left, right, preferred_element_type=F32)


def mm_nt(left, right):
    return lax.dot_general(left, right, NT, preferred_element_type=F32)


def mm_tn(left, right):
    return lax.dot_general(left, right, TN, preferred_element_type=F32)


def whole(shape):
    return pl.BlockSpec(shape, lambda *_: (0,) * len(shape))


def exchange_pairs(dp_count, shard_count, step):
    pairs = []
    for chip in range(dp_count // 2):
        for k in range(2):
            for z in range(shard_count):
                b = z ^ step
                source = (2 * chip + k) * shard_count + z
                target = (2 * chip + (b & 1)) * shard_count + 2 * k + (b >> 1)
                pairs.append((source, target))
    return pairs


def swap_cores(value, dp_count):
    return lax.ppermute(value, "dp", [(i, i ^ 1) for i in range(dp_count)])


def shift_down(value, shard_count, step):
    return lax.ppermute(value, "shard", [(i, (i - step) % shard_count) for i in range(shard_count)])


def spread_in_plane(block, dp_count):
    got = {0: block}
    for o in range(2, dp_count, 2):
        got[o] = lax.ppermute(block, "dp", [(i, i ^ o) for i in range(dp_count)])
    for o in range(0, dp_count, 2):
        got[o + 1] = swap_cores(got[o], dp_count)
    return [got[o] for o in range(dp_count)]


def gather_pieces(piece, dp_count, shard_count):
    parts = [shift_down(piece, shard_count, step) for step in range(1, shard_count)]
    return spread_in_plane(jnp.stack(parts), dp_count)


def cut_kernel(meta, x_ref, seg_ref, *outs):
    z = meta[0]
    for r in range(4):
        b = z ^ r
        for l in range(2):
            outs[r][64 * l : 64 * l + 64] = x_ref[b >> 1, l, b & 1]
        if seg_ref is not None:
            outs[r][128:144] = seg_ref[b]


def cut_chunks(meta, values, seg_rows):
    width = values.shape[-1]
    blocks = values.reshape(2, 2, 2, 64, width)
    rows = 144 if seg_rows is not None else 128
    if seg_rows is not None:
        kernel, operands = cut_kernel, (blocks, seg_rows)
    else:
        kernel = lambda meta, x_ref, *outs: cut_kernel(meta, x_ref, None, *outs)
        operands = (blocks,)
    return pl.pallas_call(
        kernel,
        grid_spec=pltpu.PrefetchScalarGridSpec(
            num_scalar_prefetch=1,
            grid=(1,),
            in_specs=[whole(operand.shape) for operand in operands],
            out_specs=[whole((rows, width))] * 4,
        ),
        out_shape=[jax.ShapeDtypeStruct((rows, width), values.dtype)] * 4,
        compiler_params=pltpu.CompilerParams(vmem_limit_bytes=VMEM_LIMIT),
        name="cut_chunks",
    )(meta, *operands)


def join_kernel(meta, c0, c1, c2, c3, out_ref):
    z = meta[0]
    for r, chunk in enumerate((c0, c1, c2, c3)):
        b = z ^ r
        for l in range(2):
            out_ref[b >> 1, l, b & 1] = chunk[64 * l : 64 * l + 64].astype(out_ref.dtype)


def join_chunks(meta, chunks, dtype):
    width = chunks[0].shape[-1]
    out = pl.pallas_call(
        join_kernel,
        grid_spec=pltpu.PrefetchScalarGridSpec(
            num_scalar_prefetch=1,
            grid=(1,),
            in_specs=[whole((128, width))] * 4,
            out_specs=whole((2, 2, 2, 64, width)),
        ),
        out_shape=jax.ShapeDtypeStruct((2, 2, 2, 64, width), dtype),
        compiler_params=pltpu.CompilerParams(vmem_limit_bytes=VMEM_LIMIT),
        name="join_chunks",
    )(meta, *chunks)
    return out.reshape(2, 256, width)


def exchange(chunks, dp_count, shard_count, back=False):
    out = []
    for r, chunk in enumerate(chunks):
        pairs = exchange_pairs(dp_count, shard_count, r)
        if back:
            pairs = [(target, source) for source, target in pairs]
        out.append(lax.ppermute(chunk, ("dp", "shard"), pairs))
    return out


def weight_copies(meta, own_ref, pieces, dest, sems, places):
    z, d = meta[0], meta[1]
    own_rows, columns = own_ref.shape
    copies = [
        pltpu.make_async_copy(
            own_ref, dest.at[pl.ds(pl.multiple_of(z * own_rows, 16), own_rows)], sems.at[0]
        )
    ]
    count = 1
    for o, piece in enumerate(pieces):
        who = d ^ o
        for step in range(3):
            shard = lax.rem(z + step + 1, 4)
            for start, row, column, rows, cols in places(who):
                copies.append(
                    pltpu.make_async_copy(
                        piece.at[step, pl.ds(start, rows)],
                        dest.at[
                            pl.ds(pl.multiple_of(shard * own_rows + row, 16), rows),
                            pl.ds(pl.multiple_of(column, 128), cols),
                        ],
                        sems.at[count],
                    )
                )
                count += 1
    return copies


def qkv_places(who):
    return [(0, (who >> 1) * 48, (who & 1) * 1152, 48, 1152)]


def out_places(who):
    return [(0, (who >> 1) * 48, (who & 1) * 384, 48, 384)]


def up_places(who):
    return [(48, 0, who * 384, 192, 384)]


def down_places(who):
    return [(0, who * 96, 0, 96, 384), (96, who * 96, 384, 96, 384)]


def chunk_copies(meta, chunks, dest, sems, flip=0):
    base = meta[2] ^ flip
    copies = []
    for r, chunk in enumerate(chunks):
        rows = pl.ds(pl.multiple_of(128 * (base ^ r), 128), 128)
        copies.append(pltpu.make_async_copy(chunk.at[pl.ds(0, 128)], dest.at[rows], sems.at[r]))
    return copies


def zero_padded(rows, position, count):
    zeros = jnp.zeros_like(rows)
    return jnp.concatenate([rows if i == position else zeros for i in range(count)], axis=0)


def qkv_kernel(meta, ids, *refs):
    own, other, w_own, pieces = refs[0:4], refs[4:8], refs[8], refs[9:17]
    ins, outs = refs[17:20], refs[20:23]
    q_ref, k_ref, v_ref, mask_ref, hot_ref = refs[23:28]
    xs, segs, weight, wsems, xsems, ssems = refs[28:]
    copies = chunk_copies(meta, own, xs.at[pl.ds(0, 512)], xsems.at[0])
    copies += chunk_copies(meta, other, xs.at[pl.ds(512, 512)], xsems.at[1], flip=1)
    for half, group in enumerate((own, other)):
        for r, chunk in enumerate(group):
            place = 4 * half + (meta[2] ^ half ^ r)
            copies.append(
                pltpu.make_async_copy(
                    chunk.at[pl.ds(128, 16), pl.ds(0, 128)], segs.at[place], ssems.at[half, r]
                )
            )
    copies += weight_copies(meta, w_own, pieces, weight, wsems, qkv_places)
    for copy in copies:
        copy.start()
    for copy in copies:
        copy.wait()
    lane = lax.broadcasted_iota(jnp.int32, (128, 128), 1)
    lane_of_head = lax.rem(lane, 64)
    as_float = lane_of_head.astype(F32)
    is_segment = lane_of_head < 16
    ones = jnp.where((lane_of_head >= 32) & (lane_of_head < 35), 1.0, 0.0)
    for t in range(8):
        row = segs[t].astype(F32)[0:1]
        column = jnp.broadcast_to(row, (128, 128)).T
        same = column == as_float
        mask_ref[128 * t : 128 * t + 128] = jnp.where(
            is_segment, jnp.where(same, 0.0, -BIG), ones
        ).astype(BF)
        if t < 4:
            hot_ref[128 * t : 128 * t + 128] = jnp.where(is_segment & same, 1.0, 0.0).astype(BF)
    mask_ref[1024:1088] = jnp.where(is_segment, -BIG, ones)[0:64].astype(BF)
    in_all = jnp.concatenate([ref[0, 0] for ref in ins], axis=0)
    out_all = [zero_padded(ref[0, 0], p, 3) for p, ref in enumerate(outs)]
    targets = (q_ref, k_ref, v_ref)
    for tile in range(4):
        rows = slice(256 * tile, 256 * tile + 256)
        x = xs[rows]
        rank = mm_nt(x, in_all).astype(BF)
        for p in range(0 if tile < 2 else 1, 3):
            value = mm(x, weight[:, 768 * p : 768 * p + 768]) + mm(rank, out_all[p])
            value = value.astype(BF)
            if p == 0:
                value = (value.astype(F32) * HD**-0.5).astype(BF)
            targets[p][rows] = value


def adapter_spec(p):
    return pl.BlockSpec((1, 1, RANK, 768), lambda i, meta, ids, p=p, n=None: (p, 0, 0, 0))


def table_spec(p, column, width):
    return pl.BlockSpec((1, 1, RANK, width), lambda i, meta, ids: (p, ids[column], 0, 0))


def hidden_spec(column, width):
    return pl.BlockSpec((1, RANK, width), lambda i, meta, ids: (ids[column], 0, 0))


def any_specs(count):
    return [pl.BlockSpec(memory_space=ANY)] * count


def project_qkv(meta, ids, own, other, w_own, pieces, table_in, table_out):
    width = w_own.shape[1] // 3
    return pl.pallas_call(
        qkv_kernel,
        grid_spec=pltpu.PrefetchScalarGridSpec(
            num_scalar_prefetch=2,
            grid=(1,),
            in_specs=any_specs(17)
            + [table_spec(p, p, width) for p in range(3)]
            + [table_spec(p, p, width) for p in range(3)],
            out_specs=[
                whole((512, width)),
                whole((1024, width)),
                whole((1024, width)),
                whole((1088, 128)),
                whole((512, 128)),
            ],
            scratch_shapes=[
                VMEM((1024, width), BF),
                VMEM((8, 16, 128), BF),
                VMEM((width, 3 * width), BF),
                pltpu.SemaphoreType.DMA((25,)),
                pltpu.SemaphoreType.DMA((2, 4)),
                pltpu.SemaphoreType.DMA((2, 4)),
            ],
        ),
        out_shape=[
            jax.ShapeDtypeStruct((512, width), BF),
            jax.ShapeDtypeStruct((1024, width), BF),
            jax.ShapeDtypeStruct((1024, width), BF),
            jax.ShapeDtypeStruct((1088, 128), BF),
            jax.ShapeDtypeStruct((512, 128), BF),
        ],
        compiler_params=pltpu.CompilerParams(vmem_limit_bytes=VMEM_LIMIT),
        cost_estimate=pl.CostEstimate(flops=8_000_000_000, bytes_accessed=14_000_000, transcendentals=0),
        name="project_qkv",
    )(meta, ids, *own, *other, w_own, *pieces, *([table_in] * 3), *([table_out] * 3))


def split_three(column):
    high = column.astype(BF).astype(F32)
    middle = (column - high).astype(BF).astype(F32)
    return high, middle, column - high - middle


def pick_rows(picks, base, low, refs, mask_ref):
    def rows(ref, position):
        return ref[pl.ds(pl.multiple_of(position * 64, 64), 64), :]

    left, left_mask, right, right_mask = (picks[base + i] for i in range(4))
    own = picks[base + 10]
    picked = []
    for ref in refs + [mask_ref]:
        is_mask = ref is mask_ref
        blocks = [
            ref[0:64],
            ref[512:576],
            rows(ref, left_mask if is_mask else left),
            rows(ref, own),
            rows(ref, right_mask if is_mask else right),
        ]
        for n in range(RANDOMS):
            blocks.append(
                jnp.where(low, rows(ref, picks[base + 4 + n]), rows(ref, picks[base + 7 + n]))
            )
        picked.append(jnp.concatenate(blocks, axis=0))
    return picked


PICK_WIDTH = 11


def by_head(block, low):
    zeros = jnp.zeros_like(block)
    return jnp.concatenate([jnp.where(low, block, zeros), jnp.where(low, zeros, block)], axis=0)


def attend_kernel(picks, q_ref, k_ref, v_ref, mask_ref, hot_ref, o_ref, extra_ref):
    pair = pl.program_id(0)
    low = lax.broadcasted_iota(jnp.int32, (64, 128), 1) < 64
    lane = lax.broadcasted_iota(jnp.int32, (128, 128), 1)

    def one_block(rows, keys, values, masks):
        queries = by_head(q_ref[rows, :], low)
        hot = by_head(hot_ref[rows, :], low)
        scores = mm_nt(
            jnp.concatenate([queries, hot], axis=1), jnp.concatenate([keys, masks], axis=1)
        )
        top = jnp.max(scores, axis=1, keepdims=True)
        weights = jnp.exp(scores - top)
        total = jnp.sum(weights, axis=1, keepdims=True)
        mixed = mm(weights.astype(BF), values) / total
        o_ref[rows, :] = jnp.where(low, mixed[0:64], mixed[64:128]).astype(BF)
        high, middle, rest = split_three(-(top + jnp.log(total)))
        extra = jnp.where(
            lane == 32, high, jnp.where(lane == 33, middle, jnp.where(lane == 34, rest, hot.astype(F32)))
        )
        return extra.astype(BF)

    for l in range(1, 8):
        base = (pair * 8 + l) * PICK_WIDTH
        keys, values, masks = pick_rows(picks, base, low, [k_ref, v_ref], mask_ref)
        extra_ref[0, l] = one_block(slice(64 * l, 64 * l + 64), keys, values, masks)
    extra_ref[0, 0] = one_block(slice(0, 64), k_ref[...], v_ref[...], mask_ref[0:1024])


def attend(picks, q, k, v, masks, hot):
    width = q.shape[1]
    pairs = width // 128
    return pl.pallas_call(
        attend_kernel,
        grid_spec=pltpu.PrefetchScalarGridSpec(
            num_scalar_prefetch=1,
            grid=(pairs,),
            in_specs=[
                pl.BlockSpec((512, 128), lambda g, _: (0, g)),
                pl.BlockSpec((1024, 128), lambda g, _: (0, g)),
                pl.BlockSpec((1024, 128), lambda g, _: (0, g)),
                whole((1088, 128)),
                whole((512, 128)),
            ],
            out_specs=[
                pl.BlockSpec((512, 128), lambda g, _: (0, g)),
                pl.BlockSpec((1, 8, 128, 128), lambda g, _: (g, 0, 0, 0)),
            ],
        ),
        out_shape=[
            jax.ShapeDtypeStruct((512, width), BF),
            jax.ShapeDtypeStruct((pairs, 8, 128, 128), BF),
        ],
        compiler_params=pltpu.CompilerParams(vmem_limit_bytes=VMEM_LIMIT),
        cost_estimate=pl.CostEstimate(flops=12_000_000_000, bytes_accessed=10_000_000, transcendentals=4_000_000),
        name="attend",
    )(picks, q, k, v, masks, hot)


def attend_back_kernel(
    picks, q_ref, k_ref, v_ref, mask_ref, extra_ref, grad_ref, mixed_ref,
    dq_ref, dk_own, dv_own, dk_other, dv_other, key_sum, value_sum,
):
    pair = pl.program_id(0)
    low = lax.broadcasted_iota(jnp.int32, (64, 128), 1) < 64
    lane = lax.broadcasted_iota(jnp.int32, (128, 128), 1)
    key_sum[...] = jnp.zeros_like(key_sum)
    value_sum[...] = jnp.zeros_like(value_sum)

    def prepare(l):
        rows = slice(64 * l, 64 * l + 64)
        queries = by_head(q_ref[rows, :], low)
        grad = grad_ref[rows, :]
        grads = by_head(grad, low)
        products = grad.astype(F32) * mixed_ref[rows, :].astype(F32)
        zeros = jnp.zeros_like(products)
        centre = jnp.concatenate(
            [
                jnp.sum(jnp.where(low, products, zeros), axis=1, keepdims=True),
                jnp.sum(jnp.where(low, zeros, products), axis=1, keepdims=True),
            ],
            axis=0,
        )
        high, middle, rest = split_three(-centre)
        grad_extra = jnp.where(
            lane == 32, high, jnp.where(lane == 33, middle, jnp.where(lane == 34, rest, 0.0))
        ).astype(BF)
        query_wide = jnp.concatenate([queries, extra_ref[0, l]], axis=1)
        grad_wide = jnp.concatenate([grads, grad_extra], axis=1)
        zero = jnp.zeros_like(queries)
        both = jnp.concatenate(
            [jnp.concatenate([queries, zero], axis=1), jnp.concatenate([zero, grads], axis=1)],
            axis=0,
        )
        return query_wide, grad_wide, both

    def one_part(prepared, keys, values, masks):
        query_wide, grad_wide, both = prepared
        shares = jnp.exp(mm_nt(jnp.concatenate([keys, masks], axis=1), query_wide))
        grad_shares = mm_nt(jnp.concatenate([values, masks], axis=1), grad_wide)
        grad_scores = (shares * grad_shares).astype(BF)
        sums = mm(jnp.concatenate([grad_scores, shares.astype(BF)], axis=1), both)
        return mm_tn(grad_scores, keys), sums

    def store_query(l, grad_query):
        dq_ref[64 * l : 64 * l + 64] = (
            jnp.where(low, grad_query[0:64], grad_query[64:128]) * HD**-0.5
        ).astype(BF)

    prepared = prepare(0)
    total = None
    for half in range(2):
        rows = slice(512 * half, 512 * half + 512)
        grad_query, sums = one_part(prepared, k_ref[rows, :], v_ref[rows, :], mask_ref[rows, :])
        key_sum[rows] += sums[:, 0:128]
        value_sum[rows] += sums[:, 128:256]
        total = grad_query if total is None else total + grad_query
    store_query(0, total)
    for l in range(1, 8):
        base = (pair * 8 + l) * PICK_WIDTH
        keys, values, masks = pick_rows(picks, base, low, [k_ref, v_ref], mask_ref)
        grad_query, sums = one_part(prepare(l), keys, values, masks)
        store_query(l, grad_query)
        for at, sum_ref in ((0, key_sum), (128, value_sum)):
            for slot, position in enumerate((0, 8, picks[base], picks[base + 10], picks[base + 2])):
                rows = pl.ds(pl.multiple_of(position * 64, 64), 64)
                sum_ref[rows, :] += sums[64 * slot : 64 * slot + 64, at : at + 128]
            for n in range(RANDOMS):
                part = sums[64 * (5 + n) : 64 * (6 + n), at : at + 128]
                zeros = jnp.zeros_like(part)
                rows = pl.ds(pl.multiple_of(picks[base + 4 + n] * 64, 64), 64)
                sum_ref[rows, :] += jnp.where(low, part, zeros)
                rows = pl.ds(pl.multiple_of(picks[base + 7 + n] * 64, 64), 64)
                sum_ref[rows, :] += jnp.where(low, zeros, part)
    dk_own[...] = key_sum[0:512]
    dv_own[...] = value_sum[0:512]
    dk_other[...] = key_sum[512:1024].astype(BF)
    dv_other[...] = value_sum[512:1024].astype(BF)


def attend_back(picks, q, k, v, masks, extra, grad, mixed):
    width = q.shape[1]
    pairs = width // 128
    half = pl.BlockSpec((512, 128), lambda g, _: (0, g))
    full = pl.BlockSpec((1024, 128), lambda g, _: (0, g))
    return pl.pallas_call(
        attend_back_kernel,
        grid_spec=pltpu.PrefetchScalarGridSpec(
            num_scalar_prefetch=1,
            grid=(pairs,),
            in_specs=[
                half,
                full,
                full,
                whole((1088, 128)),
                pl.BlockSpec((1, 8, 128, 128), lambda g, _: (g, 0, 0, 0)),
                half,
                half,
            ],
            out_specs=[half] * 5,
            scratch_shapes=[VMEM((1024, 128), F32), VMEM((1024, 128), F32)],
        ),
        out_shape=[
            jax.ShapeDtypeStruct((512, width), BF),
            jax.ShapeDtypeStruct((512, width), F32),
            jax.ShapeDtypeStruct((512, width), F32),
            jax.ShapeDtypeStruct((512, width), BF),
            jax.ShapeDtypeStruct((512, width), BF),
        ],
        compiler_params=pltpu.CompilerParams(vmem_limit_bytes=VMEM_LIMIT),
        cost_estimate=pl.CostEstimate(flops=20_000_000_000, bytes_accessed=12_000_000, transcendentals=4_000_000),
        name="attend_back",
    )(picks, q, k, v, masks, extra, grad, mixed)


def gelu_and_slope(lifted):
    z = jnp.abs(lifted) * 0.7071067811865476
    t = 1.0 / (1.0 + 0.3275911 * z)
    poly = t * (
        0.254829592
        + t * (-0.284496736 + t * (1.421413741 + t * (-1.453152027 + t * 1.061405429)))
    )
    decay = jnp.exp(-z * z)
    tail = 0.5 * poly * decay
    below = jnp.where(lifted < 0.0, tail, 1.0 - tail)
    return lifted * below, below + lifted * (decay * 0.3989422804014327)


def norm_parts(hidden):
    average = jnp.mean(hidden, axis=-1, keepdims=True)
    centred = hidden - average
    spread = jnp.mean(centred * centred, axis=-1, keepdims=True)
    inverse = lax.rsqrt(spread + EPSILON)
    return centred * inverse, inverse


def norm_back(grad, gain, normal, inverse):
    scaled = grad * gain
    return inverse * (
        scaled
        - jnp.mean(scaled, axis=-1, keepdims=True)
        - normal * jnp.mean(scaled * normal, axis=-1, keepdims=True)
    )


MID_TILE = 256
MID_PARTS = 4


def middle_kernel(meta, ids, *refs):
    xc, cots = refs[0:4], refs[4:8]
    out_own, up_own, down_own = refs[8:11]
    up_pieces, down_pieces = refs[11:19], refs[19:27]
    mixed_ref, gain1, gain2, in3, in4, in5, out3, out4, out5 = refs[27:36]
    lo0, lo1, lo2, lo3, grad_branch_ref, grad_mixed_ref, g0, g1, g2, g3 = refs[36:46]
    (
        xs, cot, w_out, w_up, w_down, active, slope, first_low, rank4, rank5, low4, low5, layer,
        s_in3, s_in4, s_in5, s_out3, s_out4, s_out5, gathered,
        osems, usems, dsems, xsems,
    ) = refs[46:]
    near = chunk_copies(meta, xc, xs, xsems.at[0]) + chunk_copies(meta, cots, cot, xsems.at[1])
    out_copies = weight_copies(meta, out_own, up_pieces, w_out, osems, out_places)
    up_copies = weight_copies(meta, up_own, up_pieces, w_up, usems, up_places)
    down_copies = weight_copies(meta, down_own, down_pieces, w_down, dsems, down_places)
    for copy in near + out_copies + up_copies + down_copies:
        copy.start()
    for copy in near + out_copies:
        copy.wait()
    for copy in up_copies + down_copies:
        copy.wait()
    for ref in (s_in3, s_in4, s_in5, s_out3, s_out4, s_out5):
        ref[...] = jnp.zeros_like(ref)
    hidden = w_up.shape[1]
    part = hidden // MID_PARTS
    a_in3, a_in4, a_out3, a_out5 = in3[0, 0], in4[0, 0], out3[0, 0], out5[0, 0]

    def tile_step(tile, carry):
        rows = pl.ds(pl.multiple_of(tile * MID_TILE, MID_TILE), MID_TILE)
        mixed = mixed_ref[rows, :]
        rank3 = mm_nt(mixed, a_in3).astype(BF)
        branch = mm(mixed, w_out[...]) + mm(rank3, a_out3)
        normal1, inverse1 = norm_parts(xs[rows, :].astype(F32) + branch)
        first = normal1 * gain1[...]
        low1 = first.astype(BF)
        r4 = mm_nt(low1, a_in4).astype(BF)
        lowered = first
        r5 = jnp.zeros((MID_TILE, RANK), F32)
        for n in range(MID_PARTS):
            cols = slice(n * part, n * part + part)
            lifted = mm(low1, w_up[:, cols]) + mm(r4, out4[0, :, cols])
            value, tangent = gelu_and_slope(lifted)
            value = value.astype(BF)
            active[:, cols] = value
            slope[:, cols] = tangent
            lowered = lowered + mm(value, w_down[cols, :])
            r5 = r5 + mm_nt(value, in5[0, :, cols])
        r5 = r5.astype(BF)
        lowered = lowered + mm(r5, a_out5)
        normal2, inverse2 = norm_parts(lowered)
        layer[rows, :] = (normal2 * gain2[...]).astype(BF)
        grad_sum = norm_back(cot[rows, :].astype(F32), gain2[...], normal2, inverse2)
        e5 = grad_sum.astype(BF)
        rg5 = mm_nt(e5, a_out5).astype(BF)
        s_out5[...] += mm_tn(r5, e5)
        grad_first = grad_sum
        rg4 = jnp.zeros((MID_TILE, RANK), F32)
        for n in range(MID_PARTS):
            cols = slice(n * part, n * part + part)
            grad_active = mm_nt(e5, w_down[cols, :]) + mm(rg5, in5[0, :, cols])
            e4 = (slope[:, cols] * grad_active).astype(BF)
            s_in5[:, cols] += mm_tn(rg5, active[:, cols])
            s_out4[:, cols] += mm_tn(r4, e4)
            grad_first = grad_first + mm_nt(e4, w_up[:, cols])
            rg4 = rg4 + mm_nt(e4, out4[0, :, cols])
        rg4 = rg4.astype(BF)
        s_in4[...] += mm_tn(rg4, low1)
        grad_first = grad_first + mm(rg4, a_in4)
        grad_branch = norm_back(grad_first, gain1[...], normal1, inverse1)
        grad_branch_ref[rows, :] = grad_branch
        e3 = grad_branch.astype(BF)
        rg3 = mm_nt(e3, a_out3).astype(BF)
        s_out3[...] += mm_tn(rank3, e3)
        s_in3[...] += mm_tn(rg3, mixed)
        grad_mixed_ref[rows, :] = (mm_nt(e3, w_out[...]) + mm(rg3, a_in3)).astype(BF)
        return carry

    lax.fori_loop(0, 512 // MID_TILE, tile_step, 0)
    base = meta[2]
    for r, ref in enumerate((lo0, lo1, lo2, lo3)):
        ref[...] = layer[pl.ds(pl.multiple_of(128 * (base ^ r), 128), 128), :]
    wide, narrow = 768, 192
    for owner in range(4):
        start = 0
        for ref, size in (
            (s_in5, wide), (s_out4, wide), (s_in3, narrow), (s_in4, narrow), (s_out3, narrow), (s_out5, narrow),
        ):
            gathered[owner, :, start : start + size] = ref[:, owner * size : owner * size + size]
            start += size
    for r, ref in enumerate((g0, g1, g2, g3)):
        ref[...] = gathered[lax.rem(meta[0] + 4 - r, 4)].astype(BF)


def middle(meta, ids, xc, cots, out_own, up_own, down_own, up_pieces, down_pieces, mixed, gain1, gain2,
           table_in, table_in_hidden, table_out, table_out_hidden):
    width, hidden = mixed.shape[1], up_own.shape[1]
    return pl.pallas_call(
        middle_kernel,
        grid_spec=pltpu.PrefetchScalarGridSpec(
            num_scalar_prefetch=2,
            grid=(1,),
            in_specs=any_specs(27)
            + [
                whole((512, width)),
                whole((1, width)),
                whole((1, width)),
                table_spec(3, 3, width),
                table_spec(4, 4, width),
                hidden_spec(5, hidden),
                table_spec(3, 3, width),
                hidden_spec(4, hidden),
                table_spec(4, 5, width),
            ],
            out_specs=[whole((128, width))] * 4
            + [whole((512, width)), whole((512, width))]
            + [whole((RANK, 2304))] * 4,
            scratch_shapes=[
                VMEM((512, width), BF),
                VMEM((512, width), BF),
                VMEM((width, width), BF),
                VMEM((width, hidden), BF),
                VMEM((hidden, width), BF),
                VMEM((MID_TILE, hidden), BF),
                VMEM((MID_TILE, hidden), F32),
                VMEM((8, 128), BF),
                VMEM((8, 128), BF),
                VMEM((8, 128), BF),
                VMEM((8, 128), BF),
                VMEM((8, 128), BF),
                VMEM((512, width), BF),
                VMEM((RANK, width), F32),
                VMEM((RANK, width), F32),
                VMEM((RANK, hidden), F32),
                VMEM((RANK, width), F32),
                VMEM((RANK, hidden), F32),
                VMEM((RANK, width), F32),
                VMEM((4, RANK, 2304), F32),
                pltpu.SemaphoreType.DMA((25,)),
                pltpu.SemaphoreType.DMA((25,)),
                pltpu.SemaphoreType.DMA((49,)),
                pltpu.SemaphoreType.DMA((2, 4)),
            ],
        ),
        out_shape=[jax.ShapeDtypeStruct((128, width), BF)] * 4
        + [jax.ShapeDtypeStruct((512, width), F32), jax.ShapeDtypeStruct((512, width), BF)]
        + [jax.ShapeDtypeStruct((RANK, 2304), BF)] * 4,
        compiler_params=pltpu.CompilerParams(vmem_limit_bytes=VMEM_LIMIT),
        cost_estimate=pl.CostEstimate(flops=20_000_000_000, bytes_accessed=22_000_000, transcendentals=4_000_000),
        name="middle",
    )(meta, ids, *xc, *cots, out_own, up_own, down_own, *up_pieces, *down_pieces, mixed, gain1, gain2,
      table_in, table_in, table_in_hidden, table_out, table_out_hidden, table_out)


def qkv_back_kernel(meta, ids, *refs):
    xc, w_own, pieces = refs[0:4], refs[4], refs[5:13]
    dq_ref, dk_own, dv_own, dk_got, dv_got, branch_ref = refs[13:19]
    ins, outs = refs[19:22], refs[22:25]
    ig = refs[25:29]
    gs = refs[29:33]
    xs, weight, result, s_in, s_out, gathered, wsems, xsems = refs[33:]
    copies = chunk_copies(meta, xc, xs, xsems)
    copies += weight_copies(meta, w_own, pieces, weight, wsems, qkv_places)
    for copy in copies:
        copy.start()
    for copy in copies:
        copy.wait()
    in_all = jnp.concatenate([ref[0, 0] for ref in ins], axis=0)
    out_all = jnp.concatenate([zero_padded(ref[0, 0], p, 3) for p, ref in enumerate(outs)], axis=1)
    for tile in range(2):
        rows = slice(256 * tile, 256 * tile + 256)
        dk = (dk_own[rows] + dk_got[rows].astype(F32)).astype(BF)
        dv = (dv_own[rows] + dv_got[rows].astype(F32)).astype(BF)
        grads = jnp.concatenate([dq_ref[rows], dk, dv], axis=1)
        x = xs[rows]
        rank = mm_nt(x, in_all).astype(BF)
        rank_grad = mm_nt(grads, out_all).astype(BF)
        result[rows] = (branch_ref[rows] + mm_nt(grads, weight[...]) + mm(rank_grad, in_all)).astype(BF)
        part_in, part_out = mm_tn(rank_grad, x), mm_tn(rank, grads)
        if tile == 0:
            s_in[...] = part_in
            s_out[...] = part_out
        else:
            s_in[...] += part_in
            s_out[...] += part_out
    base = meta[2]
    for r, ref in enumerate(ig):
        ref[...] = result[pl.ds(pl.multiple_of(128 * (base ^ r), 128), 128), :]
    for owner in range(4):
        for p in range(3):
            rows = slice(RANK * p, RANK * p + RANK)
            gathered[owner, :, 192 * p : 192 * p + 192] = s_in[rows, 192 * owner : 192 * owner + 192]
            gathered[owner, :, 192 * (3 + p) : 192 * (4 + p)] = s_out[
                rows, 768 * p + 192 * owner : 768 * p + 192 * owner + 192
            ]
    for r, ref in enumerate(gs):
        ref[...] = gathered[lax.rem(meta[0] + 4 - r, 4)].astype(BF)


def qkv_back(meta, ids, xc, w_own, pieces, dq, dk_own, dv_own, dk_got, dv_got, branch, table_in, table_out):
    width = dq.shape[1]
    return pl.pallas_call(
        qkv_back_kernel,
        grid_spec=pltpu.PrefetchScalarGridSpec(
            num_scalar_prefetch=2,
            grid=(1,),
            in_specs=any_specs(13)
            + [whole((512, width))] * 6
            + [table_spec(p, p, width) for p in range(3)]
            + [table_spec(p, p, width) for p in range(3)],
            out_specs=[whole((128, width))] * 4 + [whole((RANK, 1152))] * 4,
            scratch_shapes=[
                VMEM((512, width), BF),
                VMEM((width, 3 * width), BF),
                VMEM((512, width), BF),
                VMEM((3 * RANK, width), F32),
                VMEM((3 * RANK, 3 * width), F32),
                VMEM((4, RANK, 1152), F32),
                pltpu.SemaphoreType.DMA((25,)),
                pltpu.SemaphoreType.DMA((4,)),
            ],
        ),
        out_shape=[jax.ShapeDtypeStruct((128, width), BF)] * 4
        + [jax.ShapeDtypeStruct((RANK, 1152), BF)] * 4,
        compiler_params=pltpu.CompilerParams(vmem_limit_bytes=VMEM_LIMIT),
        cost_estimate=pl.CostEstimate(flops=5_000_000_000, bytes_accessed=10_000_000, transcendentals=0),
        name="qkv_back",
    )(meta, ids, *xc, w_own, *pieces, dq, dk_own, dv_own, dk_got, dv_got, branch,
      *([table_in] * 3), *([table_out] * 3))


def combine_kernel(meta, ids, *refs):
    mids, firsts = refs[0:8], refs[8:16]
    in_d, in_f, out_d, out_f = refs[16:20]
    for ref in (in_d, in_f, out_d, out_f):
        ref[...] = jnp.zeros_like(ref)
    z = meta[0]
    narrow, wide = 192, 768
    for chip in range(4):
        for step in range(4):
            source = lax.rem(z + step, 4)
            at = (chip * 4 + source) * 6
            chosen = [ids[at + p] for p in range(6)]
            part = mids[2 * chip][step].astype(F32) + mids[2 * chip + 1][step].astype(F32)
            in_f[chosen[5]] += part[:, 0:wide]
            out_f[chosen[4]] += part[:, wide : 2 * wide]
            start = 2 * wide
            in_d[3, chosen[3]] += part[:, start : start + narrow]
            in_d[4, chosen[4]] += part[:, start + narrow : start + 2 * narrow]
            out_d[3, chosen[3]] += part[:, start + 2 * narrow : start + 3 * narrow]
            out_d[4, chosen[5]] += part[:, start + 3 * narrow : start + 4 * narrow]
            part = firsts[2 * chip][step].astype(F32) + firsts[2 * chip + 1][step].astype(F32)
            for p in range(3):
                in_d[p, chosen[p]] += part[:, narrow * p : narrow * p + narrow]
                out_d[p, chosen[p]] += part[:, narrow * (3 + p) : narrow * (4 + p)]


def combine(meta, ids, mids, firsts, tables, narrow, wide):
    shapes = [(5, tables, RANK, narrow), (tables, RANK, wide)] * 2
    return pl.pallas_call(
        combine_kernel,
        grid_spec=pltpu.PrefetchScalarGridSpec(
            num_scalar_prefetch=2,
            grid=(1,),
            in_specs=[whole(mids[0].shape)] * 8 + [whole(firsts[0].shape)] * 8,
            out_specs=[whole(shape) for shape in shapes],
        ),
        out_shape=[jax.ShapeDtypeStruct(shape, F32) for shape in shapes],
        compiler_params=pltpu.CompilerParams(vmem_limit_bytes=VMEM_LIMIT),
        name="combine",
    )(meta, ids, *mids, *firsts)


def paired_body(
    inputs,
    segments,
    random_key_blocks,
    adapter_index_table,
    frozen_query_key_value_weight,
    frozen_output_weight,
    frozen_up_weight,
    frozen_down_weight,
    attention_norm_gain,
    feedforward_norm_gain,
    adapter_down_from_width,
    adapter_down_from_hidden,
    adapter_up_to_width,
    adapter_up_to_hidden,
    cotangent,
):
    dp_count, shard_count = lax.axis_size("dp"), lax.axis_size("shard")
    d, z = lax.axis_index("dp"), lax.axis_index("shard")
    core = d & 1
    meta = jnp.stack([z, d, 2 * (z & 1) + core]).astype(jnp.int32)

    def piece(weight, rows, columns, row, column):
        return lax.dynamic_slice(weight, (row, column), (rows, columns))

    qkv_piece = piece(frozen_query_key_value_weight, 48, 1152, (d >> 1) * 48, core * 1152)
    qkv_pieces = gather_pieces(qkv_piece, dp_count, shard_count)

    seg_rows = segments.reshape(2, 2, 2, 64).transpose(0, 2, 1, 3).reshape(4, 1, 128).astype(BF)
    seg_rows = jnp.pad(seg_rows, ((0, 0), (0, 15), (0, inputs.shape[-1] - 128)))
    own = exchange(cut_chunks(meta, inputs, seg_rows), dp_count, shard_count)
    other = [swap_cores(chunk, dp_count) for chunk in own]

    up_piece = jnp.concatenate(
        [
            piece(frozen_output_weight, 48, 384, (d >> 1) * 48, core * 384),
            piece(frozen_up_weight, 192, 384, 0, d * 384),
        ],
        axis=0,
    )
    down_piece = piece(frozen_down_weight, 96, 768, d * 96, 0)
    down_piece = jnp.concatenate([down_piece[:, 0:384], down_piece[:, 384:768]], axis=0)
    up_pieces = gather_pieces(up_piece, dp_count, shard_count)
    down_pieces = gather_pieces(down_piece, dp_count, shard_count)
    cots = exchange(cut_chunks(meta, cotangent, None), dp_count, shard_count)

    there = swap_cores(adapter_index_table, dp_count)
    column_ids = jnp.where(
        core == 0,
        jnp.concatenate([adapter_index_table, there], axis=0),
        jnp.concatenate([there, adapter_index_table], axis=0),
    )
    ids = lax.dynamic_index_in_dim(column_ids, z, 0, keepdims=False)
    plane_ids = [column_ids] + [
        lax.ppermute(column_ids, "dp", [(i, i ^ o) for i in range(dp_count)])
        for o in range(2, dp_count, 2)
    ]
    plane_ids = jnp.concatenate(plane_ids, axis=0).reshape(-1)

    local = jnp.arange(8, dtype=jnp.int32)
    block = 2 * local + core

    def place(index):
        return ((index & 1) ^ core) * 8 + (index >> 1)

    left_ok, right_ok = block - 1 >= GLOBALS, block + 1 < 16
    left = jnp.where(left_ok, place(block - 1), 0)
    right = jnp.where(right_ok, place(block + 1), 0)
    window = jnp.stack(
        [left, jnp.where(left_ok, left, 16), right, jnp.where(right_ok, right, 16)], axis=-1
    )
    drawn = lax.dynamic_index_in_dim(
        random_key_blocks.reshape(H, 8, 2, RANDOMS), core, 2, keepdims=False
    )
    drawn = place(drawn).reshape(H // 2, 2, 8, RANDOMS).transpose(0, 2, 1, 3).reshape(H // 2, 8, 2 * RANDOMS)
    picks = jnp.concatenate(
        [
            jnp.broadcast_to(window[None], (H // 2, 8, 4)),
            drawn,
            jnp.broadcast_to(local[None, :, None], (H // 2, 8, 1)),
        ],
        axis=-1,
    ).reshape(-1)

    q, k, v, masks, hot = project_qkv(
        meta, ids, own, other, frozen_query_key_value_weight, qkv_pieces,
        adapter_down_from_width, adapter_up_to_width,
    )
    mixed, extra = attend(picks, q, k, v, masks, hot)
    results = middle(
        meta, ids, own, cots, frozen_output_weight, frozen_up_weight, frozen_down_weight,
        up_pieces, down_pieces, mixed, attention_norm_gain[None], feedforward_norm_gain[None],
        adapter_down_from_width, adapter_down_from_hidden, adapter_up_to_width, adapter_up_to_hidden,
    )
    layer_chunks, grad_branch, grad_mixed, mid_grads = results[0:4], results[4], results[5], results[6:10]
    layer_out = join_chunks(meta, exchange(layer_chunks, dp_count, shard_count, back=True), BF)

    def spread(parts):
        got = [parts[0]] + [shift_down(parts[r], shard_count, r) for r in range(1, shard_count)]
        return spread_in_plane(jnp.stack(got), dp_count)

    mids = spread(mid_grads)
    dq, dk_own, dv_own, dk_other, dv_other = attend_back(
        picks, q, k, v, masks, extra, grad_mixed, mixed
    )
    dk_got, dv_got = swap_cores(dk_other, dp_count), swap_cores(dv_other, dp_count)
    results = qkv_back(
        meta, ids, own, frozen_query_key_value_weight, qkv_pieces, dq, dk_own, dv_own, dk_got, dv_got,
        grad_branch, adapter_down_from_width, adapter_up_to_width,
    )
    input_grad = join_chunks(meta, exchange(results[0:4], dp_count, shard_count, back=True), F32)
    firsts = spread(results[4:8])
    in_d, in_f, out_d, out_f = combine(
        meta, plane_ids, mids, firsts, adapter_down_from_width.shape[1], 192, 768
    )
    return (layer_out, input_grad, in_d, in_f, out_d, out_f)


def solution(mesh):
    dp_count, shard_count = mesh.shape["dp"], mesh.shape["shard"]
    paired = dp_count == 8 and shard_count == 4
    return jax.shard_map(
        paired_body if paired else general_body,
        mesh=mesh,
        in_specs=(
            P("dp", "shard", None),
            P("dp", "shard"),
            P(),
            P("dp", None),
            P("shard", None),
            P("shard", None),
            P("shard", None),
            P("shard", None),
            P(),
            P(),
            P(),
            P(),
            P(),
            P(),
            P("dp", "shard", None),
        ),
        out_specs=(
            P("dp", "shard", None),
            P("dp", "shard", None),
            P(None, None, None, "shard"),
            P(None, None, "shard"),
            P(None, None, None, "shard"),
            P(None, None, "shard"),
        ),
        check_vma=False,
    )
```

```python
import functools

import jax
import jax.numpy as jnp
from jax import lax
from jax.experimental import pallas as pl
from jax.experimental.pallas import tpu as pltpu
from jax.sharding import PartitionSpec as P

H = 12
HD = 64
BLOCK = 64
GLOBALS = 2
RANDOMS = 3


EPSILON = 1e-06
NEGATIVE = -1e30


def norm_rows(hidden, gain_vector):
    average = jnp.mean(hidden, axis=-1, keepdims=True)
    centred = hidden - average
    spread = jnp.mean(centred * centred, axis=-1, keepdims=True)
    return centred * lax.rsqrt(spread + EPSILON) * gain_vector


def gelu_exact(values):
    return jax.nn.gelu(values, approximate=False)


def dense_forward(inputs, weight):
    return jnp.einsum("sti,io->sto", inputs, weight, preferred_element_type=jnp.float32)


def dense_backward(grad_low, weight):
    return jnp.einsum("sto,io->sti", grad_low, weight, preferred_element_type=jnp.float32)


def adapt(inputs, down_rows, up_rows):
    rank_part = jnp.einsum(
        "sti,sri->str", inputs, down_rows, preferred_element_type=jnp.float32
    ).astype(jnp.bfloat16)
    return (
        rank_part,
        jnp.einsum("str,sro->sto", rank_part, up_rows, preferred_element_type=jnp.float32),
    )


def adapt_back(inputs, down_rows, up_rows, rank_part, grad_low):
    grad_up = jnp.einsum("str,sto->sro", rank_part, grad_low, preferred_element_type=jnp.float32)
    rank_grad = jnp.einsum(
        "sto,sro->str", grad_low, up_rows, preferred_element_type=jnp.float32
    ).astype(jnp.bfloat16)
    grad_down = jnp.einsum("str,sti->sri", rank_grad, inputs, preferred_element_type=jnp.float32)
    grad_inputs = jnp.einsum(
        "str,sri->sti", rank_grad, down_rows, preferred_element_type=jnp.float32
    )
    return (grad_down, grad_up, grad_inputs)


def table_sum(per_sequence, chosen, table_size):
    matches = (chosen[:, None] == jnp.arange(table_size, dtype=jnp.int32)[None, :]).astype(
        jnp.float32
    )
    return jnp.sum(matches[:, :, None, None] * per_sequence[:, None], axis=0)


def sparse_scores(query_heads, key_picked, permit, scaling):
    scores = (
        jnp.einsum(
            "shbqd,shbkd->shbqk", query_heads, key_picked, preferred_element_type=jnp.float32
        )
        * scaling
    )
    return jnp.where(permit, scores, NEGATIVE)


def global_scores(query_rows, key_rows, seg_query, seg_keys, scaling):
    scores = (
        jnp.einsum("hqd,hkd->hqk", query_rows, key_rows, preferred_element_type=jnp.float32)
        * scaling
    )
    return jnp.where((seg_query[:, None] == seg_keys[None, :])[None], scores, NEGATIVE)


def global_forward(query_rows, key_rows, value_rows, seg_query, seg_keys, scaling):
    scores = global_scores(query_rows, key_rows, seg_query, seg_keys, scaling)
    top_score = jnp.max(scores, axis=-1, keepdims=True)
    weights = jnp.exp(scores - top_score)
    totals = jnp.sum(weights, axis=-1, keepdims=True)
    shares = (weights / totals).astype(jnp.bfloat16)
    attended = jnp.einsum("hqk,hkd->hqd", shares, value_rows, preferred_element_type=jnp.float32)
    return (attended, (top_score + jnp.log(totals))[..., 0])


def global_backward(
    query_rows, key_rows, value_rows, seg_query, seg_keys, grad_rows, log_total, scaling
):
    scores = global_scores(query_rows, key_rows, seg_query, seg_keys, scaling)
    shares = jnp.exp(scores - log_total[..., None])
    share_low = shares.astype(jnp.bfloat16)
    grad_shares = jnp.einsum(
        "hqd,hkd->hqk", grad_rows, value_rows, preferred_element_type=jnp.float32
    )
    centre = jnp.sum(shares * grad_shares, axis=-1, keepdims=True)
    grad_scores = (shares * (grad_shares - centre)).astype(jnp.bfloat16)
    grad_query = (
        jnp.einsum("hqk,hkd->hqd", grad_scores, key_rows, preferred_element_type=jnp.float32)
        * scaling
    )
    grad_keys = (
        jnp.einsum("hqk,hqd->hkd", grad_scores, query_rows, preferred_element_type=jnp.float32)
        * scaling
    )
    grad_values = jnp.einsum(
        "hqk,hqd->hkd", share_low, grad_rows, preferred_element_type=jnp.float32
    )
    return (grad_query, grad_keys, grad_values, centre[..., 0])


def general_body(
    inputs,
    segments,
    random_key_blocks,
    adapter_index_table,
    frozen_query_key_value_weight,
    frozen_output_weight,
    frozen_up_weight,
    frozen_down_weight,
    attention_norm_gain,
    feedforward_norm_gain,
    adapter_down_from_width,
    adapter_down_from_hidden,
    adapter_up_to_width,
    adapter_up_to_hidden,
    cotangent,
):
    seq_count = inputs.shape[0]
    local_tokens = inputs.shape[1]
    width = inputs.shape[2]
    shard_count = lax.axis_size("shard")
    full_length = local_tokens * shard_count
    total_blocks = full_length // BLOCK
    local_blocks = local_tokens // BLOCK
    cand_count = 3 + GLOBALS + RANDOMS
    glob_rows = GLOBALS * BLOCK
    scaling = HD ** (-0.5)

    def select_adapter_table(table, table_column):
        return jnp.take(table, adapter_index_table[:, table_column], axis=0)

    adapter_tables_input = [
        select_adapter_table(adapter_down_from_width[table_column], table_column)
        for table_column in range(5)
    ] + [select_adapter_table(adapter_down_from_hidden, 5)]
    adapter_tables_output = [
        select_adapter_table(adapter_up_to_width[table_column], table_column)
        for table_column in range(4)
    ]
    adapter_tables_output = adapter_tables_output + [
        select_adapter_table(adapter_up_to_hidden, 4),
        select_adapter_table(adapter_up_to_width[4], 5),
    ]
    qkv_full, out_full = (
        lax.all_gather(frozen_query_key_value_weight, "shard", axis=0, tiled=True),
        lax.all_gather(frozen_output_weight, "shard", axis=0, tiled=True),
    )
    main_part = dense_forward(inputs, qkv_full)
    rank_parts = []
    projected = []
    for table_column in range(3):
        rank_part, extra = adapt(
            inputs, adapter_tables_input[table_column], adapter_tables_output[table_column]
        )
        rank_parts.append(rank_part)
        projected.append(
            (main_part[..., table_column * width : (table_column + 1) * width] + extra).astype(
                jnp.bfloat16
            )
        )
    seg_low = segments.astype(jnp.bfloat16)
    key_all, value_all, seg_all = (
        lax.all_gather(projected[1], "shard", axis=1, tiled=True),
        lax.all_gather(projected[2], "shard", axis=1, tiled=True),
        lax.all_gather(seg_low, "shard", axis=1, tiled=True),
    )
    shard_pos = lax.axis_index("shard")
    is_first = shard_pos == 0
    first_block = shard_pos * local_blocks
    block_ids = first_block + jnp.arange(local_blocks, dtype=jnp.int32)
    rand_local = lax.dynamic_slice_in_dim(random_key_blocks, first_block, local_blocks, axis=1)
    window_part = jnp.stack([block_ids - 1, block_ids, block_ids + 1], axis=-1)
    global_ids = jnp.broadcast_to(
        jnp.arange(GLOBALS, dtype=jnp.int32)[None, :], (local_blocks, GLOBALS)
    )
    fixed_part = jnp.concatenate([window_part, global_ids], axis=-1)
    candidates = jnp.concatenate(
        [jnp.broadcast_to(fixed_part[None], (H, local_blocks, 3 + GLOBALS)), rand_local], axis=-1
    )
    candidates = jnp.clip(candidates, 0, total_blocks - 1)
    always_true = jnp.ones((local_blocks,), dtype=bool)
    fixed_valid = jnp.stack(
        [block_ids - 1 >= GLOBALS, always_true, block_ids + 1 < total_blocks]
        + [always_true] * GLOBALS,
        axis=-1,
    )
    valid = jnp.concatenate(
        [
            jnp.broadcast_to(fixed_valid[None], (H, local_blocks, 3 + GLOBALS)),
            jnp.ones((H, local_blocks, RANDOMS), dtype=bool),
        ],
        axis=-1,
    )
    valid_keys = jnp.repeat(valid, BLOCK, axis=-1)
    query_heads = (
        projected[0].reshape(seq_count, local_blocks, BLOCK, H, HD).transpose(0, 3, 1, 2, 4)
    )
    key_source = key_all.reshape(seq_count, total_blocks, BLOCK, H, HD).transpose(0, 3, 1, 2, 4)
    value_source = value_all.reshape(seq_count, total_blocks, BLOCK, H, HD).transpose(0, 3, 1, 2, 4)
    head_index = jnp.arange(H, dtype=jnp.int32)[:, None, None]
    key_picked = key_source[:, head_index, candidates].reshape(
        seq_count, H, local_blocks, cand_count * BLOCK, HD
    )
    value_picked = value_source[:, head_index, candidates].reshape(
        seq_count, H, local_blocks, cand_count * BLOCK, HD
    )
    seg_picked = seg_all.reshape(seq_count, total_blocks, BLOCK)[:, candidates].reshape(
        seq_count, H, local_blocks, cand_count * BLOCK
    )
    seg_local = seg_low.reshape(seq_count, local_blocks, BLOCK)
    permit = valid_keys[None, :, :, None, :] & (
        seg_local[:, None, :, :, None] == seg_picked[:, :, :, None, :]
    )
    scores = sparse_scores(query_heads, key_picked, permit, scaling)
    top_score = jnp.max(scores, axis=-1, keepdims=True)
    weights = jnp.exp(scores - top_score)
    totals = jnp.sum(weights, axis=-1, keepdims=True)
    share_low = (weights / totals).astype(jnp.bfloat16)
    sparse_lse = (top_score + jnp.log(totals))[..., 0]
    sparse_out = jnp.einsum(
        "shbqk,shbkd->shbqd", share_low, value_picked, preferred_element_type=jnp.float32
    )
    key_heads = key_source.reshape(seq_count, H, full_length, HD)
    value_heads = value_source.reshape(seq_count, H, full_length, HD)
    glob_query = query_heads[:, :, :GLOBALS].reshape(seq_count, H, glob_rows, HD)
    glob_seg = seg_low[:, :glob_rows]

    def run_forward(operands):
        return lax.map(
            lambda packet: global_forward(
                packet[0], packet[1], packet[2], packet[3], packet[4], scaling
            ),
            operands,
        )

    def skip_forward(operands):
        return (
            jnp.zeros((seq_count, H, glob_rows, HD), jnp.float32),
            jnp.zeros((seq_count, H, glob_rows), jnp.float32),
        )

    global_out, global_lse = lax.cond(
        is_first, run_forward, skip_forward, (glob_query, key_heads, value_heads, glob_seg, seg_all)
    )
    glob_blocks = global_out.reshape(seq_count, H, GLOBALS, BLOCK, HD)
    head_out = jnp.concatenate(
        [jnp.where(is_first, glob_blocks, sparse_out[:, :, :GLOBALS]), sparse_out[:, :, GLOBALS:]],
        axis=2,
    )
    mixed_low = (
        head_out.transpose(0, 2, 3, 1, 4)
        .reshape(seq_count, local_tokens, width)
        .astype(jnp.bfloat16)
    )
    rank_out, extra_out = adapt(mixed_low, adapter_tables_input[3], adapter_tables_output[3])
    branch = dense_forward(mixed_low, out_full) + extra_out
    first, first_pull = jax.vjp(
        lambda hidden: norm_rows(hidden, attention_norm_gain), inputs.astype(jnp.float32) + branch
    )
    first_low = first.astype(jnp.bfloat16)
    up_full, down_full = (
        lax.all_gather(frozen_up_weight, "shard", axis=0, tiled=True),
        lax.all_gather(frozen_down_weight, "shard", axis=0, tiled=True),
    )
    rank_up, extra_up = adapt(first_low, adapter_tables_input[4], adapter_tables_output[4])
    lifted = dense_forward(first_low, up_full) + extra_up
    activated, gelu_pull = jax.vjp(gelu_exact, lifted)
    active_low = activated.astype(jnp.bfloat16)
    rank_down, extra_down = adapt(active_low, adapter_tables_input[5], adapter_tables_output[5])
    lowered = dense_forward(active_low, down_full) + extra_down
    result, final_pull = jax.vjp(
        lambda hidden: norm_rows(hidden, feedforward_norm_gain), first + lowered
    )
    layer_out = result.astype(jnp.bfloat16)
    up_back, down_back = (
        lax.all_gather(frozen_up_weight, "shard", axis=0, tiled=True),
        lax.all_gather(frozen_down_weight, "shard", axis=0, tiled=True),
    )
    grad_adapt_in = [None] * 6
    grad_adapt_out = [None] * 6
    (grad_sum,) = final_pull(cotangent.astype(jnp.float32))
    grad_lowered = grad_sum.astype(jnp.bfloat16)
    grad_adapt_in[5], grad_adapt_out[5], extra_grad = adapt_back(
        active_low, adapter_tables_input[5], adapter_tables_output[5], rank_down, grad_lowered
    )
    grad_active = dense_backward(grad_lowered, down_back) + extra_grad
    (grad_lifted,) = gelu_pull(grad_active)
    grad_lift_low = grad_lifted.astype(jnp.bfloat16)
    grad_adapt_in[4], grad_adapt_out[4], extra_grad = adapt_back(
        first_low, adapter_tables_input[4], adapter_tables_output[4], rank_up, grad_lift_low
    )
    grad_first = grad_sum + dense_backward(grad_lift_low, up_back) + extra_grad
    (grad_branch,) = first_pull(grad_first)
    grad_branch_low = grad_branch.astype(jnp.bfloat16)
    qkv_back, out_back = (
        lax.all_gather(frozen_query_key_value_weight, "shard", axis=0, tiled=True),
        lax.all_gather(frozen_output_weight, "shard", axis=0, tiled=True),
    )
    grad_adapt_in[3], grad_adapt_out[3], extra_grad = adapt_back(
        mixed_low, adapter_tables_input[3], adapter_tables_output[3], rank_out, grad_branch_low
    )
    grad_mixed = (dense_backward(grad_branch_low, out_back) + extra_grad).astype(jnp.bfloat16)
    grad_heads = grad_mixed.reshape(seq_count, local_blocks, BLOCK, H, HD).transpose(0, 3, 1, 2, 4)
    row_keep = (block_ids >= GLOBALS)[None, None, :, None, None]
    grad_sparse = jnp.where(row_keep, grad_heads, jnp.zeros_like(grad_heads))
    scores = sparse_scores(query_heads, key_picked, permit, scaling)
    shares = jnp.exp(scores - sparse_lse[..., None])
    share_low = shares.astype(jnp.bfloat16)
    grad_shares = jnp.einsum(
        "shbqd,shbkd->shbqk", grad_sparse, value_picked, preferred_element_type=jnp.float32
    )
    centre = jnp.sum(shares * grad_shares, axis=-1, keepdims=True)
    grad_scores = (shares * (grad_shares - centre)).astype(jnp.bfloat16)
    grad_query = (
        jnp.einsum(
            "shbqk,shbkd->shbqd", grad_scores, key_picked, preferred_element_type=jnp.float32
        )
        * scaling
    )
    glob_grad = grad_heads[:, :, :GLOBALS].reshape(seq_count, H, glob_rows, HD)

    def run_backward(operands):
        return lax.map(
            lambda packet: global_backward(
                packet[0], packet[1], packet[2], packet[3], packet[4], packet[5], packet[6], scaling
            ),
            operands,
        )

    def skip_backward(operands):
        return (
            jnp.zeros((seq_count, H, glob_rows, HD), jnp.float32),
            jnp.zeros((seq_count, H, full_length, HD), jnp.float32),
            jnp.zeros((seq_count, H, full_length, HD), jnp.float32),
            jnp.zeros((seq_count, H, glob_rows), jnp.float32),
        )

    glob_dq, glob_dk, glob_dv, glob_centre = lax.cond(
        is_first,
        run_backward,
        skip_backward,
        (glob_query, key_heads, value_heads, glob_seg, seg_all, glob_grad, global_lse),
    )
    grad_query = grad_query.at[:, :, :GLOBALS].add(
        glob_dq.reshape(seq_count, H, GLOBALS, BLOCK, HD)
    )
    grad_key_picked = (
        jnp.einsum(
            "shbqk,shbqd->shbkd", grad_scores, query_heads, preferred_element_type=jnp.float32
        )
        * scaling
    )
    grad_value_picked = jnp.einsum(
        "shbqk,shbqd->shbkd", share_low, grad_sparse, preferred_element_type=jnp.float32
    )
    block_shape = (seq_count, H, local_blocks, cand_count, BLOCK, HD)
    key_grad_blocks = (
        jnp.zeros((seq_count, H, total_blocks, BLOCK, HD), jnp.float32)
        .at[:, head_index, candidates]
        .add(grad_key_picked.reshape(block_shape))
    )
    value_grad_blocks = (
        jnp.zeros((seq_count, H, total_blocks, BLOCK, HD), jnp.float32)
        .at[:, head_index, candidates]
        .add(grad_value_picked.reshape(block_shape))
    )
    key_grad_full = (
        (key_grad_blocks.reshape(seq_count, H, full_length, HD) + glob_dk)
        .transpose(0, 2, 1, 3)
        .reshape(seq_count, full_length, width)
    )
    value_grad_full = (
        (value_grad_blocks.reshape(seq_count, H, full_length, HD) + glob_dv)
        .transpose(0, 2, 1, 3)
        .reshape(seq_count, full_length, width)
    )
    key_grad, value_grad = (
        lax.psum_scatter(
            key_grad_full.astype(jnp.bfloat16), "shard", scatter_dimension=1, tiled=True
        ).astype(jnp.float32),
        lax.psum_scatter(
            value_grad_full.astype(jnp.bfloat16), "shard", scatter_dimension=1, tiled=True
        ).astype(jnp.float32),
    )
    query_grad = grad_query.transpose(0, 2, 3, 1, 4).reshape(seq_count, local_tokens, width)
    grad_proj = [
        query_grad.astype(jnp.bfloat16),
        key_grad.astype(jnp.bfloat16),
        value_grad.astype(jnp.bfloat16),
    ]
    input_grad = grad_branch + dense_backward(jnp.concatenate(grad_proj, axis=-1), qkv_back)
    for table_column in range(3):
        grad_adapt_in[table_column], grad_adapt_out[table_column], extra_grad = adapt_back(
            inputs,
            adapter_tables_input[table_column],
            adapter_tables_output[table_column],
            rank_parts[table_column],
            grad_proj[table_column],
        )
        input_grad = input_grad + extra_grad
    adapter_table_count = adapter_down_from_width.shape[1]
    grad_in_d = jnp.stack(
        [
            table_sum(
                grad_adapt_in[table_column],
                adapter_index_table[:, table_column],
                adapter_table_count,
            )
            for table_column in range(5)
        ],
        axis=0,
    )
    grad_in_f = table_sum(grad_adapt_in[5], adapter_index_table[:, 5], adapter_table_count)
    out_list = [
        table_sum(
            grad_adapt_out[table_column], adapter_index_table[:, table_column], adapter_table_count
        )
        for table_column in range(4)
    ]
    grad_out_d = jnp.stack(
        out_list + [table_sum(grad_adapt_out[5], adapter_index_table[:, 5], adapter_table_count)],
        axis=0,
    )
    grad_out_f = table_sum(grad_adapt_out[4], adapter_index_table[:, 4], adapter_table_count)
    owned = (
        lax.psum_scatter(
            grad_in_d.astype(jnp.bfloat16), "shard", scatter_dimension=3, tiled=True
        ).astype(jnp.float32),
        lax.psum_scatter(
            grad_in_f.astype(jnp.bfloat16), "shard", scatter_dimension=2, tiled=True
        ).astype(jnp.float32),
        lax.psum_scatter(
            grad_out_d.astype(jnp.bfloat16), "shard", scatter_dimension=3, tiled=True
        ).astype(jnp.float32),
        lax.psum_scatter(
            grad_out_f.astype(jnp.bfloat16), "shard", scatter_dimension=2, tiled=True
        ).astype(jnp.float32),
    )
    summed = (
        lax.psum(owned[0].astype(jnp.bfloat16), "dp").astype(jnp.float32),
        lax.psum(owned[1].astype(jnp.bfloat16), "dp").astype(jnp.float32),
        lax.psum(owned[2].astype(jnp.bfloat16), "dp").astype(jnp.float32),
        lax.psum(owned[3].astype(jnp.bfloat16), "dp").astype(jnp.float32),
    )
    return (layer_out, input_grad, summed[0], summed[1], summed[2], summed[3])


BF = jnp.bfloat16
F32 = jnp.float32
NT = (((1,), (1,)), ((), ()))
TN = (((0,), (0,)), ((), ()))
BIG = 1e30
RANK = 16
ANY = pl.ANY
VMEM = pltpu.VMEM
VMEM_LIMIT = 56 * 1024 * 1024
SMALL_COST = pl.CostEstimate(flops=1_000_000, bytes_accessed=100_000, transcendentals=0)


def mm(left, right):
    return jnp.dot(left, right, preferred_element_type=F32)


def mm_nt(left, right):
    return lax.dot_general(left, right, NT, preferred_element_type=F32)


def mm_tn(left, right):
    return lax.dot_general(left, right, TN, preferred_element_type=F32)


def whole(shape):
    return pl.BlockSpec(shape, lambda *_: (0,) * len(shape))


def away_pairs(dp_count, shard_count, step):
    pairs = []
    for chip in range(dp_count // 2):
        for k in range(2):
            for z in range(shard_count):
                m = (z & 1) ^ step
                source = (2 * chip + k) * shard_count + z
                target = (2 * chip + (z >> 1)) * shard_count + 2 * k + m
                pairs.append((source, target))
    return pairs


def swap_cores(value, dp_count):
    return lax.ppermute(value, "dp", [(i, i ^ 1) for i in range(dp_count)])


def swap_shards(value, shard_count, step):
    return lax.ppermute(value, "shard", [(i, i ^ step) for i in range(shard_count)])


def spread_over_chips(block, dp_count):
    others = [lax.ppermute(block, "dp", [(i, i ^ o) for i in range(dp_count)]) for o in range(2, dp_count, 2)]
    return [block] + others


def spread_over_cores(blocks, dp_count):
    return [one for block in blocks for one in (block, swap_cores(block, dp_count))]


def spread_in_plane(block, dp_count):
    return spread_over_cores(spread_over_chips(block, dp_count), dp_count)


def join_kernel(meta, part0, part1, out_ref):
    for r, part in enumerate((part0, part1)):
        out_ref[(meta[0] & 1) ^ r] = part[...].astype(out_ref.dtype)


def join_parts(meta, parts, dtype):
    rows, width = parts[0].shape
    return pl.pallas_call(
        join_kernel,
        grid_spec=pltpu.PrefetchScalarGridSpec(
            num_scalar_prefetch=1,
            grid=(1,),
            in_specs=[whole((rows, width))] * 2,
            out_specs=whole((2, rows, width)),
        ),
        out_shape=jax.ShapeDtypeStruct((2, rows, width), dtype),
        compiler_params=pltpu.CompilerParams(vmem_limit_bytes=VMEM_LIMIT),
        cost_estimate=SMALL_COST,
        name="join_parts",
    )(meta, *parts)


def send_away(parts, dp_count, shard_count):
    return [
        lax.ppermute(part, ("dp", "shard"), away_pairs(dp_count, shard_count, r))
        for r, part in enumerate(parts)
    ]


def weight_copies(meta, own_ref, pieces, dest, sems, places):
    z, d = meta[0], meta[1]
    own_rows, columns = own_ref.shape
    copies = [
        pltpu.make_async_copy(
            own_ref, dest.at[pl.ds(pl.multiple_of(z * own_rows, 16), own_rows)], sems.at[0]
        )
    ]
    count = 1
    for o, piece in enumerate(pieces):
        who = d ^ o
        for step in range(3):
            shard = z ^ (step + 1)
            for start, row, column, rows, cols in places(who):
                copies.append(
                    pltpu.make_async_copy(
                        piece.at[step, pl.ds(start, rows)],
                        dest.at[
                            pl.ds(pl.multiple_of(shard * own_rows + row, 16), rows),
                            pl.ds(pl.multiple_of(column, 128), cols),
                        ],
                        sems.at[count],
                    )
                )
                count += 1
    return copies


def qkv_places(who):
    return [(0, (who >> 1) * 48, (who & 1) * 1152, 48, 1152)]


def out_places(who):
    return [(0, (who >> 1) * 48, (who & 1) * 384, 48, 384)]


def up_places(who):
    return [(48, 0, who * 384, 192, 384)]


def down_places(who):
    return [(0, who * 96, 0, 96, 384), (96, who * 96, 384, 96, 384)]


def token_copies(meta, messages, dest, sems):
    copies = []
    for at, message in enumerate(messages):
        row = 512 * (at >> 1) + 256 * ((meta[0] & 1) ^ (at & 1))
        copies.append(
            pltpu.make_async_copy(
                message.at[pl.ds(0, 256)], dest.at[pl.ds(pl.multiple_of(row, 256), 256)], sems.at[at]
            )
        )
    return copies


def zero_padded(rows, position, count):
    zeros = jnp.zeros_like(rows)
    return jnp.concatenate([rows if i == position else zeros for i in range(count)], axis=0)


def qkv_kernel(meta, ids, *refs):
    messages, w_own, pieces = refs[0:4], refs[4], refs[5:13]
    ins, outs = refs[13:16], refs[16:19]
    q_ref, k_ref, v_ref, mask_ref, hot_ref, own_ref = refs[19:25]
    xs, segs, weight, wsems, xsems, ssems = refs[25:]
    copies = token_copies(meta, messages, xs, xsems)
    for at, message in enumerate(messages):
        copies.append(
            pltpu.make_async_copy(
                message.at[pl.ds(256, 16), pl.ds(0, 256)],
                segs.at[2 * (at >> 1) + ((meta[0] & 1) ^ (at & 1))],
                ssems.at[at],
            )
        )
    copies += weight_copies(meta, w_own, pieces, weight, wsems, qkv_places)
    for copy in copies:
        copy.start()
    for copy in copies:
        copy.wait()
    lane = lax.broadcasted_iota(jnp.int32, (128, 128), 1)
    lane_of_head = lax.rem(lane, 64)
    as_float = lane_of_head.astype(F32)
    is_segment = lane_of_head < 16
    ones = jnp.where((lane_of_head >= 32) & (lane_of_head < 35), 1.0, 0.0)
    for place in range(4):
        row = segs[place].astype(F32)[0:1]
        for half in range(2):
            column = jnp.broadcast_to(row[:, 128 * half : 128 * half + 128], (128, 128)).T
            same = column == as_float
            mask = jnp.where(is_segment, jnp.where(same, 0.0, -BIG), ones).astype(BF)
            hot = jnp.where(is_segment & same, 1.0, 0.0).astype(BF)
            rows = slice(256 * place + 128 * half, 256 * place + 128 * half + 128)
            mask_ref[rows] = mask
            if place < 2:
                hot_ref[rows] = hot
    mask_ref[1024:1088] = jnp.where(is_segment, -BIG, ones)[0:64].astype(BF)
    own_ref[...] = xs[0:512]
    in_all = jnp.concatenate([ref[0, 0] for ref in ins], axis=0)
    out_all = [zero_padded(ref[0, 0], p, 3) for p, ref in enumerate(outs)]
    targets = (q_ref, k_ref, v_ref)
    for tile in range(4):
        rows = slice(256 * tile, 256 * tile + 256)
        x = xs[rows]
        rank = mm_nt(x, in_all).astype(BF)
        for p in range(0 if tile < 2 else 1, 3):
            value = mm(x, weight[:, 768 * p : 768 * p + 768]) + mm(rank, out_all[p])
            value = value.astype(BF)
            if p == 0:
                value = (value.astype(F32) * HD**-0.5).astype(BF)
            targets[p][rows] = value


def table_spec(p, column, width):
    return pl.BlockSpec((1, 1, RANK, width), lambda i, meta, ids: (p, ids[column], 0, 0))


def hidden_spec(column, width):
    return pl.BlockSpec((1, RANK, width), lambda i, meta, ids: (ids[column], 0, 0))


def any_specs(count):
    return [pl.BlockSpec(memory_space=ANY)] * count


def project_qkv(meta, ids, messages, w_own, pieces, table_in, table_out):
    width = w_own.shape[1] // 3
    return pl.pallas_call(
        qkv_kernel,
        grid_spec=pltpu.PrefetchScalarGridSpec(
            num_scalar_prefetch=2,
            grid=(1,),
            in_specs=any_specs(13)
            + [table_spec(p, p, width) for p in range(3)]
            + [table_spec(p, p, width) for p in range(3)],
            out_specs=[
                whole((512, width)),
                whole((1024, width)),
                whole((1024, width)),
                whole((1088, 128)),
                whole((512, 128)),
                whole((512, width)),
            ],
            scratch_shapes=[
                VMEM((1024, width), BF),
                VMEM((4, 16, 256), BF),
                VMEM((width, 3 * width), BF),
                pltpu.SemaphoreType.DMA((25,)),
                pltpu.SemaphoreType.DMA((4,)),
                pltpu.SemaphoreType.DMA((4,)),
            ],
        ),
        out_shape=[
            jax.ShapeDtypeStruct((512, width), BF),
            jax.ShapeDtypeStruct((1024, width), BF),
            jax.ShapeDtypeStruct((1024, width), BF),
            jax.ShapeDtypeStruct((1088, 128), BF),
            jax.ShapeDtypeStruct((512, 128), BF),
            jax.ShapeDtypeStruct((512, width), BF),
        ],
        compiler_params=pltpu.CompilerParams(vmem_limit_bytes=VMEM_LIMIT),
        cost_estimate=SMALL_COST,
        name="project_qkv",
    )(meta, ids, *messages, w_own, *pieces, *([table_in] * 3), *([table_out] * 3))


def split_three(column):
    high = column.astype(BF).astype(F32)
    middle = (column - high).astype(BF).astype(F32)
    return high, middle, column - high - middle


def pick_rows(picks, base, low, refs, mask_ref):
    def rows(ref, position, count=64):
        return ref[pl.ds(pl.multiple_of(position * 64, 64), count), :]

    left, left_mask, right, right_mask = (picks[base + i] for i in range(4))
    own, first = picks[base + 10], picks[base + 11]
    picked = []
    for ref in refs + [mask_ref]:
        is_mask = ref is mask_ref
        blocks = [
            rows(ref, first, 128),
            rows(ref, left_mask if is_mask else left),
            rows(ref, own),
            rows(ref, right_mask if is_mask else right),
        ]
        for n in range(RANDOMS):
            blocks.append(
                jnp.where(low, rows(ref, picks[base + 4 + n]), rows(ref, picks[base + 7 + n]))
            )
        picked.append(jnp.concatenate(blocks, axis=0))
    return picked


PICK_WIDTH = 12


def by_head(block, low):
    zeros = jnp.zeros_like(block)
    return jnp.concatenate([jnp.where(low, block, zeros), jnp.where(low, zeros, block)], axis=0)


def attend_kernel(first, picks, q_ref, k_ref, v_ref, mask_ref, hot_ref, o_ref, extra_ref):
    pair = pl.program_id(0) + first
    low = lax.broadcasted_iota(jnp.int32, (64, 128), 1) < 64
    lane = lax.broadcasted_iota(jnp.int32, (128, 128), 1)

    def one_block(rows, keys, values, masks):
        queries = by_head(q_ref[rows, :], low)
        hot = by_head(hot_ref[rows, :], low)
        scores = mm_nt(
            jnp.concatenate([queries, hot], axis=1), jnp.concatenate([keys, masks], axis=1)
        )
        top = jnp.max(scores, axis=1, keepdims=True)
        weights = jnp.exp(scores - top)
        total = jnp.sum(weights, axis=1, keepdims=True)
        mixed = mm(weights.astype(BF), values) / total
        o_ref[rows, :] = jnp.where(low, mixed[0:64], mixed[64:128]).astype(BF)
        high, middle, rest = split_three(-(top + jnp.log(total)))
        extra = jnp.where(
            lane == 32, high, jnp.where(lane == 33, middle, jnp.where(lane == 34, rest, hot.astype(F32)))
        )
        return extra.astype(BF)

    def sparse_block(l):
        base = (pair * 8 + l) * PICK_WIDTH
        keys, values, masks = pick_rows(picks, base, low, [k_ref, v_ref], mask_ref)
        extra_ref[0, l] = one_block(slice(64 * l, 64 * l + 64), keys, values, masks)

    holds_globals = picks[PICK_WIDTH * 48] == 0

    @pl.when(holds_globals)
    def _():
        for l in range(GLOBALS):
            extra_ref[0, l] = one_block(slice(64 * l, 64 * l + 64), k_ref[...], v_ref[...], mask_ref[0:1024])

    @pl.when(jnp.logical_not(holds_globals))
    def _():
        for l in range(GLOBALS):
            sparse_block(l)

    for l in range(GLOBALS, 8):
        sparse_block(l)


def attend(first, count, picks, q, k, v, masks, hot):
    from_first = lambda g, _: (0, g + first)
    return pl.pallas_call(
        functools.partial(attend_kernel, first),
        grid_spec=pltpu.PrefetchScalarGridSpec(
            num_scalar_prefetch=1,
            grid=(count,),
            in_specs=[
                pl.BlockSpec((512, 128), from_first),
                pl.BlockSpec((1024, 128), from_first),
                pl.BlockSpec((1024, 128), from_first),
                whole((1088, 128)),
                whole((512, 128)),
            ],
            out_specs=[
                pl.BlockSpec((512, 128), lambda g, _: (0, g)),
                pl.BlockSpec((1, 8, 128, 128), lambda g, _: (g, 0, 0, 0)),
            ],
        ),
        out_shape=[
            jax.ShapeDtypeStruct((512, 128 * count), BF),
            jax.ShapeDtypeStruct((count, 8, 128, 128), BF),
        ],
        compiler_params=pltpu.CompilerParams(vmem_limit_bytes=VMEM_LIMIT),
        cost_estimate=SMALL_COST,
        name="attend",
    )(picks, q, k, v, masks, hot)


def attend_back_kernel(
    first, picks, q_ref, k_ref, v_ref, mask_ref, extra_ref, grad_ref, mixed_ref,
    dq_ref, dk_own, dv_own, other_ref, key_sum, value_sum,
):
    pair = pl.program_id(0) + first
    low = lax.broadcasted_iota(jnp.int32, (64, 128), 1) < 64
    lane = lax.broadcasted_iota(jnp.int32, (128, 128), 1)
    key_sum[...] = jnp.zeros_like(key_sum)
    value_sum[...] = jnp.zeros_like(value_sum)

    def prepare(l):
        rows = slice(64 * l, 64 * l + 64)
        queries = by_head(q_ref[rows, :], low)
        grad = grad_ref[rows, :]
        grads = by_head(grad, low)
        products = grad.astype(F32) * mixed_ref[rows, :].astype(F32)
        zeros = jnp.zeros_like(products)
        centre = jnp.concatenate(
            [
                jnp.sum(jnp.where(low, products, zeros), axis=1, keepdims=True),
                jnp.sum(jnp.where(low, zeros, products), axis=1, keepdims=True),
            ],
            axis=0,
        )
        high, middle, rest = split_three(-centre)
        grad_extra = jnp.where(
            lane == 32, high, jnp.where(lane == 33, middle, jnp.where(lane == 34, rest, 0.0))
        ).astype(BF)
        query_wide = jnp.concatenate([queries, extra_ref[0, l]], axis=1)
        grad_wide = jnp.concatenate([grads, grad_extra], axis=1)
        zero = jnp.zeros_like(queries)
        both = jnp.concatenate(
            [jnp.concatenate([queries, zero], axis=1), jnp.concatenate([zero, grads], axis=1)],
            axis=0,
        )
        return query_wide, grad_wide, both

    def one_part(prepared, keys, values, masks):
        query_wide, grad_wide, both = prepared
        shares = jnp.exp(mm_nt(jnp.concatenate([keys, masks], axis=1), query_wide))
        grad_shares = mm_nt(jnp.concatenate([values, masks], axis=1), grad_wide)
        grad_scores = (shares * grad_shares).astype(BF)
        sums = mm(jnp.concatenate([grad_scores, shares.astype(BF)], axis=1), both)
        return mm_tn(grad_scores, keys), sums

    def store_query(l, grad_query):
        dq_ref[64 * l : 64 * l + 64] = (
            jnp.where(low, grad_query[0:64], grad_query[64:128]) * HD**-0.5
        ).astype(BF)

    def dense_block(l):
        prepared = prepare(l)
        total = None
        for half in range(2):
            rows = slice(512 * half, 512 * half + 512)
            grad_query, sums = one_part(prepared, k_ref[rows, :], v_ref[rows, :], mask_ref[rows, :])
            key_sum[rows] += sums[:, 0:128]
            value_sum[rows] += sums[:, 128:256]
            total = grad_query if total is None else total + grad_query
        store_query(l, total)

    def sparse_block(l):
        base = (pair * 8 + l) * PICK_WIDTH
        keys, values, masks = pick_rows(picks, base, low, [k_ref, v_ref], mask_ref)
        grad_query, sums = one_part(prepare(l), keys, values, masks)
        store_query(l, grad_query)

        def rows(position, count=64):
            return pl.ds(pl.multiple_of(position * 64, 64), count)

        for at, sum_ref in ((0, key_sum), (128, value_sum)):
            sum_ref[rows(picks[base + 11], 128), :] += sums[0:128, at : at + 128]
            for slot, position in enumerate((picks[base], picks[base + 10], picks[base + 2])):
                sum_ref[rows(position), :] += sums[64 * slot + 128 : 64 * slot + 192, at : at + 128]
            for n in range(RANDOMS):
                part = sums[64 * (5 + n) : 64 * (6 + n), at : at + 128]
                zeros = jnp.zeros_like(part)
                sum_ref[rows(picks[base + 4 + n]), :] += jnp.where(low, part, zeros)
                sum_ref[rows(picks[base + 7 + n]), :] += jnp.where(low, zeros, part)

    holds_globals = picks[PICK_WIDTH * 48] == 0

    @pl.when(holds_globals)
    def _():
        for l in range(GLOBALS):
            dense_block(l)

    @pl.when(jnp.logical_not(holds_globals))
    def _():
        for l in range(GLOBALS):
            sparse_block(l)

    for l in range(GLOBALS, 8):
        sparse_block(l)
    dk_own[...] = key_sum[0:512]
    dv_own[...] = value_sum[0:512]
    other_ref[0] = key_sum[512:1024].astype(BF)
    other_ref[1] = value_sum[512:1024].astype(BF)


def attend_back(first, count, picks, q, k, v, masks, extra, grad, mixed):
    from_first = lambda g, _: (0, g + first)
    half = pl.BlockSpec((512, 128), lambda g, _: (0, g))
    return pl.pallas_call(
        functools.partial(attend_back_kernel, first),
        grid_spec=pltpu.PrefetchScalarGridSpec(
            num_scalar_prefetch=1,
            grid=(count,),
            in_specs=[
                pl.BlockSpec((512, 128), from_first),
                pl.BlockSpec((1024, 128), from_first),
                pl.BlockSpec((1024, 128), from_first),
                whole((1088, 128)),
                pl.BlockSpec((1, 8, 128, 128), lambda g, _: (g, 0, 0, 0)),
                pl.BlockSpec((512, 128), from_first),
                half,
            ],
            out_specs=[half] * 3 + [pl.BlockSpec((2, 512, 128), lambda g, _: (0, 0, g))],
            scratch_shapes=[VMEM((1024, 128), F32), VMEM((1024, 128), F32)],
        ),
        out_shape=[
            jax.ShapeDtypeStruct((512, 128 * count), BF),
            jax.ShapeDtypeStruct((512, 128 * count), F32),
            jax.ShapeDtypeStruct((512, 128 * count), F32),
            jax.ShapeDtypeStruct((2, 512, 128 * count), BF),
        ],
        compiler_params=pltpu.CompilerParams(vmem_limit_bytes=VMEM_LIMIT),
        cost_estimate=SMALL_COST,
        name="attend_back",
    )(picks, q, k, v, masks, extra, grad, mixed)


def gelu_and_slope(lifted):
    z = jnp.abs(lifted) * 0.7071067811865476
    t = 1.0 / (1.0 + 0.3275911 * z)
    poly = t * (
        0.254829592
        + t * (-0.284496736 + t * (1.421413741 + t * (-1.453152027 + t * 1.061405429)))
    )
    decay = jnp.exp(-z * z)
    tail = 0.5 * poly * decay
    below = jnp.where(lifted < 0.0, tail, 1.0 - tail)
    return lifted * below, below + lifted * (decay * 0.3989422804014327)


def norm_parts(hidden):
    average = jnp.mean(hidden, axis=-1, keepdims=True)
    centred = hidden - average
    spread = jnp.mean(centred * centred, axis=-1, keepdims=True)
    inverse = lax.rsqrt(spread + EPSILON)
    return centred * inverse, inverse


def norm_back(grad, gain, normal, inverse):
    scaled = grad * gain
    return inverse * (
        scaled
        - jnp.mean(scaled, axis=-1, keepdims=True)
        - normal * jnp.mean(scaled * normal, axis=-1, keepdims=True)
    )


MID_TILE = 256
MID_PARTS = 4


def first_half_kernel(meta, ids, *refs):
    out_own, up_own, up_pieces = refs[0], refs[1], refs[2:10]
    x_ref, mixed_ref, gain1, in3, in4, out3, out4 = refs[10:17]
    normal_ref, inverse_ref, active, slope = refs[17:21]
    w_out, w_up, osems, usems = refs[21:]
    out_copies = weight_copies(meta, out_own, up_pieces, w_out, osems, out_places)
    up_copies = weight_copies(meta, up_own, up_pieces, w_up, usems, up_places)
    is_first = pl.program_id(0) == 0

    @pl.when(is_first)
    def _():
        for copy in out_copies + up_copies:
            copy.start()
        for copy in out_copies:
            copy.wait()

    mixed = mixed_ref[...]
    rank3 = mm_nt(mixed, in3[0, 0]).astype(BF)
    branch = mm(mixed, w_out[...]) + mm(rank3, out3[0, 0])
    normal, inverse = norm_parts(x_ref[...].astype(F32) + branch)
    normal_ref[...] = normal
    inverse_ref[...] = jnp.broadcast_to(inverse, inverse_ref.shape)
    low = (normal * gain1[...]).astype(BF)
    rank4 = mm_nt(low, in4[0, 0]).astype(BF)

    @pl.when(is_first)
    def _():
        for copy in up_copies:
            copy.wait()

    part = w_up.shape[1] // MID_PARTS
    for n in range(MID_PARTS):
        cols = slice(n * part, n * part + part)
        lifted = mm(low, w_up[:, cols]) + mm(rank4, out4[0, :, cols])
        value, tangent = gelu_and_slope(lifted)
        active[:, cols] = value.astype(BF)
        slope[:, cols] = tangent.astype(BF)


def first_half(meta, ids, out_own, up_own, up_pieces, x, mixed, gain1, table_in, table_out, table_out_hidden):
    width, hidden = x.shape[1], up_own.shape[1]
    tile = lambda columns: pl.BlockSpec((MID_TILE, columns), lambda i, *_: (i, 0))
    return pl.pallas_call(
        first_half_kernel,
        grid_spec=pltpu.PrefetchScalarGridSpec(
            num_scalar_prefetch=2,
            grid=(512 // MID_TILE,),
            in_specs=any_specs(10)
            + [
                tile(width),
                tile(width),
                whole((1, width)),
                table_spec(3, 3, width),
                table_spec(4, 4, width),
                table_spec(3, 3, width),
                hidden_spec(4, hidden),
            ],
            out_specs=[tile(width), tile(128), tile(hidden), tile(hidden)],
            scratch_shapes=[
                VMEM((width, width), BF),
                VMEM((width, hidden), BF),
                pltpu.SemaphoreType.DMA((25,)),
                pltpu.SemaphoreType.DMA((25,)),
            ],
        ),
        out_shape=[
            jax.ShapeDtypeStruct((512, width), F32),
            jax.ShapeDtypeStruct((512, 128), F32),
            jax.ShapeDtypeStruct((512, hidden), BF),
            jax.ShapeDtypeStruct((512, hidden), BF),
        ],
        compiler_params=pltpu.CompilerParams(vmem_limit_bytes=VMEM_LIMIT),
        cost_estimate=SMALL_COST,
        name="first_half",
    )(meta, ids, out_own, up_own, *up_pieces, x, mixed, gain1, table_in, table_in, table_out, table_out_hidden)


def second_half_kernel(meta, ids, *refs):
    cots, out_own, up_own, down_own = refs[0:2], refs[2], refs[3], refs[4]
    up_pieces, down_pieces = refs[5:13], refs[13:21]
    normal_ref, inverse_ref, active, slope, mixed_ref = refs[21:26]
    gain1, gain2, in3, in4, in5, out3, out4, out5 = refs[26:34]
    layer_parts, grad_branch_ref, grad_mixed_ref, grad_parts = refs[34:36], refs[36], refs[37], refs[38:42]
    (
        cot, w_out, w_up, w_down, layer,
        s_in3, s_in4, s_in5, s_out3, s_out4, s_out5, gathered,
        osems, usems, dsems, xsems,
    ) = refs[42:]
    tile = pl.program_id(0)
    is_first = tile == 0
    near = token_copies(meta, cots, cot, xsems)
    out_copies = weight_copies(meta, out_own, up_pieces, w_out, osems, out_places)
    up_copies = weight_copies(meta, up_own, up_pieces, w_up, usems, up_places)
    down_copies = weight_copies(meta, down_own, down_pieces, w_down, dsems, down_places)

    @pl.when(is_first)
    def _():
        for copy in down_copies + near + up_copies + out_copies:
            copy.start()
        for ref in (s_in3, s_in4, s_in5, s_out3, s_out4, s_out5):
            ref[...] = jnp.zeros_like(ref)
        for copy in down_copies + near:
            copy.wait()

    part = w_up.shape[1] // MID_PARTS
    a_in3, a_in4, a_out3, a_out5 = in3[0, 0], in4[0, 0], out3[0, 0], out5[0, 0]
    rows = pl.ds(pl.multiple_of(tile * MID_TILE, MID_TILE), MID_TILE)
    normal1 = normal_ref[...]
    inverse1 = inverse_ref[:, 0:1]
    first = normal1 * gain1[...]
    low1 = first.astype(BF)
    r4 = mm_nt(low1, a_in4).astype(BF)
    r5 = mm_nt(active[...], in5[0]).astype(BF)
    lowered = first + mm(active[...], w_down[...]) + mm(r5, a_out5)
    normal2, inverse2 = norm_parts(lowered)
    layer[rows, :] = (normal2 * gain2[...]).astype(BF)
    grad_sum = norm_back(cot[rows, :].astype(F32), gain2[...], normal2, inverse2)
    e5 = grad_sum.astype(BF)
    rg5 = mm_nt(e5, a_out5).astype(BF)
    s_out5[...] += mm_tn(r5, e5)

    @pl.when(is_first)
    def _():
        for copy in up_copies + out_copies:
            copy.wait()

    grad_first = grad_sum
    rg4 = jnp.zeros((MID_TILE, RANK), F32)
    for n in range(MID_PARTS):
        cols = slice(n * part, n * part + part)
        grad_active = mm_nt(e5, w_down[cols, :]) + mm(rg5, in5[0, :, cols])
        e4 = (slope[:, cols].astype(F32) * grad_active).astype(BF)
        s_in5[:, cols] += mm_tn(rg5, active[:, cols])
        s_out4[:, cols] += mm_tn(r4, e4)
        grad_first = grad_first + mm_nt(e4, w_up[:, cols])
        rg4 = rg4 + mm_nt(e4, out4[0, :, cols])
    rg4 = rg4.astype(BF)
    s_in4[...] += mm_tn(rg4, low1)
    grad_first = grad_first + mm(rg4, a_in4)
    grad_branch = norm_back(grad_first, gain1[...], normal1, inverse1)
    grad_branch_ref[...] = grad_branch
    e3 = grad_branch.astype(BF)
    mixed = mixed_ref[...]
    rank3 = mm_nt(mixed, a_in3).astype(BF)
    rg3 = mm_nt(e3, a_out3).astype(BF)
    s_out3[...] += mm_tn(rank3, e3)
    s_in3[...] += mm_tn(rg3, mixed)
    grad_mixed_ref[...] = (mm_nt(e3, w_out[...]) + mm(rg3, a_in3)).astype(BF)

    @pl.when(tile == 512 // MID_TILE - 1)
    def _():
        wide, narrow = 768, 192
        for owner in range(4):
            start = 0
            for ref, size in (
                (s_in5, wide), (s_out4, wide), (s_in3, narrow), (s_in4, narrow), (s_out3, narrow), (s_out5, narrow),
            ):
                row, column = 16 * (start // 768), start % 768
                gathered[owner, row : row + 16, column : column + size] = ref[:, owner * size : owner * size + size]
                start += size
        lane = lax.broadcasted_iota(jnp.int32, (16, 128), 1)
        id_rows = jnp.zeros((16, 128), F32)
        for p in range(6):
            id_rows = jnp.where(lane == p, ids[p].astype(F32), id_rows)
        for r, ref in enumerate(layer_parts):
            ref[...] = layer[pl.ds(pl.multiple_of(256 * ((meta[0] & 1) ^ r), 256), 256), :]
        for r, ref in enumerate(grad_parts):
            ref[0:48] = gathered[meta[0] ^ r].astype(BF)
            ref[48:64] = jnp.zeros((16, 768), BF)
            ref[48:64, 0:128] = id_rows.astype(BF)


def second_half(meta, ids, cots, out_own, up_own, down_own, up_pieces, down_pieces, normal, inverse, active, slope,
                mixed, gain1, gain2, table_in, table_in_hidden, table_out, table_out_hidden):
    width, hidden = normal.shape[1], up_own.shape[1]
    tile = lambda columns: pl.BlockSpec((MID_TILE, columns), lambda i, *_: (i, 0))
    return pl.pallas_call(
        second_half_kernel,
        grid_spec=pltpu.PrefetchScalarGridSpec(
            num_scalar_prefetch=2,
            grid=(512 // MID_TILE,),
            in_specs=any_specs(21)
            + [
                tile(width),
                tile(128),
                tile(hidden),
                tile(hidden),
                tile(width),
                whole((1, width)),
                whole((1, width)),
                table_spec(3, 3, width),
                table_spec(4, 4, width),
                hidden_spec(5, hidden),
                table_spec(3, 3, width),
                hidden_spec(4, hidden),
                table_spec(4, 5, width),
            ],
            out_specs=[whole((256, width))] * 2 + [tile(width), tile(width)] + [whole((64, width))] * 4,
            scratch_shapes=[
                VMEM((512, width), BF),
                VMEM((width, width), BF),
                VMEM((width, hidden), BF),
                VMEM((hidden, width), BF),
                VMEM((512, width), BF),
                VMEM((RANK, width), F32),
                VMEM((RANK, width), F32),
                VMEM((RANK, hidden), F32),
                VMEM((RANK, width), F32),
                VMEM((RANK, hidden), F32),
                VMEM((RANK, width), F32),
                VMEM((4, 3 * RANK, 768), F32),
                pltpu.SemaphoreType.DMA((25,)),
                pltpu.SemaphoreType.DMA((25,)),
                pltpu.SemaphoreType.DMA((49,)),
                pltpu.SemaphoreType.DMA((2,)),
            ],
        ),
        out_shape=[jax.ShapeDtypeStruct((256, width), BF)] * 2
        + [jax.ShapeDtypeStruct((512, width), F32), jax.ShapeDtypeStruct((512, width), BF)]
        + [jax.ShapeDtypeStruct((64, width), BF)] * 4,
        compiler_params=pltpu.CompilerParams(vmem_limit_bytes=VMEM_LIMIT),
        cost_estimate=SMALL_COST,
        name="second_half",
    )(meta, ids, *cots, out_own, up_own, down_own, *up_pieces, *down_pieces, normal, inverse, active, slope, mixed,
      gain1, gain2, table_in, table_in, table_in_hidden, table_out, table_out_hidden, table_out)


def first_grads_kernel(meta, ids, *refs):
    xs, dq_ref, dk_ref, dv_ref, got_ref = refs[0:5]
    ins, outs = refs[5:8], refs[8:11]
    grads_ref, rank_grad_ref = refs[11:13]
    gs = refs[13:17]
    s_in, s_out, gathered = refs[17:]
    in_all = jnp.concatenate([ref[0, 0] for ref in ins], axis=0)
    out_all = jnp.concatenate([zero_padded(ref[0, 0], p, 3) for p, ref in enumerate(outs)], axis=1)
    for tile in range(2):
        rows = slice(256 * tile, 256 * tile + 256)
        grads = jnp.concatenate(
            [dq_ref[rows]]
            + [(ref[rows] + got_ref[n, rows].astype(F32)).astype(BF) for n, ref in enumerate((dk_ref, dv_ref))],
            axis=1,
        )
        grads_ref[rows] = grads
        x = xs[rows]
        rank = mm_nt(x, in_all).astype(BF)
        rank_grad = mm_nt(grads, out_all).astype(BF)
        rank_grad_ref[rows] = rank_grad
        part_in, part_out = mm_tn(rank_grad, x), mm_tn(rank, grads)
        if tile == 0:
            s_in[...] = part_in
            s_out[...] = part_out
        else:
            s_in[...] += part_in
            s_out[...] += part_out
    for owner in range(4):
        for p in range(3):
            rows = slice(RANK * p, RANK * p + RANK)
            gathered[owner, :, 192 * p : 192 * p + 192] = s_in[rows, 192 * owner : 192 * owner + 192]
            gathered[owner, :, 192 * (3 + p) : 192 * (4 + p)] = s_out[
                rows, 768 * p + 192 * owner : 768 * p + 192 * owner + 192
            ]
    for r, ref in enumerate(gs):
        ref[...] = gathered[meta[0] ^ r].astype(BF)


def first_grads(meta, ids, x, dq, dk, dv, got, table_in, table_out):
    width = x.shape[1]
    return pl.pallas_call(
        first_grads_kernel,
        grid_spec=pltpu.PrefetchScalarGridSpec(
            num_scalar_prefetch=2,
            grid=(1,),
            in_specs=[whole((512, width))] * 4
            + [whole((2, 512, width))]
            + [table_spec(p, p, width) for p in range(3)] * 2,
            out_specs=[whole((512, 3 * width)), whole((512, 3 * RANK))] + [whole((RANK, 1152))] * 4,
            scratch_shapes=[
                VMEM((3 * RANK, width), F32),
                VMEM((3 * RANK, 3 * width), F32),
                VMEM((4, RANK, 1152), F32),
            ],
        ),
        out_shape=[jax.ShapeDtypeStruct((512, 3 * width), BF), jax.ShapeDtypeStruct((512, 3 * RANK), BF)]
        + [jax.ShapeDtypeStruct((RANK, 1152), BF)] * 4,
        compiler_params=pltpu.CompilerParams(vmem_limit_bytes=VMEM_LIMIT),
        cost_estimate=SMALL_COST,
        name="first_grads",
    )(meta, ids, x, dq, dk, dv, got, *([table_in] * 3), *([table_out] * 3))


def input_grad_kernel(meta, ids, *refs):
    w_own, pieces = refs[0], refs[1:9]
    branch_ref, grads_ref, rank_grad_ref = refs[9:12]
    ins, parts = refs[12:15], refs[15:17]
    weight, wsems = refs[17:]
    copies = weight_copies(meta, w_own, pieces, weight, wsems, qkv_places)
    for copy in copies:
        copy.start()
    for copy in copies:
        copy.wait()
    in_all = jnp.concatenate([ref[0, 0] for ref in ins], axis=0)
    for r, ref in enumerate(parts):
        rows = pl.ds(pl.multiple_of(256 * ((meta[0] & 1) ^ r), 256), 256)
        ref[...] = (
            branch_ref[rows, :] + mm_nt(grads_ref[rows, :], weight[...]) + mm(rank_grad_ref[rows, :], in_all)
        ).astype(BF)


def project_back(meta, ids, w_own, pieces, branch, grads, rank_grad, table_in):
    width = branch.shape[1]
    return pl.pallas_call(
        input_grad_kernel,
        grid_spec=pltpu.PrefetchScalarGridSpec(
            num_scalar_prefetch=2,
            grid=(1,),
            in_specs=any_specs(9)
            + [whole((512, width)), whole((512, 3 * width)), whole((512, 3 * RANK))]
            + [table_spec(p, p, width) for p in range(3)],
            out_specs=[whole((256, width))] * 2,
            scratch_shapes=[VMEM((width, 3 * width), BF), pltpu.SemaphoreType.DMA((25,))],
        ),
        out_shape=[jax.ShapeDtypeStruct((256, width), BF)] * 2,
        compiler_params=pltpu.CompilerParams(vmem_limit_bytes=VMEM_LIMIT),
        cost_estimate=SMALL_COST,
        name="project_back",
    )(meta, ids, w_own, *pieces, branch, grads, rank_grad, *([table_in] * 3))


def combine_middle_kernel(ids, *refs):
    messages = refs[0:8]
    in_d, in_f, out_d, out_f = refs[8:12]
    for ref in (in_d, in_f, out_d, out_f):
        ref[...] = jnp.zeros_like(ref)
    narrow = in_d.shape[-1]
    for o in range(8):
        for r in range(4):
            chosen = [ids[(o * 4 + r) * 6 + p] for p in range(3, 6)]
            part = messages[o][r].astype(F32)
            in_f[chosen[2]] += part[0:16]
            out_f[chosen[1]] += part[16:32]
            for at, (ref, p, which) in enumerate(
                ((in_d, 3, 0), (in_d, 4, 1), (out_d, 3, 0), (out_d, 4, 2))
            ):
                ref[p, chosen[which]] += part[32:48, narrow * at : narrow * at + narrow]


def combine_middle(ids, messages, tables, narrow, wide):
    shapes = [(5, tables, RANK, narrow), (tables, RANK, wide)] * 2
    return pl.pallas_call(
        combine_middle_kernel,
        grid_spec=pltpu.PrefetchScalarGridSpec(
            num_scalar_prefetch=1,
            grid=(1,),
            in_specs=[whole(message.shape) for message in messages],
            out_specs=[whole(shape) for shape in shapes],
        ),
        out_shape=[jax.ShapeDtypeStruct(shape, F32) for shape in shapes],
        compiler_params=pltpu.CompilerParams(vmem_limit_bytes=VMEM_LIMIT),
        cost_estimate=SMALL_COST,
        name="combine_middle",
    )(ids, *messages)


def combine_first_kernel(ids, *refs):
    messages = refs[0:8]
    in_d, out_d = refs[10:12]
    for n, ref in enumerate((in_d, out_d)):
        ref[...] = refs[8 + n][...]
    narrow = in_d.shape[-1]
    for o in range(8):
        for r in range(4):
            part = messages[o][r].astype(F32)
            for p in range(3):
                chosen = ids[(o * 4 + r) * 6 + p]
                in_d[p, chosen] += part[:, narrow * p : narrow * p + narrow]
                out_d[p, chosen] += part[:, narrow * (3 + p) : narrow * (4 + p)]


def combine_first(ids, messages, in_d, out_d):
    return pl.pallas_call(
        combine_first_kernel,
        grid_spec=pltpu.PrefetchScalarGridSpec(
            num_scalar_prefetch=1,
            grid=(1,),
            in_specs=[whole(message.shape) for message in messages] + [whole(in_d.shape)] * 2,
            out_specs=[whole(in_d.shape)] * 2,
        ),
        out_shape=[jax.ShapeDtypeStruct(in_d.shape, F32)] * 2,
        compiler_params=pltpu.CompilerParams(vmem_limit_bytes=VMEM_LIMIT),
        name="combine_first",
    )(ids, *messages, in_d, out_d)


def after(value, *others):
    return lax.optimization_barrier((value, *others))[0]


def beside(work, transfers, values, moved):
    given = lax.optimization_barrier((tuple(values), tuple(moved)))
    return lax.optimization_barrier((tuple(work(*given[0])), tuple(transfers(*given[1]))))


def paired_body(
    inputs,
    segments,
    random_key_blocks,
    adapter_index_table,
    frozen_query_key_value_weight,
    frozen_output_weight,
    frozen_up_weight,
    frozen_down_weight,
    attention_norm_gain,
    feedforward_norm_gain,
    adapter_down_from_width,
    adapter_down_from_hidden,
    adapter_up_to_width,
    adapter_up_to_hidden,
    cotangent,
):
    dp_count, shard_count = lax.axis_size("dp"), lax.axis_size("shard")
    d, z = lax.axis_index("dp"), lax.axis_index("shard")
    core = d & 1
    meta = jnp.stack([z, d]).astype(jnp.int32)

    def piece(weight, rows, columns, row, column):
        return lax.dynamic_slice(weight, (row, column), (rows, columns))

    def fetch(part):
        return [swap_shards(part, shard_count, step) for step in range(1, shard_count)]

    qkv_own = jnp.stack(fetch(piece(frozen_query_key_value_weight, 48, 1152, (d >> 1) * 48, core * 1152)))

    def slices(values):
        return [lax.dynamic_index_in_dim(values, (z & 1) ^ r, 0, keepdims=False) for r in range(2)]

    seg_rows = jnp.pad(segments.astype(BF)[:, None, :], ((0, 0), (0, 15), (0, inputs.shape[-1] - 256)))
    own = send_away(slices(jnp.concatenate([inputs, seg_rows], axis=1)), dp_count, shard_count)
    tokens = own + [swap_cores(part, dp_count) for part in own]
    qkv_pieces = spread_in_plane(qkv_own, dp_count)

    up_piece = jnp.concatenate(
        [
            piece(frozen_output_weight, 48, 384, (d >> 1) * 48, core * 384),
            piece(frozen_up_weight, 192, 384, 0, d * 384),
        ],
        axis=0,
    )
    down_piece = piece(frozen_down_weight, 96, 768, d * 96, 0)
    down_piece = jnp.concatenate([down_piece[:, 0:384], down_piece[:, 384:768]], axis=0)
    there = swap_cores(adapter_index_table, dp_count)
    column_ids = jnp.where(
        core == 0,
        jnp.concatenate([adapter_index_table, there], axis=0),
        jnp.concatenate([there, adapter_index_table], axis=0),
    )
    ids = lax.dynamic_index_in_dim(column_ids, z, 0, keepdims=False)

    local = jnp.arange(8, dtype=jnp.int32)
    block = 8 * core + local

    def place(index):
        return ((index >> 3) ^ core) * 8 + (index & 7)

    left_ok, right_ok = block - 1 >= GLOBALS, block + 1 < 16
    left = jnp.where(left_ok, place(block - 1), 0)
    right = jnp.where(right_ok, place(block + 1), 0)
    window = jnp.stack(
        [left, jnp.where(left_ok, left, 16), right, jnp.where(right_ok, right, 16)], axis=-1
    )
    drawn = place(lax.dynamic_slice_in_dim(random_key_blocks, 8 * core, 8, axis=1))
    drawn = drawn.reshape(H // 2, 2, 8, RANDOMS).transpose(0, 2, 1, 3).reshape(H // 2, 8, 2 * RANDOMS)
    picks = jnp.concatenate(
        [
            jnp.broadcast_to(window[None], (H // 2, 8, 4)),
            drawn,
            jnp.broadcast_to(local[None, :, None], (H // 2, 8, 1)),
            jnp.broadcast_to(8 * core, (H // 2, 8, 1)),
        ],
        axis=-1,
    ).reshape(-1)
    picks = jnp.concatenate([picks, core[None]]).astype(jnp.int32)

    def work(*given):
        return project_qkv(
            meta, ids, given[0:4], frozen_query_key_value_weight, given[4:],
            adapter_down_from_width, adapter_up_to_width,
        )

    (q, k, v, masks, hot, x), up_own = beside(work, fetch, (*tokens, *qkv_pieces), (up_piece,))
    pairs = H // 2
    (mixed, extra), moved = beside(
        lambda *given: attend(0, pairs, picks, *given),
        lambda block, part: (*spread_over_chips(block, dp_count), *fetch(part)),
        (q, k, v, masks, hot),
        (jnp.stack(up_own), down_piece),
    )
    up_pieces, down_own = moved[0 : dp_count // 2], jnp.stack(moved[dp_count // 2 :])
    up_pieces = spread_over_cores(up_pieces, dp_count)
    gain1, gain2 = attention_norm_gain[None], feedforward_norm_gain[None]

    def work(mixed, *pieces):
        return first_half(
            meta, ids, frozen_output_weight, frozen_up_weight, pieces, x, mixed, gain1,
            adapter_down_from_width, adapter_up_to_width, adapter_up_to_hidden,
        )

    (normal, inverse, active, slope), (*down_pieces, cot_a, cot_b) = beside(
        work,
        lambda block, values: (
            *spread_over_chips(block, dp_count), *send_away(slices(values), dp_count, shard_count)
        ),
        (mixed, *up_pieces),
        (down_own, cotangent),
    )
    down_pieces = spread_over_cores(down_pieces, dp_count)
    cots = (cot_a, cot_b)
    results = second_half(
        meta, ids, cots, frozen_output_weight, frozen_up_weight, frozen_down_weight, up_pieces, down_pieces,
        normal, inverse, active, slope, mixed, gain1, gain2,
        adapter_down_from_width, adapter_down_from_hidden, adapter_up_to_width, adapter_up_to_hidden,
    )
    grad_branch, parts = results[2], results[5:8]
    (dq, dk, dv, other_sums), moved = beside(
        lambda grad: attend_back(0, pairs, picks, q, k, v, masks, extra, grad, mixed),
        lambda layer_a, layer_b, *parts: (
            *send_away((layer_a, layer_b), dp_count, shard_count),
            *(swap_shards(part, shard_count, step + 1) for step, part in enumerate(parts)),
        ),
        (results[3],),
        (*results[0:2], *parts),
    )
    got = swap_cores(other_sums, dp_count)
    layer_out = join_parts(meta, moved[0:2], BF)
    messages = jnp.stack([results[4], *moved[2:5]])

    def work(got):
        grads, rank_grad, own, *parts = first_grads(
            meta, ids, x, dq, dk, dv, got, adapter_down_from_width, adapter_up_to_width
        )
        input_parts, moved = beside(
            lambda grads: project_back(
                meta, ids, frozen_query_key_value_weight, qkv_pieces, grad_branch, grads, rank_grad,
                adapter_down_from_width,
            ),
            lambda *parts: tuple(swap_shards(part, shard_count, step + 1) for step, part in enumerate(parts)),
            (grads,),
            parts,
        )
        return (*input_parts, own, *moved)

    (*input_parts, own, first_a, first_b, first_c), messages = beside(
        work, lambda block: spread_over_chips(block, dp_count), (got,), (messages,)
    )
    messages = spread_over_cores(messages, dp_count)
    chosen = jnp.stack([message[:, 48, 0:6] for message in messages]).astype(jnp.int32).reshape(-1)
    (in_d, in_f, out_d, out_f), firsts = beside(
        lambda *messages: combine_middle(chosen, messages, adapter_down_from_width.shape[1], 192, 768),
        lambda block: spread_over_chips(block, dp_count),
        messages,
        (jnp.stack([own, first_a, first_b, first_c]),),
    )
    firsts = spread_over_cores(firsts, dp_count)
    input_grad = join_parts(meta, send_away(input_parts, dp_count, shard_count), F32)
    in_d, out_d = combine_first(chosen, firsts, in_d, out_d)
    return (layer_out, input_grad, in_d, in_f, out_d, out_f)


def solution(mesh):
    dp_count, shard_count = mesh.shape["dp"], mesh.shape["shard"]
    paired = dp_count == 8 and shard_count == 4
    return jax.shard_map(
        paired_body if paired else general_body,
        mesh=mesh,
        in_specs=(
            P("dp", "shard", None),
            P("dp", "shard"),
            P(),
            P("dp", None),
            P("shard", None),
            P("shard", None),
            P("shard", None),
            P("shard", None),
            P(),
            P(),
            P(),
            P(),
            P(),
            P(),
            P("dp", "shard", None),
        ),
        out_specs=(
            P("dp", "shard", None),
            P("dp", "shard", None),
            P(None, None, None, "shard"),
            P(None, None, "shard"),
            P(None, None, None, "shard"),
            P(None, None, "shard"),
        ),
        check_vma=False,
    )
```

```python
import functools

import jax
import jax.numpy as jnp
from jax import lax
from jax.experimental import pallas as pl
from jax.experimental.pallas import tpu as pltpu
from jax.sharding import PartitionSpec as P

H = 12
HD = 64
BLOCK = 64
GLOBALS = 2
RANDOMS = 3


EPSILON = 1e-06
NEGATIVE = -1e30


def norm_rows(hidden, gain_vector):
    average = jnp.mean(hidden, axis=-1, keepdims=True)
    centred = hidden - average
    spread = jnp.mean(centred * centred, axis=-1, keepdims=True)
    return centred * lax.rsqrt(spread + EPSILON) * gain_vector


def gelu_exact(values):
    return jax.nn.gelu(values, approximate=False)


def dense_forward(inputs, weight):
    return jnp.einsum("sti,io->sto", inputs, weight, preferred_element_type=jnp.float32)


def dense_backward(grad_low, weight):
    return jnp.einsum("sto,io->sti", grad_low, weight, preferred_element_type=jnp.float32)


def adapt(inputs, down_rows, up_rows):
    rank_part = jnp.einsum(
        "sti,sri->str", inputs, down_rows, preferred_element_type=jnp.float32
    ).astype(jnp.bfloat16)
    return (
        rank_part,
        jnp.einsum("str,sro->sto", rank_part, up_rows, preferred_element_type=jnp.float32),
    )


def adapt_back(inputs, down_rows, up_rows, rank_part, grad_low):
    grad_up = jnp.einsum("str,sto->sro", rank_part, grad_low, preferred_element_type=jnp.float32)
    rank_grad = jnp.einsum(
        "sto,sro->str", grad_low, up_rows, preferred_element_type=jnp.float32
    ).astype(jnp.bfloat16)
    grad_down = jnp.einsum("str,sti->sri", rank_grad, inputs, preferred_element_type=jnp.float32)
    grad_inputs = jnp.einsum(
        "str,sri->sti", rank_grad, down_rows, preferred_element_type=jnp.float32
    )
    return (grad_down, grad_up, grad_inputs)


def table_sum(per_sequence, chosen, table_size):
    matches = (chosen[:, None] == jnp.arange(table_size, dtype=jnp.int32)[None, :]).astype(
        jnp.float32
    )
    return jnp.sum(matches[:, :, None, None] * per_sequence[:, None], axis=0)


def sparse_scores(query_heads, key_picked, permit, scaling):
    scores = (
        jnp.einsum(
            "shbqd,shbkd->shbqk", query_heads, key_picked, preferred_element_type=jnp.float32
        )
        * scaling
    )
    return jnp.where(permit, scores, NEGATIVE)


def global_scores(query_rows, key_rows, seg_query, seg_keys, scaling):
    scores = (
        jnp.einsum("hqd,hkd->hqk", query_rows, key_rows, preferred_element_type=jnp.float32)
        * scaling
    )
    return jnp.where((seg_query[:, None] == seg_keys[None, :])[None], scores, NEGATIVE)


def global_forward(query_rows, key_rows, value_rows, seg_query, seg_keys, scaling):
    scores = global_scores(query_rows, key_rows, seg_query, seg_keys, scaling)
    top_score = jnp.max(scores, axis=-1, keepdims=True)
    weights = jnp.exp(scores - top_score)
    totals = jnp.sum(weights, axis=-1, keepdims=True)
    shares = (weights / totals).astype(jnp.bfloat16)
    attended = jnp.einsum("hqk,hkd->hqd", shares, value_rows, preferred_element_type=jnp.float32)
    return (attended, (top_score + jnp.log(totals))[..., 0])


def global_backward(
    query_rows, key_rows, value_rows, seg_query, seg_keys, grad_rows, log_total, scaling
):
    scores = global_scores(query_rows, key_rows, seg_query, seg_keys, scaling)
    shares = jnp.exp(scores - log_total[..., None])
    share_low = shares.astype(jnp.bfloat16)
    grad_shares = jnp.einsum(
        "hqd,hkd->hqk", grad_rows, value_rows, preferred_element_type=jnp.float32
    )
    centre = jnp.sum(shares * grad_shares, axis=-1, keepdims=True)
    grad_scores = (shares * (grad_shares - centre)).astype(jnp.bfloat16)
    grad_query = (
        jnp.einsum("hqk,hkd->hqd", grad_scores, key_rows, preferred_element_type=jnp.float32)
        * scaling
    )
    grad_keys = (
        jnp.einsum("hqk,hqd->hkd", grad_scores, query_rows, preferred_element_type=jnp.float32)
        * scaling
    )
    grad_values = jnp.einsum(
        "hqk,hqd->hkd", share_low, grad_rows, preferred_element_type=jnp.float32
    )
    return (grad_query, grad_keys, grad_values, centre[..., 0])


def general_body(
    inputs,
    segments,
    random_key_blocks,
    adapter_index_table,
    frozen_query_key_value_weight,
    frozen_output_weight,
    frozen_up_weight,
    frozen_down_weight,
    attention_norm_gain,
    feedforward_norm_gain,
    adapter_down_from_width,
    adapter_down_from_hidden,
    adapter_up_to_width,
    adapter_up_to_hidden,
    cotangent,
):
    seq_count = inputs.shape[0]
    local_tokens = inputs.shape[1]
    width = inputs.shape[2]
    shard_count = lax.axis_size("shard")
    full_length = local_tokens * shard_count
    total_blocks = full_length // BLOCK
    local_blocks = local_tokens // BLOCK
    cand_count = 3 + GLOBALS + RANDOMS
    glob_rows = GLOBALS * BLOCK
    scaling = HD ** (-0.5)

    def select_adapter_table(table, table_column):
        return jnp.take(table, adapter_index_table[:, table_column], axis=0)

    adapter_tables_input = [
        select_adapter_table(adapter_down_from_width[table_column], table_column)
        for table_column in range(5)
    ] + [select_adapter_table(adapter_down_from_hidden, 5)]
    adapter_tables_output = [
        select_adapter_table(adapter_up_to_width[table_column], table_column)
        for table_column in range(4)
    ]
    adapter_tables_output = adapter_tables_output + [
        select_adapter_table(adapter_up_to_hidden, 4),
        select_adapter_table(adapter_up_to_width[4], 5),
    ]
    qkv_full, out_full = (
        lax.all_gather(frozen_query_key_value_weight, "shard", axis=0, tiled=True),
        lax.all_gather(frozen_output_weight, "shard", axis=0, tiled=True),
    )
    main_part = dense_forward(inputs, qkv_full)
    rank_parts = []
    projected = []
    for table_column in range(3):
        rank_part, extra = adapt(
            inputs, adapter_tables_input[table_column], adapter_tables_output[table_column]
        )
        rank_parts.append(rank_part)
        projected.append(
            (main_part[..., table_column * width : (table_column + 1) * width] + extra).astype(
                jnp.bfloat16
            )
        )
    seg_low = segments.astype(jnp.bfloat16)
    key_all, value_all, seg_all = (
        lax.all_gather(projected[1], "shard", axis=1, tiled=True),
        lax.all_gather(projected[2], "shard", axis=1, tiled=True),
        lax.all_gather(seg_low, "shard", axis=1, tiled=True),
    )
    shard_pos = lax.axis_index("shard")
    is_first = shard_pos == 0
    first_block = shard_pos * local_blocks
    block_ids = first_block + jnp.arange(local_blocks, dtype=jnp.int32)
    rand_local = lax.dynamic_slice_in_dim(random_key_blocks, first_block, local_blocks, axis=1)
    window_part = jnp.stack([block_ids - 1, block_ids, block_ids + 1], axis=-1)
    global_ids = jnp.broadcast_to(
        jnp.arange(GLOBALS, dtype=jnp.int32)[None, :], (local_blocks, GLOBALS)
    )
    fixed_part = jnp.concatenate([window_part, global_ids], axis=-1)
    candidates = jnp.concatenate(
        [jnp.broadcast_to(fixed_part[None], (H, local_blocks, 3 + GLOBALS)), rand_local], axis=-1
    )
    candidates = jnp.clip(candidates, 0, total_blocks - 1)
    always_true = jnp.ones((local_blocks,), dtype=bool)
    fixed_valid = jnp.stack(
        [block_ids - 1 >= GLOBALS, always_true, block_ids + 1 < total_blocks]
        + [always_true] * GLOBALS,
        axis=-1,
    )
    valid = jnp.concatenate(
        [
            jnp.broadcast_to(fixed_valid[None], (H, local_blocks, 3 + GLOBALS)),
            jnp.ones((H, local_blocks, RANDOMS), dtype=bool),
        ],
        axis=-1,
    )
    valid_keys = jnp.repeat(valid, BLOCK, axis=-1)
    query_heads = (
        projected[0].reshape(seq_count, local_blocks, BLOCK, H, HD).transpose(0, 3, 1, 2, 4)
    )
    key_source = key_all.reshape(seq_count, total_blocks, BLOCK, H, HD).transpose(0, 3, 1, 2, 4)
    value_source = value_all.reshape(seq_count, total_blocks, BLOCK, H, HD).transpose(0, 3, 1, 2, 4)
    head_index = jnp.arange(H, dtype=jnp.int32)[:, None, None]
    key_picked = key_source[:, head_index, candidates].reshape(
        seq_count, H, local_blocks, cand_count * BLOCK, HD
    )
    value_picked = value_source[:, head_index, candidates].reshape(
        seq_count, H, local_blocks, cand_count * BLOCK, HD
    )
    seg_picked = seg_all.reshape(seq_count, total_blocks, BLOCK)[:, candidates].reshape(
        seq_count, H, local_blocks, cand_count * BLOCK
    )
    seg_local = seg_low.reshape(seq_count, local_blocks, BLOCK)
    permit = valid_keys[None, :, :, None, :] & (
        seg_local[:, None, :, :, None] == seg_picked[:, :, :, None, :]
    )
    scores = sparse_scores(query_heads, key_picked, permit, scaling)
    top_score = jnp.max(scores, axis=-1, keepdims=True)
    weights = jnp.exp(scores - top_score)
    totals = jnp.sum(weights, axis=-1, keepdims=True)
    share_low = (weights / totals).astype(jnp.bfloat16)
    sparse_lse = (top_score + jnp.log(totals))[..., 0]
    sparse_out = jnp.einsum(
        "shbqk,shbkd->shbqd", share_low, value_picked, preferred_element_type=jnp.float32
    )
    key_heads = key_source.reshape(seq_count, H, full_length, HD)
    value_heads = value_source.reshape(seq_count, H, full_length, HD)
    glob_query = query_heads[:, :, :GLOBALS].reshape(seq_count, H, glob_rows, HD)
    glob_seg = seg_low[:, :glob_rows]

    def run_forward(operands):
        return lax.map(
            lambda packet: global_forward(
                packet[0], packet[1], packet[2], packet[3], packet[4], scaling
            ),
            operands,
        )

    def skip_forward(operands):
        return (
            jnp.zeros((seq_count, H, glob_rows, HD), jnp.float32),
            jnp.zeros((seq_count, H, glob_rows), jnp.float32),
        )

    global_out, global_lse = lax.cond(
        is_first, run_forward, skip_forward, (glob_query, key_heads, value_heads, glob_seg, seg_all)
    )
    glob_blocks = global_out.reshape(seq_count, H, GLOBALS, BLOCK, HD)
    head_out = jnp.concatenate(
        [jnp.where(is_first, glob_blocks, sparse_out[:, :, :GLOBALS]), sparse_out[:, :, GLOBALS:]],
        axis=2,
    )
    mixed_low = (
        head_out.transpose(0, 2, 3, 1, 4)
        .reshape(seq_count, local_tokens, width)
        .astype(jnp.bfloat16)
    )
    rank_out, extra_out = adapt(mixed_low, adapter_tables_input[3], adapter_tables_output[3])
    branch = dense_forward(mixed_low, out_full) + extra_out
    first, first_pull = jax.vjp(
        lambda hidden: norm_rows(hidden, attention_norm_gain), inputs.astype(jnp.float32) + branch
    )
    first_low = first.astype(jnp.bfloat16)
    up_full, down_full = (
        lax.all_gather(frozen_up_weight, "shard", axis=0, tiled=True),
        lax.all_gather(frozen_down_weight, "shard", axis=0, tiled=True),
    )
    rank_up, extra_up = adapt(first_low, adapter_tables_input[4], adapter_tables_output[4])
    lifted = dense_forward(first_low, up_full) + extra_up
    activated, gelu_pull = jax.vjp(gelu_exact, lifted)
    active_low = activated.astype(jnp.bfloat16)
    rank_down, extra_down = adapt(active_low, adapter_tables_input[5], adapter_tables_output[5])
    lowered = dense_forward(active_low, down_full) + extra_down
    result, final_pull = jax.vjp(
        lambda hidden: norm_rows(hidden, feedforward_norm_gain), first + lowered
    )
    layer_out = result.astype(jnp.bfloat16)
    up_back, down_back = (
        lax.all_gather(frozen_up_weight, "shard", axis=0, tiled=True),
        lax.all_gather(frozen_down_weight, "shard", axis=0, tiled=True),
    )
    grad_adapt_in = [None] * 6
    grad_adapt_out = [None] * 6
    (grad_sum,) = final_pull(cotangent.astype(jnp.float32))
    grad_lowered = grad_sum.astype(jnp.bfloat16)
    grad_adapt_in[5], grad_adapt_out[5], extra_grad = adapt_back(
        active_low, adapter_tables_input[5], adapter_tables_output[5], rank_down, grad_lowered
    )
    grad_active = dense_backward(grad_lowered, down_back) + extra_grad
    (grad_lifted,) = gelu_pull(grad_active)
    grad_lift_low = grad_lifted.astype(jnp.bfloat16)
    grad_adapt_in[4], grad_adapt_out[4], extra_grad = adapt_back(
        first_low, adapter_tables_input[4], adapter_tables_output[4], rank_up, grad_lift_low
    )
    grad_first = grad_sum + dense_backward(grad_lift_low, up_back) + extra_grad
    (grad_branch,) = first_pull(grad_first)
    grad_branch_low = grad_branch.astype(jnp.bfloat16)
    qkv_back, out_back = (
        lax.all_gather(frozen_query_key_value_weight, "shard", axis=0, tiled=True),
        lax.all_gather(frozen_output_weight, "shard", axis=0, tiled=True),
    )
    grad_adapt_in[3], grad_adapt_out[3], extra_grad = adapt_back(
        mixed_low, adapter_tables_input[3], adapter_tables_output[3], rank_out, grad_branch_low
    )
    grad_mixed = (dense_backward(grad_branch_low, out_back) + extra_grad).astype(jnp.bfloat16)
    grad_heads = grad_mixed.reshape(seq_count, local_blocks, BLOCK, H, HD).transpose(0, 3, 1, 2, 4)
    row_keep = (block_ids >= GLOBALS)[None, None, :, None, None]
    grad_sparse = jnp.where(row_keep, grad_heads, jnp.zeros_like(grad_heads))
    scores = sparse_scores(query_heads, key_picked, permit, scaling)
    shares = jnp.exp(scores - sparse_lse[..., None])
    share_low = shares.astype(jnp.bfloat16)
    grad_shares = jnp.einsum(
        "shbqd,shbkd->shbqk", grad_sparse, value_picked, preferred_element_type=jnp.float32
    )
    centre = jnp.sum(shares * grad_shares, axis=-1, keepdims=True)
    grad_scores = (shares * (grad_shares - centre)).astype(jnp.bfloat16)
    grad_query = (
        jnp.einsum(
            "shbqk,shbkd->shbqd", grad_scores, key_picked, preferred_element_type=jnp.float32
        )
        * scaling
    )
    glob_grad = grad_heads[:, :, :GLOBALS].reshape(seq_count, H, glob_rows, HD)

    def run_backward(operands):
        return lax.map(
            lambda packet: global_backward(
                packet[0], packet[1], packet[2], packet[3], packet[4], packet[5], packet[6], scaling
            ),
            operands,
        )

    def skip_backward(operands):
        return (
            jnp.zeros((seq_count, H, glob_rows, HD), jnp.float32),
            jnp.zeros((seq_count, H, full_length, HD), jnp.float32),
            jnp.zeros((seq_count, H, full_length, HD), jnp.float32),
            jnp.zeros((seq_count, H, glob_rows), jnp.float32),
        )

    glob_dq, glob_dk, glob_dv, glob_centre = lax.cond(
        is_first,
        run_backward,
        skip_backward,
        (glob_query, key_heads, value_heads, glob_seg, seg_all, glob_grad, global_lse),
    )
    grad_query = grad_query.at[:, :, :GLOBALS].add(
        glob_dq.reshape(seq_count, H, GLOBALS, BLOCK, HD)
    )
    grad_key_picked = (
        jnp.einsum(
            "shbqk,shbqd->shbkd", grad_scores, query_heads, preferred_element_type=jnp.float32
        )
        * scaling
    )
    grad_value_picked = jnp.einsum(
        "shbqk,shbqd->shbkd", share_low, grad_sparse, preferred_element_type=jnp.float32
    )
    block_shape = (seq_count, H, local_blocks, cand_count, BLOCK, HD)
    key_grad_blocks = (
        jnp.zeros((seq_count, H, total_blocks, BLOCK, HD), jnp.float32)
        .at[:, head_index, candidates]
        .add(grad_key_picked.reshape(block_shape))
    )
    value_grad_blocks = (
        jnp.zeros((seq_count, H, total_blocks, BLOCK, HD), jnp.float32)
        .at[:, head_index, candidates]
        .add(grad_value_picked.reshape(block_shape))
    )
    key_grad_full = (
        (key_grad_blocks.reshape(seq_count, H, full_length, HD) + glob_dk)
        .transpose(0, 2, 1, 3)
        .reshape(seq_count, full_length, width)
    )
    value_grad_full = (
        (value_grad_blocks.reshape(seq_count, H, full_length, HD) + glob_dv)
        .transpose(0, 2, 1, 3)
        .reshape(seq_count, full_length, width)
    )
    key_grad, value_grad = (
        lax.psum_scatter(
            key_grad_full.astype(jnp.bfloat16), "shard", scatter_dimension=1, tiled=True
        ).astype(jnp.float32),
        lax.psum_scatter(
            value_grad_full.astype(jnp.bfloat16), "shard", scatter_dimension=1, tiled=True
        ).astype(jnp.float32),
    )
    query_grad = grad_query.transpose(0, 2, 3, 1, 4).reshape(seq_count, local_tokens, width)
    grad_proj = [
        query_grad.astype(jnp.bfloat16),
        key_grad.astype(jnp.bfloat16),
        value_grad.astype(jnp.bfloat16),
    ]
    input_grad = grad_branch + dense_backward(jnp.concatenate(grad_proj, axis=-1), qkv_back)
    for table_column in range(3):
        grad_adapt_in[table_column], grad_adapt_out[table_column], extra_grad = adapt_back(
            inputs,
            adapter_tables_input[table_column],
            adapter_tables_output[table_column],
            rank_parts[table_column],
            grad_proj[table_column],
        )
        input_grad = input_grad + extra_grad
    adapter_table_count = adapter_down_from_width.shape[1]
    grad_in_d = jnp.stack(
        [
            table_sum(
                grad_adapt_in[table_column],
                adapter_index_table[:, table_column],
                adapter_table_count,
            )
            for table_column in range(5)
        ],
        axis=0,
    )
    grad_in_f = table_sum(grad_adapt_in[5], adapter_index_table[:, 5], adapter_table_count)
    out_list = [
        table_sum(
            grad_adapt_out[table_column], adapter_index_table[:, table_column], adapter_table_count
        )
        for table_column in range(4)
    ]
    grad_out_d = jnp.stack(
        out_list + [table_sum(grad_adapt_out[5], adapter_index_table[:, 5], adapter_table_count)],
        axis=0,
    )
    grad_out_f = table_sum(grad_adapt_out[4], adapter_index_table[:, 4], adapter_table_count)
    owned = (
        lax.psum_scatter(
            grad_in_d.astype(jnp.bfloat16), "shard", scatter_dimension=3, tiled=True
        ).astype(jnp.float32),
        lax.psum_scatter(
            grad_in_f.astype(jnp.bfloat16), "shard", scatter_dimension=2, tiled=True
        ).astype(jnp.float32),
        lax.psum_scatter(
            grad_out_d.astype(jnp.bfloat16), "shard", scatter_dimension=3, tiled=True
        ).astype(jnp.float32),
        lax.psum_scatter(
            grad_out_f.astype(jnp.bfloat16), "shard", scatter_dimension=2, tiled=True
        ).astype(jnp.float32),
    )
    summed = (
        lax.psum(owned[0].astype(jnp.bfloat16), "dp").astype(jnp.float32),
        lax.psum(owned[1].astype(jnp.bfloat16), "dp").astype(jnp.float32),
        lax.psum(owned[2].astype(jnp.bfloat16), "dp").astype(jnp.float32),
        lax.psum(owned[3].astype(jnp.bfloat16), "dp").astype(jnp.float32),
    )
    return (layer_out, input_grad, summed[0], summed[1], summed[2], summed[3])


BF = jnp.bfloat16
F32 = jnp.float32
NT = (((1,), (1,)), ((), ()))
TN = (((0,), (0,)), ((), ()))
BIG = 1e30
RANK = 16
ANY = pl.ANY
VMEM = pltpu.VMEM
MEBI = 1024 * 1024
SMALL_COST = pl.CostEstimate(flops=1_000_000, bytes_accessed=100_000, transcendentals=0)


def mm(left, right):
    return jnp.dot(left, right, preferred_element_type=F32)


def mm_nt(left, right):
    return lax.dot_general(left, right, NT, preferred_element_type=F32)


def mm_tn(left, right):
    return lax.dot_general(left, right, TN, preferred_element_type=F32)


def whole(shape):
    return pl.BlockSpec(shape, lambda *_: (0,) * len(shape))


def away_pairs(dp_count, shard_count, step):
    pairs = []
    for chip in range(dp_count // 2):
        for k in range(2):
            for z in range(shard_count):
                m = (z & 1) ^ step
                source = (2 * chip + k) * shard_count + z
                target = (2 * chip + (z >> 1)) * shard_count + 2 * k + m
                pairs.append((source, target))
    return pairs


def swap_cores(value, dp_count):
    return lax.ppermute(value, "dp", [(i, i ^ 1) for i in range(dp_count)])


def swap_shards(value, shard_count, step):
    return lax.ppermute(value, "shard", [(i, i ^ step) for i in range(shard_count)])


def spread_over_chips(block, dp_count):
    others = [lax.ppermute(block, "dp", [(i, i ^ o) for i in range(dp_count)]) for o in range(2, dp_count, 2)]
    return [block] + others


def swap_chips(block, dp_count, offset):
    return lax.ppermute(block, "dp", [(i, i ^ offset) for i in range(dp_count)])


def spread_over_cores(blocks, dp_count):
    return [one for block in blocks for one in (block, swap_cores(block, dp_count))]


def spread_in_plane(block, dp_count):
    return spread_over_cores(spread_over_chips(block, dp_count), dp_count)


def join_kernel(meta, part0, part1, out_ref):
    for r, part in enumerate((part0, part1)):
        out_ref[(meta[0] & 1) ^ r] = part[...].astype(out_ref.dtype)


def join_parts(meta, parts, dtype):
    rows, width = parts[0].shape
    return pl.pallas_call(
        join_kernel,
        grid_spec=pltpu.PrefetchScalarGridSpec(
            num_scalar_prefetch=1,
            grid=(1,),
            in_specs=[whole((rows, width))] * 2,
            out_specs=whole((2, rows, width)),
        ),
        out_shape=jax.ShapeDtypeStruct((2, rows, width), dtype),
        compiler_params=pltpu.CompilerParams(vmem_limit_bytes=30 * MEBI),
        cost_estimate=SMALL_COST,
        name="join_parts",
    )(meta, *parts)


def send_away(parts, dp_count, shard_count):
    return [
        lax.ppermute(part, ("dp", "shard"), away_pairs(dp_count, shard_count, r))
        for r, part in enumerate(parts)
    ]


def weight_copies(meta, own_ref, pieces, dest, sems, places):
    z, d = meta[0], meta[1]
    own_rows, columns = own_ref.shape
    copies = [
        pltpu.make_async_copy(
            own_ref, dest.at[pl.ds(pl.multiple_of(z * own_rows, 16), own_rows)], sems.at[0]
        )
    ]
    count = 1
    for o, piece in enumerate(pieces):
        who = d ^ o
        for step in range(3):
            shard = z ^ (step + 1)
            for start, row, column, rows, cols in places(who):
                copies.append(
                    pltpu.make_async_copy(
                        piece.at[step, pl.ds(start, rows)],
                        dest.at[
                            pl.ds(pl.multiple_of(shard * own_rows + row, 16), rows),
                            pl.ds(pl.multiple_of(column, 128), cols),
                        ],
                        sems.at[count],
                    )
                )
                count += 1
    return copies


def qkv_places(who):
    return [(0, (who >> 1) * 48, (who & 1) * 1152, 48, 1152)]


def out_places(who):
    return [(0, (who >> 1) * 48, (who & 1) * 384, 48, 384)]


def up_places(who):
    return [(48, 0, who * 384, 192, 384)]


def down_places(who):
    return [(0, who * 96, 0, 96, 384), (96, who * 96, 384, 96, 384)]


def token_copies(meta, messages, dest, sems):
    copies = []
    for at, message in enumerate(messages):
        row = 512 * (at >> 1) + 256 * ((meta[0] & 1) ^ (at & 1))
        copies.append(
            pltpu.make_async_copy(
                message.at[pl.ds(0, 256)], dest.at[pl.ds(pl.multiple_of(row, 256), 256)], sems.at[at]
            )
        )
    return copies


def zero_padded(rows, position, count):
    zeros = jnp.zeros_like(rows)
    return jnp.concatenate([rows if i == position else zeros for i in range(count)], axis=0)


def qkv_kernel(meta, ids, *refs):
    messages, w_own, pieces = refs[0:4], refs[4], refs[5:13]
    ins, outs = refs[13:16], refs[16:19]
    q_ref, k_ref, v_ref, mask_ref, hot_ref, own_ref = refs[19:25]
    xs, segs, weight, wsems, xsems, ssems = refs[25:]
    copies = token_copies(meta, messages, xs, xsems)
    for at, message in enumerate(messages):
        copies.append(
            pltpu.make_async_copy(
                message.at[pl.ds(256, 16), pl.ds(0, 256)],
                segs.at[2 * (at >> 1) + ((meta[0] & 1) ^ (at & 1))],
                ssems.at[at],
            )
        )
    copies += weight_copies(meta, w_own, pieces, weight, wsems, qkv_places)
    for copy in copies:
        copy.start()
    for copy in copies:
        copy.wait()
    lane = lax.broadcasted_iota(jnp.int32, (128, 128), 1)
    lane_of_head = lax.rem(lane, 64)
    as_float = lane_of_head.astype(F32)
    is_segment = lane_of_head < 16
    row_block = lax.broadcasted_iota(jnp.int32, (128, 128), 0) // 64
    for place in range(4):
        row = segs[place].astype(F32)[0:1]
        for half in range(2):
            column = jnp.broadcast_to(row[:, 128 * half : 128 * half + 128], (128, 128)).T
            same = column == as_float
            block_lane = lane_of_head == 16 + 4 * place + 2 * half + row_block
            rows = slice(256 * place + 128 * half, 256 * place + 128 * half + 128)
            mask_ref[rows] = jnp.where(
                is_segment, jnp.where(same, 0.0, -BIG), jnp.where(block_lane, 1.0, 0.0)
            ).astype(BF)
            if place < 2:
                hot_ref[rows] = jnp.where(is_segment & same, 1.0, 0.0).astype(BF)
    own_ref[...] = xs[0:512]
    in_all = jnp.concatenate([ref[0, 0] for ref in ins], axis=0)
    out_all = [zero_padded(ref[0, 0], p, 3) for p, ref in enumerate(outs)]
    targets = (q_ref, k_ref, v_ref)
    for tile in range(4):
        rows = slice(256 * tile, 256 * tile + 256)
        x = xs[rows]
        rank = mm_nt(x, in_all).astype(BF)
        for p in range(0 if tile < 2 else 1, 3):
            value = mm(x, weight[:, 768 * p : 768 * p + 768]) + mm(rank, out_all[p])
            value = value.astype(BF)
            if p == 0:
                value = (value.astype(F32) * HD**-0.5).astype(BF)
            targets[p][rows] = value


def table_spec(p, column, width):
    return pl.BlockSpec((1, 1, RANK, width), lambda i, meta, ids: (p, ids[column], 0, 0))


def hidden_spec(column, width):
    return pl.BlockSpec((1, RANK, width), lambda i, meta, ids: (ids[column], 0, 0))


def any_specs(count):
    return [pl.BlockSpec(memory_space=ANY)] * count


def project_qkv(meta, ids, messages, w_own, pieces, table_in, table_out):
    width = w_own.shape[1] // 3
    return pl.pallas_call(
        qkv_kernel,
        grid_spec=pltpu.PrefetchScalarGridSpec(
            num_scalar_prefetch=2,
            grid=(1,),
            in_specs=any_specs(13)
            + [table_spec(p, p, width) for p in range(3)]
            + [table_spec(p, p, width) for p in range(3)],
            out_specs=[
                whole((512, width)),
                whole((1024, width)),
                whole((1024, width)),
                whole((1024, 128)),
                whole((512, 128)),
                whole((512, width)),
            ],
            scratch_shapes=[
                VMEM((1024, width), BF),
                VMEM((4, 16, 256), BF),
                VMEM((width, 3 * width), BF),
                pltpu.SemaphoreType.DMA((25,)),
                pltpu.SemaphoreType.DMA((4,)),
                pltpu.SemaphoreType.DMA((4,)),
            ],
        ),
        out_shape=[
            jax.ShapeDtypeStruct((512, width), BF),
            jax.ShapeDtypeStruct((1024, width), BF),
            jax.ShapeDtypeStruct((1024, width), BF),
            jax.ShapeDtypeStruct((1024, 128), BF),
            jax.ShapeDtypeStruct((512, 128), BF),
            jax.ShapeDtypeStruct((512, width), BF),
        ],
        compiler_params=pltpu.CompilerParams(vmem_limit_bytes=56 * MEBI),
        cost_estimate=SMALL_COST,
        name="project_qkv",
    )(meta, ids, *messages, w_own, *pieces, *([table_in] * 3), *([table_out] * 3))


def attend_kernel(q_ref, k_ref, v_ref, mask_ref, hot_ref, closed_ref, o_ref, p_ref):
    low = lax.broadcasted_iota(jnp.int32, (512, 128), 1) < 64
    low_keys = lax.broadcasted_iota(jnp.int32, (1024, 128), 1) < 64
    closed = jnp.concatenate(
        [jnp.broadcast_to(closed_ref[0, l : l + 1], (64, 128)) for l in range(8)], axis=0
    )
    extra = (hot_ref[...].astype(F32) + closed).astype(BF)
    q, k, v, masks = q_ref[...], k_ref[...], v_ref[...], mask_ref[...]
    wide = [(jnp.where(low, q, extra), jnp.where(low_keys, k, masks)), (jnp.where(low, extra, q), jnp.where(low_keys, masks, k))]
    size = 512
    units = [(start, head) for start in range(0, 512, size) for head in range(2)]
    raw = lambda unit: mm_nt(wide[unit[1]][0][unit[0] : unit[0] + size], wide[unit[1]][1])
    ahead = raw(units[0])
    mixed = {}
    for n, (start, head) in enumerate(units):
        scores = ahead
        if n + 1 < len(units):
            ahead = raw(units[n + 1])
        weights = jnp.exp(scores - jnp.max(scores, axis=1, keepdims=True))
        shares = (weights * (1.0 / jnp.sum(weights, axis=1, keepdims=True))).astype(BF)
        p_ref[head, start : start + size] = shares
        mixed[head] = mm(shares, v)
        if head == 1:
            o_ref[start : start + size] = jnp.where(low[0:size], mixed[0], mixed[1]).astype(BF)


def attend(q, k, v, masks, hot, closed):
    width = q.shape[1]
    pairs = width // 128
    half = pl.BlockSpec((512, 128), lambda g: (0, g))
    full = pl.BlockSpec((1024, 128), lambda g: (0, g))
    return pl.pallas_call(
        attend_kernel,
        grid=(pairs,),
        in_specs=[
            half,
            full,
            full,
            whole((1024, 128)),
            whole((512, 128)),
            pl.BlockSpec((1, 8, 128), lambda g: (g, 0, 0)),
        ],
        out_specs=[half, pl.BlockSpec((2, 512, 1024), lambda g: (g, 0, 0))],
        out_shape=[
            jax.ShapeDtypeStruct((512, width), BF),
            jax.ShapeDtypeStruct((2 * pairs, 512, 1024), BF),
        ],
        compiler_params=pltpu.CompilerParams(vmem_limit_bytes=56 * MEBI),
        cost_estimate=SMALL_COST,
        name="attend",
    )(q, k, v, masks, hot, closed)


def attend_back_kernel(q_ref, k_ref, v_ref, p_ref, grad_ref, mixed_ref, dq_ref, dk_own, dv_own, other_ref):
    low = lax.broadcasted_iota(jnp.int32, (512, 128), 1) < 64
    q, k, v, grad = q_ref[...], k_ref[...], v_ref[...], grad_ref[...]
    products = grad.astype(F32) * mixed_ref[...].astype(F32)
    q_turned, grad_turned = q.T, grad.T
    zeros, none = jnp.zeros_like(grad), jnp.zeros_like(products)
    dq, dk, dv = [], [], []
    for head in range(2):
        mine = low if head == 0 else jnp.logical_not(low)
        centre = jnp.sum(jnp.where(mine, products, none), axis=1, keepdims=True)
        grad_shares = mm_nt(jnp.where(mine, grad, zeros), v)
        shares = p_ref[head]
        grad_scores = (shares.astype(F32) * (grad_shares - centre)).astype(BF)
        rows = slice(64 * head, 64 * head + 64)
        dq.append(mm(grad_scores, k))
        dk.append(mm(q_turned[rows], grad_scores))
        dv.append(mm(grad_turned[rows], shares))
    dq_ref[...] = (jnp.where(low, dq[0], dq[1]) * HD**-0.5).astype(BF)
    dk = jnp.concatenate(dk, axis=0).T
    dv = jnp.concatenate(dv, axis=0).T
    dk_own[...] = dk[0:512]
    dv_own[...] = dv[0:512]
    other_ref[0] = dk[512:1024].astype(BF)
    other_ref[1] = dv[512:1024].astype(BF)


def attend_back(q, k, v, shares, grad, mixed):
    width = q.shape[1]
    half = pl.BlockSpec((512, 128), lambda g: (0, g))
    full = pl.BlockSpec((1024, 128), lambda g: (0, g))
    return pl.pallas_call(
        attend_back_kernel,
        grid=(width // 128,),
        in_specs=[half, full, full, pl.BlockSpec((2, 512, 1024), lambda g: (g, 0, 0)), half, half],
        out_specs=[half] * 3 + [pl.BlockSpec((2, 512, 128), lambda g: (0, 0, g))],
        out_shape=[
            jax.ShapeDtypeStruct((512, width), BF),
            jax.ShapeDtypeStruct((512, width), F32),
            jax.ShapeDtypeStruct((512, width), F32),
            jax.ShapeDtypeStruct((2, 512, width), BF),
        ],
        compiler_params=pltpu.CompilerParams(vmem_limit_bytes=56 * MEBI),
        cost_estimate=SMALL_COST,
        name="attend_back",
    )(q, k, v, shares, grad, mixed)


def gelu_and_slope(lifted):
    z = jnp.abs(lifted) * 0.7071067811865476
    t = 1.0 / (1.0 + 0.3275911 * z)
    poly = t * (
        0.254829592
        + t * (-0.284496736 + t * (1.421413741 + t * (-1.453152027 + t * 1.061405429)))
    )
    decay = jnp.exp(-z * z)
    tail = 0.5 * poly * decay
    below = jnp.where(lifted < 0.0, tail, 1.0 - tail)
    return lifted * below, below + lifted * (decay * 0.3989422804014327)


def norm_parts(hidden):
    average = jnp.mean(hidden, axis=-1, keepdims=True)
    centred = hidden - average
    spread = jnp.mean(centred * centred, axis=-1, keepdims=True)
    inverse = lax.rsqrt(spread + EPSILON)
    return centred * inverse, inverse


def norm_back(grad, gain, normal, inverse):
    scaled = grad * gain
    return inverse * (
        scaled
        - jnp.mean(scaled, axis=-1, keepdims=True)
        - normal * jnp.mean(scaled * normal, axis=-1, keepdims=True)
    )


MID_TILE = 256
MID_PARTS = 4


def first_half_kernel(meta, ids, *refs):
    out_own, up_own, up_pieces = refs[0], refs[1], refs[2:10]
    x_ref, mixed_ref, gain1, in3, in4, out3, out4 = refs[10:17]
    normal_ref, inverse_ref, active, slope = refs[17:21]
    w_out, w_up, osems, usems = refs[21:]
    out_copies = weight_copies(meta, out_own, up_pieces, w_out, osems, out_places)
    up_copies = weight_copies(meta, up_own, up_pieces, w_up, usems, up_places)
    is_first = pl.program_id(0) == 0

    @pl.when(is_first)
    def _():
        for copy in out_copies + up_copies:
            copy.start()
        for copy in out_copies:
            copy.wait()

    mixed = mixed_ref[...]
    rank3 = mm_nt(mixed, in3[0, 0]).astype(BF)
    branch = mm(mixed, w_out[...]) + mm(rank3, out3[0, 0])
    normal, inverse = norm_parts(x_ref[...].astype(F32) + branch)
    normal_ref[...] = normal
    inverse_ref[...] = jnp.broadcast_to(inverse, inverse_ref.shape)
    low = (normal * gain1[...]).astype(BF)
    rank4 = mm_nt(low, in4[0, 0]).astype(BF)

    @pl.when(is_first)
    def _():
        for copy in up_copies:
            copy.wait()

    part = w_up.shape[1] // MID_PARTS
    for n in range(MID_PARTS):
        cols = slice(n * part, n * part + part)
        lifted = mm(low, w_up[:, cols]) + mm(rank4, out4[0, :, cols])
        value, tangent = gelu_and_slope(lifted)
        active[:, cols] = value.astype(BF)
        slope[:, cols] = tangent.astype(BF)


def first_half(meta, ids, out_own, up_own, up_pieces, x, mixed, gain1, table_in, table_out, table_out_hidden):
    width, hidden = x.shape[1], up_own.shape[1]
    tile = lambda columns: pl.BlockSpec((MID_TILE, columns), lambda i, *_: (i, 0))
    return pl.pallas_call(
        first_half_kernel,
        grid_spec=pltpu.PrefetchScalarGridSpec(
            num_scalar_prefetch=2,
            grid=(512 // MID_TILE,),
            in_specs=any_specs(10)
            + [
                tile(width),
                tile(width),
                whole((1, width)),
                table_spec(3, 3, width),
                table_spec(4, 4, width),
                table_spec(3, 3, width),
                hidden_spec(4, hidden),
            ],
            out_specs=[tile(width), tile(128), tile(hidden), tile(hidden)],
            scratch_shapes=[
                VMEM((width, width), BF),
                VMEM((width, hidden), BF),
                pltpu.SemaphoreType.DMA((25,)),
                pltpu.SemaphoreType.DMA((25,)),
            ],
        ),
        out_shape=[
            jax.ShapeDtypeStruct((512, width), F32),
            jax.ShapeDtypeStruct((512, 128), F32),
            jax.ShapeDtypeStruct((512, hidden), BF),
            jax.ShapeDtypeStruct((512, hidden), BF),
        ],
        compiler_params=pltpu.CompilerParams(vmem_limit_bytes=56 * MEBI),
        cost_estimate=SMALL_COST,
        name="first_half",
    )(meta, ids, out_own, up_own, *up_pieces, x, mixed, gain1, table_in, table_in, table_out, table_out_hidden)


def second_half_kernel(meta, ids, *refs):
    cots, out_own, up_own, down_own = refs[0:2], refs[2], refs[3], refs[4]
    up_pieces, down_pieces = refs[5:13], refs[13:21]
    normal_ref, inverse_ref, active, slope, mixed_ref = refs[21:26]
    gain1, gain2, in3, in4, in5, out3, out4, out5 = refs[26:34]
    layer_parts, grad_branch_ref, grad_mixed_ref, grad_parts = refs[34:36], refs[36], refs[37], refs[38:42]
    (
        cot, w_out, w_up, w_down, layer,
        s_in3, s_in4, s_in5, s_out3, s_out4, s_out5, gathered,
        osems, usems, dsems, xsems,
    ) = refs[42:]
    tile = pl.program_id(0)
    is_first = tile == 0
    near = token_copies(meta, cots, cot, xsems)
    out_copies = weight_copies(meta, out_own, up_pieces, w_out, osems, out_places)
    up_copies = weight_copies(meta, up_own, up_pieces, w_up, usems, up_places)
    down_copies = weight_copies(meta, down_own, down_pieces, w_down, dsems, down_places)

    @pl.when(is_first)
    def _():
        for copy in down_copies + near + up_copies + out_copies:
            copy.start()
        for ref in (s_in3, s_in4, s_in5, s_out3, s_out4, s_out5):
            ref[...] = jnp.zeros_like(ref)
        for copy in down_copies + near:
            copy.wait()

    part = w_up.shape[1] // MID_PARTS
    a_in3, a_in4, a_out3, a_out5 = in3[0, 0], in4[0, 0], out3[0, 0], out5[0, 0]
    rows = pl.ds(pl.multiple_of(tile * MID_TILE, MID_TILE), MID_TILE)
    normal1 = normal_ref[...]
    inverse1 = inverse_ref[:, 0:1]
    first = normal1 * gain1[...]
    low1 = first.astype(BF)
    r4 = mm_nt(low1, a_in4).astype(BF)
    r5 = mm_nt(active[...], in5[0]).astype(BF)
    lowered = first + mm(active[...], w_down[...]) + mm(r5, a_out5)
    normal2, inverse2 = norm_parts(lowered)
    layer[rows, :] = (normal2 * gain2[...]).astype(BF)
    grad_sum = norm_back(cot[rows, :].astype(F32), gain2[...], normal2, inverse2)
    e5 = grad_sum.astype(BF)
    rg5 = mm_nt(e5, a_out5).astype(BF)
    s_out5[...] += mm_tn(r5, e5)

    @pl.when(is_first)
    def _():
        for copy in up_copies + out_copies:
            copy.wait()

    grad_first = grad_sum
    rg4 = jnp.zeros((MID_TILE, RANK), F32)
    for n in range(MID_PARTS):
        cols = slice(n * part, n * part + part)
        grad_active = mm_nt(e5, w_down[cols, :]) + mm(rg5, in5[0, :, cols])
        e4 = (slope[:, cols].astype(F32) * grad_active).astype(BF)
        s_in5[:, cols] += mm_tn(rg5, active[:, cols])
        s_out4[:, cols] += mm_tn(r4, e4)
        grad_first = grad_first + mm_nt(e4, w_up[:, cols])
        rg4 = rg4 + mm_nt(e4, out4[0, :, cols])
    rg4 = rg4.astype(BF)
    s_in4[...] += mm_tn(rg4, low1)
    grad_first = grad_first + mm(rg4, a_in4)
    grad_branch = norm_back(grad_first, gain1[...], normal1, inverse1)
    grad_branch_ref[...] = grad_branch
    e3 = grad_branch.astype(BF)
    mixed = mixed_ref[...]
    rank3 = mm_nt(mixed, a_in3).astype(BF)
    rg3 = mm_nt(e3, a_out3).astype(BF)
    s_out3[...] += mm_tn(rank3, e3)
    s_in3[...] += mm_tn(rg3, mixed)
    grad_mixed_ref[...] = (mm_nt(e3, w_out[...]) + mm(rg3, a_in3)).astype(BF)

    @pl.when(tile == 512 // MID_TILE - 1)
    def _():
        wide, narrow = 768, 192
        for owner in range(4):
            start = 0
            for ref, size in (
                (s_in5, wide), (s_out4, wide), (s_in3, narrow), (s_in4, narrow), (s_out3, narrow), (s_out5, narrow),
            ):
                row, column = 16 * (start // 768), start % 768
                gathered[owner, row : row + 16, column : column + size] = ref[:, owner * size : owner * size + size]
                start += size
        lane = lax.broadcasted_iota(jnp.int32, (16, 128), 1)
        id_rows = jnp.zeros((16, 128), F32)
        for p in range(6):
            id_rows = jnp.where(lane == p, ids[p].astype(F32), id_rows)
        for r, ref in enumerate(layer_parts):
            ref[...] = layer[pl.ds(pl.multiple_of(256 * ((meta[0] & 1) ^ r), 256), 256), :]
        for r, ref in enumerate(grad_parts):
            ref[0:48] = gathered[meta[0] ^ r].astype(BF)
            ref[48:64] = jnp.zeros((16, 768), BF)
            ref[48:64, 0:128] = id_rows.astype(BF)


def second_half(meta, ids, cots, out_own, up_own, down_own, up_pieces, down_pieces, normal, inverse, active, slope,
                mixed, gain1, gain2, table_in, table_in_hidden, table_out, table_out_hidden):
    width, hidden = normal.shape[1], up_own.shape[1]
    tile = lambda columns: pl.BlockSpec((MID_TILE, columns), lambda i, *_: (i, 0))
    return pl.pallas_call(
        second_half_kernel,
        grid_spec=pltpu.PrefetchScalarGridSpec(
            num_scalar_prefetch=2,
            grid=(512 // MID_TILE,),
            in_specs=any_specs(21)
            + [
                tile(width),
                tile(128),
                tile(hidden),
                tile(hidden),
                tile(width),
                whole((1, width)),
                whole((1, width)),
                table_spec(3, 3, width),
                table_spec(4, 4, width),
                hidden_spec(5, hidden),
                table_spec(3, 3, width),
                hidden_spec(4, hidden),
                table_spec(4, 5, width),
            ],
            out_specs=[whole((256, width))] * 2 + [tile(width), tile(width)] + [whole((64, width))] * 4,
            scratch_shapes=[
                VMEM((512, width), BF),
                VMEM((width, width), BF),
                VMEM((width, hidden), BF),
                VMEM((hidden, width), BF),
                VMEM((512, width), BF),
                VMEM((RANK, width), F32),
                VMEM((RANK, width), F32),
                VMEM((RANK, hidden), F32),
                VMEM((RANK, width), F32),
                VMEM((RANK, hidden), F32),
                VMEM((RANK, width), F32),
                VMEM((4, 3 * RANK, 768), F32),
                pltpu.SemaphoreType.DMA((25,)),
                pltpu.SemaphoreType.DMA((25,)),
                pltpu.SemaphoreType.DMA((49,)),
                pltpu.SemaphoreType.DMA((2,)),
            ],
        ),
        out_shape=[jax.ShapeDtypeStruct((256, width), BF)] * 2
        + [jax.ShapeDtypeStruct((512, width), F32), jax.ShapeDtypeStruct((512, width), BF)]
        + [jax.ShapeDtypeStruct((64, width), BF)] * 4,
        compiler_params=pltpu.CompilerParams(vmem_limit_bytes=56 * MEBI),
        cost_estimate=SMALL_COST,
        name="second_half",
    )(meta, ids, *cots, out_own, up_own, down_own, *up_pieces, *down_pieces, normal, inverse, active, slope, mixed,
      gain1, gain2, table_in, table_in, table_in_hidden, table_out, table_out_hidden, table_out)


def first_grads_kernel(meta, ids, *refs):
    xs, dq_ref, dk_ref, dv_ref, got_ref = refs[0:5]
    ins, outs = refs[5:8], refs[8:11]
    grads_ref, rank_grad_ref = refs[11:13]
    gs = refs[13:17]
    s_in, s_out, gathered = refs[17:]
    in_all = jnp.concatenate([ref[0, 0] for ref in ins], axis=0)
    out_all = jnp.concatenate([zero_padded(ref[0, 0], p, 3) for p, ref in enumerate(outs)], axis=1)
    for tile in range(2):
        rows = slice(256 * tile, 256 * tile + 256)
        grads = jnp.concatenate(
            [dq_ref[rows]]
            + [(ref[rows] + got_ref[n, rows].astype(F32)).astype(BF) for n, ref in enumerate((dk_ref, dv_ref))],
            axis=1,
        )
        grads_ref[rows] = grads
        x = xs[rows]
        rank = mm_nt(x, in_all).astype(BF)
        rank_grad = mm_nt(grads, out_all).astype(BF)
        rank_grad_ref[rows] = rank_grad
        part_in, part_out = mm_tn(rank_grad, x), mm_tn(rank, grads)
        if tile == 0:
            s_in[...] = part_in
            s_out[...] = part_out
        else:
            s_in[...] += part_in
            s_out[...] += part_out
    for owner in range(4):
        for p in range(3):
            rows = slice(RANK * p, RANK * p + RANK)
            gathered[owner, :, 192 * p : 192 * p + 192] = s_in[rows, 192 * owner : 192 * owner + 192]
            gathered[owner, :, 192 * (3 + p) : 192 * (4 + p)] = s_out[
                rows, 768 * p + 192 * owner : 768 * p + 192 * owner + 192
            ]
    for r, ref in enumerate(gs):
        ref[...] = gathered[meta[0] ^ r].astype(BF)


def first_grads(meta, ids, x, dq, dk, dv, got, table_in, table_out):
    width = x.shape[1]
    return pl.pallas_call(
        first_grads_kernel,
        grid_spec=pltpu.PrefetchScalarGridSpec(
            num_scalar_prefetch=2,
            grid=(1,),
            in_specs=[whole((512, width))] * 4
            + [whole((2, 512, width))]
            + [table_spec(p, p, width) for p in range(3)] * 2,
            out_specs=[whole((512, 3 * width)), whole((512, 3 * RANK))] + [whole((RANK, 1152))] * 4,
            scratch_shapes=[
                VMEM((3 * RANK, width), F32),
                VMEM((3 * RANK, 3 * width), F32),
                VMEM((4, RANK, 1152), F32),
            ],
        ),
        out_shape=[jax.ShapeDtypeStruct((512, 3 * width), BF), jax.ShapeDtypeStruct((512, 3 * RANK), BF)]
        + [jax.ShapeDtypeStruct((RANK, 1152), BF)] * 4,
        compiler_params=pltpu.CompilerParams(vmem_limit_bytes=30 * MEBI),
        cost_estimate=SMALL_COST,
        name="first_grads",
    )(meta, ids, x, dq, dk, dv, got, *([table_in] * 3), *([table_out] * 3))


def input_grad_kernel(meta, ids, *refs):
    w_own, pieces = refs[0], refs[1:9]
    branch_ref, grads_ref, rank_grad_ref = refs[9:12]
    ins, parts = refs[12:15], refs[15:17]
    weight, wsems = refs[17:]
    copies = weight_copies(meta, w_own, pieces, weight, wsems, qkv_places)
    for copy in copies:
        copy.start()
    for copy in copies:
        copy.wait()
    in_all = jnp.concatenate([ref[0, 0] for ref in ins], axis=0)
    for r, ref in enumerate(parts):
        rows = pl.ds(pl.multiple_of(256 * ((meta[0] & 1) ^ r), 256), 256)
        ref[...] = (
            branch_ref[rows, :] + mm_nt(grads_ref[rows, :], weight[...]) + mm(rank_grad_ref[rows, :], in_all)
        ).astype(BF)


def project_back(meta, ids, w_own, pieces, branch, grads, rank_grad, table_in):
    width = branch.shape[1]
    return pl.pallas_call(
        input_grad_kernel,
        grid_spec=pltpu.PrefetchScalarGridSpec(
            num_scalar_prefetch=2,
            grid=(1,),
            in_specs=any_specs(9)
            + [whole((512, width)), whole((512, 3 * width)), whole((512, 3 * RANK))]
            + [table_spec(p, p, width) for p in range(3)],
            out_specs=[whole((256, width))] * 2,
            scratch_shapes=[VMEM((width, 3 * width), BF), pltpu.SemaphoreType.DMA((25,))],
        ),
        out_shape=[jax.ShapeDtypeStruct((256, width), BF)] * 2,
        compiler_params=pltpu.CompilerParams(vmem_limit_bytes=30 * MEBI),
        cost_estimate=SMALL_COST,
        name="project_back",
    )(meta, ids, w_own, *pieces, branch, grads, rank_grad, *([table_in] * 3))


def combine_middle_kernel(ids, own, other, in_d, in_f, out_d, out_f):
    for ref in (in_d, in_f, out_d, out_f):
        ref[...] = jnp.zeros_like(ref)
    narrow = in_d.shape[-1]
    for chip in range(4):
        for r in range(4):
            chosen = [ids[(chip * 4 + r) * 6 + p] for p in range(3, 6)]
            part = own[chip, r].astype(F32) + other[chip, r].astype(F32)
            in_f[chosen[2]] += part[0:16]
            out_f[chosen[1]] += part[16:32]
            for at, (ref, p, which) in enumerate(
                ((in_d, 3, 0), (in_d, 4, 1), (out_d, 3, 0), (out_d, 4, 2))
            ):
                ref[p, chosen[which]] += part[32:48, narrow * at : narrow * at + narrow]


def combine_middle(ids, own, other, tables, narrow, wide):
    shapes = [(5, tables, RANK, narrow), (tables, RANK, wide)] * 2
    return pl.pallas_call(
        combine_middle_kernel,
        grid_spec=pltpu.PrefetchScalarGridSpec(
            num_scalar_prefetch=1,
            grid=(1,),
            in_specs=[whole(own.shape)] * 2,
            out_specs=[whole(shape) for shape in shapes],
        ),
        out_shape=[jax.ShapeDtypeStruct(shape, F32) for shape in shapes],
        compiler_params=pltpu.CompilerParams(vmem_limit_bytes=30 * MEBI),
        cost_estimate=SMALL_COST,
        name="combine_middle",
    )(ids, own, other)


def combine_first_kernel(ids, own, other, in_before, out_before, in_d, out_d):
    narrow = in_d.shape[-1]
    for ref, before in ((in_d, in_before), (out_d, out_before)):
        ref[0:3] = jnp.zeros((3, *ref.shape[1:]), F32)
        ref[3:5] = before[3:5]
    for chip in range(4):
        for r in range(4):
            part = own[chip, r].astype(F32) + other[chip, r].astype(F32)
            for p in range(3):
                chosen = ids[(chip * 4 + r) * 6 + p]
                in_d[p, chosen] += part[:, narrow * p : narrow * p + narrow]
                out_d[p, chosen] += part[:, narrow * (3 + p) : narrow * (4 + p)]


def combine_first(ids, own, other, in_d, out_d):
    return pl.pallas_call(
        combine_first_kernel,
        grid_spec=pltpu.PrefetchScalarGridSpec(
            num_scalar_prefetch=1,
            grid=(1,),
            in_specs=[whole(own.shape)] * 2 + [whole(in_d.shape)] * 2,
            out_specs=[whole(in_d.shape)] * 2,
        ),
        out_shape=[jax.ShapeDtypeStruct(in_d.shape, F32)] * 2,
        compiler_params=pltpu.CompilerParams(vmem_limit_bytes=30 * MEBI),
        cost_estimate=SMALL_COST,
        name="combine_first",
    )(ids, own, other, in_d, out_d)


def after(value, *others):
    return lax.optimization_barrier((value, *others))[0]


def beside(work, transfers, values, moved):
    given = lax.optimization_barrier((tuple(values), tuple(moved)))
    return lax.optimization_barrier((tuple(work(*given[0])), tuple(transfers(*given[1]))))


def paired_body(
    inputs,
    segments,
    random_key_blocks,
    adapter_index_table,
    frozen_query_key_value_weight,
    frozen_output_weight,
    frozen_up_weight,
    frozen_down_weight,
    attention_norm_gain,
    feedforward_norm_gain,
    adapter_down_from_width,
    adapter_down_from_hidden,
    adapter_up_to_width,
    adapter_up_to_hidden,
    cotangent,
):
    dp_count, shard_count = lax.axis_size("dp"), lax.axis_size("shard")
    d, z = lax.axis_index("dp"), lax.axis_index("shard")
    core = d & 1
    meta = jnp.stack([z, d]).astype(jnp.int32)

    def piece(weight, rows, columns, row, column):
        return lax.dynamic_slice(weight, (row, column), (rows, columns))

    def fetch(part):
        return [swap_shards(part, shard_count, step) for step in range(1, shard_count)]

    def slices(values):
        return [lax.dynamic_index_in_dim(values, (z & 1) ^ r, 0, keepdims=False) for r in range(2)]

    def chips(block, *offsets):
        return [swap_chips(block, dp_count, offset) for offset in offsets]

    def swap(block):
        return swap_cores(block, dp_count)

    qkv_own = jnp.stack(fetch(piece(frozen_query_key_value_weight, 48, 1152, (d >> 1) * 48, core * 1152)))
    up_piece = jnp.concatenate(
        [
            piece(frozen_output_weight, 48, 384, (d >> 1) * 48, core * 384),
            piece(frozen_up_weight, 192, 384, 0, d * 384),
        ],
        axis=0,
    )
    up_own = jnp.stack(fetch(up_piece))
    down_piece = piece(frozen_down_weight, 96, 768, d * 96, 0)
    down_piece = jnp.concatenate([down_piece[:, 0:384], down_piece[:, 384:768]], axis=0)
    qkv_x, qkv_y = chips(qkv_own, 2, 4)
    seg_rows = jnp.pad(segments.astype(BF)[:, None, :], ((0, 0), (0, 15), (0, inputs.shape[-1] - 256)))
    own = send_away(
        slices(after(jnp.concatenate([inputs, seg_rows], axis=1), up_own)), dp_count, shard_count
    )
    tokens = own + [swap(part) for part in own]
    (qkv_xy,) = chips(qkv_x, 4)
    qkv_pieces = spread_over_cores((qkv_own, qkv_x, qkv_y, qkv_xy), dp_count)
    up_x, up_y = chips(up_own, 2, 4)
    there = swap_cores(adapter_index_table, dp_count)
    column_ids = jnp.where(
        core == 0,
        jnp.concatenate([adapter_index_table, there], axis=0),
        jnp.concatenate([there, adapter_index_table], axis=0),
    )
    ids = lax.dynamic_index_in_dim(column_ids, z, 0, keepdims=False)

    blocks = jnp.arange(16, dtype=jnp.int32)
    query_block = (8 * core + blocks[0:8])[None, :, None]
    key_block = jnp.where(blocks < 8, 8 * core + blocks, 8 * (1 - core) + blocks - 8)[None, None, :]
    drawn = lax.dynamic_slice_in_dim(random_key_blocks, 8 * core, 8, axis=1)
    allowed = (jnp.abs(query_block - key_block) <= 1) | (query_block < GLOBALS) | (key_block < GLOBALS)
    for n in range(RANDOMS):
        allowed = allowed | (drawn[:, :, n : n + 1] == key_block)
    closed = jnp.pad(jnp.where(allowed, 0.0, -BIG), ((0, 0), (0, 0), (16, 32)))
    closed = closed.reshape(H // 2, 2, 8, 64)
    closed = jnp.concatenate([closed[:, 1], closed[:, 0]], axis=-1)

    def work(*given):
        return project_qkv(
            meta, ids, given[0:4], frozen_query_key_value_weight, given[4:],
            adapter_down_from_width, adapter_up_to_width,
        )

    (q, k, v, masks, hot, x), (up_xy, up_there, *down_own) = beside(
        work,
        lambda up_own, up_x, up_y, part: (*chips(up_x, 4), swap(up_own), *fetch(part)),
        (*tokens, *qkv_pieces),
        (up_own, up_x, up_y, down_piece),
    )
    down_own = jnp.stack(down_own)
    (mixed, shares), (down_x, down_y, *others) = beside(
        lambda *given: attend(*given, closed),
        lambda block, *ups: (*chips(block, 2, 4), *(swap(up) for up in ups)),
        (q, k, v, masks, hot),
        (down_own, up_x, up_y, up_xy),
    )
    up_pieces = (up_own, up_there, up_x, others[0], up_y, others[1], up_xy, others[2])
    gain1, gain2 = attention_norm_gain[None], feedforward_norm_gain[None]

    def work(mixed, *pieces):
        return first_half(
            meta, ids, frozen_output_weight, frozen_up_weight, pieces, x, mixed, gain1,
            adapter_down_from_width, adapter_up_to_width, adapter_up_to_hidden,
        )

    (normal, inverse, active, slope), (down_xy, cot_a, cot_b, down_there, down_x_there) = beside(
        work,
        lambda own, down_x, values: (
            *chips(down_x, 4), *send_away(slices(values), dp_count, shard_count), swap(own), swap(down_x)
        ),
        (mixed, *up_pieces),
        (down_own, down_x, cotangent),
    )
    down_pieces = (down_own, down_there, down_x, down_x_there, down_y, swap(down_y), down_xy, swap(down_xy))
    cots = (cot_a, cot_b)
    results = second_half(
        meta, ids, cots, frozen_output_weight, frozen_up_weight, frozen_down_weight, up_pieces, down_pieces,
        normal, inverse, active, slope, mixed, gain1, gain2,
        adapter_down_from_width, adapter_down_from_hidden, adapter_up_to_width, adapter_up_to_hidden,
    )
    grad_branch = results[2]

    def home(r, part):
        return lax.ppermute(part, ("dp", "shard"), away_pairs(dp_count, shard_count, r))

    def swap_over_shards(*parts):
        return [swap_shards(part, shard_count, step + 1) for step, part in enumerate(parts)]

    (dq, dk, dv, other_sums), (layer_a, *moved) = beside(
        lambda grad: attend_back(q, k, v, shares, grad, mixed),
        lambda part, *parts: (home(0, part), *swap_over_shards(*parts)),
        (results[3],),
        (results[0], *results[5:8]),
    )
    messages = jnp.stack([results[4], *moved])

    (grads, rank_grad, *first_parts), (layer_b, message_x, message_y) = beside(
        lambda other_sums: first_grads(
            meta, ids, x, dq, dk, dv, swap(other_sums), adapter_down_from_width, adapter_up_to_width
        ),
        lambda part, block: (home(1, part), *chips(block, 2, 4)),
        (other_sums,),
        (results[1], messages),
    )
    input_parts, (message_xy, *moved) = beside(
        lambda grads: project_back(
            meta, ids, frozen_query_key_value_weight, qkv_pieces, grad_branch, grads, rank_grad,
            adapter_down_from_width,
        ),
        lambda block, *parts: (*chips(block, 4), *swap_over_shards(*parts)),
        (grads,),
        (message_x, *first_parts[1:]),
    )
    firsts = jnp.stack([first_parts[0], *moved])

    (blocks,), (part_a, others, *firsts_got) = beside(
        lambda *blocks: blocks,
        lambda part, blocks, block: (home(0, part), swap(blocks), *chips(block, 2, 4, 6)),
        (jnp.stack([messages, message_x, message_y, message_xy]),),
        (input_parts[0], jnp.stack([messages, message_x, message_y, message_xy]), firsts),
    )

    def work(blocks, others, firsts, layer_a, layer_b):
        chosen = blocks[:, :, 48, 0:6].astype(jnp.int32).reshape(-1)
        layer_out = join_parts(meta, (layer_a, layer_b), BF)
        in_d, in_f, out_d, out_f = combine_middle(
            chosen, blocks, others, adapter_down_from_width.shape[1], 192, 768
        )
        in_d, out_d = combine_first(chosen, firsts, swap(firsts), in_d, out_d)
        return layer_out, in_d, in_f, out_d, out_f

    (layer_out, in_d, in_f, out_d, out_f), (part_b,) = beside(
        work,
        lambda part: (home(1, part),),
        (blocks, others, jnp.stack([firsts, *firsts_got]), layer_a, layer_b),
        (input_parts[1],),
    )
    return (layer_out, join_parts(meta, (part_a, part_b), F32), in_d, in_f, out_d, out_f)


def solution(mesh):
    dp_count, shard_count = mesh.shape["dp"], mesh.shape["shard"]
    paired = dp_count == 8 and shard_count == 4
    return jax.shard_map(
        paired_body if paired else general_body,
        mesh=mesh,
        in_specs=(
            P("dp", "shard", None),
            P("dp", "shard"),
            P(),
            P("dp", None),
            P("shard", None),
            P("shard", None),
            P("shard", None),
            P("shard", None),
            P(),
            P(),
            P(),
            P(),
            P(),
            P(),
            P("dp", "shard", None),
        ),
        out_specs=(
            P("dp", "shard", None),
            P("dp", "shard", None),
            P(None, None, None, "shard"),
            P(None, None, "shard"),
            P(None, None, None, "shard"),
            P(None, None, "shard"),
        ),
        check_vma=False,
    )
```

```python
import functools

import jax
import jax.numpy as jnp
from jax import lax
from jax.experimental import pallas as pl
from jax.experimental.pallas import tpu as pltpu
from jax.sharding import PartitionSpec as P

H = 12
HD = 64
BLOCK = 64
GLOBALS = 2
RANDOMS = 3


EPSILON = 1e-06
NEGATIVE = -1e30


def norm_rows(hidden, gain_vector):
    average = jnp.mean(hidden, axis=-1, keepdims=True)
    centred = hidden - average
    spread = jnp.mean(centred * centred, axis=-1, keepdims=True)
    return centred * lax.rsqrt(spread + EPSILON) * gain_vector


def gelu_exact(values):
    return jax.nn.gelu(values, approximate=False)


def dense_forward(inputs, weight):
    return jnp.einsum("sti,io->sto", inputs, weight, preferred_element_type=jnp.float32)


def dense_backward(grad_low, weight):
    return jnp.einsum("sto,io->sti", grad_low, weight, preferred_element_type=jnp.float32)


def adapt(inputs, down_rows, up_rows):
    rank_part = jnp.einsum(
        "sti,sri->str", inputs, down_rows, preferred_element_type=jnp.float32
    ).astype(jnp.bfloat16)
    return (
        rank_part,
        jnp.einsum("str,sro->sto", rank_part, up_rows, preferred_element_type=jnp.float32),
    )


def adapt_back(inputs, down_rows, up_rows, rank_part, grad_low):
    grad_up = jnp.einsum("str,sto->sro", rank_part, grad_low, preferred_element_type=jnp.float32)
    rank_grad = jnp.einsum(
        "sto,sro->str", grad_low, up_rows, preferred_element_type=jnp.float32
    ).astype(jnp.bfloat16)
    grad_down = jnp.einsum("str,sti->sri", rank_grad, inputs, preferred_element_type=jnp.float32)
    grad_inputs = jnp.einsum(
        "str,sri->sti", rank_grad, down_rows, preferred_element_type=jnp.float32
    )
    return (grad_down, grad_up, grad_inputs)


def table_sum(per_sequence, chosen, table_size):
    matches = (chosen[:, None] == jnp.arange(table_size, dtype=jnp.int32)[None, :]).astype(
        jnp.float32
    )
    return jnp.sum(matches[:, :, None, None] * per_sequence[:, None], axis=0)


def sparse_scores(query_heads, key_picked, permit, scaling):
    scores = (
        jnp.einsum(
            "shbqd,shbkd->shbqk", query_heads, key_picked, preferred_element_type=jnp.float32
        )
        * scaling
    )
    return jnp.where(permit, scores, NEGATIVE)


def global_scores(query_rows, key_rows, seg_query, seg_keys, scaling):
    scores = (
        jnp.einsum("hqd,hkd->hqk", query_rows, key_rows, preferred_element_type=jnp.float32)
        * scaling
    )
    return jnp.where((seg_query[:, None] == seg_keys[None, :])[None], scores, NEGATIVE)


def global_forward(query_rows, key_rows, value_rows, seg_query, seg_keys, scaling):
    scores = global_scores(query_rows, key_rows, seg_query, seg_keys, scaling)
    top_score = jnp.max(scores, axis=-1, keepdims=True)
    weights = jnp.exp(scores - top_score)
    totals = jnp.sum(weights, axis=-1, keepdims=True)
    shares = (weights / totals).astype(jnp.bfloat16)
    attended = jnp.einsum("hqk,hkd->hqd", shares, value_rows, preferred_element_type=jnp.float32)
    return (attended, (top_score + jnp.log(totals))[..., 0])


def global_backward(
    query_rows, key_rows, value_rows, seg_query, seg_keys, grad_rows, log_total, scaling
):
    scores = global_scores(query_rows, key_rows, seg_query, seg_keys, scaling)
    shares = jnp.exp(scores - log_total[..., None])
    share_low = shares.astype(jnp.bfloat16)
    grad_shares = jnp.einsum(
        "hqd,hkd->hqk", grad_rows, value_rows, preferred_element_type=jnp.float32
    )
    centre = jnp.sum(shares * grad_shares, axis=-1, keepdims=True)
    grad_scores = (shares * (grad_shares - centre)).astype(jnp.bfloat16)
    grad_query = (
        jnp.einsum("hqk,hkd->hqd", grad_scores, key_rows, preferred_element_type=jnp.float32)
        * scaling
    )
    grad_keys = (
        jnp.einsum("hqk,hqd->hkd", grad_scores, query_rows, preferred_element_type=jnp.float32)
        * scaling
    )
    grad_values = jnp.einsum(
        "hqk,hqd->hkd", share_low, grad_rows, preferred_element_type=jnp.float32
    )
    return (grad_query, grad_keys, grad_values, centre[..., 0])


def general_body(
    inputs,
    segments,
    random_key_blocks,
    adapter_index_table,
    frozen_query_key_value_weight,
    frozen_output_weight,
    frozen_up_weight,
    frozen_down_weight,
    attention_norm_gain,
    feedforward_norm_gain,
    adapter_down_from_width,
    adapter_down_from_hidden,
    adapter_up_to_width,
    adapter_up_to_hidden,
    cotangent,
):
    seq_count = inputs.shape[0]
    local_tokens = inputs.shape[1]
    width = inputs.shape[2]
    shard_count = lax.axis_size("shard")
    full_length = local_tokens * shard_count
    total_blocks = full_length // BLOCK
    local_blocks = local_tokens // BLOCK
    cand_count = 3 + GLOBALS + RANDOMS
    glob_rows = GLOBALS * BLOCK
    scaling = HD ** (-0.5)

    def select_adapter_table(table, table_column):
        return jnp.take(table, adapter_index_table[:, table_column], axis=0)

    adapter_tables_input = [
        select_adapter_table(adapter_down_from_width[table_column], table_column)
        for table_column in range(5)
    ] + [select_adapter_table(adapter_down_from_hidden, 5)]
    adapter_tables_output = [
        select_adapter_table(adapter_up_to_width[table_column], table_column)
        for table_column in range(4)
    ]
    adapter_tables_output = adapter_tables_output + [
        select_adapter_table(adapter_up_to_hidden, 4),
        select_adapter_table(adapter_up_to_width[4], 5),
    ]
    qkv_full, out_full = (
        lax.all_gather(frozen_query_key_value_weight, "shard", axis=0, tiled=True),
        lax.all_gather(frozen_output_weight, "shard", axis=0, tiled=True),
    )
    main_part = dense_forward(inputs, qkv_full)
    rank_parts = []
    projected = []
    for table_column in range(3):
        rank_part, extra = adapt(
            inputs, adapter_tables_input[table_column], adapter_tables_output[table_column]
        )
        rank_parts.append(rank_part)
        projected.append(
            (main_part[..., table_column * width : (table_column + 1) * width] + extra).astype(
                jnp.bfloat16
            )
        )
    seg_low = segments.astype(jnp.bfloat16)
    key_all, value_all, seg_all = (
        lax.all_gather(projected[1], "shard", axis=1, tiled=True),
        lax.all_gather(projected[2], "shard", axis=1, tiled=True),
        lax.all_gather(seg_low, "shard", axis=1, tiled=True),
    )
    shard_pos = lax.axis_index("shard")
    is_first = shard_pos == 0
    first_block = shard_pos * local_blocks
    block_ids = first_block + jnp.arange(local_blocks, dtype=jnp.int32)
    rand_local = lax.dynamic_slice_in_dim(random_key_blocks, first_block, local_blocks, axis=1)
    window_part = jnp.stack([block_ids - 1, block_ids, block_ids + 1], axis=-1)
    global_ids = jnp.broadcast_to(
        jnp.arange(GLOBALS, dtype=jnp.int32)[None, :], (local_blocks, GLOBALS)
    )
    fixed_part = jnp.concatenate([window_part, global_ids], axis=-1)
    candidates = jnp.concatenate(
        [jnp.broadcast_to(fixed_part[None], (H, local_blocks, 3 + GLOBALS)), rand_local], axis=-1
    )
    candidates = jnp.clip(candidates, 0, total_blocks - 1)
    always_true = jnp.ones((local_blocks,), dtype=bool)
    fixed_valid = jnp.stack(
        [block_ids - 1 >= GLOBALS, always_true, block_ids + 1 < total_blocks]
        + [always_true] * GLOBALS,
        axis=-1,
    )
    valid = jnp.concatenate(
        [
            jnp.broadcast_to(fixed_valid[None], (H, local_blocks, 3 + GLOBALS)),
            jnp.ones((H, local_blocks, RANDOMS), dtype=bool),
        ],
        axis=-1,
    )
    valid_keys = jnp.repeat(valid, BLOCK, axis=-1)
    query_heads = (
        projected[0].reshape(seq_count, local_blocks, BLOCK, H, HD).transpose(0, 3, 1, 2, 4)
    )
    key_source = key_all.reshape(seq_count, total_blocks, BLOCK, H, HD).transpose(0, 3, 1, 2, 4)
    value_source = value_all.reshape(seq_count, total_blocks, BLOCK, H, HD).transpose(0, 3, 1, 2, 4)
    head_index = jnp.arange(H, dtype=jnp.int32)[:, None, None]
    key_picked = key_source[:, head_index, candidates].reshape(
        seq_count, H, local_blocks, cand_count * BLOCK, HD
    )
    value_picked = value_source[:, head_index, candidates].reshape(
        seq_count, H, local_blocks, cand_count * BLOCK, HD
    )
    seg_picked = seg_all.reshape(seq_count, total_blocks, BLOCK)[:, candidates].reshape(
        seq_count, H, local_blocks, cand_count * BLOCK
    )
    seg_local = seg_low.reshape(seq_count, local_blocks, BLOCK)
    permit = valid_keys[None, :, :, None, :] & (
        seg_local[:, None, :, :, None] == seg_picked[:, :, :, None, :]
    )
    scores = sparse_scores(query_heads, key_picked, permit, scaling)
    top_score = jnp.max(scores, axis=-1, keepdims=True)
    weights = jnp.exp(scores - top_score)
    totals = jnp.sum(weights, axis=-1, keepdims=True)
    share_low = (weights / totals).astype(jnp.bfloat16)
    sparse_lse = (top_score + jnp.log(totals))[..., 0]
    sparse_out = jnp.einsum(
        "shbqk,shbkd->shbqd", share_low, value_picked, preferred_element_type=jnp.float32
    )
    key_heads = key_source.reshape(seq_count, H, full_length, HD)
    value_heads = value_source.reshape(seq_count, H, full_length, HD)
    glob_query = query_heads[:, :, :GLOBALS].reshape(seq_count, H, glob_rows, HD)
    glob_seg = seg_low[:, :glob_rows]

    def run_forward(operands):
        return lax.map(
            lambda packet: global_forward(
                packet[0], packet[1], packet[2], packet[3], packet[4], scaling
            ),
            operands,
        )

    def skip_forward(operands):
        return (
            jnp.zeros((seq_count, H, glob_rows, HD), jnp.float32),
            jnp.zeros((seq_count, H, glob_rows), jnp.float32),
        )

    global_out, global_lse = lax.cond(
        is_first, run_forward, skip_forward, (glob_query, key_heads, value_heads, glob_seg, seg_all)
    )
    glob_blocks = global_out.reshape(seq_count, H, GLOBALS, BLOCK, HD)
    head_out = jnp.concatenate(
        [jnp.where(is_first, glob_blocks, sparse_out[:, :, :GLOBALS]), sparse_out[:, :, GLOBALS:]],
        axis=2,
    )
    mixed_low = (
        head_out.transpose(0, 2, 3, 1, 4)
        .reshape(seq_count, local_tokens, width)
        .astype(jnp.bfloat16)
    )
    rank_out, extra_out = adapt(mixed_low, adapter_tables_input[3], adapter_tables_output[3])
    branch = dense_forward(mixed_low, out_full) + extra_out
    first, first_pull = jax.vjp(
        lambda hidden: norm_rows(hidden, attention_norm_gain), inputs.astype(jnp.float32) + branch
    )
    first_low = first.astype(jnp.bfloat16)
    up_full, down_full = (
        lax.all_gather(frozen_up_weight, "shard", axis=0, tiled=True),
        lax.all_gather(frozen_down_weight, "shard", axis=0, tiled=True),
    )
    rank_up, extra_up = adapt(first_low, adapter_tables_input[4], adapter_tables_output[4])
    lifted = dense_forward(first_low, up_full) + extra_up
    activated, gelu_pull = jax.vjp(gelu_exact, lifted)
    active_low = activated.astype(jnp.bfloat16)
    rank_down, extra_down = adapt(active_low, adapter_tables_input[5], adapter_tables_output[5])
    lowered = dense_forward(active_low, down_full) + extra_down
    result, final_pull = jax.vjp(
        lambda hidden: norm_rows(hidden, feedforward_norm_gain), first + lowered
    )
    layer_out = result.astype(jnp.bfloat16)
    up_back, down_back = (
        lax.all_gather(frozen_up_weight, "shard", axis=0, tiled=True),
        lax.all_gather(frozen_down_weight, "shard", axis=0, tiled=True),
    )
    grad_adapt_in = [None] * 6
    grad_adapt_out = [None] * 6
    (grad_sum,) = final_pull(cotangent.astype(jnp.float32))
    grad_lowered = grad_sum.astype(jnp.bfloat16)
    grad_adapt_in[5], grad_adapt_out[5], extra_grad = adapt_back(
        active_low, adapter_tables_input[5], adapter_tables_output[5], rank_down, grad_lowered
    )
    grad_active = dense_backward(grad_lowered, down_back) + extra_grad
    (grad_lifted,) = gelu_pull(grad_active)
    grad_lift_low = grad_lifted.astype(jnp.bfloat16)
    grad_adapt_in[4], grad_adapt_out[4], extra_grad = adapt_back(
        first_low, adapter_tables_input[4], adapter_tables_output[4], rank_up, grad_lift_low
    )
    grad_first = grad_sum + dense_backward(grad_lift_low, up_back) + extra_grad
    (grad_branch,) = first_pull(grad_first)
    grad_branch_low = grad_branch.astype(jnp.bfloat16)
    qkv_back, out_back = (
        lax.all_gather(frozen_query_key_value_weight, "shard", axis=0, tiled=True),
        lax.all_gather(frozen_output_weight, "shard", axis=0, tiled=True),
    )
    grad_adapt_in[3], grad_adapt_out[3], extra_grad = adapt_back(
        mixed_low, adapter_tables_input[3], adapter_tables_output[3], rank_out, grad_branch_low
    )
    grad_mixed = (dense_backward(grad_branch_low, out_back) + extra_grad).astype(jnp.bfloat16)
    grad_heads = grad_mixed.reshape(seq_count, local_blocks, BLOCK, H, HD).transpose(0, 3, 1, 2, 4)
    row_keep = (block_ids >= GLOBALS)[None, None, :, None, None]
    grad_sparse = jnp.where(row_keep, grad_heads, jnp.zeros_like(grad_heads))
    scores = sparse_scores(query_heads, key_picked, permit, scaling)
    shares = jnp.exp(scores - sparse_lse[..., None])
    share_low = shares.astype(jnp.bfloat16)
    grad_shares = jnp.einsum(
        "shbqd,shbkd->shbqk", grad_sparse, value_picked, preferred_element_type=jnp.float32
    )
    centre = jnp.sum(shares * grad_shares, axis=-1, keepdims=True)
    grad_scores = (shares * (grad_shares - centre)).astype(jnp.bfloat16)
    grad_query = (
        jnp.einsum(
            "shbqk,shbkd->shbqd", grad_scores, key_picked, preferred_element_type=jnp.float32
        )
        * scaling
    )
    glob_grad = grad_heads[:, :, :GLOBALS].reshape(seq_count, H, glob_rows, HD)

    def run_backward(operands):
        return lax.map(
            lambda packet: global_backward(
                packet[0], packet[1], packet[2], packet[3], packet[4], packet[5], packet[6], scaling
            ),
            operands,
        )

    def skip_backward(operands):
        return (
            jnp.zeros((seq_count, H, glob_rows, HD), jnp.float32),
            jnp.zeros((seq_count, H, full_length, HD), jnp.float32),
            jnp.zeros((seq_count, H, full_length, HD), jnp.float32),
            jnp.zeros((seq_count, H, glob_rows), jnp.float32),
        )

    glob_dq, glob_dk, glob_dv, glob_centre = lax.cond(
        is_first,
        run_backward,
        skip_backward,
        (glob_query, key_heads, value_heads, glob_seg, seg_all, glob_grad, global_lse),
    )
    grad_query = grad_query.at[:, :, :GLOBALS].add(
        glob_dq.reshape(seq_count, H, GLOBALS, BLOCK, HD)
    )
    grad_key_picked = (
        jnp.einsum(
            "shbqk,shbqd->shbkd", grad_scores, query_heads, preferred_element_type=jnp.float32
        )
        * scaling
    )
    grad_value_picked = jnp.einsum(
        "shbqk,shbqd->shbkd", share_low, grad_sparse, preferred_element_type=jnp.float32
    )
    block_shape = (seq_count, H, local_blocks, cand_count, BLOCK, HD)
    key_grad_blocks = (
        jnp.zeros((seq_count, H, total_blocks, BLOCK, HD), jnp.float32)
        .at[:, head_index, candidates]
        .add(grad_key_picked.reshape(block_shape))
    )
    value_grad_blocks = (
        jnp.zeros((seq_count, H, total_blocks, BLOCK, HD), jnp.float32)
        .at[:, head_index, candidates]
        .add(grad_value_picked.reshape(block_shape))
    )
    key_grad_full = (
        (key_grad_blocks.reshape(seq_count, H, full_length, HD) + glob_dk)
        .transpose(0, 2, 1, 3)
        .reshape(seq_count, full_length, width)
    )
    value_grad_full = (
        (value_grad_blocks.reshape(seq_count, H, full_length, HD) + glob_dv)
        .transpose(0, 2, 1, 3)
        .reshape(seq_count, full_length, width)
    )
    key_grad, value_grad = (
        lax.psum_scatter(
            key_grad_full.astype(jnp.bfloat16), "shard", scatter_dimension=1, tiled=True
        ).astype(jnp.float32),
        lax.psum_scatter(
            value_grad_full.astype(jnp.bfloat16), "shard", scatter_dimension=1, tiled=True
        ).astype(jnp.float32),
    )
    query_grad = grad_query.transpose(0, 2, 3, 1, 4).reshape(seq_count, local_tokens, width)
    grad_proj = [
        query_grad.astype(jnp.bfloat16),
        key_grad.astype(jnp.bfloat16),
        value_grad.astype(jnp.bfloat16),
    ]
    input_grad = grad_branch + dense_backward(jnp.concatenate(grad_proj, axis=-1), qkv_back)
    for table_column in range(3):
        grad_adapt_in[table_column], grad_adapt_out[table_column], extra_grad = adapt_back(
            inputs,
            adapter_tables_input[table_column],
            adapter_tables_output[table_column],
            rank_parts[table_column],
            grad_proj[table_column],
        )
        input_grad = input_grad + extra_grad
    adapter_table_count = adapter_down_from_width.shape[1]
    grad_in_d = jnp.stack(
        [
            table_sum(
                grad_adapt_in[table_column],
                adapter_index_table[:, table_column],
                adapter_table_count,
            )
            for table_column in range(5)
        ],
        axis=0,
    )
    grad_in_f = table_sum(grad_adapt_in[5], adapter_index_table[:, 5], adapter_table_count)
    out_list = [
        table_sum(
            grad_adapt_out[table_column], adapter_index_table[:, table_column], adapter_table_count
        )
        for table_column in range(4)
    ]
    grad_out_d = jnp.stack(
        out_list + [table_sum(grad_adapt_out[5], adapter_index_table[:, 5], adapter_table_count)],
        axis=0,
    )
    grad_out_f = table_sum(grad_adapt_out[4], adapter_index_table[:, 4], adapter_table_count)
    owned = (
        lax.psum_scatter(
            grad_in_d.astype(jnp.bfloat16), "shard", scatter_dimension=3, tiled=True
        ).astype(jnp.float32),
        lax.psum_scatter(
            grad_in_f.astype(jnp.bfloat16), "shard", scatter_dimension=2, tiled=True
        ).astype(jnp.float32),
        lax.psum_scatter(
            grad_out_d.astype(jnp.bfloat16), "shard", scatter_dimension=3, tiled=True
        ).astype(jnp.float32),
        lax.psum_scatter(
            grad_out_f.astype(jnp.bfloat16), "shard", scatter_dimension=2, tiled=True
        ).astype(jnp.float32),
    )
    summed = (
        lax.psum(owned[0].astype(jnp.bfloat16), "dp").astype(jnp.float32),
        lax.psum(owned[1].astype(jnp.bfloat16), "dp").astype(jnp.float32),
        lax.psum(owned[2].astype(jnp.bfloat16), "dp").astype(jnp.float32),
        lax.psum(owned[3].astype(jnp.bfloat16), "dp").astype(jnp.float32),
    )
    return (layer_out, input_grad, summed[0], summed[1], summed[2], summed[3])


BF = jnp.bfloat16
F32 = jnp.float32
NT = (((1,), (1,)), ((), ()))
TN = (((0,), (0,)), ((), ()))
BIG = 1e30
RANK = 16
ANY = pl.ANY
VMEM = pltpu.VMEM
MEBI = 1024 * 1024
SMALL_COST = pl.CostEstimate(flops=1_000_000, bytes_accessed=100_000, transcendentals=0)


def mm(left, right):
    return jnp.dot(left, right, preferred_element_type=F32)


def mm_nt(left, right):
    return lax.dot_general(left, right, NT, preferred_element_type=F32)


def mm_tn(left, right):
    return lax.dot_general(left, right, TN, preferred_element_type=F32)


def whole(shape):
    return pl.BlockSpec(shape, lambda *_: (0,) * len(shape))


def away_pairs(dp_count, shard_count, step):
    pairs = []
    for chip in range(dp_count // 2):
        for k in range(2):
            for z in range(shard_count):
                m = (z & 1) ^ step
                source = (2 * chip + k) * shard_count + z
                target = (2 * chip + (z >> 1)) * shard_count + 2 * k + m
                pairs.append((source, target))
    return pairs


def swap_cores(value, dp_count):
    return lax.ppermute(value, "dp", [(i, i ^ 1) for i in range(dp_count)])


def swap_shards(value, shard_count, step):
    return lax.ppermute(value, "shard", [(i, i ^ step) for i in range(shard_count)])


def spread_over_chips(block, dp_count):
    others = [lax.ppermute(block, "dp", [(i, i ^ o) for i in range(dp_count)]) for o in range(2, dp_count, 2)]
    return [block] + others


def swap_chips(block, dp_count, offset):
    return lax.ppermute(block, "dp", [(i, i ^ offset) for i in range(dp_count)])


def spread_over_cores(blocks, dp_count):
    return [one for block in blocks for one in (block, swap_cores(block, dp_count))]


def spread_in_plane(block, dp_count):
    return spread_over_cores(spread_over_chips(block, dp_count), dp_count)


def join_kernel(meta, part0, part1, out_ref):
    for r, part in enumerate((part0, part1)):
        out_ref[(meta[0] & 1) ^ r] = part[...].astype(out_ref.dtype)


def join_parts(meta, parts, dtype):
    rows, width = parts[0].shape
    return pl.pallas_call(
        join_kernel,
        grid_spec=pltpu.PrefetchScalarGridSpec(
            num_scalar_prefetch=1,
            grid=(1,),
            in_specs=[whole((rows, width))] * 2,
            out_specs=whole((2, rows, width)),
        ),
        out_shape=jax.ShapeDtypeStruct((2, rows, width), dtype),
        compiler_params=pltpu.CompilerParams(vmem_limit_bytes=30 * MEBI),
        cost_estimate=SMALL_COST,
        name="join_parts",
    )(meta, *parts)


def send_away(parts, dp_count, shard_count):
    return [
        lax.ppermute(part, ("dp", "shard"), away_pairs(dp_count, shard_count, r))
        for r, part in enumerate(parts)
    ]


def weight_copies(meta, own_ref, pieces, dest, sems, places):
    z, d = meta[0], meta[1]
    own_rows, columns = own_ref.shape
    copies = [
        pltpu.make_async_copy(
            own_ref, dest.at[pl.ds(pl.multiple_of(z * own_rows, 16), own_rows)], sems.at[0]
        )
    ]
    count = 1
    for o, parts in enumerate(pieces):
        who = d ^ o
        for step in range(3):
            shard = z ^ (step + 1)
            for start, row, column, rows, cols in places(who):
                for piece, first in parts:
                    low, high = max(start, first), min(start + rows, first + piece.shape[1])
                    if low >= high:
                        continue
                    copies.append(
                        pltpu.make_async_copy(
                            piece.at[step, pl.ds(low - first, high - low)],
                            dest.at[
                                pl.ds(pl.multiple_of(shard * own_rows + row + low - start, 16), high - low),
                                pl.ds(pl.multiple_of(column, 128), cols),
                            ],
                            sems.at[count],
                        )
                    )
                    count += 1
    return copies


def one_each(refs):
    return [[(ref, 0)] for ref in refs]


UP_SPLIT = 128


def up_parts(refs):
    return one_each(refs[0:6]) + [[(refs[6], 0), (refs[7], UP_SPLIT)], [(refs[8], 0), (refs[9], UP_SPLIT)]]


def qkv_places(who):
    return [(0, (who >> 1) * 48, (who & 1) * 1152, 48, 1152)]


def out_places(who):
    return [(0, (who >> 1) * 48, (who & 1) * 384, 48, 384)]


def up_places(who):
    return [(48, 0, who * 384, 192, 384)]


def down_places(who):
    return [(0, who * 96, 0, 96, 384), (96, who * 96, 384, 96, 384)]


def token_copies(meta, messages, dest, sems):
    copies = []
    for at, message in enumerate(messages):
        row = 512 * (at >> 1) + 256 * ((meta[0] & 1) ^ (at & 1))
        copies.append(
            pltpu.make_async_copy(
                message.at[pl.ds(0, 256)], dest.at[pl.ds(pl.multiple_of(row, 256), 256)], sems.at[at]
            )
        )
    return copies


def zero_padded(rows, position, count):
    zeros = jnp.zeros_like(rows)
    return jnp.concatenate([rows if i == position else zeros for i in range(count)], axis=0)


def qkv_kernel(meta, ids, *refs):
    messages, w_own, pieces = refs[0:4], refs[4], one_each(refs[5:13])
    ins, outs = refs[13:16], refs[16:19]
    q_ref, k_ref, v_ref, mask_ref, hot_ref, own_ref = refs[19:25]
    xs, segs, weight, wsems, xsems, ssems = refs[25:]
    copies = token_copies(meta, messages, xs, xsems)
    for at, message in enumerate(messages):
        copies.append(
            pltpu.make_async_copy(
                message.at[pl.ds(256, 16), pl.ds(0, 256)],
                segs.at[2 * (at >> 1) + ((meta[0] & 1) ^ (at & 1))],
                ssems.at[at],
            )
        )
    copies += weight_copies(meta, w_own, pieces, weight, wsems, qkv_places)
    for copy in copies:
        copy.start()
    for copy in copies:
        copy.wait()
    lane = lax.broadcasted_iota(jnp.int32, (128, 128), 1)
    lane_of_head = lax.rem(lane, 64)
    as_float = lane_of_head.astype(F32)
    is_segment = lane_of_head < 16
    row_block = lax.broadcasted_iota(jnp.int32, (128, 128), 0) // 64
    for place in range(4):
        row = segs[place].astype(F32)[0:1]
        for half in range(2):
            column = jnp.broadcast_to(row[:, 128 * half : 128 * half + 128], (128, 128)).T
            same = column == as_float
            block_lane = lane_of_head == 16 + 4 * place + 2 * half + row_block
            rows = slice(256 * place + 128 * half, 256 * place + 128 * half + 128)
            mask_ref[rows] = jnp.where(
                is_segment, jnp.where(same, 0.0, -BIG), jnp.where(block_lane, 1.0, 0.0)
            ).astype(BF)
            if place < 2:
                hot_ref[rows] = jnp.where(is_segment & same, 1.0, 0.0).astype(BF)
    own_ref[...] = xs[0:512]
    in_all = jnp.concatenate([ref[0, 0] for ref in ins], axis=0)
    out_all = [zero_padded(ref[0, 0], p, 3) for p, ref in enumerate(outs)]
    targets = (q_ref, k_ref, v_ref)
    for tile in range(4):
        rows = slice(256 * tile, 256 * tile + 256)
        x = xs[rows]
        rank = mm_nt(x, in_all).astype(BF)
        for p in range(0 if tile < 2 else 1, 3):
            value = mm(x, weight[:, 768 * p : 768 * p + 768]) + mm(rank, out_all[p])
            value = value.astype(BF)
            if p == 0:
                value = (value.astype(F32) * HD**-0.5).astype(BF)
            targets[p][rows] = value


def table_spec(p, column, width):
    return pl.BlockSpec((1, 1, RANK, width), lambda i, meta, ids: (p, ids[column], 0, 0))


def hidden_spec(column, width):
    return pl.BlockSpec((1, RANK, width), lambda i, meta, ids: (ids[column], 0, 0))


def any_specs(count):
    return [pl.BlockSpec(memory_space=ANY)] * count


def project_qkv(meta, ids, messages, w_own, pieces, table_in, table_out):
    width = w_own.shape[1] // 3
    return pl.pallas_call(
        qkv_kernel,
        grid_spec=pltpu.PrefetchScalarGridSpec(
            num_scalar_prefetch=2,
            grid=(1,),
            in_specs=any_specs(13)
            + [table_spec(p, p, width) for p in range(3)]
            + [table_spec(p, p, width) for p in range(3)],
            out_specs=[
                whole((512, width)),
                whole((1024, width)),
                whole((1024, width)),
                whole((1024, 128)),
                whole((512, 128)),
                whole((512, width)),
            ],
            scratch_shapes=[
                VMEM((1024, width), BF),
                VMEM((4, 16, 256), BF),
                VMEM((width, 3 * width), BF),
                pltpu.SemaphoreType.DMA((25,)),
                pltpu.SemaphoreType.DMA((4,)),
                pltpu.SemaphoreType.DMA((4,)),
            ],
        ),
        out_shape=[
            jax.ShapeDtypeStruct((512, width), BF),
            jax.ShapeDtypeStruct((1024, width), BF),
            jax.ShapeDtypeStruct((1024, width), BF),
            jax.ShapeDtypeStruct((1024, 128), BF),
            jax.ShapeDtypeStruct((512, 128), BF),
            jax.ShapeDtypeStruct((512, width), BF),
        ],
        compiler_params=pltpu.CompilerParams(vmem_limit_bytes=56 * MEBI),
        cost_estimate=SMALL_COST,
        name="project_qkv",
    )(meta, ids, *messages, w_own, *pieces, *([table_in] * 3), *([table_out] * 3))


def attend_kernel(q_ref, k_ref, v_ref, mask_ref, hot_ref, closed_ref, o_ref, p_ref):
    low = lax.broadcasted_iota(jnp.int32, (512, 128), 1) < 64
    low_keys = lax.broadcasted_iota(jnp.int32, (1024, 128), 1) < 64
    closed = jnp.concatenate(
        [jnp.broadcast_to(closed_ref[0, l : l + 1], (64, 128)) for l in range(8)], axis=0
    )
    extra = (hot_ref[...].astype(F32) + closed).astype(BF)
    q, k, v, masks = q_ref[...], k_ref[...], v_ref[...], mask_ref[...]
    wide = [(jnp.where(low, q, extra), jnp.where(low_keys, k, masks)), (jnp.where(low, extra, q), jnp.where(low_keys, masks, k))]
    size = 512
    units = [(start, head) for start in range(0, 512, size) for head in range(2)]
    raw = lambda unit: mm_nt(wide[unit[1]][0][unit[0] : unit[0] + size], wide[unit[1]][1])
    ahead = raw(units[0])
    mixed = {}
    for n, (start, head) in enumerate(units):
        scores = ahead
        if n + 1 < len(units):
            ahead = raw(units[n + 1])
        weights = jnp.exp(scores - jnp.max(scores, axis=1, keepdims=True))
        shares = (weights * (1.0 / jnp.sum(weights, axis=1, keepdims=True))).astype(BF)
        p_ref[head, start : start + size] = shares
        mixed[head] = mm(shares, v)
        if head == 1:
            o_ref[start : start + size] = jnp.where(low[0:size], mixed[0], mixed[1]).astype(BF)


def attend(q, k, v, masks, hot, closed):
    width = q.shape[1]
    pairs = width // 128
    half = pl.BlockSpec((512, 128), lambda g: (0, g))
    full = pl.BlockSpec((1024, 128), lambda g: (0, g))
    return pl.pallas_call(
        attend_kernel,
        grid=(pairs,),
        in_specs=[
            half,
            full,
            full,
            whole((1024, 128)),
            whole((512, 128)),
            pl.BlockSpec((1, 8, 128), lambda g: (g, 0, 0)),
        ],
        out_specs=[half, pl.BlockSpec((2, 512, 1024), lambda g: (g, 0, 0))],
        out_shape=[
            jax.ShapeDtypeStruct((512, width), BF),
            jax.ShapeDtypeStruct((2 * pairs, 512, 1024), BF),
        ],
        compiler_params=pltpu.CompilerParams(vmem_limit_bytes=56 * MEBI),
        cost_estimate=SMALL_COST,
        name="attend",
    )(q, k, v, masks, hot, closed)


def attend_back_kernel(q_ref, k_ref, v_ref, p_ref, grad_ref, mixed_ref, dq_ref, dk_own, dv_own, other_ref):
    low = lax.broadcasted_iota(jnp.int32, (512, 128), 1) < 64
    q, k, v, grad = q_ref[...], k_ref[...], v_ref[...], grad_ref[...]
    products = grad.astype(F32) * mixed_ref[...].astype(F32)
    q_turned, grad_turned = q.T, grad.T
    zeros, none = jnp.zeros_like(grad), jnp.zeros_like(products)
    dq, dk, dv = [], [], []
    for head in range(2):
        mine = low if head == 0 else jnp.logical_not(low)
        centre = jnp.sum(jnp.where(mine, products, none), axis=1, keepdims=True)
        grad_shares = mm_nt(jnp.where(mine, grad, zeros), v)
        shares = p_ref[head]
        grad_scores = (shares.astype(F32) * (grad_shares - centre)).astype(BF)
        rows = slice(64 * head, 64 * head + 64)
        dq.append(mm(grad_scores, k))
        dk.append(mm(q_turned[rows], grad_scores))
        dv.append(mm(grad_turned[rows], shares))
    dq_ref[...] = (jnp.where(low, dq[0], dq[1]) * HD**-0.5).astype(BF)
    dk = jnp.concatenate(dk, axis=0).T
    dv = jnp.concatenate(dv, axis=0).T
    dk_own[...] = dk[0:512].astype(BF)
    dv_own[...] = dv[0:512].astype(BF)
    other_ref[0] = dk[512:1024].astype(BF)
    other_ref[1] = dv[512:1024].astype(BF)


def attend_back(q, k, v, shares, grad, mixed):
    width = q.shape[1]
    half = pl.BlockSpec((512, 128), lambda g: (0, g))
    full = pl.BlockSpec((1024, 128), lambda g: (0, g))
    return pl.pallas_call(
        attend_back_kernel,
        grid=(width // 128,),
        in_specs=[half, full, full, pl.BlockSpec((2, 512, 1024), lambda g: (g, 0, 0)), half, half],
        out_specs=[half] * 3 + [pl.BlockSpec((2, 512, 128), lambda g: (0, 0, g))],
        out_shape=[
            jax.ShapeDtypeStruct((512, width), BF),
            jax.ShapeDtypeStruct((512, width), BF),
            jax.ShapeDtypeStruct((512, width), BF),
            jax.ShapeDtypeStruct((2, 512, width), BF),
        ],
        compiler_params=pltpu.CompilerParams(vmem_limit_bytes=56 * MEBI),
        cost_estimate=SMALL_COST,
        name="attend_back",
    )(q, k, v, shares, grad, mixed)


def gelu_and_slope(lifted):
    size = jnp.abs(lifted)
    t = 1.0 / (1.0 + 0.23164189 * size)
    poly = t * (
        0.127414796 + t * (-0.142248368 + t * (0.7107068705 + t * (-0.7265760135 + t * 0.5307027145)))
    )
    decay = jnp.exp2(lifted * lifted * -0.7213475204444817)
    tail = poly * decay
    below = jnp.where(lifted < 0.0, tail, 1.0 - tail)
    return jnp.maximum(lifted, 0.0) - size * tail, below + lifted * (decay * 0.3989422804014327)


def norm_parts(hidden):
    average = jnp.mean(hidden, axis=-1, keepdims=True)
    centred = hidden - average
    spread = jnp.mean(centred * centred, axis=-1, keepdims=True)
    inverse = lax.rsqrt(spread + EPSILON)
    return centred * inverse, inverse


def norm_back(grad, gain, normal, inverse):
    scaled = grad * gain
    return inverse * (
        scaled
        - jnp.mean(scaled, axis=-1, keepdims=True)
        - normal * jnp.mean(scaled * normal, axis=-1, keepdims=True)
    )


MID_TILE = 256
MID_PARTS = 4


def first_half_kernel(meta, ids, *refs):
    out_own, up_own, up_pieces = refs[0], refs[1], up_parts(refs[2:12])
    x_ref, mixed_ref, gain1, in3, in4, out3, out4 = refs[12:19]
    normal_ref, inverse_ref, active, slope = refs[19:23]
    w_out, w_up, osems, usems = refs[23:]
    out_copies = weight_copies(meta, out_own, up_pieces, w_out, osems, out_places)
    up_copies = weight_copies(meta, up_own, up_pieces, w_up, usems, up_places)
    is_first = pl.program_id(0) == 0

    @pl.when(is_first)
    def _():
        for copy in out_copies + up_copies:
            copy.start()
        for copy in out_copies:
            copy.wait()

    mixed = mixed_ref[...]
    rank3 = mm_nt(mixed, in3[0, 0]).astype(BF)
    branch = mm(mixed, w_out[...]) + mm(rank3, out3[0, 0])
    normal, inverse = norm_parts(x_ref[...].astype(F32) + branch)
    normal_ref[...] = normal
    inverse_ref[...] = jnp.broadcast_to(inverse, inverse_ref.shape)
    low = (normal * gain1[...][None]).astype(BF)
    rank4 = mm_nt(low, in4[0, 0]).astype(BF)

    @pl.when(is_first)
    def _():
        for copy in up_copies:
            copy.wait()

    part = w_up.shape[1] // MID_PARTS
    columns = [slice(n * part, n * part + part) for n in range(MID_PARTS)]
    lift = lambda cols: mm(low, w_up[:, cols]) + mm(rank4, out4[0, :, cols])
    ahead = lift(columns[0])
    for n, cols in enumerate(columns):
        lifted = ahead
        if n + 1 < MID_PARTS:
            ahead = lift(columns[n + 1])
        value, tangent = gelu_and_slope(lifted)
        active[:, cols] = value.astype(BF)
        slope[:, cols] = tangent.astype(BF)


def first_half(meta, ids, out_own, up_own, up_pieces, x, mixed, gain1, table_in, table_out, table_out_hidden):
    width, hidden = x.shape[1], up_own.shape[1]
    tile = lambda columns: pl.BlockSpec((MID_TILE, columns), lambda i, *_: (i, 0))
    return pl.pallas_call(
        first_half_kernel,
        grid_spec=pltpu.PrefetchScalarGridSpec(
            num_scalar_prefetch=2,
            grid=(512 // MID_TILE,),
            in_specs=any_specs(12)
            + [
                tile(width),
                tile(width),
                whole((width,)),
                table_spec(3, 3, width),
                table_spec(4, 4, width),
                table_spec(3, 3, width),
                hidden_spec(4, hidden),
            ],
            out_specs=[tile(width), tile(128), tile(hidden), tile(hidden)],
            scratch_shapes=[
                VMEM((width, width), BF),
                VMEM((width, hidden), BF),
                pltpu.SemaphoreType.DMA((25,)),
                pltpu.SemaphoreType.DMA((31,)),
            ],
        ),
        out_shape=[
            jax.ShapeDtypeStruct((512, width), F32),
            jax.ShapeDtypeStruct((512, 128), F32),
            jax.ShapeDtypeStruct((512, hidden), BF),
            jax.ShapeDtypeStruct((512, hidden), BF),
        ],
        compiler_params=pltpu.CompilerParams(vmem_limit_bytes=56 * MEBI),
        cost_estimate=SMALL_COST,
        name="first_half",
    )(meta, ids, out_own, up_own, *up_pieces, x, mixed, gain1, table_in, table_in, table_out, table_out_hidden)


def write_halves(meta, gathered, groups, own_half, other_half):
    core = meta[1] & 1
    for r in range(4):
        for half, ref in enumerate((own_half, other_half)):
            rows = [
                gathered[meta[0] ^ r, pl.ds(pl.multiple_of(16 * group + 8 * (core ^ half), 8), 8), :]
                for group in range(groups)
            ]
            ref[r] = jnp.concatenate(rows, axis=0).astype(ref.dtype)


def second_half_kernel(meta, ids, *refs):
    cots, out_own, up_own, down_own = refs[0:2], refs[2], refs[3], refs[4]
    up_pieces, down_pieces = up_parts(refs[5:15]), one_each(refs[15:23])
    normal_ref, inverse_ref, active, slope, mixed_ref = refs[23:28]
    gain1, gain2, in3, in4, in5, out3, out4, out5 = refs[28:36]
    layer_parts, grad_branch_ref, grad_mixed_ref, own_half, other_half = refs[36:38], refs[38], refs[39], refs[40], refs[41]
    (
        cot, w_out, w_up, w_down, layer,
        s_in3, s_in4, s_in5, s_out3, s_out4, s_out5, gathered,
        osems, usems, dsems, xsems,
    ) = refs[42:]
    tile = pl.program_id(0)
    is_first = tile == 0
    near = token_copies(meta, cots, cot, xsems)
    out_copies = weight_copies(meta, out_own, up_pieces, w_out, osems, out_places)
    up_copies = weight_copies(meta, up_own, up_pieces, w_up, usems, up_places)
    down_copies = weight_copies(meta, down_own, down_pieces, w_down, dsems, down_places)

    @pl.when(is_first)
    def _():
        for copy in down_copies + near + up_copies + out_copies:
            copy.start()
        for ref in (s_in3, s_in4, s_in5, s_out3, s_out4, s_out5):
            ref[...] = jnp.zeros_like(ref)
        for copy in down_copies + near:
            copy.wait()

    part = w_up.shape[1] // MID_PARTS
    a_in3, a_in4, a_out3, a_out5 = in3[0, 0], in4[0, 0], out3[0, 0], out5[0, 0]
    rows = pl.ds(pl.multiple_of(tile * MID_TILE, MID_TILE), MID_TILE)
    normal1 = normal_ref[...]
    inverse1 = inverse_ref[:, 0:1]
    first = normal1 * gain1[...][None]
    low1 = first.astype(BF)
    r4 = mm_nt(low1, a_in4).astype(BF)
    r5 = mm_nt(active[...], in5[0]).astype(BF)
    lowered = first + mm(active[...], w_down[...]) + mm(r5, a_out5)
    normal2, inverse2 = norm_parts(lowered)
    layer[rows, :] = (normal2 * gain2[...][None]).astype(BF)
    grad_sum = norm_back(cot[rows, :].astype(F32), gain2[...][None], normal2, inverse2)
    e5 = grad_sum.astype(BF)
    rg5 = mm_nt(e5, a_out5).astype(BF)
    s_out5[...] += mm_tn(r5, e5)

    @pl.when(is_first)
    def _():
        for copy in up_copies + out_copies:
            copy.wait()

    grad_first = grad_sum
    rg4 = jnp.zeros((MID_TILE, RANK), F32)
    for n in range(MID_PARTS):
        cols = slice(n * part, n * part + part)
        grad_active = mm_nt(e5, w_down[cols, :]) + mm(rg5, in5[0, :, cols])
        e4 = (slope[:, cols].astype(F32) * grad_active).astype(BF)
        s_in5[:, cols] += mm_tn(rg5, active[:, cols])
        s_out4[:, cols] += mm_tn(r4, e4)
        grad_first = grad_first + mm_nt(e4, w_up[:, cols])
        rg4 = rg4 + mm_nt(e4, out4[0, :, cols])
    rg4 = rg4.astype(BF)
    s_in4[...] += mm_tn(rg4, low1)
    grad_first = grad_first + mm(rg4, a_in4)
    grad_branch = norm_back(grad_first, gain1[...][None], normal1, inverse1)
    grad_branch_ref[...] = grad_branch
    e3 = grad_branch.astype(BF)
    mixed = mixed_ref[...]
    rank3 = mm_nt(mixed, a_in3).astype(BF)
    rg3 = mm_nt(e3, a_out3).astype(BF)
    s_out3[...] += mm_tn(rank3, e3)
    s_in3[...] += mm_tn(rg3, mixed)
    grad_mixed_ref[...] = (mm_nt(e3, w_out[...]) + mm(rg3, a_in3)).astype(BF)

    @pl.when(tile == 512 // MID_TILE - 1)
    def _():
        wide, narrow = 768, 192
        for owner in range(4):
            start = 0
            for ref, size in (
                (s_in5, wide), (s_out4, wide), (s_in3, narrow), (s_in4, narrow), (s_out3, narrow), (s_out5, narrow),
            ):
                row, column = 16 * (start // 768), start % 768
                gathered[owner, row : row + 16, column : column + size] = ref[:, owner * size : owner * size + size]
                start += size
        for r, ref in enumerate(layer_parts):
            ref[...] = layer[pl.ds(pl.multiple_of(256 * ((meta[0] & 1) ^ r), 256), 256), :]
        write_halves(meta, gathered, 3, own_half, other_half)


def second_half(meta, ids, cots, out_own, up_own, down_own, up_pieces, down_pieces, normal, inverse, active, slope,
                mixed, gain1, gain2, table_in, table_in_hidden, table_out, table_out_hidden):
    width, hidden = normal.shape[1], up_own.shape[1]
    tile = lambda columns: pl.BlockSpec((MID_TILE, columns), lambda i, *_: (i, 0))
    return pl.pallas_call(
        second_half_kernel,
        grid_spec=pltpu.PrefetchScalarGridSpec(
            num_scalar_prefetch=2,
            grid=(512 // MID_TILE,),
            in_specs=any_specs(23)
            + [
                tile(width),
                tile(128),
                tile(hidden),
                tile(hidden),
                tile(width),
                whole((width,)),
                whole((width,)),
                table_spec(3, 3, width),
                table_spec(4, 4, width),
                hidden_spec(5, hidden),
                table_spec(3, 3, width),
                hidden_spec(4, hidden),
                table_spec(4, 5, width),
            ],
            out_specs=[whole((256, width))] * 2 + [tile(width), tile(width)] + [whole((4, 24, width))] * 2,
            scratch_shapes=[
                VMEM((512, width), BF),
                VMEM((width, width), BF),
                VMEM((width, hidden), BF),
                VMEM((hidden, width), BF),
                VMEM((512, width), BF),
                VMEM((RANK, width), F32),
                VMEM((RANK, width), F32),
                VMEM((RANK, hidden), F32),
                VMEM((RANK, width), F32),
                VMEM((RANK, hidden), F32),
                VMEM((RANK, width), F32),
                VMEM((4, 3 * RANK, 768), F32),
                pltpu.SemaphoreType.DMA((25,)),
                pltpu.SemaphoreType.DMA((31,)),
                pltpu.SemaphoreType.DMA((49,)),
                pltpu.SemaphoreType.DMA((2,)),
            ],
        ),
        out_shape=[jax.ShapeDtypeStruct((256, width), BF)] * 2
        + [jax.ShapeDtypeStruct((512, width), F32), jax.ShapeDtypeStruct((512, width), BF)]
        + [jax.ShapeDtypeStruct((4, 24, width), F32), jax.ShapeDtypeStruct((4, 24, width), BF)],
        compiler_params=pltpu.CompilerParams(vmem_limit_bytes=56 * MEBI),
        cost_estimate=SMALL_COST,
        name="second_half",
    )(meta, ids, *cots, out_own, up_own, down_own, *up_pieces, *down_pieces, normal, inverse, active, slope, mixed,
      gain1, gain2, table_in, table_in, table_in_hidden, table_out, table_out_hidden, table_out)


def first_grads_kernel(meta, ids, *refs):
    xs, dq_ref, dk_ref, dv_ref, got_ref = refs[0:5]
    ins, outs = refs[5:8], refs[8:11]
    grads_ref, rank_grad_ref = refs[11:13]
    own_half, other_half = refs[13:15]
    s_in, s_out, gathered = refs[15:]
    in_all = jnp.concatenate([ref[0, 0] for ref in ins], axis=0)
    out_all = jnp.concatenate([zero_padded(ref[0, 0], p, 3) for p, ref in enumerate(outs)], axis=1)
    for tile in range(2):
        rows = slice(256 * tile, 256 * tile + 256)
        grads = jnp.concatenate(
            [dq_ref[rows]]
            + [(ref[rows].astype(F32) + got_ref[n, rows].astype(F32)).astype(BF) for n, ref in enumerate((dk_ref, dv_ref))],
            axis=1,
        )
        grads_ref[rows] = grads
        x = xs[rows]
        rank = mm_nt(x, in_all).astype(BF)
        rank_grad = mm_nt(grads, out_all).astype(BF)
        rank_grad_ref[rows] = rank_grad
        part_in, part_out = mm_tn(rank_grad, x), mm_tn(rank, grads)
        if tile == 0:
            s_in[...] = part_in
            s_out[...] = part_out
        else:
            s_in[...] += part_in
            s_out[...] += part_out
    gathered[...] = jnp.zeros_like(gathered)
    for owner in range(4):
        for p in range(3):
            rows, columns = slice(RANK * p, RANK * p + RANK), slice(192 * owner, 192 * owner + 192)
            gathered[owner, 0:16, 192 * p : 192 * p + 192] = s_in[rows, columns]
            columns = slice(768 * p + 192 * owner, 768 * p + 192 * owner + 192)
            at = (0, 576) if p == 0 else (16, 192 * (p - 1))
            gathered[owner, at[0] : at[0] + 16, at[1] : at[1] + 192] = s_out[rows, columns]
    write_halves(meta, gathered, 2, own_half, other_half)


def first_grads(meta, ids, x, dq, dk, dv, got, table_in, table_out):
    width = x.shape[1]
    return pl.pallas_call(
        first_grads_kernel,
        grid_spec=pltpu.PrefetchScalarGridSpec(
            num_scalar_prefetch=2,
            grid=(1,),
            in_specs=[whole((512, width))] * 4
            + [whole((2, 512, width))]
            + [table_spec(p, p, width) for p in range(3)] * 2,
            out_specs=[whole((512, 3 * width)), whole((512, 3 * RANK))] + [whole((4, 16, width))] * 2,
            scratch_shapes=[
                VMEM((3 * RANK, width), F32),
                VMEM((3 * RANK, 3 * width), F32),
                VMEM((4, 2 * RANK, 768), F32),
            ],
        ),
        out_shape=[jax.ShapeDtypeStruct((512, 3 * width), BF), jax.ShapeDtypeStruct((512, 3 * RANK), BF)]
        + [jax.ShapeDtypeStruct((4, 16, width), F32), jax.ShapeDtypeStruct((4, 16, width), BF)],
        compiler_params=pltpu.CompilerParams(vmem_limit_bytes=30 * MEBI),
        cost_estimate=SMALL_COST,
        name="first_grads",
    )(meta, ids, x, dq, dk, dv, got, *([table_in] * 3), *([table_out] * 3))


def input_grad_kernel(meta, ids, *refs):
    w_own, pieces = refs[0], one_each(refs[1:9])
    branch_ref, grads_ref, rank_grad_ref = refs[9:12]
    ins, parts = refs[12:15], refs[15:17]
    weight, wsems = refs[17:]
    copies = weight_copies(meta, w_own, pieces, weight, wsems, qkv_places)
    for copy in copies:
        copy.start()
    for copy in copies:
        copy.wait()
    in_all = jnp.concatenate([ref[0, 0] for ref in ins], axis=0)
    for r, ref in enumerate(parts):
        rows = pl.ds(pl.multiple_of(256 * ((meta[0] & 1) ^ r), 256), 256)
        ref[...] = (
            branch_ref[rows, :] + mm_nt(grads_ref[rows, :], weight[...]) + mm(rank_grad_ref[rows, :], in_all)
        ).astype(BF)


def project_back(meta, ids, w_own, pieces, branch, grads, rank_grad, table_in):
    width = branch.shape[1]
    return pl.pallas_call(
        input_grad_kernel,
        grid_spec=pltpu.PrefetchScalarGridSpec(
            num_scalar_prefetch=2,
            grid=(1,),
            in_specs=any_specs(9)
            + [whole((512, width)), whole((512, 3 * width)), whole((512, 3 * RANK))]
            + [table_spec(p, p, width) for p in range(3)],
            out_specs=[whole((256, width))] * 2,
            scratch_shapes=[VMEM((width, 3 * width), BF), pltpu.SemaphoreType.DMA((25,))],
        ),
        out_shape=[jax.ShapeDtypeStruct((256, width), BF)] * 2,
        compiler_params=pltpu.CompilerParams(vmem_limit_bytes=30 * MEBI),
        cost_estimate=SMALL_COST,
        name="project_back",
    )(meta, ids, w_own, *pieces, branch, grads, rank_grad, *([table_in] * 3))


def sum_cores_kernel(ids, mid_own, mid_other, first_own, first_other, *messages):
    row = lax.broadcasted_iota(jnp.int32, (16, 768), 0)
    lane = lax.broadcasted_iota(jnp.int32, (16, 768), 1)
    for r, ref in enumerate(messages):
        mid = mid_own[r] + mid_other[r].astype(F32)
        first = first_own[r] + first_other[r].astype(F32)
        for p in range(6):
            first = jnp.where((row >= 8) & (lane == 384 + p), ids[p].astype(F32), first)
        ref[...] = jnp.concatenate([mid, first], axis=0).astype(BF)


def sum_cores(ids, *halves):
    width = halves[0].shape[-1]
    return pl.pallas_call(
        sum_cores_kernel,
        grid_spec=pltpu.PrefetchScalarGridSpec(
            num_scalar_prefetch=1,
            grid=(1,),
            in_specs=[whole(half.shape) for half in halves],
            out_specs=[whole((40, width))] * 4,
        ),
        out_shape=[jax.ShapeDtypeStruct((40, width), BF)] * 4,
        compiler_params=pltpu.CompilerParams(vmem_limit_bytes=30 * MEBI),
        cost_estimate=SMALL_COST,
        name="sum_cores",
    )(ids, *halves)


def combine_kernel(ids, meta, own, other, in_d, in_f, out_d, out_f):
    for ref in (in_d, in_f, out_d, out_f):
        ref[...] = jnp.zeros_like(ref)
    narrow = in_d.shape[-1]
    for chip in range(4):
        for r in range(4):
            chosen = [ids[(chip * 4 + r) * 6 + p] for p in range(6)]
            for half, messages in enumerate((own, other)):
                ranks = pl.ds(pl.multiple_of(8 * ((meta[1] & 1) ^ half), 8), 8)
                part = messages[chip, r].astype(F32)
                in_f[chosen[5], ranks, :] += part[0:8]
                out_f[chosen[4], ranks, :] += part[8:16]
                for at, (ref, p, which) in enumerate(
                    (
                        (in_d, 3, 3), (in_d, 4, 4), (out_d, 3, 3), (out_d, 4, 5),
                        (in_d, 0, 0), (in_d, 1, 1), (in_d, 2, 2), (out_d, 0, 0),
                        (out_d, 1, 1), (out_d, 2, 2),
                    )
                ):
                    row, column = 16 + 8 * (at // 4), narrow * (at % 4)
                    ref[p, chosen[which], ranks, :] += part[row : row + 8, column : column + narrow]


def combine(ids, meta, own, other, tables, narrow, wide):
    shapes = [(5, tables, RANK, narrow), (tables, RANK, wide)] * 2
    return pl.pallas_call(
        combine_kernel,
        grid_spec=pltpu.PrefetchScalarGridSpec(
            num_scalar_prefetch=2,
            grid=(1,),
            in_specs=[whole(own.shape)] * 2,
            out_specs=[whole(shape) for shape in shapes],
        ),
        out_shape=[jax.ShapeDtypeStruct(shape, F32) for shape in shapes],
        compiler_params=pltpu.CompilerParams(vmem_limit_bytes=30 * MEBI),
        cost_estimate=SMALL_COST,
        name="combine",
    )(ids, meta, own, other)


def after(value, *others):
    return lax.optimization_barrier((value, *others))[0]


def beside(work, transfers, values, moved):
    given = lax.optimization_barrier((tuple(values), tuple(moved)))
    return lax.optimization_barrier((tuple(work(*given[0])), tuple(transfers(*given[1]))))


def paired_body(
    inputs,
    segments,
    random_key_blocks,
    adapter_index_table,
    frozen_query_key_value_weight,
    frozen_output_weight,
    frozen_up_weight,
    frozen_down_weight,
    attention_norm_gain,
    feedforward_norm_gain,
    adapter_down_from_width,
    adapter_down_from_hidden,
    adapter_up_to_width,
    adapter_up_to_hidden,
    cotangent,
):
    dp_count, shard_count = lax.axis_size("dp"), lax.axis_size("shard")
    d, z = lax.axis_index("dp"), lax.axis_index("shard")
    core = d & 1
    meta = jnp.stack([z, d]).astype(jnp.int32)

    def piece(weight, rows, columns, row, column):
        return lax.dynamic_slice(weight, (row, column), (rows, columns))

    def fetch(part):
        return [swap_shards(part, shard_count, step) for step in range(1, shard_count)]

    def slices(values):
        return [lax.dynamic_index_in_dim(values, (z & 1) ^ r, 0, keepdims=False) for r in range(2)]

    def chips(block, *offsets):
        return [swap_chips(block, dp_count, offset) for offset in offsets]

    def swap(block):
        return swap_cores(block, dp_count)

    qkv_own = jnp.stack(fetch(piece(frozen_query_key_value_weight, 48, 1152, (d >> 1) * 48, core * 1152)))
    up_piece = jnp.concatenate(
        [
            piece(frozen_output_weight, 48, 384, (d >> 1) * 48, core * 384),
            piece(frozen_up_weight, 192, 384, 0, d * 384),
        ],
        axis=0,
    )
    down_piece = piece(frozen_down_weight, 96, 768, d * 96, 0)
    down_piece = jnp.concatenate([down_piece[:, 0:384], down_piece[:, 384:768]], axis=0)
    seg_rows = jnp.pad(segments.astype(BF)[:, None, :], ((0, 0), (0, 15), (0, inputs.shape[-1] - 256)))
    own = send_away(slices(jnp.concatenate([inputs, seg_rows], axis=1)), dp_count, shard_count)
    there = swap_cores(adapter_index_table, dp_count)
    column_ids = jnp.where(
        core == 0,
        jnp.concatenate([adapter_index_table, there], axis=0),
        jnp.concatenate([there, adapter_index_table], axis=0),
    )
    ids = lax.dynamic_index_in_dim(column_ids, z, 0, keepdims=False)

    blocks = jnp.arange(16, dtype=jnp.int32)
    query_block = (8 * core + blocks[0:8])[None, :, None]
    key_block = jnp.where(blocks < 8, 8 * core + blocks, 8 * (1 - core) + blocks - 8)[None, None, :]
    drawn = lax.dynamic_slice_in_dim(random_key_blocks, 8 * core, 8, axis=1)
    allowed = (jnp.abs(query_block - key_block) <= 1) | (query_block < GLOBALS) | (key_block < GLOBALS)
    for n in range(RANDOMS):
        allowed = allowed | (drawn[:, :, n : n + 1] == key_block)
    closed = jnp.pad(jnp.where(allowed, 0.0, -BIG), ((0, 0), (0, 0), (16, 32)))
    closed = closed.reshape(H // 2, 2, 8, 64)
    closed = jnp.concatenate([closed[:, 1], closed[:, 0]], axis=-1)

    own, meta, closed, up_piece, down_piece = lax.optimization_barrier(
        (own, meta, closed, up_piece, down_piece)
    )
    tokens = own + [swap(part) for part in own]
    qkv_pieces = spread_over_cores((qkv_own, *chips(qkv_own, 2, 4, 6)), dp_count)
    up_own = fetch(after(up_piece, *own))

    def work(*given):
        return project_qkv(
            meta, ids, given[0:4], frozen_query_key_value_weight, given[4:],
            adapter_down_from_width, adapter_up_to_width,
        )

    (q, k, v, masks, hot, x), up_own = lax.optimization_barrier((work(*tokens, *qkv_pieces), up_own))
    up_own = jnp.stack(up_own)
    (mixed, shares), (up_x, up_y, *down_own) = beside(
        lambda *given: attend(*given, closed),
        lambda block, part: (*chips(block, 2, 4), *fetch(part)),
        (q, k, v, masks, hot),
        (up_own, down_piece),
    )
    down_own = jnp.stack(down_own)
    mixed, up_a, up_b, *others = lax.optimization_barrier(
        (
            mixed,
            *chips(up_x[:, 0:UP_SPLIT], 4),
            *chips(up_y[:, UP_SPLIT:], 2),
            swap(up_own),
            swap(up_x),
            swap(up_y),
        )
    )
    up_pieces = (up_own, others[0], up_x, others[1], up_y, others[2], up_a, up_b, swap(up_a), swap(up_b))
    gain1, gain2 = attention_norm_gain, feedforward_norm_gain

    def work(mixed, *pieces):
        return first_half(
            meta, ids, frozen_output_weight, frozen_up_weight, pieces, x, mixed, gain1,
            adapter_down_from_width, adapter_up_to_width, adapter_up_to_hidden,
        )

    (normal, inverse, active, slope), (*down_pieces, cot_a, cot_b) = beside(
        work,
        lambda block, values: (*chips(block, 2, 4, 6), *send_away(slices(values), dp_count, shard_count)),
        (mixed, *up_pieces),
        (after(down_own, up_a, up_b), cotangent),
    )
    down_pieces = spread_over_cores((down_own, *down_pieces), dp_count)
    cots = (cot_a, cot_b)
    results = second_half(
        meta, ids, cots, frozen_output_weight, frozen_up_weight, frozen_down_weight, up_pieces, down_pieces,
        normal, inverse, active, slope, mixed, gain1, gain2,
        adapter_down_from_width, adapter_down_from_hidden, adapter_up_to_width, adapter_up_to_hidden,
    )
    grad_branch = results[2]

    def home(r, part):
        return lax.ppermute(part, ("dp", "shard"), away_pairs(dp_count, shard_count, r))

    def swap_over_shards(*parts):
        return [swap_shards(part, shard_count, step + 1) for step, part in enumerate(parts)]

    (dq, dk, dv, other_sums), (layer_a, layer_b) = beside(
        lambda grad: attend_back(q, k, v, shares, grad, mixed),
        lambda part_a, part_b: (home(0, part_a), home(1, part_b)),
        (results[3],),
        results[0:2],
    )
    grads, rank_grad, first_own, first_other = first_grads(
        meta, ids, x, dq, dk, dv, swap(other_sums), adapter_down_from_width, adapter_up_to_width
    )
    input_parts, (first_other, mid_other) = beside(
        lambda grads: project_back(
            meta, ids, frozen_query_key_value_weight, qkv_pieces, grad_branch, grads, rank_grad,
            adapter_down_from_width,
        ),
        lambda *halves: [swap(half) for half in halves],
        (grads,),
        (first_other, results[5]),
    )
    message, *others = sum_cores(ids, results[4], mid_other, first_own, first_other)
    (layer_out,), moved = beside(
        lambda *parts: (join_parts(meta, parts, BF),),
        swap_over_shards,
        (layer_a, layer_b),
        others,
    )
    messages = jnp.stack([message, *moved])
    _, (part_a, part_b, *moved) = beside(
        lambda: (),
        lambda part_a, part_b, block: (home(0, part_a), home(1, part_b), *chips(block, 2, 4, 6)),
        (),
        (*input_parts, messages),
    )
    messages = jnp.stack([messages, *moved])
    chosen = messages[:, :, 32, 384:390].astype(jnp.int32).reshape(-1)
    in_d, in_f, out_d, out_f = combine(
        chosen, meta, messages, swap(messages), adapter_down_from_width.shape[1], 192, 768
    )
    return (layer_out, join_parts(meta, (part_a, part_b), F32), in_d, in_f, out_d, out_f)


def solution(mesh):
    dp_count, shard_count = mesh.shape["dp"], mesh.shape["shard"]
    paired = dp_count == 8 and shard_count == 4
    return jax.shard_map(
        paired_body if paired else general_body,
        mesh=mesh,
        in_specs=(
            P("dp", "shard", None),
            P("dp", "shard"),
            P(),
            P("dp", None),
            P("shard", None),
            P("shard", None),
            P("shard", None),
            P("shard", None),
            P(),
            P(),
            P(),
            P(),
            P(),
            P(),
            P("dp", "shard", None),
        ),
        out_specs=(
            P("dp", "shard", None),
            P("dp", "shard", None),
            P(None, None, None, "shard"),
            P(None, None, "shard"),
            P(None, None, None, "shard"),
            P(None, None, "shard"),
        ),
        check_vma=False,
    )
```

```python
import functools

import jax
import jax.numpy as jnp
from jax import lax
from jax.experimental import pallas as pl
from jax.experimental.pallas import tpu as pltpu
from jax.sharding import PartitionSpec as P

H = 12
HD = 64
BLOCK = 64
GLOBALS = 2
RANDOMS = 3


EPSILON = 1e-06
NEGATIVE = -1e30


def norm_rows(hidden, gain_vector):
    average = jnp.mean(hidden, axis=-1, keepdims=True)
    centred = hidden - average
    spread = jnp.mean(centred * centred, axis=-1, keepdims=True)
    return centred * lax.rsqrt(spread + EPSILON) * gain_vector


def gelu_exact(values):
    return jax.nn.gelu(values, approximate=False)


def dense_forward(inputs, weight):
    return jnp.einsum("sti,io->sto", inputs, weight, preferred_element_type=jnp.float32)


def dense_backward(grad_low, weight):
    return jnp.einsum("sto,io->sti", grad_low, weight, preferred_element_type=jnp.float32)


def adapt(inputs, down_rows, up_rows):
    rank_part = jnp.einsum(
        "sti,sri->str", inputs, down_rows, preferred_element_type=jnp.float32
    ).astype(jnp.bfloat16)
    return (
        rank_part,
        jnp.einsum("str,sro->sto", rank_part, up_rows, preferred_element_type=jnp.float32),
    )


def adapt_back(inputs, down_rows, up_rows, rank_part, grad_low):
    grad_up = jnp.einsum("str,sto->sro", rank_part, grad_low, preferred_element_type=jnp.float32)
    rank_grad = jnp.einsum(
        "sto,sro->str", grad_low, up_rows, preferred_element_type=jnp.float32
    ).astype(jnp.bfloat16)
    grad_down = jnp.einsum("str,sti->sri", rank_grad, inputs, preferred_element_type=jnp.float32)
    grad_inputs = jnp.einsum(
        "str,sri->sti", rank_grad, down_rows, preferred_element_type=jnp.float32
    )
    return (grad_down, grad_up, grad_inputs)


def table_sum(per_sequence, chosen, table_size):
    matches = (chosen[:, None] == jnp.arange(table_size, dtype=jnp.int32)[None, :]).astype(
        jnp.float32
    )
    return jnp.sum(matches[:, :, None, None] * per_sequence[:, None], axis=0)


def sparse_scores(query_heads, key_picked, permit, scaling):
    scores = (
        jnp.einsum(
            "shbqd,shbkd->shbqk", query_heads, key_picked, preferred_element_type=jnp.float32
        )
        * scaling
    )
    return jnp.where(permit, scores, NEGATIVE)


def global_scores(query_rows, key_rows, seg_query, seg_keys, scaling):
    scores = (
        jnp.einsum("hqd,hkd->hqk", query_rows, key_rows, preferred_element_type=jnp.float32)
        * scaling
    )
    return jnp.where((seg_query[:, None] == seg_keys[None, :])[None], scores, NEGATIVE)


def global_forward(query_rows, key_rows, value_rows, seg_query, seg_keys, scaling):
    scores = global_scores(query_rows, key_rows, seg_query, seg_keys, scaling)
    top_score = jnp.max(scores, axis=-1, keepdims=True)
    weights = jnp.exp(scores - top_score)
    totals = jnp.sum(weights, axis=-1, keepdims=True)
    shares = (weights / totals).astype(jnp.bfloat16)
    attended = jnp.einsum("hqk,hkd->hqd", shares, value_rows, preferred_element_type=jnp.float32)
    return (attended, (top_score + jnp.log(totals))[..., 0])


def global_backward(
    query_rows, key_rows, value_rows, seg_query, seg_keys, grad_rows, log_total, scaling
):
    scores = global_scores(query_rows, key_rows, seg_query, seg_keys, scaling)
    shares = jnp.exp(scores - log_total[..., None])
    share_low = shares.astype(jnp.bfloat16)
    grad_shares = jnp.einsum(
        "hqd,hkd->hqk", grad_rows, value_rows, preferred_element_type=jnp.float32
    )
    centre = jnp.sum(shares * grad_shares, axis=-1, keepdims=True)
    grad_scores = (shares * (grad_shares - centre)).astype(jnp.bfloat16)
    grad_query = (
        jnp.einsum("hqk,hkd->hqd", grad_scores, key_rows, preferred_element_type=jnp.float32)
        * scaling
    )
    grad_keys = (
        jnp.einsum("hqk,hqd->hkd", grad_scores, query_rows, preferred_element_type=jnp.float32)
        * scaling
    )
    grad_values = jnp.einsum(
        "hqk,hqd->hkd", share_low, grad_rows, preferred_element_type=jnp.float32
    )
    return (grad_query, grad_keys, grad_values, centre[..., 0])


def general_body(
    inputs,
    segments,
    random_key_blocks,
    adapter_index_table,
    frozen_query_key_value_weight,
    frozen_output_weight,
    frozen_up_weight,
    frozen_down_weight,
    attention_norm_gain,
    feedforward_norm_gain,
    adapter_down_from_width,
    adapter_down_from_hidden,
    adapter_up_to_width,
    adapter_up_to_hidden,
    cotangent,
):
    seq_count = inputs.shape[0]
    local_tokens = inputs.shape[1]
    width = inputs.shape[2]
    shard_count = lax.axis_size("shard")
    full_length = local_tokens * shard_count
    total_blocks = full_length // BLOCK
    local_blocks = local_tokens // BLOCK
    cand_count = 3 + GLOBALS + RANDOMS
    glob_rows = GLOBALS * BLOCK
    scaling = HD ** (-0.5)

    def select_adapter_table(table, table_column):
        return jnp.take(table, adapter_index_table[:, table_column], axis=0)

    adapter_tables_input = [
        select_adapter_table(adapter_down_from_width[table_column], table_column)
        for table_column in range(5)
    ] + [select_adapter_table(adapter_down_from_hidden, 5)]
    adapter_tables_output = [
        select_adapter_table(adapter_up_to_width[table_column], table_column)
        for table_column in range(4)
    ]
    adapter_tables_output = adapter_tables_output + [
        select_adapter_table(adapter_up_to_hidden, 4),
        select_adapter_table(adapter_up_to_width[4], 5),
    ]
    qkv_full, out_full = (
        lax.all_gather(frozen_query_key_value_weight, "shard", axis=0, tiled=True),
        lax.all_gather(frozen_output_weight, "shard", axis=0, tiled=True),
    )
    main_part = dense_forward(inputs, qkv_full)
    rank_parts = []
    projected = []
    for table_column in range(3):
        rank_part, extra = adapt(
            inputs, adapter_tables_input[table_column], adapter_tables_output[table_column]
        )
        rank_parts.append(rank_part)
        projected.append(
            (main_part[..., table_column * width : (table_column + 1) * width] + extra).astype(
                jnp.bfloat16
            )
        )
    seg_low = segments.astype(jnp.bfloat16)
    key_all, value_all, seg_all = (
        lax.all_gather(projected[1], "shard", axis=1, tiled=True),
        lax.all_gather(projected[2], "shard", axis=1, tiled=True),
        lax.all_gather(seg_low, "shard", axis=1, tiled=True),
    )
    shard_pos = lax.axis_index("shard")
    is_first = shard_pos == 0
    first_block = shard_pos * local_blocks
    block_ids = first_block + jnp.arange(local_blocks, dtype=jnp.int32)
    rand_local = lax.dynamic_slice_in_dim(random_key_blocks, first_block, local_blocks, axis=1)
    window_part = jnp.stack([block_ids - 1, block_ids, block_ids + 1], axis=-1)
    global_ids = jnp.broadcast_to(
        jnp.arange(GLOBALS, dtype=jnp.int32)[None, :], (local_blocks, GLOBALS)
    )
    fixed_part = jnp.concatenate([window_part, global_ids], axis=-1)
    candidates = jnp.concatenate(
        [jnp.broadcast_to(fixed_part[None], (H, local_blocks, 3 + GLOBALS)), rand_local], axis=-1
    )
    candidates = jnp.clip(candidates, 0, total_blocks - 1)
    always_true = jnp.ones((local_blocks,), dtype=bool)
    fixed_valid = jnp.stack(
        [block_ids - 1 >= GLOBALS, always_true, block_ids + 1 < total_blocks]
        + [always_true] * GLOBALS,
        axis=-1,
    )
    valid = jnp.concatenate(
        [
            jnp.broadcast_to(fixed_valid[None], (H, local_blocks, 3 + GLOBALS)),
            jnp.ones((H, local_blocks, RANDOMS), dtype=bool),
        ],
        axis=-1,
    )
    valid_keys = jnp.repeat(valid, BLOCK, axis=-1)
    query_heads = (
        projected[0].reshape(seq_count, local_blocks, BLOCK, H, HD).transpose(0, 3, 1, 2, 4)
    )
    key_source = key_all.reshape(seq_count, total_blocks, BLOCK, H, HD).transpose(0, 3, 1, 2, 4)
    value_source = value_all.reshape(seq_count, total_blocks, BLOCK, H, HD).transpose(0, 3, 1, 2, 4)
    head_index = jnp.arange(H, dtype=jnp.int32)[:, None, None]
    key_picked = key_source[:, head_index, candidates].reshape(
        seq_count, H, local_blocks, cand_count * BLOCK, HD
    )
    value_picked = value_source[:, head_index, candidates].reshape(
        seq_count, H, local_blocks, cand_count * BLOCK, HD
    )
    seg_picked = seg_all.reshape(seq_count, total_blocks, BLOCK)[:, candidates].reshape(
        seq_count, H, local_blocks, cand_count * BLOCK
    )
    seg_local = seg_low.reshape(seq_count, local_blocks, BLOCK)
    permit = valid_keys[None, :, :, None, :] & (
        seg_local[:, None, :, :, None] == seg_picked[:, :, :, None, :]
    )
    scores = sparse_scores(query_heads, key_picked, permit, scaling)
    top_score = jnp.max(scores, axis=-1, keepdims=True)
    weights = jnp.exp(scores - top_score)
    totals = jnp.sum(weights, axis=-1, keepdims=True)
    share_low = (weights / totals).astype(jnp.bfloat16)
    sparse_lse = (top_score + jnp.log(totals))[..., 0]
    sparse_out = jnp.einsum(
        "shbqk,shbkd->shbqd", share_low, value_picked, preferred_element_type=jnp.float32
    )
    key_heads = key_source.reshape(seq_count, H, full_length, HD)
    value_heads = value_source.reshape(seq_count, H, full_length, HD)
    glob_query = query_heads[:, :, :GLOBALS].reshape(seq_count, H, glob_rows, HD)
    glob_seg = seg_low[:, :glob_rows]

    def run_forward(operands):
        return lax.map(
            lambda packet: global_forward(
                packet[0], packet[1], packet[2], packet[3], packet[4], scaling
            ),
            operands,
        )

    def skip_forward(operands):
        return (
            jnp.zeros((seq_count, H, glob_rows, HD), jnp.float32),
            jnp.zeros((seq_count, H, glob_rows), jnp.float32),
        )

    global_out, global_lse = lax.cond(
        is_first, run_forward, skip_forward, (glob_query, key_heads, value_heads, glob_seg, seg_all)
    )
    glob_blocks = global_out.reshape(seq_count, H, GLOBALS, BLOCK, HD)
    head_out = jnp.concatenate(
        [jnp.where(is_first, glob_blocks, sparse_out[:, :, :GLOBALS]), sparse_out[:, :, GLOBALS:]],
        axis=2,
    )
    mixed_low = (
        head_out.transpose(0, 2, 3, 1, 4)
        .reshape(seq_count, local_tokens, width)
        .astype(jnp.bfloat16)
    )
    rank_out, extra_out = adapt(mixed_low, adapter_tables_input[3], adapter_tables_output[3])
    branch = dense_forward(mixed_low, out_full) + extra_out
    first, first_pull = jax.vjp(
        lambda hidden: norm_rows(hidden, attention_norm_gain), inputs.astype(jnp.float32) + branch
    )
    first_low = first.astype(jnp.bfloat16)
    up_full, down_full = (
        lax.all_gather(frozen_up_weight, "shard", axis=0, tiled=True),
        lax.all_gather(frozen_down_weight, "shard", axis=0, tiled=True),
    )
    rank_up, extra_up = adapt(first_low, adapter_tables_input[4], adapter_tables_output[4])
    lifted = dense_forward(first_low, up_full) + extra_up
    activated, gelu_pull = jax.vjp(gelu_exact, lifted)
    active_low = activated.astype(jnp.bfloat16)
    rank_down, extra_down = adapt(active_low, adapter_tables_input[5], adapter_tables_output[5])
    lowered = dense_forward(active_low, down_full) + extra_down
    result, final_pull = jax.vjp(
        lambda hidden: norm_rows(hidden, feedforward_norm_gain), first + lowered
    )
    layer_out = result.astype(jnp.bfloat16)
    up_back, down_back = (
        lax.all_gather(frozen_up_weight, "shard", axis=0, tiled=True),
        lax.all_gather(frozen_down_weight, "shard", axis=0, tiled=True),
    )
    grad_adapt_in = [None] * 6
    grad_adapt_out = [None] * 6
    (grad_sum,) = final_pull(cotangent.astype(jnp.float32))
    grad_lowered = grad_sum.astype(jnp.bfloat16)
    grad_adapt_in[5], grad_adapt_out[5], extra_grad = adapt_back(
        active_low, adapter_tables_input[5], adapter_tables_output[5], rank_down, grad_lowered
    )
    grad_active = dense_backward(grad_lowered, down_back) + extra_grad
    (grad_lifted,) = gelu_pull(grad_active)
    grad_lift_low = grad_lifted.astype(jnp.bfloat16)
    grad_adapt_in[4], grad_adapt_out[4], extra_grad = adapt_back(
        first_low, adapter_tables_input[4], adapter_tables_output[4], rank_up, grad_lift_low
    )
    grad_first = grad_sum + dense_backward(grad_lift_low, up_back) + extra_grad
    (grad_branch,) = first_pull(grad_first)
    grad_branch_low = grad_branch.astype(jnp.bfloat16)
    qkv_back, out_back = (
        lax.all_gather(frozen_query_key_value_weight, "shard", axis=0, tiled=True),
        lax.all_gather(frozen_output_weight, "shard", axis=0, tiled=True),
    )
    grad_adapt_in[3], grad_adapt_out[3], extra_grad = adapt_back(
        mixed_low, adapter_tables_input[3], adapter_tables_output[3], rank_out, grad_branch_low
    )
    grad_mixed = (dense_backward(grad_branch_low, out_back) + extra_grad).astype(jnp.bfloat16)
    grad_heads = grad_mixed.reshape(seq_count, local_blocks, BLOCK, H, HD).transpose(0, 3, 1, 2, 4)
    row_keep = (block_ids >= GLOBALS)[None, None, :, None, None]
    grad_sparse = jnp.where(row_keep, grad_heads, jnp.zeros_like(grad_heads))
    scores = sparse_scores(query_heads, key_picked, permit, scaling)
    shares = jnp.exp(scores - sparse_lse[..., None])
    share_low = shares.astype(jnp.bfloat16)
    grad_shares = jnp.einsum(
        "shbqd,shbkd->shbqk", grad_sparse, value_picked, preferred_element_type=jnp.float32
    )
    centre = jnp.sum(shares * grad_shares, axis=-1, keepdims=True)
    grad_scores = (shares * (grad_shares - centre)).astype(jnp.bfloat16)
    grad_query = (
        jnp.einsum(
            "shbqk,shbkd->shbqd", grad_scores, key_picked, preferred_element_type=jnp.float32
        )
        * scaling
    )
    glob_grad = grad_heads[:, :, :GLOBALS].reshape(seq_count, H, glob_rows, HD)

    def run_backward(operands):
        return lax.map(
            lambda packet: global_backward(
                packet[0], packet[1], packet[2], packet[3], packet[4], packet[5], packet[6], scaling
            ),
            operands,
        )

    def skip_backward(operands):
        return (
            jnp.zeros((seq_count, H, glob_rows, HD), jnp.float32),
            jnp.zeros((seq_count, H, full_length, HD), jnp.float32),
            jnp.zeros((seq_count, H, full_length, HD), jnp.float32),
            jnp.zeros((seq_count, H, glob_rows), jnp.float32),
        )

    glob_dq, glob_dk, glob_dv, glob_centre = lax.cond(
        is_first,
        run_backward,
        skip_backward,
        (glob_query, key_heads, value_heads, glob_seg, seg_all, glob_grad, global_lse),
    )
    grad_query = grad_query.at[:, :, :GLOBALS].add(
        glob_dq.reshape(seq_count, H, GLOBALS, BLOCK, HD)
    )
    grad_key_picked = (
        jnp.einsum(
            "shbqk,shbqd->shbkd", grad_scores, query_heads, preferred_element_type=jnp.float32
        )
        * scaling
    )
    grad_value_picked = jnp.einsum(
        "shbqk,shbqd->shbkd", share_low, grad_sparse, preferred_element_type=jnp.float32
    )
    block_shape = (seq_count, H, local_blocks, cand_count, BLOCK, HD)
    key_grad_blocks = (
        jnp.zeros((seq_count, H, total_blocks, BLOCK, HD), jnp.float32)
        .at[:, head_index, candidates]
        .add(grad_key_picked.reshape(block_shape))
    )
    value_grad_blocks = (
        jnp.zeros((seq_count, H, total_blocks, BLOCK, HD), jnp.float32)
        .at[:, head_index, candidates]
        .add(grad_value_picked.reshape(block_shape))
    )
    key_grad_full = (
        (key_grad_blocks.reshape(seq_count, H, full_length, HD) + glob_dk)
        .transpose(0, 2, 1, 3)
        .reshape(seq_count, full_length, width)
    )
    value_grad_full = (
        (value_grad_blocks.reshape(seq_count, H, full_length, HD) + glob_dv)
        .transpose(0, 2, 1, 3)
        .reshape(seq_count, full_length, width)
    )
    key_grad, value_grad = (
        lax.psum_scatter(
            key_grad_full.astype(jnp.bfloat16), "shard", scatter_dimension=1, tiled=True
        ).astype(jnp.float32),
        lax.psum_scatter(
            value_grad_full.astype(jnp.bfloat16), "shard", scatter_dimension=1, tiled=True
        ).astype(jnp.float32),
    )
    query_grad = grad_query.transpose(0, 2, 3, 1, 4).reshape(seq_count, local_tokens, width)
    grad_proj = [
        query_grad.astype(jnp.bfloat16),
        key_grad.astype(jnp.bfloat16),
        value_grad.astype(jnp.bfloat16),
    ]
    input_grad = grad_branch + dense_backward(jnp.concatenate(grad_proj, axis=-1), qkv_back)
    for table_column in range(3):
        grad_adapt_in[table_column], grad_adapt_out[table_column], extra_grad = adapt_back(
            inputs,
            adapter_tables_input[table_column],
            adapter_tables_output[table_column],
            rank_parts[table_column],
            grad_proj[table_column],
        )
        input_grad = input_grad + extra_grad
    adapter_table_count = adapter_down_from_width.shape[1]
    grad_in_d = jnp.stack(
        [
            table_sum(
                grad_adapt_in[table_column],
                adapter_index_table[:, table_column],
                adapter_table_count,
            )
            for table_column in range(5)
        ],
        axis=0,
    )
    grad_in_f = table_sum(grad_adapt_in[5], adapter_index_table[:, 5], adapter_table_count)
    out_list = [
        table_sum(
            grad_adapt_out[table_column], adapter_index_table[:, table_column], adapter_table_count
        )
        for table_column in range(4)
    ]
    grad_out_d = jnp.stack(
        out_list + [table_sum(grad_adapt_out[5], adapter_index_table[:, 5], adapter_table_count)],
        axis=0,
    )
    grad_out_f = table_sum(grad_adapt_out[4], adapter_index_table[:, 4], adapter_table_count)
    owned = (
        lax.psum_scatter(
            grad_in_d.astype(jnp.bfloat16), "shard", scatter_dimension=3, tiled=True
        ).astype(jnp.float32),
        lax.psum_scatter(
            grad_in_f.astype(jnp.bfloat16), "shard", scatter_dimension=2, tiled=True
        ).astype(jnp.float32),
        lax.psum_scatter(
            grad_out_d.astype(jnp.bfloat16), "shard", scatter_dimension=3, tiled=True
        ).astype(jnp.float32),
        lax.psum_scatter(
            grad_out_f.astype(jnp.bfloat16), "shard", scatter_dimension=2, tiled=True
        ).astype(jnp.float32),
    )
    summed = (
        lax.psum(owned[0].astype(jnp.bfloat16), "dp").astype(jnp.float32),
        lax.psum(owned[1].astype(jnp.bfloat16), "dp").astype(jnp.float32),
        lax.psum(owned[2].astype(jnp.bfloat16), "dp").astype(jnp.float32),
        lax.psum(owned[3].astype(jnp.bfloat16), "dp").astype(jnp.float32),
    )
    return (layer_out, input_grad, summed[0], summed[1], summed[2], summed[3])


BF = jnp.bfloat16
F32 = jnp.float32
NT = (((1,), (1,)), ((), ()))
TN = (((0,), (0,)), ((), ()))
BIG = 1e30
RANK = 16
ANY = pl.ANY
VMEM = pltpu.VMEM
MEBI = 1024 * 1024
SMALL_COST = pl.CostEstimate(flops=1_000_000, bytes_accessed=100_000, transcendentals=0)


def mm(left, right):
    return jnp.dot(left, right, preferred_element_type=F32)


def mm_nt(left, right):
    return lax.dot_general(left, right, NT, preferred_element_type=F32)


def mm_tn(left, right):
    return lax.dot_general(left, right, TN, preferred_element_type=F32)


def whole(shape):
    return pl.BlockSpec(shape, lambda *_: (0,) * len(shape))


def away_pairs(dp_count, shard_count, step):
    pairs = []
    for chip in range(dp_count // 2):
        for k in range(2):
            for z in range(shard_count):
                m = (z & 1) ^ step
                source = (2 * chip + k) * shard_count + z
                target = (2 * chip + (z >> 1)) * shard_count + 2 * k + m
                pairs.append((source, target))
    return pairs


def swap_cores(value, dp_count):
    return lax.ppermute(value, "dp", [(i, i ^ 1) for i in range(dp_count)])


def swap_shards(value, shard_count, step):
    return lax.ppermute(value, "shard", [(i, i ^ step) for i in range(shard_count)])


def spread_over_chips(block, dp_count):
    others = [lax.ppermute(block, "dp", [(i, i ^ o) for i in range(dp_count)]) for o in range(2, dp_count, 2)]
    return [block] + others


def swap_chips(block, dp_count, offset):
    return lax.ppermute(block, "dp", [(i, i ^ offset) for i in range(dp_count)])


def spread_over_cores(blocks, dp_count):
    return [one for block in blocks for one in (block, swap_cores(block, dp_count))]


def spread_in_plane(block, dp_count):
    return spread_over_cores(spread_over_chips(block, dp_count), dp_count)


def join_kernel(meta, part0, part1, out_ref):
    for r, part in enumerate((part0, part1)):
        out_ref[(meta[0] & 1) ^ r] = part[...].astype(out_ref.dtype)


def join_parts(meta, parts, dtype):
    rows, width = parts[0].shape
    return pl.pallas_call(
        join_kernel,
        grid_spec=pltpu.PrefetchScalarGridSpec(
            num_scalar_prefetch=1,
            grid=(1,),
            in_specs=[whole((rows, width))] * 2,
            out_specs=whole((2, rows, width)),
        ),
        out_shape=jax.ShapeDtypeStruct((2, rows, width), dtype),
        compiler_params=pltpu.CompilerParams(vmem_limit_bytes=30 * MEBI),
        cost_estimate=SMALL_COST,
        name="join_parts",
    )(meta, *parts)


def send_away(parts, dp_count, shard_count):
    return [
        lax.ppermute(part, ("dp", "shard"), away_pairs(dp_count, shard_count, r))
        for r, part in enumerate(parts)
    ]


def weight_copies(meta, own_ref, pieces, dest, sems, places):
    z, d = meta[0], meta[1]
    own_rows, columns = own_ref.shape
    copies = [
        pltpu.make_async_copy(
            own_ref, dest.at[pl.ds(pl.multiple_of(z * own_rows, 16), own_rows)], sems.at[0]
        )
    ]
    count = 1
    for o, parts in enumerate(pieces):
        who = d ^ o
        for step in range(3):
            shard = z ^ (step + 1)
            for start, row, column, rows, cols in places(who):
                for piece, first in parts:
                    low, high = max(start, first), min(start + rows, first + piece.shape[1])
                    if low >= high:
                        continue
                    copies.append(
                        pltpu.make_async_copy(
                            piece.at[step, pl.ds(low - first, high - low)],
                            dest.at[
                                pl.ds(pl.multiple_of(shard * own_rows + row + low - start, 16), high - low),
                                pl.ds(pl.multiple_of(column, 128), cols),
                            ],
                            sems.at[count],
                        )
                    )
                    count += 1
    return copies


def one_each(refs):
    return [[(ref, 0)] for ref in refs]


UP_SPLIT = 128


def up_parts(refs):
    return one_each(refs[0:6]) + [[(refs[6], 0), (refs[7], UP_SPLIT)], [(refs[8], 0), (refs[9], UP_SPLIT)]]


def qkv_places(who):
    return [(0, (who >> 1) * 48, (who & 1) * 1152, 48, 1152)]


def out_places(who):
    return [(0, (who >> 1) * 48, (who & 1) * 384, 48, 384)]


def up_places(who):
    return [(48, 0, who * 384, 192, 384)]


def down_places(who):
    return [(0, who * 96, 0, 96, 384), (96, who * 96, 384, 96, 384)]


def token_copies(meta, messages, dest, sems):
    copies = []
    for at, message in enumerate(messages):
        row = 512 * (at >> 1) + 256 * ((meta[0] & 1) ^ (at & 1))
        copies.append(
            pltpu.make_async_copy(
                message.at[pl.ds(0, 256)], dest.at[pl.ds(pl.multiple_of(row, 256), 256)], sems.at[at]
            )
        )
    return copies


def zero_padded(rows, position, count):
    zeros = jnp.zeros_like(rows)
    return jnp.concatenate([rows if i == position else zeros for i in range(count)], axis=0)


def qkv_kernel(meta, ids, *refs):
    messages, w_own, pieces = refs[0:4], refs[4], one_each(refs[5:13])
    ins, outs = refs[13:16], refs[16:19]
    q_ref, k_ref, v_ref, mask_ref, hot_ref, own_ref = refs[19:25]
    xs, segs, weight, wsems, xsems, ssems = refs[25:]
    copies = token_copies(meta, messages, xs, xsems)
    for at, message in enumerate(messages):
        copies.append(
            pltpu.make_async_copy(
                message.at[pl.ds(256, 16), pl.ds(0, 256)],
                segs.at[2 * (at >> 1) + ((meta[0] & 1) ^ (at & 1))],
                ssems.at[at],
            )
        )
    copies += weight_copies(meta, w_own, pieces, weight, wsems, qkv_places)
    for copy in copies:
        copy.start()
    for copy in copies:
        copy.wait()
    lane = lax.broadcasted_iota(jnp.int32, (128, 128), 1)
    lane_of_head = lax.rem(lane, 64)
    as_float = lane_of_head.astype(F32)
    is_segment = lane_of_head < 16
    row_block = lax.broadcasted_iota(jnp.int32, (128, 128), 0) // 64
    for place in range(4):
        row = segs[place].astype(F32)[0:1]
        for half in range(2):
            column = jnp.broadcast_to(row[:, 128 * half : 128 * half + 128], (128, 128)).T
            same = column == as_float
            block_lane = lane_of_head == 16 + 4 * place + 2 * half + row_block
            rows = slice(256 * place + 128 * half, 256 * place + 128 * half + 128)
            mask_ref[rows] = jnp.where(
                is_segment, jnp.where(same, 0.0, -BIG), jnp.where(block_lane, 1.0, 0.0)
            ).astype(BF)
            if place < 2:
                hot_ref[rows] = jnp.where(is_segment & same, 1.0, 0.0).astype(BF)
    own_ref[...] = xs[0:512]
    in_all = jnp.concatenate([ref[0, 0] for ref in ins], axis=0)
    out_all = [zero_padded(ref[0, 0], p, 3) for p, ref in enumerate(outs)]
    targets = (q_ref, k_ref, v_ref)
    for tile in range(4):
        rows = slice(256 * tile, 256 * tile + 256)
        x = xs[rows]
        rank = mm_nt(x, in_all).astype(BF)
        for p in range(0 if tile < 2 else 1, 3):
            value = mm(x, weight[:, 768 * p : 768 * p + 768]) + mm(rank, out_all[p])
            value = value.astype(BF)
            if p == 0:
                value = (value.astype(F32) * HD**-0.5).astype(BF)
            targets[p][rows] = value


def table_spec(p, column, width):
    return pl.BlockSpec((1, 1, RANK, width), lambda i, meta, ids: (p, ids[column], 0, 0))


def hidden_spec(column, width):
    return pl.BlockSpec((1, RANK, width), lambda i, meta, ids: (ids[column], 0, 0))


def any_specs(count):
    return [pl.BlockSpec(memory_space=ANY)] * count


def project_qkv(meta, ids, messages, w_own, pieces, table_in, table_out):
    width = w_own.shape[1] // 3
    return pl.pallas_call(
        qkv_kernel,
        grid_spec=pltpu.PrefetchScalarGridSpec(
            num_scalar_prefetch=2,
            grid=(1,),
            in_specs=any_specs(13)
            + [table_spec(p, p, width) for p in range(3)]
            + [table_spec(p, p, width) for p in range(3)],
            out_specs=[
                whole((512, width)),
                whole((1024, width)),
                whole((1024, width)),
                whole((1024, 128)),
                whole((512, 128)),
                whole((512, width)),
            ],
            scratch_shapes=[
                VMEM((1024, width), BF),
                VMEM((4, 16, 256), BF),
                VMEM((width, 3 * width), BF),
                pltpu.SemaphoreType.DMA((25,)),
                pltpu.SemaphoreType.DMA((4,)),
                pltpu.SemaphoreType.DMA((4,)),
            ],
        ),
        out_shape=[
            jax.ShapeDtypeStruct((512, width), BF),
            jax.ShapeDtypeStruct((1024, width), BF),
            jax.ShapeDtypeStruct((1024, width), BF),
            jax.ShapeDtypeStruct((1024, 128), BF),
            jax.ShapeDtypeStruct((512, 128), BF),
            jax.ShapeDtypeStruct((512, width), BF),
        ],
        compiler_params=pltpu.CompilerParams(vmem_limit_bytes=56 * MEBI),
        cost_estimate=SMALL_COST,
        name="project_qkv",
    )(meta, ids, *messages, w_own, *pieces, *([table_in] * 3), *([table_out] * 3))


def attend_kernel(q_ref, k_ref, v_ref, mask_ref, hot_ref, closed_ref, o_ref, p_ref):
    low = lax.broadcasted_iota(jnp.int32, (512, 128), 1) < 64
    low_keys = lax.broadcasted_iota(jnp.int32, (1024, 128), 1) < 64
    closed = jnp.concatenate(
        [jnp.broadcast_to(closed_ref[0, l : l + 1], (64, 128)) for l in range(8)], axis=0
    )
    extra = (hot_ref[...].astype(F32) + closed).astype(BF)
    q, k, v, masks = q_ref[...], k_ref[...], v_ref[...], mask_ref[...]
    wide = [(jnp.where(low, q, extra), jnp.where(low_keys, k, masks)), (jnp.where(low, extra, q), jnp.where(low_keys, masks, k))]
    size = 512
    units = [(start, head) for start in range(0, 512, size) for head in range(2)]
    raw = lambda unit: mm_nt(wide[unit[1]][0][unit[0] : unit[0] + size], wide[unit[1]][1])
    ahead = raw(units[0])
    mixed = {}
    for n, (start, head) in enumerate(units):
        scores = ahead
        if n + 1 < len(units):
            ahead = raw(units[n + 1])
        weights = jnp.exp(scores - jnp.max(scores, axis=1, keepdims=True))
        shares = (weights * (1.0 / jnp.sum(weights, axis=1, keepdims=True))).astype(BF)
        p_ref[head, start : start + size] = shares
        mixed[head] = mm(shares, v)
        if head == 1:
            o_ref[start : start + size] = jnp.where(low[0:size], mixed[0], mixed[1]).astype(BF)


def attend(q, k, v, masks, hot, closed):
    width = q.shape[1]
    pairs = width // 128
    half = pl.BlockSpec((512, 128), lambda g: (0, g))
    full = pl.BlockSpec((1024, 128), lambda g: (0, g))
    return pl.pallas_call(
        attend_kernel,
        grid=(pairs,),
        in_specs=[
            half,
            full,
            full,
            whole((1024, 128)),
            whole((512, 128)),
            pl.BlockSpec((1, 8, 128), lambda g: (g, 0, 0)),
        ],
        out_specs=[half, pl.BlockSpec((2, 512, 1024), lambda g: (g, 0, 0))],
        out_shape=[
            jax.ShapeDtypeStruct((512, width), BF),
            jax.ShapeDtypeStruct((2 * pairs, 512, 1024), BF),
        ],
        compiler_params=pltpu.CompilerParams(vmem_limit_bytes=56 * MEBI),
        cost_estimate=SMALL_COST,
        name="attend",
    )(q, k, v, masks, hot, closed)


def attend_back_kernel(q_ref, k_ref, v_ref, p_ref, grad_ref, mixed_ref, dq_ref, dk_own, dv_own, other_ref):
    low = lax.broadcasted_iota(jnp.int32, (512, 128), 1) < 64
    q, k, v, grad = q_ref[...], k_ref[...], v_ref[...], grad_ref[...]
    products = grad.astype(F32) * mixed_ref[...].astype(F32)
    q_turned, grad_turned = q.T, grad.T
    zeros, none = jnp.zeros_like(grad), jnp.zeros_like(products)
    dq, dk, dv = [], [], []
    for head in range(2):
        mine = low if head == 0 else jnp.logical_not(low)
        centre = jnp.sum(jnp.where(mine, products, none), axis=1, keepdims=True)
        grad_shares = mm_nt(jnp.where(mine, grad, zeros), v)
        shares = p_ref[head]
        grad_scores = (shares.astype(F32) * (grad_shares - centre)).astype(BF)
        rows = slice(64 * head, 64 * head + 64)
        dq.append(mm(grad_scores, k))
        dk.append(mm(q_turned[rows], grad_scores))
        dv.append(mm(grad_turned[rows], shares))
    dq_ref[...] = (jnp.where(low, dq[0], dq[1]) * HD**-0.5).astype(BF)
    dk = jnp.concatenate(dk, axis=0).T
    dv = jnp.concatenate(dv, axis=0).T
    dk_own[...] = dk[0:512].astype(BF)
    dv_own[...] = dv[0:512].astype(BF)
    other_ref[0] = dk[512:1024].astype(BF)
    other_ref[1] = dv[512:1024].astype(BF)


def attend_back(q, k, v, shares, grad, mixed):
    width = q.shape[1]
    half = pl.BlockSpec((512, 128), lambda g: (0, g))
    full = pl.BlockSpec((1024, 128), lambda g: (0, g))
    return pl.pallas_call(
        attend_back_kernel,
        grid=(width // 128,),
        in_specs=[half, full, full, pl.BlockSpec((2, 512, 1024), lambda g: (g, 0, 0)), half, half],
        out_specs=[half] * 3 + [pl.BlockSpec((2, 512, 128), lambda g: (0, 0, g))],
        out_shape=[
            jax.ShapeDtypeStruct((512, width), BF),
            jax.ShapeDtypeStruct((512, width), BF),
            jax.ShapeDtypeStruct((512, width), BF),
            jax.ShapeDtypeStruct((2, 512, width), BF),
        ],
        compiler_params=pltpu.CompilerParams(vmem_limit_bytes=45 * MEBI),
        cost_estimate=SMALL_COST,
        name="attend_back",
    )(q, k, v, shares, grad, mixed)


def gelu_and_slope(lifted):
    size = jnp.abs(lifted)
    t = 1.0 / (1.0 + 0.23164189 * size)
    poly = t * (
        0.127414796 + t * (-0.142248368 + t * (0.7107068705 + t * (-0.7265760135 + t * 0.5307027145)))
    )
    decay = jnp.exp2(lifted * lifted * -0.7213475204444817)
    tail = poly * decay
    below = jnp.where(lifted < 0.0, tail, 1.0 - tail)
    return jnp.maximum(lifted, 0.0) - size * tail, below + lifted * (decay * 0.3989422804014327)


def norm_parts(hidden):
    average = jnp.mean(hidden, axis=-1, keepdims=True)
    centred = hidden - average
    spread = jnp.mean(centred * centred, axis=-1, keepdims=True)
    inverse = lax.rsqrt(spread + EPSILON)
    return centred * inverse, inverse


def norm_back(grad, gain, normal, inverse):
    scaled = grad * gain
    return inverse * (
        scaled
        - jnp.mean(scaled, axis=-1, keepdims=True)
        - normal * jnp.mean(scaled * normal, axis=-1, keepdims=True)
    )


MID_TILE = 256
MID_PARTS = 4


def first_half_kernel(meta, ids, *refs):
    out_own, up_own, up_pieces = refs[0], refs[1], up_parts(refs[2:12])
    x_ref, mixed_ref, gain1, in3, in4, out3, out4 = refs[12:19]
    normal_ref, inverse_ref, active, slope = refs[19:23]
    w_out, w_up, osems, usems = refs[23:]
    out_copies = weight_copies(meta, out_own, up_pieces, w_out, osems, out_places)
    up_copies = weight_copies(meta, up_own, up_pieces, w_up, usems, up_places)
    is_first = pl.program_id(0) == 0

    @pl.when(is_first)
    def _():
        for copy in out_copies + up_copies:
            copy.start()
        for copy in out_copies:
            copy.wait()

    mixed = mixed_ref[...]
    rank3 = mm_nt(mixed, in3[0, 0]).astype(BF)
    branch = mm(mixed, w_out[...]) + mm(rank3, out3[0, 0])
    normal, inverse = norm_parts(x_ref[...].astype(F32) + branch)
    normal_ref[...] = normal
    inverse_ref[...] = jnp.broadcast_to(inverse, inverse_ref.shape)
    low = (normal * gain1[...][None]).astype(BF)
    rank4 = mm_nt(low, in4[0, 0]).astype(BF)

    @pl.when(is_first)
    def _():
        for copy in up_copies:
            copy.wait()

    part = w_up.shape[1] // MID_PARTS
    columns = [slice(n * part, n * part + part) for n in range(MID_PARTS)]
    lift = lambda cols: mm(low, w_up[:, cols]) + mm(rank4, out4[0, :, cols])
    ahead = lift(columns[0])
    for n, cols in enumerate(columns):
        lifted = ahead
        if n + 1 < MID_PARTS:
            ahead = lift(columns[n + 1])
        value, tangent = gelu_and_slope(lifted)
        active[:, cols] = value.astype(BF)
        slope[:, cols] = tangent.astype(BF)


def first_half(meta, ids, out_own, up_own, up_pieces, x, mixed, gain1, table_in, table_out, table_out_hidden):
    width, hidden = x.shape[1], up_own.shape[1]
    tile = lambda columns: pl.BlockSpec((MID_TILE, columns), lambda i, *_: (i, 0))
    return pl.pallas_call(
        first_half_kernel,
        grid_spec=pltpu.PrefetchScalarGridSpec(
            num_scalar_prefetch=2,
            grid=(512 // MID_TILE,),
            in_specs=any_specs(12)
            + [
                tile(width),
                tile(width),
                whole((width,)),
                table_spec(3, 3, width),
                table_spec(4, 4, width),
                table_spec(3, 3, width),
                hidden_spec(4, hidden),
            ],
            out_specs=[tile(width), tile(128), tile(hidden), tile(hidden)],
            scratch_shapes=[
                VMEM((width, width), BF),
                VMEM((width, hidden), BF),
                pltpu.SemaphoreType.DMA((25,)),
                pltpu.SemaphoreType.DMA((31,)),
            ],
        ),
        out_shape=[
            jax.ShapeDtypeStruct((512, width), F32),
            jax.ShapeDtypeStruct((512, 128), F32),
            jax.ShapeDtypeStruct((512, hidden), BF),
            jax.ShapeDtypeStruct((512, hidden), BF),
        ],
        compiler_params=pltpu.CompilerParams(vmem_limit_bytes=50 * MEBI),
        cost_estimate=SMALL_COST,
        name="first_half",
    )(meta, ids, out_own, up_own, *up_pieces, x, mixed, gain1, table_in, table_in, table_out, table_out_hidden)


def write_halves(meta, gathered, groups, own_half, other_half):
    core = meta[1] & 1
    for r in range(4):
        for half, ref in enumerate((own_half, other_half)):
            rows = [
                gathered[meta[0] ^ r, pl.ds(pl.multiple_of(16 * group + 8 * (core ^ half), 8), 8), :]
                for group in range(groups)
            ]
            ref[r] = jnp.concatenate(rows, axis=0).astype(ref.dtype)


def second_half_kernel(meta, ids, *refs):
    cots, out_own, up_own, down_own = refs[0:2], refs[2], refs[3], refs[4]
    up_pieces, down_pieces = up_parts(refs[5:15]), one_each(refs[15:23])
    normal_ref, inverse_ref, active, slope, mixed_ref = refs[23:28]
    gain1, gain2, in3, in4, in5, out3, out4, out5 = refs[28:36]
    layer_parts, grad_branch_ref, grad_mixed_ref, own_half, other_half = refs[36:38], refs[38], refs[39], refs[40], refs[41]
    (
        cot, w_out, w_up, w_down, layer,
        s_in3, s_in4, s_in5, s_out3, s_out4, s_out5, gathered,
        osems, usems, dsems, xsems,
    ) = refs[42:]
    tile = pl.program_id(0)
    is_first = tile == 0
    near = token_copies(meta, cots, cot, xsems)
    out_copies = weight_copies(meta, out_own, up_pieces, w_out, osems, out_places)
    up_copies = weight_copies(meta, up_own, up_pieces, w_up, usems, up_places)
    down_copies = weight_copies(meta, down_own, down_pieces, w_down, dsems, down_places)

    @pl.when(is_first)
    def _():
        for copy in down_copies + near + up_copies + out_copies:
            copy.start()
        for ref in (s_in3, s_in4, s_in5, s_out3, s_out4, s_out5):
            ref[...] = jnp.zeros_like(ref)
        for copy in down_copies + near:
            copy.wait()

    part = w_up.shape[1] // MID_PARTS
    a_in3, a_in4, a_out3, a_out5 = in3[0, 0], in4[0, 0], out3[0, 0], out5[0, 0]
    rows = pl.ds(pl.multiple_of(tile * MID_TILE, MID_TILE), MID_TILE)
    normal1 = normal_ref[...]
    inverse1 = inverse_ref[:, 0:1]
    first = normal1 * gain1[...][None]
    low1 = first.astype(BF)
    r4 = mm_nt(low1, a_in4).astype(BF)
    r5 = mm_nt(active[...], in5[0]).astype(BF)
    lowered = first + mm(active[...], w_down[...]) + mm(r5, a_out5)
    normal2, inverse2 = norm_parts(lowered)
    layer[rows, :] = (normal2 * gain2[...][None]).astype(BF)
    grad_sum = norm_back(cot[rows, :].astype(F32), gain2[...][None], normal2, inverse2)
    e5 = grad_sum.astype(BF)
    rg5 = mm_nt(e5, a_out5).astype(BF)
    s_out5[...] += mm_tn(r5, e5)

    @pl.when(is_first)
    def _():
        for copy in up_copies + out_copies:
            copy.wait()

    grad_first = grad_sum
    rg4 = jnp.zeros((MID_TILE, RANK), F32)
    for n in range(MID_PARTS):
        cols = slice(n * part, n * part + part)
        grad_active = mm_nt(e5, w_down[cols, :]) + mm(rg5, in5[0, :, cols])
        e4 = (slope[:, cols].astype(F32) * grad_active).astype(BF)
        s_in5[:, cols] += mm_tn(rg5, active[:, cols])
        s_out4[:, cols] += mm_tn(r4, e4)
        grad_first = grad_first + mm_nt(e4, w_up[:, cols])
        rg4 = rg4 + mm_nt(e4, out4[0, :, cols])
    rg4 = rg4.astype(BF)
    s_in4[...] += mm_tn(rg4, low1)
    grad_first = grad_first + mm(rg4, a_in4)
    grad_branch = norm_back(grad_first, gain1[...][None], normal1, inverse1)
    grad_branch_ref[...] = grad_branch
    e3 = grad_branch.astype(BF)
    mixed = mixed_ref[...]
    rank3 = mm_nt(mixed, a_in3).astype(BF)
    rg3 = mm_nt(e3, a_out3).astype(BF)
    s_out3[...] += mm_tn(rank3, e3)
    s_in3[...] += mm_tn(rg3, mixed)
    grad_mixed_ref[...] = (mm_nt(e3, w_out[...]) + mm(rg3, a_in3)).astype(BF)

    @pl.when(tile == 512 // MID_TILE - 1)
    def _():
        wide, narrow = 768, 192
        for owner in range(4):
            start = 0
            for ref, size in (
                (s_in5, wide), (s_out4, wide), (s_in3, narrow), (s_in4, narrow), (s_out3, narrow), (s_out5, narrow),
            ):
                row, column = 16 * (start // 768), start % 768
                gathered[owner, row : row + 16, column : column + size] = ref[:, owner * size : owner * size + size]
                start += size
        for r, ref in enumerate(layer_parts):
            ref[...] = layer[pl.ds(pl.multiple_of(256 * ((meta[0] & 1) ^ r), 256), 256), :]
        write_halves(meta, gathered, 3, own_half, other_half)


def second_half(meta, ids, cots, out_own, up_own, down_own, up_pieces, down_pieces, normal, inverse, active, slope,
                mixed, gain1, gain2, table_in, table_in_hidden, table_out, table_out_hidden):
    width, hidden = normal.shape[1], up_own.shape[1]
    tile = lambda columns: pl.BlockSpec((MID_TILE, columns), lambda i, *_: (i, 0))
    return pl.pallas_call(
        second_half_kernel,
        grid_spec=pltpu.PrefetchScalarGridSpec(
            num_scalar_prefetch=2,
            grid=(512 // MID_TILE,),
            in_specs=any_specs(23)
            + [
                tile(width),
                tile(128),
                tile(hidden),
                tile(hidden),
                tile(width),
                whole((width,)),
                whole((width,)),
                table_spec(3, 3, width),
                table_spec(4, 4, width),
                hidden_spec(5, hidden),
                table_spec(3, 3, width),
                hidden_spec(4, hidden),
                table_spec(4, 5, width),
            ],
            out_specs=[whole((256, width))] * 2 + [tile(width), tile(width)] + [whole((4, 24, width))] * 2,
            scratch_shapes=[
                VMEM((512, width), BF),
                VMEM((width, width), BF),
                VMEM((width, hidden), BF),
                VMEM((hidden, width), BF),
                VMEM((512, width), BF),
                VMEM((RANK, width), F32),
                VMEM((RANK, width), F32),
                VMEM((RANK, hidden), F32),
                VMEM((RANK, width), F32),
                VMEM((RANK, hidden), F32),
                VMEM((RANK, width), F32),
                VMEM((4, 3 * RANK, 768), F32),
                pltpu.SemaphoreType.DMA((25,)),
                pltpu.SemaphoreType.DMA((31,)),
                pltpu.SemaphoreType.DMA((49,)),
                pltpu.SemaphoreType.DMA((2,)),
            ],
        ),
        out_shape=[jax.ShapeDtypeStruct((256, width), BF)] * 2
        + [jax.ShapeDtypeStruct((512, width), F32), jax.ShapeDtypeStruct((512, width), BF)]
        + [jax.ShapeDtypeStruct((4, 24, width), F32), jax.ShapeDtypeStruct((4, 24, width), BF)],
        compiler_params=pltpu.CompilerParams(vmem_limit_bytes=56 * MEBI),
        cost_estimate=SMALL_COST,
        name="second_half",
    )(meta, ids, *cots, out_own, up_own, down_own, *up_pieces, *down_pieces, normal, inverse, active, slope, mixed,
      gain1, gain2, table_in, table_in, table_in_hidden, table_out, table_out_hidden, table_out)


def first_grads_kernel(meta, ids, *refs):
    xs, dq_ref, dk_ref, dv_ref, got_ref = refs[0:5]
    ins, outs = refs[5:8], refs[8:11]
    grads_ref, rank_grad_ref = refs[11:13]
    own_half, other_half = refs[13:15]
    s_in, s_out, gathered = refs[15:]
    in_all = jnp.concatenate([ref[0, 0] for ref in ins], axis=0)
    out_all = jnp.concatenate([zero_padded(ref[0, 0], p, 3) for p, ref in enumerate(outs)], axis=1)
    for tile in range(2):
        rows = slice(256 * tile, 256 * tile + 256)
        grads = jnp.concatenate(
            [dq_ref[rows]]
            + [(ref[rows].astype(F32) + got_ref[n, rows].astype(F32)).astype(BF) for n, ref in enumerate((dk_ref, dv_ref))],
            axis=1,
        )
        grads_ref[rows] = grads
        x = xs[rows]
        rank = mm_nt(x, in_all).astype(BF)
        rank_grad = mm_nt(grads, out_all).astype(BF)
        rank_grad_ref[rows] = rank_grad
        part_in, part_out = mm_tn(rank_grad, x), mm_tn(rank, grads)
        if tile == 0:
            s_in[...] = part_in
            s_out[...] = part_out
        else:
            s_in[...] += part_in
            s_out[...] += part_out
    gathered[...] = jnp.zeros_like(gathered)
    for owner in range(4):
        for p in range(3):
            rows, columns = slice(RANK * p, RANK * p + RANK), slice(192 * owner, 192 * owner + 192)
            gathered[owner, 0:16, 192 * p : 192 * p + 192] = s_in[rows, columns]
            columns = slice(768 * p + 192 * owner, 768 * p + 192 * owner + 192)
            at = (0, 576) if p == 0 else (16, 192 * (p - 1))
            gathered[owner, at[0] : at[0] + 16, at[1] : at[1] + 192] = s_out[rows, columns]
    write_halves(meta, gathered, 2, own_half, other_half)


def first_grads(meta, ids, x, dq, dk, dv, got, table_in, table_out):
    width = x.shape[1]
    return pl.pallas_call(
        first_grads_kernel,
        grid_spec=pltpu.PrefetchScalarGridSpec(
            num_scalar_prefetch=2,
            grid=(1,),
            in_specs=[whole((512, width))] * 4
            + [whole((2, 512, width))]
            + [table_spec(p, p, width) for p in range(3)] * 2,
            out_specs=[whole((512, 3 * width)), whole((512, 3 * RANK))] + [whole((4, 16, width))] * 2,
            scratch_shapes=[
                VMEM((3 * RANK, width), F32),
                VMEM((3 * RANK, 3 * width), F32),
                VMEM((4, 2 * RANK, 768), F32),
            ],
        ),
        out_shape=[jax.ShapeDtypeStruct((512, 3 * width), BF), jax.ShapeDtypeStruct((512, 3 * RANK), BF)]
        + [jax.ShapeDtypeStruct((4, 16, width), F32), jax.ShapeDtypeStruct((4, 16, width), BF)],
        compiler_params=pltpu.CompilerParams(vmem_limit_bytes=30 * MEBI),
        cost_estimate=SMALL_COST,
        name="first_grads",
    )(meta, ids, x, dq, dk, dv, got, *([table_in] * 3), *([table_out] * 3))


def input_grad_kernel(meta, ids, *refs):
    w_own, pieces = refs[0], one_each(refs[1:9])
    branch_ref, grads_ref, rank_grad_ref = refs[9:12]
    ins, parts = refs[12:15], refs[15:17]
    weight, wsems = refs[17:]
    copies = weight_copies(meta, w_own, pieces, weight, wsems, qkv_places)
    for copy in copies:
        copy.start()
    for copy in copies:
        copy.wait()
    in_all = jnp.concatenate([ref[0, 0] for ref in ins], axis=0)
    for r, ref in enumerate(parts):
        rows = pl.ds(pl.multiple_of(256 * ((meta[0] & 1) ^ r), 256), 256)
        ref[...] = (
            branch_ref[rows, :] + mm_nt(grads_ref[rows, :], weight[...]) + mm(rank_grad_ref[rows, :], in_all)
        ).astype(BF)


def project_back(meta, ids, w_own, pieces, branch, grads, rank_grad, table_in):
    width = branch.shape[1]
    return pl.pallas_call(
        input_grad_kernel,
        grid_spec=pltpu.PrefetchScalarGridSpec(
            num_scalar_prefetch=2,
            grid=(1,),
            in_specs=any_specs(9)
            + [whole((512, width)), whole((512, 3 * width)), whole((512, 3 * RANK))]
            + [table_spec(p, p, width) for p in range(3)],
            out_specs=[whole((256, width))] * 2,
            scratch_shapes=[VMEM((width, 3 * width), BF), pltpu.SemaphoreType.DMA((25,))],
        ),
        out_shape=[jax.ShapeDtypeStruct((256, width), BF)] * 2,
        compiler_params=pltpu.CompilerParams(vmem_limit_bytes=30 * MEBI),
        cost_estimate=SMALL_COST,
        name="project_back",
    )(meta, ids, w_own, *pieces, branch, grads, rank_grad, *([table_in] * 3))


def sum_cores_kernel(ids, mid_own, mid_other, first_own, first_other, *messages):
    row = lax.broadcasted_iota(jnp.int32, (16, 768), 0)
    lane = lax.broadcasted_iota(jnp.int32, (16, 768), 1)
    for r, ref in enumerate(messages):
        mid = mid_own[r] + mid_other[r].astype(F32)
        first = first_own[r] + first_other[r].astype(F32)
        for p in range(6):
            first = jnp.where((row >= 8) & (lane == 384 + p), ids[p].astype(F32), first)
        ref[...] = jnp.concatenate([mid, first], axis=0).astype(BF)


def sum_cores(ids, *halves):
    width = halves[0].shape[-1]
    return pl.pallas_call(
        sum_cores_kernel,
        grid_spec=pltpu.PrefetchScalarGridSpec(
            num_scalar_prefetch=1,
            grid=(1,),
            in_specs=[whole(half.shape) for half in halves],
            out_specs=[whole((40, width))] * 4,
        ),
        out_shape=[jax.ShapeDtypeStruct((40, width), BF)] * 4,
        compiler_params=pltpu.CompilerParams(vmem_limit_bytes=30 * MEBI),
        cost_estimate=SMALL_COST,
        name="sum_cores",
    )(ids, *halves)


def combine_kernel(ids, meta, own, other, in_d, in_f, out_d, out_f):
    for ref in (in_d, in_f, out_d, out_f):
        ref[...] = jnp.zeros_like(ref)
    narrow = in_d.shape[-1]
    for chip in range(4):
        for r in range(4):
            chosen = [ids[(chip * 4 + r) * 6 + p] for p in range(6)]
            for half, messages in enumerate((own, other)):
                ranks = pl.ds(pl.multiple_of(8 * ((meta[1] & 1) ^ half), 8), 8)
                part = messages[chip, r].astype(F32)
                in_f[chosen[5], ranks, :] += part[0:8]
                out_f[chosen[4], ranks, :] += part[8:16]
                for at, (ref, p, which) in enumerate(
                    (
                        (in_d, 3, 3), (in_d, 4, 4), (out_d, 3, 3), (out_d, 4, 5),
                        (in_d, 0, 0), (in_d, 1, 1), (in_d, 2, 2), (out_d, 0, 0),
                        (out_d, 1, 1), (out_d, 2, 2),
                    )
                ):
                    row, column = 16 + 8 * (at // 4), narrow * (at % 4)
                    ref[p, chosen[which], ranks, :] += part[row : row + 8, column : column + narrow]


def combine(ids, meta, own, other, tables, narrow, wide):
    shapes = [(5, tables, RANK, narrow), (tables, RANK, wide)] * 2
    return pl.pallas_call(
        combine_kernel,
        grid_spec=pltpu.PrefetchScalarGridSpec(
            num_scalar_prefetch=2,
            grid=(1,),
            in_specs=[whole(own.shape)] * 2,
            out_specs=[whole(shape) for shape in shapes],
        ),
        out_shape=[jax.ShapeDtypeStruct(shape, F32) for shape in shapes],
        compiler_params=pltpu.CompilerParams(vmem_limit_bytes=30 * MEBI),
        cost_estimate=SMALL_COST,
        name="combine",
    )(ids, meta, own, other)


def after(value, *others):
    return lax.optimization_barrier((value, *others))[0]


def beside(work, transfers, values, moved):
    given = lax.optimization_barrier((tuple(values), tuple(moved)))
    return lax.optimization_barrier((tuple(work(*given[0])), tuple(transfers(*given[1]))))


def paired_body(
    inputs,
    segments,
    random_key_blocks,
    adapter_index_table,
    frozen_query_key_value_weight,
    frozen_output_weight,
    frozen_up_weight,
    frozen_down_weight,
    attention_norm_gain,
    feedforward_norm_gain,
    adapter_down_from_width,
    adapter_down_from_hidden,
    adapter_up_to_width,
    adapter_up_to_hidden,
    cotangent,
):
    dp_count, shard_count = lax.axis_size("dp"), lax.axis_size("shard")
    d, z = lax.axis_index("dp"), lax.axis_index("shard")
    core = d & 1
    meta = jnp.stack([z, d]).astype(jnp.int32)

    def piece(weight, rows, columns, row, column):
        return lax.dynamic_slice(weight, (row, column), (rows, columns))

    def fetch(part):
        return [swap_shards(part, shard_count, step) for step in range(1, shard_count)]

    def slices(values):
        return [lax.dynamic_index_in_dim(values, (z & 1) ^ r, 0, keepdims=False) for r in range(2)]

    def chips(block, *offsets):
        return [swap_chips(block, dp_count, offset) for offset in offsets]

    def swap(block):
        return swap_cores(block, dp_count)

    qkv_own = jnp.stack(fetch(piece(frozen_query_key_value_weight, 48, 1152, (d >> 1) * 48, core * 1152)))
    up_piece = jnp.concatenate(
        [
            piece(frozen_output_weight, 48, 384, (d >> 1) * 48, core * 384),
            piece(frozen_up_weight, 192, 384, 0, d * 384),
        ],
        axis=0,
    )
    down_piece = piece(frozen_down_weight, 96, 768, d * 96, 0)
    down_piece = jnp.concatenate([down_piece[:, 0:384], down_piece[:, 384:768]], axis=0)
    seg_rows = jnp.pad(segments.astype(BF)[:, None, :], ((0, 0), (0, 15), (0, inputs.shape[-1] - 256)))
    own = send_away(slices(jnp.concatenate([inputs, seg_rows], axis=1)), dp_count, shard_count)
    there = swap_cores(adapter_index_table, dp_count)
    column_ids = jnp.where(
        core == 0,
        jnp.concatenate([adapter_index_table, there], axis=0),
        jnp.concatenate([there, adapter_index_table], axis=0),
    )
    ids = lax.dynamic_index_in_dim(column_ids, z, 0, keepdims=False)

    blocks = jnp.arange(16, dtype=jnp.int32)
    query_block = (8 * core + blocks[0:8])[None, :, None]
    key_block = jnp.where(blocks < 8, 8 * core + blocks, 8 * (1 - core) + blocks - 8)[None, None, :]
    drawn = lax.dynamic_slice_in_dim(random_key_blocks, 8 * core, 8, axis=1)
    allowed = (jnp.abs(query_block - key_block) <= 1) | (query_block < GLOBALS) | (key_block < GLOBALS)
    for n in range(RANDOMS):
        allowed = allowed | (drawn[:, :, n : n + 1] == key_block)
    closed = jnp.pad(jnp.where(allowed, 0.0, -BIG), ((0, 0), (0, 0), (16, 32)))
    closed = closed.reshape(H // 2, 2, 8, 64)
    closed = jnp.concatenate([closed[:, 1], closed[:, 0]], axis=-1)

    qkv_own, meta, up_piece = lax.optimization_barrier((qkv_own, meta, up_piece))
    tokens = own + [swap(part) for part in own]
    qkv_x, qkv_y, qkv_xy = chips(qkv_own, 2, 4, 6)
    qkv_xy, closed, down_piece, ids = lax.optimization_barrier((qkv_xy, closed, down_piece, ids))
    qkv_pieces = spread_over_cores((qkv_own, qkv_x, qkv_y, qkv_xy), dp_count)
    up_own = fetch(after(up_piece, *own))

    def work(*given):
        return project_qkv(
            meta, ids, given[0:4], frozen_query_key_value_weight, given[4:],
            adapter_down_from_width, adapter_up_to_width,
        )

    (q, k, v, masks, hot, x), up_own = lax.optimization_barrier((work(*tokens, *qkv_pieces), up_own))
    up_own = jnp.stack(up_own)
    (mixed, shares), (up_x, up_y, up_there, down_1, down_2) = beside(
        lambda *given: attend(*given, closed),
        lambda block, part: (
            *chips(block, 2, 4), swap(block), swap_shards(part, shard_count, 1), swap_shards(part, shard_count, 2)
        ),
        (q, k, v, masks, hot),
        (up_own, down_piece),
    )
    mixed, up_a, up_b, up_x_there, up_y_there, down_3 = lax.optimization_barrier(
        (
            mixed,
            *chips(up_x[:, 0:UP_SPLIT], 4),
            *chips(up_y[:, UP_SPLIT:], 2),
            swap(up_x),
            swap(up_y),
            swap_shards(after(down_piece, mixed), shard_count, 3),
        )
    )
    down_own = jnp.stack([down_1, down_2, down_3])
    up_pieces = (up_own, up_there, up_x, up_x_there, up_y, up_y_there, up_a, up_b, swap(up_a), swap(up_b))
    gain1, gain2 = attention_norm_gain, feedforward_norm_gain

    def work(mixed, *pieces):
        return first_half(
            meta, ids, frozen_output_weight, frozen_up_weight, pieces, x, mixed, gain1,
            adapter_down_from_width, adapter_up_to_width, adapter_up_to_hidden,
        )

    (normal, inverse, active, slope), (*down_pieces, cot_a, cot_b) = beside(
        work,
        lambda block, values: (*chips(block, 2, 4, 6), *send_away(slices(values), dp_count, shard_count)),
        (mixed, *up_pieces),
        (after(down_own, up_a, up_b), cotangent),
    )
    down_pieces = spread_over_cores((down_own, *down_pieces), dp_count)
    cots = (cot_a, cot_b)
    results = second_half(
        meta, ids, cots, frozen_output_weight, frozen_up_weight, frozen_down_weight, up_pieces, down_pieces,
        normal, inverse, active, slope, mixed, gain1, gain2,
        adapter_down_from_width, adapter_down_from_hidden, adapter_up_to_width, adapter_up_to_hidden,
    )
    grad_branch = results[2]

    def home(r, part):
        return lax.ppermute(part, ("dp", "shard"), away_pairs(dp_count, shard_count, r))

    def swap_over_shards(*parts):
        return [swap_shards(part, shard_count, step + 1) for step, part in enumerate(parts)]

    (dq, dk, dv, other_sums), (layer_a, layer_b) = beside(
        lambda grad: attend_back(q, k, v, shares, grad, mixed),
        lambda part_a, part_b: (home(0, part_a), home(1, part_b)),
        (results[3],),
        results[0:2],
    )
    grads, rank_grad, first_own, first_other = first_grads(
        meta, ids, x, dq, dk, dv, swap(other_sums), adapter_down_from_width, adapter_up_to_width
    )
    input_parts, (first_other, mid_other) = beside(
        lambda grads: project_back(
            meta, ids, frozen_query_key_value_weight, qkv_pieces, grad_branch, grads, rank_grad,
            adapter_down_from_width,
        ),
        lambda *halves: [swap(half) for half in halves],
        (grads,),
        (first_other, results[5]),
    )
    message, *others = sum_cores(ids, results[4], mid_other, first_own, first_other)
    (layer_out,), moved = beside(
        lambda *parts: (join_parts(meta, parts, BF),),
        swap_over_shards,
        (layer_a, layer_b),
        others,
    )
    messages = jnp.stack([message, *moved])
    _, (part_a, part_b, *moved) = beside(
        lambda: (),
        lambda part_a, part_b, block: (home(0, part_a), home(1, part_b), *chips(block, 2, 4, 6)),
        (),
        (*input_parts, messages),
    )
    messages = jnp.stack([messages, *moved])
    chosen = messages[:, :, 32, 384:390].astype(jnp.int32).reshape(-1)
    in_d, in_f, out_d, out_f = combine(
        chosen, meta, messages, swap(messages), adapter_down_from_width.shape[1], 192, 768
    )
    return (layer_out, join_parts(meta, (part_a, part_b), F32), in_d, in_f, out_d, out_f)


def solution(mesh):
    dp_count, shard_count = mesh.shape["dp"], mesh.shape["shard"]
    paired = dp_count == 8 and shard_count == 4
    return jax.shard_map(
        paired_body if paired else general_body,
        mesh=mesh,
        in_specs=(
            P("dp", "shard", None),
            P("dp", "shard"),
            P(),
            P("dp", None),
            P("shard", None),
            P("shard", None),
            P("shard", None),
            P("shard", None),
            P(),
            P(),
            P(),
            P(),
            P(),
            P(),
            P("dp", "shard", None),
        ),
        out_specs=(
            P("dp", "shard", None),
            P("dp", "shard", None),
            P(None, None, None, "shard"),
            P(None, None, "shard"),
            P(None, None, None, "shard"),
            P(None, None, "shard"),
        ),
        check_vma=False,
    )
```

```python
import functools

import jax
import jax.numpy as jnp
from jax import lax
from jax.experimental import pallas as pl
from jax.experimental.pallas import tpu as pltpu
from jax.sharding import PartitionSpec as P

H = 12
HD = 64
BLOCK = 64
GLOBALS = 2
RANDOMS = 3


EPSILON = 1e-06
NEGATIVE = -1e30


def norm_rows(hidden, gain_vector):
    average = jnp.mean(hidden, axis=-1, keepdims=True)
    centred = hidden - average
    spread = jnp.mean(centred * centred, axis=-1, keepdims=True)
    return centred * lax.rsqrt(spread + EPSILON) * gain_vector


def gelu_exact(values):
    return jax.nn.gelu(values, approximate=False)


def dense_forward(inputs, weight):
    return jnp.einsum("sti,io->sto", inputs, weight, preferred_element_type=jnp.float32)


def dense_backward(grad_low, weight):
    return jnp.einsum("sto,io->sti", grad_low, weight, preferred_element_type=jnp.float32)


def adapt(inputs, down_rows, up_rows):
    rank_part = jnp.einsum(
        "sti,sri->str", inputs, down_rows, preferred_element_type=jnp.float32
    ).astype(jnp.bfloat16)
    return (
        rank_part,
        jnp.einsum("str,sro->sto", rank_part, up_rows, preferred_element_type=jnp.float32),
    )


def adapt_back(inputs, down_rows, up_rows, rank_part, grad_low):
    grad_up = jnp.einsum("str,sto->sro", rank_part, grad_low, preferred_element_type=jnp.float32)
    rank_grad = jnp.einsum(
        "sto,sro->str", grad_low, up_rows, preferred_element_type=jnp.float32
    ).astype(jnp.bfloat16)
    grad_down = jnp.einsum("str,sti->sri", rank_grad, inputs, preferred_element_type=jnp.float32)
    grad_inputs = jnp.einsum(
        "str,sri->sti", rank_grad, down_rows, preferred_element_type=jnp.float32
    )
    return (grad_down, grad_up, grad_inputs)


def table_sum(per_sequence, chosen, table_size):
    matches = (chosen[:, None] == jnp.arange(table_size, dtype=jnp.int32)[None, :]).astype(
        jnp.float32
    )
    return jnp.sum(matches[:, :, None, None] * per_sequence[:, None], axis=0)


def sparse_scores(query_heads, key_picked, permit, scaling):
    scores = (
        jnp.einsum(
            "shbqd,shbkd->shbqk", query_heads, key_picked, preferred_element_type=jnp.float32
        )
        * scaling
    )
    return jnp.where(permit, scores, NEGATIVE)


def global_scores(query_rows, key_rows, seg_query, seg_keys, scaling):
    scores = (
        jnp.einsum("hqd,hkd->hqk", query_rows, key_rows, preferred_element_type=jnp.float32)
        * scaling
    )
    return jnp.where((seg_query[:, None] == seg_keys[None, :])[None], scores, NEGATIVE)


def global_forward(query_rows, key_rows, value_rows, seg_query, seg_keys, scaling):
    scores = global_scores(query_rows, key_rows, seg_query, seg_keys, scaling)
    top_score = jnp.max(scores, axis=-1, keepdims=True)
    weights = jnp.exp(scores - top_score)
    totals = jnp.sum(weights, axis=-1, keepdims=True)
    shares = (weights / totals).astype(jnp.bfloat16)
    attended = jnp.einsum("hqk,hkd->hqd", shares, value_rows, preferred_element_type=jnp.float32)
    return (attended, (top_score + jnp.log(totals))[..., 0])


def global_backward(
    query_rows, key_rows, value_rows, seg_query, seg_keys, grad_rows, log_total, scaling
):
    scores = global_scores(query_rows, key_rows, seg_query, seg_keys, scaling)
    shares = jnp.exp(scores - log_total[..., None])
    share_low = shares.astype(jnp.bfloat16)
    grad_shares = jnp.einsum(
        "hqd,hkd->hqk", grad_rows, value_rows, preferred_element_type=jnp.float32
    )
    centre = jnp.sum(shares * grad_shares, axis=-1, keepdims=True)
    grad_scores = (shares * (grad_shares - centre)).astype(jnp.bfloat16)
    grad_query = (
        jnp.einsum("hqk,hkd->hqd", grad_scores, key_rows, preferred_element_type=jnp.float32)
        * scaling
    )
    grad_keys = (
        jnp.einsum("hqk,hqd->hkd", grad_scores, query_rows, preferred_element_type=jnp.float32)
        * scaling
    )
    grad_values = jnp.einsum(
        "hqk,hqd->hkd", share_low, grad_rows, preferred_element_type=jnp.float32
    )
    return (grad_query, grad_keys, grad_values, centre[..., 0])


def general_body(
    inputs,
    segments,
    random_key_blocks,
    adapter_index_table,
    frozen_query_key_value_weight,
    frozen_output_weight,
    frozen_up_weight,
    frozen_down_weight,
    attention_norm_gain,
    feedforward_norm_gain,
    adapter_down_from_width,
    adapter_down_from_hidden,
    adapter_up_to_width,
    adapter_up_to_hidden,
    cotangent,
):
    seq_count = inputs.shape[0]
    local_tokens = inputs.shape[1]
    width = inputs.shape[2]
    shard_count = lax.axis_size("shard")
    full_length = local_tokens * shard_count
    total_blocks = full_length // BLOCK
    local_blocks = local_tokens // BLOCK
    cand_count = 3 + GLOBALS + RANDOMS
    glob_rows = GLOBALS * BLOCK
    scaling = HD ** (-0.5)

    def select_adapter_table(table, table_column):
        return jnp.take(table, adapter_index_table[:, table_column], axis=0)

    adapter_tables_input = [
        select_adapter_table(adapter_down_from_width[table_column], table_column)
        for table_column in range(5)
    ] + [select_adapter_table(adapter_down_from_hidden, 5)]
    adapter_tables_output = [
        select_adapter_table(adapter_up_to_width[table_column], table_column)
        for table_column in range(4)
    ]
    adapter_tables_output = adapter_tables_output + [
        select_adapter_table(adapter_up_to_hidden, 4),
        select_adapter_table(adapter_up_to_width[4], 5),
    ]
    qkv_full, out_full = (
        lax.all_gather(frozen_query_key_value_weight, "shard", axis=0, tiled=True),
        lax.all_gather(frozen_output_weight, "shard", axis=0, tiled=True),
    )
    main_part = dense_forward(inputs, qkv_full)
    rank_parts = []
    projected = []
    for table_column in range(3):
        rank_part, extra = adapt(
            inputs, adapter_tables_input[table_column], adapter_tables_output[table_column]
        )
        rank_parts.append(rank_part)
        projected.append(
            (main_part[..., table_column * width : (table_column + 1) * width] + extra).astype(
                jnp.bfloat16
            )
        )
    seg_low = segments.astype(jnp.bfloat16)
    key_all, value_all, seg_all = (
        lax.all_gather(projected[1], "shard", axis=1, tiled=True),
        lax.all_gather(projected[2], "shard", axis=1, tiled=True),
        lax.all_gather(seg_low, "shard", axis=1, tiled=True),
    )
    shard_pos = lax.axis_index("shard")
    is_first = shard_pos == 0
    first_block = shard_pos * local_blocks
    block_ids = first_block + jnp.arange(local_blocks, dtype=jnp.int32)
    rand_local = lax.dynamic_slice_in_dim(random_key_blocks, first_block, local_blocks, axis=1)
    window_part = jnp.stack([block_ids - 1, block_ids, block_ids + 1], axis=-1)
    global_ids = jnp.broadcast_to(
        jnp.arange(GLOBALS, dtype=jnp.int32)[None, :], (local_blocks, GLOBALS)
    )
    fixed_part = jnp.concatenate([window_part, global_ids], axis=-1)
    candidates = jnp.concatenate(
        [jnp.broadcast_to(fixed_part[None], (H, local_blocks, 3 + GLOBALS)), rand_local], axis=-1
    )
    candidates = jnp.clip(candidates, 0, total_blocks - 1)
    always_true = jnp.ones((local_blocks,), dtype=bool)
    fixed_valid = jnp.stack(
        [block_ids - 1 >= GLOBALS, always_true, block_ids + 1 < total_blocks]
        + [always_true] * GLOBALS,
        axis=-1,
    )
    valid = jnp.concatenate(
        [
            jnp.broadcast_to(fixed_valid[None], (H, local_blocks, 3 + GLOBALS)),
            jnp.ones((H, local_blocks, RANDOMS), dtype=bool),
        ],
        axis=-1,
    )
    valid_keys = jnp.repeat(valid, BLOCK, axis=-1)
    query_heads = (
        projected[0].reshape(seq_count, local_blocks, BLOCK, H, HD).transpose(0, 3, 1, 2, 4)
    )
    key_source = key_all.reshape(seq_count, total_blocks, BLOCK, H, HD).transpose(0, 3, 1, 2, 4)
    value_source = value_all.reshape(seq_count, total_blocks, BLOCK, H, HD).transpose(0, 3, 1, 2, 4)
    head_index = jnp.arange(H, dtype=jnp.int32)[:, None, None]
    key_picked = key_source[:, head_index, candidates].reshape(
        seq_count, H, local_blocks, cand_count * BLOCK, HD
    )
    value_picked = value_source[:, head_index, candidates].reshape(
        seq_count, H, local_blocks, cand_count * BLOCK, HD
    )
    seg_picked = seg_all.reshape(seq_count, total_blocks, BLOCK)[:, candidates].reshape(
        seq_count, H, local_blocks, cand_count * BLOCK
    )
    seg_local = seg_low.reshape(seq_count, local_blocks, BLOCK)
    permit = valid_keys[None, :, :, None, :] & (
        seg_local[:, None, :, :, None] == seg_picked[:, :, :, None, :]
    )
    scores = sparse_scores(query_heads, key_picked, permit, scaling)
    top_score = jnp.max(scores, axis=-1, keepdims=True)
    weights = jnp.exp(scores - top_score)
    totals = jnp.sum(weights, axis=-1, keepdims=True)
    share_low = (weights / totals).astype(jnp.bfloat16)
    sparse_lse = (top_score + jnp.log(totals))[..., 0]
    sparse_out = jnp.einsum(
        "shbqk,shbkd->shbqd", share_low, value_picked, preferred_element_type=jnp.float32
    )
    key_heads = key_source.reshape(seq_count, H, full_length, HD)
    value_heads = value_source.reshape(seq_count, H, full_length, HD)
    glob_query = query_heads[:, :, :GLOBALS].reshape(seq_count, H, glob_rows, HD)
    glob_seg = seg_low[:, :glob_rows]

    def run_forward(operands):
        return lax.map(
            lambda packet: global_forward(
                packet[0], packet[1], packet[2], packet[3], packet[4], scaling
            ),
            operands,
        )

    def skip_forward(operands):
        return (
            jnp.zeros((seq_count, H, glob_rows, HD), jnp.float32),
            jnp.zeros((seq_count, H, glob_rows), jnp.float32),
        )

    global_out, global_lse = lax.cond(
        is_first, run_forward, skip_forward, (glob_query, key_heads, value_heads, glob_seg, seg_all)
    )
    glob_blocks = global_out.reshape(seq_count, H, GLOBALS, BLOCK, HD)
    head_out = jnp.concatenate(
        [jnp.where(is_first, glob_blocks, sparse_out[:, :, :GLOBALS]), sparse_out[:, :, GLOBALS:]],
        axis=2,
    )
    mixed_low = (
        head_out.transpose(0, 2, 3, 1, 4)
        .reshape(seq_count, local_tokens, width)
        .astype(jnp.bfloat16)
    )
    rank_out, extra_out = adapt(mixed_low, adapter_tables_input[3], adapter_tables_output[3])
    branch = dense_forward(mixed_low, out_full) + extra_out
    first, first_pull = jax.vjp(
        lambda hidden: norm_rows(hidden, attention_norm_gain), inputs.astype(jnp.float32) + branch
    )
    first_low = first.astype(jnp.bfloat16)
    up_full, down_full = (
        lax.all_gather(frozen_up_weight, "shard", axis=0, tiled=True),
        lax.all_gather(frozen_down_weight, "shard", axis=0, tiled=True),
    )
    rank_up, extra_up = adapt(first_low, adapter_tables_input[4], adapter_tables_output[4])
    lifted = dense_forward(first_low, up_full) + extra_up
    activated, gelu_pull = jax.vjp(gelu_exact, lifted)
    active_low = activated.astype(jnp.bfloat16)
    rank_down, extra_down = adapt(active_low, adapter_tables_input[5], adapter_tables_output[5])
    lowered = dense_forward(active_low, down_full) + extra_down
    result, final_pull = jax.vjp(
        lambda hidden: norm_rows(hidden, feedforward_norm_gain), first + lowered
    )
    layer_out = result.astype(jnp.bfloat16)
    up_back, down_back = (
        lax.all_gather(frozen_up_weight, "shard", axis=0, tiled=True),
        lax.all_gather(frozen_down_weight, "shard", axis=0, tiled=True),
    )
    grad_adapt_in = [None] * 6
    grad_adapt_out = [None] * 6
    (grad_sum,) = final_pull(cotangent.astype(jnp.float32))
    grad_lowered = grad_sum.astype(jnp.bfloat16)
    grad_adapt_in[5], grad_adapt_out[5], extra_grad = adapt_back(
        active_low, adapter_tables_input[5], adapter_tables_output[5], rank_down, grad_lowered
    )
    grad_active = dense_backward(grad_lowered, down_back) + extra_grad
    (grad_lifted,) = gelu_pull(grad_active)
    grad_lift_low = grad_lifted.astype(jnp.bfloat16)
    grad_adapt_in[4], grad_adapt_out[4], extra_grad = adapt_back(
        first_low, adapter_tables_input[4], adapter_tables_output[4], rank_up, grad_lift_low
    )
    grad_first = grad_sum + dense_backward(grad_lift_low, up_back) + extra_grad
    (grad_branch,) = first_pull(grad_first)
    grad_branch_low = grad_branch.astype(jnp.bfloat16)
    qkv_back, out_back = (
        lax.all_gather(frozen_query_key_value_weight, "shard", axis=0, tiled=True),
        lax.all_gather(frozen_output_weight, "shard", axis=0, tiled=True),
    )
    grad_adapt_in[3], grad_adapt_out[3], extra_grad = adapt_back(
        mixed_low, adapter_tables_input[3], adapter_tables_output[3], rank_out, grad_branch_low
    )
    grad_mixed = (dense_backward(grad_branch_low, out_back) + extra_grad).astype(jnp.bfloat16)
    grad_heads = grad_mixed.reshape(seq_count, local_blocks, BLOCK, H, HD).transpose(0, 3, 1, 2, 4)
    row_keep = (block_ids >= GLOBALS)[None, None, :, None, None]
    grad_sparse = jnp.where(row_keep, grad_heads, jnp.zeros_like(grad_heads))
    scores = sparse_scores(query_heads, key_picked, permit, scaling)
    shares = jnp.exp(scores - sparse_lse[..., None])
    share_low = shares.astype(jnp.bfloat16)
    grad_shares = jnp.einsum(
        "shbqd,shbkd->shbqk", grad_sparse, value_picked, preferred_element_type=jnp.float32
    )
    centre = jnp.sum(shares * grad_shares, axis=-1, keepdims=True)
    grad_scores = (shares * (grad_shares - centre)).astype(jnp.bfloat16)
    grad_query = (
        jnp.einsum(
            "shbqk,shbkd->shbqd", grad_scores, key_picked, preferred_element_type=jnp.float32
        )
        * scaling
    )
    glob_grad = grad_heads[:, :, :GLOBALS].reshape(seq_count, H, glob_rows, HD)

    def run_backward(operands):
        return lax.map(
            lambda packet: global_backward(
                packet[0], packet[1], packet[2], packet[3], packet[4], packet[5], packet[6], scaling
            ),
            operands,
        )

    def skip_backward(operands):
        return (
            jnp.zeros((seq_count, H, glob_rows, HD), jnp.float32),
            jnp.zeros((seq_count, H, full_length, HD), jnp.float32),
            jnp.zeros((seq_count, H, full_length, HD), jnp.float32),
            jnp.zeros((seq_count, H, glob_rows), jnp.float32),
        )

    glob_dq, glob_dk, glob_dv, glob_centre = lax.cond(
        is_first,
        run_backward,
        skip_backward,
        (glob_query, key_heads, value_heads, glob_seg, seg_all, glob_grad, global_lse),
    )
    grad_query = grad_query.at[:, :, :GLOBALS].add(
        glob_dq.reshape(seq_count, H, GLOBALS, BLOCK, HD)
    )
    grad_key_picked = (
        jnp.einsum(
            "shbqk,shbqd->shbkd", grad_scores, query_heads, preferred_element_type=jnp.float32
        )
        * scaling
    )
    grad_value_picked = jnp.einsum(
        "shbqk,shbqd->shbkd", share_low, grad_sparse, preferred_element_type=jnp.float32
    )
    block_shape = (seq_count, H, local_blocks, cand_count, BLOCK, HD)
    key_grad_blocks = (
        jnp.zeros((seq_count, H, total_blocks, BLOCK, HD), jnp.float32)
        .at[:, head_index, candidates]
        .add(grad_key_picked.reshape(block_shape))
    )
    value_grad_blocks = (
        jnp.zeros((seq_count, H, total_blocks, BLOCK, HD), jnp.float32)
        .at[:, head_index, candidates]
        .add(grad_value_picked.reshape(block_shape))
    )
    key_grad_full = (
        (key_grad_blocks.reshape(seq_count, H, full_length, HD) + glob_dk)
        .transpose(0, 2, 1, 3)
        .reshape(seq_count, full_length, width)
    )
    value_grad_full = (
        (value_grad_blocks.reshape(seq_count, H, full_length, HD) + glob_dv)
        .transpose(0, 2, 1, 3)
        .reshape(seq_count, full_length, width)
    )
    key_grad, value_grad = (
        lax.psum_scatter(
            key_grad_full.astype(jnp.bfloat16), "shard", scatter_dimension=1, tiled=True
        ).astype(jnp.float32),
        lax.psum_scatter(
            value_grad_full.astype(jnp.bfloat16), "shard", scatter_dimension=1, tiled=True
        ).astype(jnp.float32),
    )
    query_grad = grad_query.transpose(0, 2, 3, 1, 4).reshape(seq_count, local_tokens, width)
    grad_proj = [
        query_grad.astype(jnp.bfloat16),
        key_grad.astype(jnp.bfloat16),
        value_grad.astype(jnp.bfloat16),
    ]
    input_grad = grad_branch + dense_backward(jnp.concatenate(grad_proj, axis=-1), qkv_back)
    for table_column in range(3):
        grad_adapt_in[table_column], grad_adapt_out[table_column], extra_grad = adapt_back(
            inputs,
            adapter_tables_input[table_column],
            adapter_tables_output[table_column],
            rank_parts[table_column],
            grad_proj[table_column],
        )
        input_grad = input_grad + extra_grad
    adapter_table_count = adapter_down_from_width.shape[1]
    grad_in_d = jnp.stack(
        [
            table_sum(
                grad_adapt_in[table_column],
                adapter_index_table[:, table_column],
                adapter_table_count,
            )
            for table_column in range(5)
        ],
        axis=0,
    )
    grad_in_f = table_sum(grad_adapt_in[5], adapter_index_table[:, 5], adapter_table_count)
    out_list = [
        table_sum(
            grad_adapt_out[table_column], adapter_index_table[:, table_column], adapter_table_count
        )
        for table_column in range(4)
    ]
    grad_out_d = jnp.stack(
        out_list + [table_sum(grad_adapt_out[5], adapter_index_table[:, 5], adapter_table_count)],
        axis=0,
    )
    grad_out_f = table_sum(grad_adapt_out[4], adapter_index_table[:, 4], adapter_table_count)
    owned = (
        lax.psum_scatter(
            grad_in_d.astype(jnp.bfloat16), "shard", scatter_dimension=3, tiled=True
        ).astype(jnp.float32),
        lax.psum_scatter(
            grad_in_f.astype(jnp.bfloat16), "shard", scatter_dimension=2, tiled=True
        ).astype(jnp.float32),
        lax.psum_scatter(
            grad_out_d.astype(jnp.bfloat16), "shard", scatter_dimension=3, tiled=True
        ).astype(jnp.float32),
        lax.psum_scatter(
            grad_out_f.astype(jnp.bfloat16), "shard", scatter_dimension=2, tiled=True
        ).astype(jnp.float32),
    )
    summed = (
        lax.psum(owned[0].astype(jnp.bfloat16), "dp").astype(jnp.float32),
        lax.psum(owned[1].astype(jnp.bfloat16), "dp").astype(jnp.float32),
        lax.psum(owned[2].astype(jnp.bfloat16), "dp").astype(jnp.float32),
        lax.psum(owned[3].astype(jnp.bfloat16), "dp").astype(jnp.float32),
    )
    return (layer_out, input_grad, summed[0], summed[1], summed[2], summed[3])


BF = jnp.bfloat16
F32 = jnp.float32
NT = (((1,), (1,)), ((), ()))
TN = (((0,), (0,)), ((), ()))
BIG = 1e30
RANK = 16
ANY = pl.ANY
VMEM = pltpu.VMEM
MEBI = 1024 * 1024
SMALL_COST = pl.CostEstimate(flops=1_000_000, bytes_accessed=100_000, transcendentals=0)


def mm(left, right):
    return jnp.dot(left, right, preferred_element_type=F32)


def mm_nt(left, right):
    return lax.dot_general(left, right, NT, preferred_element_type=F32)


def mm_tn(left, right):
    return lax.dot_general(left, right, TN, preferred_element_type=F32)


def whole(shape):
    return pl.BlockSpec(shape, lambda *_: (0,) * len(shape))


def away_pairs(dp_count, shard_count, step):
    pairs = []
    for chip in range(dp_count // 2):
        for k in range(2):
            for z in range(shard_count):
                m = (z & 1) ^ step
                source = (2 * chip + k) * shard_count + z
                target = (2 * chip + (z >> 1)) * shard_count + 2 * k + m
                pairs.append((source, target))
    return pairs


def swap_cores(value, dp_count):
    return lax.ppermute(value, "dp", [(i, i ^ 1) for i in range(dp_count)])


def swap_shards(value, shard_count, step):
    return lax.ppermute(value, "shard", [(i, i ^ step) for i in range(shard_count)])


def spread_over_chips(block, dp_count):
    others = [lax.ppermute(block, "dp", [(i, i ^ o) for i in range(dp_count)]) for o in range(2, dp_count, 2)]
    return [block] + others


def swap_chips(block, dp_count, offset):
    return lax.ppermute(block, "dp", [(i, i ^ offset) for i in range(dp_count)])


def spread_over_cores(blocks, dp_count):
    return [one for block in blocks for one in (block, swap_cores(block, dp_count))]


def spread_in_plane(block, dp_count):
    return spread_over_cores(spread_over_chips(block, dp_count), dp_count)


def join_kernel(meta, part0, part1, out_ref):
    for r, part in enumerate((part0, part1)):
        out_ref[(meta[0] & 1) ^ r] = part[...].astype(out_ref.dtype)


def join_parts(meta, parts, dtype):
    rows, width = parts[0].shape
    return pl.pallas_call(
        join_kernel,
        grid_spec=pltpu.PrefetchScalarGridSpec(
            num_scalar_prefetch=1,
            grid=(1,),
            in_specs=[whole((rows, width))] * 2,
            out_specs=whole((2, rows, width)),
        ),
        out_shape=jax.ShapeDtypeStruct((2, rows, width), dtype),
        compiler_params=pltpu.CompilerParams(vmem_limit_bytes=30 * MEBI),
        cost_estimate=SMALL_COST,
        name="join_parts",
    )(meta, *parts)


def send_away(parts, dp_count, shard_count):
    return [
        lax.ppermute(part, ("dp", "shard"), away_pairs(dp_count, shard_count, r))
        for r, part in enumerate(parts)
    ]


def weight_copies(meta, own_ref, pieces, dest, sems, places):
    z, d = meta[0], meta[1]
    own_rows, columns = own_ref.shape
    copies = [
        pltpu.make_async_copy(
            own_ref, dest.at[pl.ds(pl.multiple_of(z * own_rows, 16), own_rows)], sems.at[0]
        )
    ]
    count = 1
    for o, parts in enumerate(pieces):
        who = d ^ o
        for step in range(3):
            shard = z ^ (step + 1)
            for start, row, column, rows, cols in places(who):
                for piece, first in parts:
                    low, high = max(start, first), min(start + rows, first + piece.shape[1])
                    if low >= high:
                        continue
                    copies.append(
                        pltpu.make_async_copy(
                            piece.at[step, pl.ds(low - first, high - low)],
                            dest.at[
                                pl.ds(pl.multiple_of(shard * own_rows + row + low - start, 16), high - low),
                                pl.ds(pl.multiple_of(column, 128), cols),
                            ],
                            sems.at[count],
                        )
                    )
                    count += 1
    return copies


def one_each(refs):
    return [[(ref, 0)] for ref in refs]


UP_SPLIT = 128


def up_parts(refs):
    return one_each(refs[0:6]) + [[(refs[6], 0), (refs[7], UP_SPLIT)], [(refs[8], 0), (refs[9], UP_SPLIT)]]


def qkv_places(who):
    return [(0, (who >> 1) * 48, (who & 1) * 1152, 48, 1152)]


def out_places(who):
    return [(0, (who >> 1) * 48, (who & 1) * 384, 48, 384)]


def up_places(who):
    return [(48, 0, who * 384, 192, 384)]


def down_places(who):
    return [(0, who * 96, 0, 96, 384), (96, who * 96, 384, 96, 384)]


def token_copies(meta, messages, dest, sems):
    copies = []
    for at, message in enumerate(messages):
        row = 512 * (at >> 1) + 256 * ((meta[0] & 1) ^ (at & 1))
        copies.append(
            pltpu.make_async_copy(
                message.at[pl.ds(0, 256)], dest.at[pl.ds(pl.multiple_of(row, 256), 256)], sems.at[at]
            )
        )
    return copies


def zero_padded(rows, position, count):
    zeros = jnp.zeros_like(rows)
    return jnp.concatenate([rows if i == position else zeros for i in range(count)], axis=0)


def qkv_kernel(meta, ids, *refs):
    messages, w_own, pieces = refs[0:4], refs[4], one_each(refs[5:13])
    ins, outs = refs[13:16], refs[16:19]
    q_ref, k_ref, v_ref, mask_ref, hot_ref, own_ref = refs[19:25]
    xs, segs, weight, wsems, xsems, ssems = refs[25:]
    copies = token_copies(meta, messages, xs, xsems)
    for at, message in enumerate(messages):
        copies.append(
            pltpu.make_async_copy(
                message.at[pl.ds(256, 16), pl.ds(0, 256)],
                segs.at[2 * (at >> 1) + ((meta[0] & 1) ^ (at & 1))],
                ssems.at[at],
            )
        )
    copies += weight_copies(meta, w_own, pieces, weight, wsems, qkv_places)
    for copy in copies:
        copy.start()
    for copy in copies:
        copy.wait()
    lane = lax.broadcasted_iota(jnp.int32, (128, 128), 1)
    lane_of_head = lax.rem(lane, 64)
    as_float = lane_of_head.astype(F32)
    is_segment = lane_of_head < 16
    row_block = lax.broadcasted_iota(jnp.int32, (128, 128), 0) // 64
    for place in range(4):
        row = segs[place].astype(F32)[0:1]
        for half in range(2):
            column = jnp.broadcast_to(row[:, 128 * half : 128 * half + 128], (128, 128)).T
            same = column == as_float
            block_lane = lane_of_head == 16 + 4 * place + 2 * half + row_block
            rows = slice(256 * place + 128 * half, 256 * place + 128 * half + 128)
            mask_ref[rows] = jnp.where(
                is_segment, jnp.where(same, 0.0, -BIG), jnp.where(block_lane, 1.0, 0.0)
            ).astype(BF)
            if place < 2:
                hot_ref[rows] = jnp.where(is_segment & same, 1.0, 0.0).astype(BF)
    own_ref[...] = xs[0:512]
    in_all = jnp.concatenate([ref[0, 0] for ref in ins], axis=0)
    out_all = [zero_padded(ref[0, 0], p, 3) for p, ref in enumerate(outs)]
    targets = (q_ref, k_ref, v_ref)
    for tile in range(4):
        rows = slice(256 * tile, 256 * tile + 256)
        x = xs[rows]
        rank = mm_nt(x, in_all).astype(BF)
        for p in range(0 if tile < 2 else 1, 3):
            value = mm(x, weight[:, 768 * p : 768 * p + 768]) + mm(rank, out_all[p])
            value = value.astype(BF)
            if p == 0:
                value = (value.astype(F32) * HD**-0.5).astype(BF)
            targets[p][rows] = value


def table_spec(p, column, width):
    return pl.BlockSpec((1, 1, RANK, width), lambda i, meta, ids: (p, ids[column], 0, 0))


def hidden_spec(column, width):
    return pl.BlockSpec((1, RANK, width), lambda i, meta, ids: (ids[column], 0, 0))


def any_specs(count):
    return [pl.BlockSpec(memory_space=ANY)] * count


def project_qkv(meta, ids, messages, w_own, pieces, table_in, table_out):
    width = w_own.shape[1] // 3
    return pl.pallas_call(
        qkv_kernel,
        grid_spec=pltpu.PrefetchScalarGridSpec(
            num_scalar_prefetch=2,
            grid=(1,),
            in_specs=any_specs(13)
            + [table_spec(p, p, width) for p in range(3)]
            + [table_spec(p, p, width) for p in range(3)],
            out_specs=[
                whole((512, width)),
                whole((1024, width)),
                whole((1024, width)),
                whole((1024, 128)),
                whole((512, 128)),
                whole((512, width)),
            ],
            scratch_shapes=[
                VMEM((1024, width), BF),
                VMEM((4, 16, 256), BF),
                VMEM((width, 3 * width), BF),
                pltpu.SemaphoreType.DMA((25,)),
                pltpu.SemaphoreType.DMA((4,)),
                pltpu.SemaphoreType.DMA((4,)),
            ],
        ),
        out_shape=[
            jax.ShapeDtypeStruct((512, width), BF),
            jax.ShapeDtypeStruct((1024, width), BF),
            jax.ShapeDtypeStruct((1024, width), BF),
            jax.ShapeDtypeStruct((1024, 128), BF),
            jax.ShapeDtypeStruct((512, 128), BF),
            jax.ShapeDtypeStruct((512, width), BF),
        ],
        compiler_params=pltpu.CompilerParams(vmem_limit_bytes=48 * MEBI),
        cost_estimate=SMALL_COST,
        name="project_qkv",
    )(meta, ids, *messages, w_own, *pieces, *([table_in] * 3), *([table_out] * 3))


def attend_kernel(q_ref, k_ref, v_ref, mask_ref, hot_ref, closed_ref, o_ref, p_ref):
    low = lax.broadcasted_iota(jnp.int32, (512, 128), 1) < 64
    low_keys = lax.broadcasted_iota(jnp.int32, (1024, 128), 1) < 64
    closed = jnp.concatenate(
        [jnp.broadcast_to(closed_ref[0, l : l + 1], (64, 128)) for l in range(8)], axis=0
    )
    extra = (hot_ref[...].astype(F32) + closed).astype(BF)
    q, k, v, masks = q_ref[...], k_ref[...], v_ref[...], mask_ref[...]
    wide = [(jnp.where(low, q, extra), jnp.where(low_keys, k, masks)), (jnp.where(low, extra, q), jnp.where(low_keys, masks, k))]
    size = 512
    units = [(start, head) for start in range(0, 512, size) for head in range(2)]
    raw = lambda unit: mm_nt(wide[unit[1]][0][unit[0] : unit[0] + size], wide[unit[1]][1])
    ahead = raw(units[0])
    mixed = {}
    for n, (start, head) in enumerate(units):
        scores = ahead
        if n + 1 < len(units):
            ahead = raw(units[n + 1])
        weights = jnp.exp(scores - jnp.max(scores, axis=1, keepdims=True))
        shares = (weights * (1.0 / jnp.sum(weights, axis=1, keepdims=True))).astype(BF)
        p_ref[head, start : start + size] = shares
        mixed[head] = mm(shares, v)
        if head == 1:
            o_ref[start : start + size] = jnp.where(low[0:size], mixed[0], mixed[1]).astype(BF)


def attend_more_kernel(q_ref, k_ref, v_ref, mask_ref, hot_ref, closed_ref, mixed, shares, o_ref, p_ref):
    del mixed, shares
    attend_kernel(q_ref, k_ref, v_ref, mask_ref, hot_ref, closed_ref, o_ref, p_ref)


def attend(first, pairs, q, k, v, masks, hot, closed, *before):
    width = q.shape[1]
    half = pl.BlockSpec((512, 128), lambda g: (0, g + first))
    full = pl.BlockSpec((1024, 128), lambda g: (0, g + first))
    return pl.pallas_call(
        attend_more_kernel if before else attend_kernel,
        grid=(pairs,),
        in_specs=[
            half,
            full,
            full,
            whole((1024, 128)),
            whole((512, 128)),
            pl.BlockSpec((1, 8, 128), lambda g: (g + first, 0, 0)),
        ]
        + any_specs(len(before)),
        out_specs=[half, pl.BlockSpec((2, 512, 1024), lambda g: (g + first, 0, 0))],
        out_shape=[
            jax.ShapeDtypeStruct((512, width), BF),
            jax.ShapeDtypeStruct((width // 64, 512, 1024), BF),
        ],
        input_output_aliases={6 + n: n for n in range(len(before))},
        compiler_params=pltpu.CompilerParams(vmem_limit_bytes=56 * MEBI),
        cost_estimate=SMALL_COST,
        name="attend",
    )(q, k, v, masks, hot, closed, *before)


def attend_back_kernel(q_ref, k_ref, v_ref, p_ref, grad_ref, mixed_ref, dq_ref, dk_own, dv_own, other_ref):
    low = lax.broadcasted_iota(jnp.int32, (512, 128), 1) < 64
    q, k, v, grad = q_ref[...], k_ref[...], v_ref[...], grad_ref[...]
    products = grad.astype(F32) * mixed_ref[...].astype(F32)
    q_turned, grad_turned = q.T, grad.T
    zeros, none = jnp.zeros_like(grad), jnp.zeros_like(products)
    dq, dk, dv = [], [], []
    for head in range(2):
        mine = low if head == 0 else jnp.logical_not(low)
        centre = jnp.sum(jnp.where(mine, products, none), axis=1, keepdims=True)
        grad_shares = mm_nt(jnp.where(mine, grad, zeros), v)
        shares = p_ref[head]
        grad_scores = (shares.astype(F32) * (grad_shares - centre)).astype(BF)
        rows = slice(64 * head, 64 * head + 64)
        dq.append(mm(grad_scores, k))
        dk.append(mm(q_turned[rows], grad_scores))
        dv.append(mm(grad_turned[rows], shares))
    dq_ref[...] = (jnp.where(low, dq[0], dq[1]) * HD**-0.5).astype(BF)
    dk = jnp.concatenate(dk, axis=0).T
    dv = jnp.concatenate(dv, axis=0).T
    dk_own[...] = dk[0:512].astype(BF)
    dv_own[...] = dv[0:512].astype(BF)
    other_ref[0] = dk[512:1024].astype(BF)
    other_ref[1] = dv[512:1024].astype(BF)


def attend_back(q, k, v, shares, grad, mixed):
    width = q.shape[1]
    half = pl.BlockSpec((512, 128), lambda g: (0, g))
    full = pl.BlockSpec((1024, 128), lambda g: (0, g))
    return pl.pallas_call(
        attend_back_kernel,
        grid=(width // 128,),
        in_specs=[half, full, full, pl.BlockSpec((2, 512, 1024), lambda g: (g, 0, 0)), half, half],
        out_specs=[half] * 3 + [pl.BlockSpec((2, 512, 128), lambda g: (0, 0, g))],
        out_shape=[
            jax.ShapeDtypeStruct((512, width), BF),
            jax.ShapeDtypeStruct((512, width), BF),
            jax.ShapeDtypeStruct((512, width), BF),
            jax.ShapeDtypeStruct((2, 512, width), BF),
        ],
        compiler_params=pltpu.CompilerParams(vmem_limit_bytes=40 * MEBI),
        cost_estimate=SMALL_COST,
        name="attend_back",
    )(q, k, v, shares, grad, mixed)


def gelu_and_slope(lifted):
    size = jnp.abs(lifted)
    t = 1.0 / (1.0 + 0.23164189 * size)
    poly = t * (
        0.127414796 + t * (-0.142248368 + t * (0.7107068705 + t * (-0.7265760135 + t * 0.5307027145)))
    )
    decay = jnp.exp2(lifted * lifted * -0.7213475204444817)
    tail = poly * decay
    below = jnp.where(lifted < 0.0, tail, 1.0 - tail)
    return jnp.maximum(lifted, 0.0) - size * tail, below + lifted * (decay * 0.3989422804014327)


def norm_parts(hidden):
    average = jnp.mean(hidden, axis=-1, keepdims=True)
    centred = hidden - average
    spread = jnp.mean(centred * centred, axis=-1, keepdims=True)
    inverse = lax.rsqrt(spread + EPSILON)
    return centred * inverse, inverse


def norm_back(grad, gain, normal, inverse):
    scaled = grad * gain
    return inverse * (
        scaled
        - jnp.mean(scaled, axis=-1, keepdims=True)
        - normal * jnp.mean(scaled * normal, axis=-1, keepdims=True)
    )


MID_TILE = 256
MID_PARTS = 4


def first_half_kernel(meta, ids, *refs):
    out_own, up_own, up_pieces = refs[0], refs[1], up_parts(refs[2:12])
    x_ref, mixed_ref, gain1, in3, in4, out3, out4 = refs[12:19]
    normal_ref, inverse_ref, active, slope = refs[19:23]
    w_out, w_up, osems, usems = refs[23:]
    out_copies = weight_copies(meta, out_own, up_pieces, w_out, osems, out_places)
    up_copies = weight_copies(meta, up_own, up_pieces, w_up, usems, up_places)
    is_first = pl.program_id(0) == 0

    @pl.when(is_first)
    def _():
        for copy in out_copies + up_copies:
            copy.start()
        for copy in out_copies:
            copy.wait()

    mixed = mixed_ref[...]
    rank3 = mm_nt(mixed, in3[0, 0]).astype(BF)
    branch = mm(mixed, w_out[...]) + mm(rank3, out3[0, 0])
    normal, inverse = norm_parts(x_ref[...].astype(F32) + branch)
    normal_ref[...] = normal
    inverse_ref[...] = jnp.broadcast_to(inverse, inverse_ref.shape)
    low = (normal * gain1[...][None]).astype(BF)
    rank4 = mm_nt(low, in4[0, 0]).astype(BF)

    @pl.when(is_first)
    def _():
        for copy in up_copies:
            copy.wait()

    part = w_up.shape[1] // MID_PARTS
    columns = [slice(n * part, n * part + part) for n in range(MID_PARTS)]
    lift = lambda cols: mm(low, w_up[:, cols]) + mm(rank4, out4[0, :, cols])
    ahead = lift(columns[0])
    for n, cols in enumerate(columns):
        lifted = ahead
        if n + 1 < MID_PARTS:
            ahead = lift(columns[n + 1])
        value, tangent = gelu_and_slope(lifted)
        active[:, cols] = value.astype(BF)
        slope[:, cols] = tangent.astype(BF)


def first_half(meta, ids, out_own, up_own, up_pieces, x, mixed, gain1, table_in, table_out, table_out_hidden):
    width, hidden = x.shape[1], up_own.shape[1]
    tile = lambda columns: pl.BlockSpec((MID_TILE, columns), lambda i, *_: (i, 0))
    return pl.pallas_call(
        first_half_kernel,
        grid_spec=pltpu.PrefetchScalarGridSpec(
            num_scalar_prefetch=2,
            grid=(512 // MID_TILE,),
            in_specs=any_specs(12)
            + [
                tile(width),
                tile(width),
                whole((width,)),
                table_spec(3, 3, width),
                table_spec(4, 4, width),
                table_spec(3, 3, width),
                hidden_spec(4, hidden),
            ],
            out_specs=[tile(width), tile(128), tile(hidden), tile(hidden)],
            scratch_shapes=[
                VMEM((width, width), BF),
                VMEM((width, hidden), BF),
                pltpu.SemaphoreType.DMA((25,)),
                pltpu.SemaphoreType.DMA((31,)),
            ],
        ),
        out_shape=[
            jax.ShapeDtypeStruct((512, width), F32),
            jax.ShapeDtypeStruct((512, 128), F32),
            jax.ShapeDtypeStruct((512, hidden), BF),
            jax.ShapeDtypeStruct((512, hidden), BF),
        ],
        compiler_params=pltpu.CompilerParams(vmem_limit_bytes=44 * MEBI),
        cost_estimate=SMALL_COST,
        name="first_half",
    )(meta, ids, out_own, up_own, *up_pieces, x, mixed, gain1, table_in, table_in, table_out, table_out_hidden)


def write_halves(meta, gathered, groups, own_half, other_half):
    core = meta[1] & 1
    for r in range(4):
        for half, ref in enumerate((own_half, other_half)):
            rows = [
                gathered[meta[0] ^ r, pl.ds(pl.multiple_of(16 * group + 8 * (core ^ half), 8), 8), :]
                for group in range(groups)
            ]
            ref[r] = jnp.concatenate(rows, axis=0).astype(ref.dtype)


def second_half_kernel(meta, ids, *refs):
    cots, out_own, up_own, down_own = refs[0:2], refs[2], refs[3], refs[4]
    up_pieces, down_pieces = up_parts(refs[5:15]), one_each(refs[15:23])
    normal_ref, inverse_ref, active, slope, mixed_ref = refs[23:28]
    gain1, gain2, in3, in4, in5, out3, out4, out5 = refs[28:36]
    layer_parts, grad_branch_ref, grad_mixed_ref, own_half, other_half = refs[36:38], refs[38], refs[39], refs[40], refs[41]
    (
        cot, w_out, w_up, w_down, layer,
        s_in3, s_in4, s_in5, s_out3, s_out4, s_out5, gathered,
        osems, usems, dsems, xsems,
    ) = refs[42:]
    tile = pl.program_id(0)
    is_first = tile == 0
    near = token_copies(meta, cots, cot, xsems)
    out_copies = weight_copies(meta, out_own, up_pieces, w_out, osems, out_places)
    up_copies = weight_copies(meta, up_own, up_pieces, w_up, usems, up_places)
    down_copies = weight_copies(meta, down_own, down_pieces, w_down, dsems, down_places)

    @pl.when(is_first)
    def _():
        for copy in down_copies + near + up_copies + out_copies:
            copy.start()
        for ref in (s_in3, s_in4, s_in5, s_out3, s_out4, s_out5):
            ref[...] = jnp.zeros_like(ref)
        for copy in down_copies + near:
            copy.wait()

    part = w_up.shape[1] // MID_PARTS
    a_in3, a_in4, a_out3, a_out5 = in3[0, 0], in4[0, 0], out3[0, 0], out5[0, 0]
    rows = pl.ds(pl.multiple_of(tile * MID_TILE, MID_TILE), MID_TILE)
    normal1 = normal_ref[...]
    inverse1 = inverse_ref[:, 0:1]
    first = normal1 * gain1[...][None]
    low1 = first.astype(BF)
    r4 = mm_nt(low1, a_in4).astype(BF)
    r5 = mm_nt(active[...], in5[0]).astype(BF)
    lowered = first + mm(active[...], w_down[...]) + mm(r5, a_out5)
    normal2, inverse2 = norm_parts(lowered)
    layer[rows, :] = (normal2 * gain2[...][None]).astype(BF)
    grad_sum = norm_back(cot[rows, :].astype(F32), gain2[...][None], normal2, inverse2)
    e5 = grad_sum.astype(BF)
    rg5 = mm_nt(e5, a_out5).astype(BF)
    s_out5[...] += mm_tn(r5, e5)

    @pl.when(is_first)
    def _():
        for copy in up_copies + out_copies:
            copy.wait()

    grad_first = grad_sum
    rg4 = jnp.zeros((MID_TILE, RANK), F32)
    for n in range(MID_PARTS):
        cols = slice(n * part, n * part + part)
        grad_active = mm_nt(e5, w_down[cols, :]) + mm(rg5, in5[0, :, cols])
        e4 = (slope[:, cols].astype(F32) * grad_active).astype(BF)
        s_in5[:, cols] += mm_tn(rg5, active[:, cols])
        s_out4[:, cols] += mm_tn(r4, e4)
        grad_first = grad_first + mm_nt(e4, w_up[:, cols])
        rg4 = rg4 + mm_nt(e4, out4[0, :, cols])
    rg4 = rg4.astype(BF)
    s_in4[...] += mm_tn(rg4, low1)
    grad_first = grad_first + mm(rg4, a_in4)
    grad_branch = norm_back(grad_first, gain1[...][None], normal1, inverse1)
    grad_branch_ref[...] = grad_branch
    e3 = grad_branch.astype(BF)
    mixed = mixed_ref[...]
    rank3 = mm_nt(mixed, a_in3).astype(BF)
    rg3 = mm_nt(e3, a_out3).astype(BF)
    s_out3[...] += mm_tn(rank3, e3)
    s_in3[...] += mm_tn(rg3, mixed)
    grad_mixed_ref[...] = (mm_nt(e3, w_out[...]) + mm(rg3, a_in3)).astype(BF)

    @pl.when(tile == 512 // MID_TILE - 1)
    def _():
        wide, narrow = 768, 192
        for owner in range(4):
            start = 0
            for ref, size in (
                (s_in5, wide), (s_out4, wide), (s_in3, narrow), (s_in4, narrow), (s_out3, narrow), (s_out5, narrow),
            ):
                row, column = 16 * (start // 768), start % 768
                gathered[owner, row : row + 16, column : column + size] = ref[:, owner * size : owner * size + size]
                start += size
        for r, ref in enumerate(layer_parts):
            ref[...] = layer[pl.ds(pl.multiple_of(256 * ((meta[0] & 1) ^ r), 256), 256), :]
        write_halves(meta, gathered, 3, own_half, other_half)


def second_half(meta, ids, cots, out_own, up_own, down_own, up_pieces, down_pieces, normal, inverse, active, slope,
                mixed, gain1, gain2, table_in, table_in_hidden, table_out, table_out_hidden):
    width, hidden = normal.shape[1], up_own.shape[1]
    tile = lambda columns: pl.BlockSpec((MID_TILE, columns), lambda i, *_: (i, 0))
    return pl.pallas_call(
        second_half_kernel,
        grid_spec=pltpu.PrefetchScalarGridSpec(
            num_scalar_prefetch=2,
            grid=(512 // MID_TILE,),
            in_specs=any_specs(23)
            + [
                tile(width),
                tile(128),
                tile(hidden),
                tile(hidden),
                tile(width),
                whole((width,)),
                whole((width,)),
                table_spec(3, 3, width),
                table_spec(4, 4, width),
                hidden_spec(5, hidden),
                table_spec(3, 3, width),
                hidden_spec(4, hidden),
                table_spec(4, 5, width),
            ],
            out_specs=[whole((256, width))] * 2 + [tile(width), tile(width)] + [whole((4, 24, width))] * 2,
            scratch_shapes=[
                VMEM((512, width), BF),
                VMEM((width, width), BF),
                VMEM((width, hidden), BF),
                VMEM((hidden, width), BF),
                VMEM((512, width), BF),
                VMEM((RANK, width), F32),
                VMEM((RANK, width), F32),
                VMEM((RANK, hidden), F32),
                VMEM((RANK, width), F32),
                VMEM((RANK, hidden), F32),
                VMEM((RANK, width), F32),
                VMEM((4, 3 * RANK, 768), F32),
                pltpu.SemaphoreType.DMA((25,)),
                pltpu.SemaphoreType.DMA((31,)),
                pltpu.SemaphoreType.DMA((49,)),
                pltpu.SemaphoreType.DMA((2,)),
            ],
        ),
        out_shape=[jax.ShapeDtypeStruct((256, width), BF)] * 2
        + [jax.ShapeDtypeStruct((512, width), F32), jax.ShapeDtypeStruct((512, width), BF)]
        + [jax.ShapeDtypeStruct((4, 24, width), F32), jax.ShapeDtypeStruct((4, 24, width), BF)],
        compiler_params=pltpu.CompilerParams(vmem_limit_bytes=56 * MEBI),
        cost_estimate=SMALL_COST,
        name="second_half",
    )(meta, ids, *cots, out_own, up_own, down_own, *up_pieces, *down_pieces, normal, inverse, active, slope, mixed,
      gain1, gain2, table_in, table_in, table_in_hidden, table_out, table_out_hidden, table_out)


def first_grads_kernel(meta, ids, *refs):
    xs, dq_ref, dk_ref, dv_ref, got_ref = refs[0:5]
    ins, outs = refs[5:8], refs[8:11]
    grads_ref, rank_grad_ref = refs[11:13]
    own_half, other_half = refs[13:15]
    s_in, s_out, gathered = refs[15:]
    in_all = jnp.concatenate([ref[0, 0] for ref in ins], axis=0)
    out_all = jnp.concatenate([zero_padded(ref[0, 0], p, 3) for p, ref in enumerate(outs)], axis=1)
    for tile in range(2):
        rows = slice(256 * tile, 256 * tile + 256)
        grads = jnp.concatenate(
            [dq_ref[rows]]
            + [(ref[rows].astype(F32) + got_ref[n, rows].astype(F32)).astype(BF) for n, ref in enumerate((dk_ref, dv_ref))],
            axis=1,
        )
        grads_ref[rows] = grads
        x = xs[rows]
        rank = mm_nt(x, in_all).astype(BF)
        rank_grad = mm_nt(grads, out_all).astype(BF)
        rank_grad_ref[rows] = rank_grad
        part_in, part_out = mm_tn(rank_grad, x), mm_tn(rank, grads)
        if tile == 0:
            s_in[...] = part_in
            s_out[...] = part_out
        else:
            s_in[...] += part_in
            s_out[...] += part_out
    gathered[...] = jnp.zeros_like(gathered)
    for owner in range(4):
        for p in range(3):
            rows, columns = slice(RANK * p, RANK * p + RANK), slice(192 * owner, 192 * owner + 192)
            gathered[owner, 0:16, 192 * p : 192 * p + 192] = s_in[rows, columns]
            columns = slice(768 * p + 192 * owner, 768 * p + 192 * owner + 192)
            at = (0, 576) if p == 0 else (16, 192 * (p - 1))
            gathered[owner, at[0] : at[0] + 16, at[1] : at[1] + 192] = s_out[rows, columns]
    write_halves(meta, gathered, 2, own_half, other_half)


def first_grads(meta, ids, x, dq, dk, dv, got, table_in, table_out):
    width = x.shape[1]
    return pl.pallas_call(
        first_grads_kernel,
        grid_spec=pltpu.PrefetchScalarGridSpec(
            num_scalar_prefetch=2,
            grid=(1,),
            in_specs=[whole((512, width))] * 4
            + [whole((2, 512, width))]
            + [table_spec(p, p, width) for p in range(3)] * 2,
            out_specs=[whole((512, 3 * width)), whole((512, 3 * RANK))] + [whole((4, 16, width))] * 2,
            scratch_shapes=[
                VMEM((3 * RANK, width), F32),
                VMEM((3 * RANK, 3 * width), F32),
                VMEM((4, 2 * RANK, 768), F32),
            ],
        ),
        out_shape=[jax.ShapeDtypeStruct((512, 3 * width), BF), jax.ShapeDtypeStruct((512, 3 * RANK), BF)]
        + [jax.ShapeDtypeStruct((4, 16, width), F32), jax.ShapeDtypeStruct((4, 16, width), BF)],
        compiler_params=pltpu.CompilerParams(vmem_limit_bytes=30 * MEBI),
        cost_estimate=SMALL_COST,
        name="first_grads",
    )(meta, ids, x, dq, dk, dv, got, *([table_in] * 3), *([table_out] * 3))


def input_grad_kernel(meta, ids, *refs):
    w_own, pieces = refs[0], one_each(refs[1:9])
    branch_ref, grads_ref, rank_grad_ref = refs[9:12]
    ins, parts = refs[12:15], refs[15:17]
    weight, wsems = refs[17:]
    copies = weight_copies(meta, w_own, pieces, weight, wsems, qkv_places)
    for copy in copies:
        copy.start()
    for copy in copies:
        copy.wait()
    in_all = jnp.concatenate([ref[0, 0] for ref in ins], axis=0)
    for r, ref in enumerate(parts):
        rows = pl.ds(pl.multiple_of(256 * ((meta[0] & 1) ^ r), 256), 256)
        ref[...] = (
            branch_ref[rows, :] + mm_nt(grads_ref[rows, :], weight[...]) + mm(rank_grad_ref[rows, :], in_all)
        ).astype(BF)


def project_back(meta, ids, w_own, pieces, branch, grads, rank_grad, table_in):
    width = branch.shape[1]
    return pl.pallas_call(
        input_grad_kernel,
        grid_spec=pltpu.PrefetchScalarGridSpec(
            num_scalar_prefetch=2,
            grid=(1,),
            in_specs=any_specs(9)
            + [whole((512, width)), whole((512, 3 * width)), whole((512, 3 * RANK))]
            + [table_spec(p, p, width) for p in range(3)],
            out_specs=[whole((256, width))] * 2,
            scratch_shapes=[VMEM((width, 3 * width), BF), pltpu.SemaphoreType.DMA((25,))],
        ),
        out_shape=[jax.ShapeDtypeStruct((256, width), BF)] * 2,
        compiler_params=pltpu.CompilerParams(vmem_limit_bytes=30 * MEBI),
        cost_estimate=SMALL_COST,
        name="project_back",
    )(meta, ids, w_own, *pieces, branch, grads, rank_grad, *([table_in] * 3))


def sum_cores_kernel(ids, mid_own, mid_other, first_own, first_other, *messages):
    row = lax.broadcasted_iota(jnp.int32, (16, 768), 0)
    lane = lax.broadcasted_iota(jnp.int32, (16, 768), 1)
    for r, ref in enumerate(messages):
        mid = mid_own[r] + mid_other[r].astype(F32)
        first = first_own[r] + first_other[r].astype(F32)
        for p in range(6):
            first = jnp.where((row >= 8) & (lane == 384 + p), ids[p].astype(F32), first)
        ref[...] = jnp.concatenate([mid, first], axis=0).astype(BF)


def sum_cores(ids, *halves):
    width = halves[0].shape[-1]
    return pl.pallas_call(
        sum_cores_kernel,
        grid_spec=pltpu.PrefetchScalarGridSpec(
            num_scalar_prefetch=1,
            grid=(1,),
            in_specs=[whole(half.shape) for half in halves],
            out_specs=[whole((40, width))] * 4,
        ),
        out_shape=[jax.ShapeDtypeStruct((40, width), BF)] * 4,
        compiler_params=pltpu.CompilerParams(vmem_limit_bytes=30 * MEBI),
        cost_estimate=SMALL_COST,
        name="sum_cores",
    )(ids, *halves)


def combine_kernel(ids, meta, own, other, in_d, in_f, out_d, out_f):
    for ref in (in_d, in_f, out_d, out_f):
        ref[...] = jnp.zeros_like(ref)
    narrow = in_d.shape[-1]
    for chip in range(4):
        for r in range(4):
            chosen = [ids[(chip * 4 + r) * 6 + p] for p in range(6)]
            for half, messages in enumerate((own, other)):
                ranks = pl.ds(pl.multiple_of(8 * ((meta[1] & 1) ^ half), 8), 8)
                part = messages[chip, r].astype(F32)
                in_f[chosen[5], ranks, :] += part[0:8]
                out_f[chosen[4], ranks, :] += part[8:16]
                for at, (ref, p, which) in enumerate(
                    (
                        (in_d, 3, 3), (in_d, 4, 4), (out_d, 3, 3), (out_d, 4, 5),
                        (in_d, 0, 0), (in_d, 1, 1), (in_d, 2, 2), (out_d, 0, 0),
                        (out_d, 1, 1), (out_d, 2, 2),
                    )
                ):
                    row, column = 16 + 8 * (at // 4), narrow * (at % 4)
                    ref[p, chosen[which], ranks, :] += part[row : row + 8, column : column + narrow]


def combine(ids, meta, own, other, tables, narrow, wide):
    shapes = [(5, tables, RANK, narrow), (tables, RANK, wide)] * 2
    return pl.pallas_call(
        combine_kernel,
        grid_spec=pltpu.PrefetchScalarGridSpec(
            num_scalar_prefetch=2,
            grid=(1,),
            in_specs=[whole(own.shape)] * 2,
            out_specs=[whole(shape) for shape in shapes],
        ),
        out_shape=[jax.ShapeDtypeStruct(shape, F32) for shape in shapes],
        compiler_params=pltpu.CompilerParams(vmem_limit_bytes=30 * MEBI),
        cost_estimate=SMALL_COST,
        name="combine",
    )(ids, meta, own, other)


def after(value, *others):
    return lax.optimization_barrier((value, *others))[0]


def beside(work, transfers, values, moved):
    given = lax.optimization_barrier((tuple(values), tuple(moved)))
    return lax.optimization_barrier((tuple(work(*given[0])), tuple(transfers(*given[1]))))


def paired_body(
    inputs,
    segments,
    random_key_blocks,
    adapter_index_table,
    frozen_query_key_value_weight,
    frozen_output_weight,
    frozen_up_weight,
    frozen_down_weight,
    attention_norm_gain,
    feedforward_norm_gain,
    adapter_down_from_width,
    adapter_down_from_hidden,
    adapter_up_to_width,
    adapter_up_to_hidden,
    cotangent,
):
    dp_count, shard_count = lax.axis_size("dp"), lax.axis_size("shard")
    d, z = lax.axis_index("dp"), lax.axis_index("shard")
    core = d & 1
    meta = jnp.stack([z, d]).astype(jnp.int32)

    def piece(weight, rows, columns, row, column):
        return lax.dynamic_slice(weight, (row, column), (rows, columns))

    def fetch(part):
        return [swap_shards(part, shard_count, step) for step in range(1, shard_count)]

    def slices(values):
        return [lax.dynamic_index_in_dim(values, (z & 1) ^ r, 0, keepdims=False) for r in range(2)]

    def chips(block, *offsets):
        return [swap_chips(block, dp_count, offset) for offset in offsets]

    def swap(block):
        return swap_cores(block, dp_count)

    qkv_own = jnp.stack(fetch(piece(frozen_query_key_value_weight, 48, 1152, (d >> 1) * 48, core * 1152)))
    up_piece = jnp.concatenate(
        [
            piece(frozen_output_weight, 48, 384, (d >> 1) * 48, core * 384),
            piece(frozen_up_weight, 192, 384, 0, d * 384),
        ],
        axis=0,
    )
    down_piece = piece(frozen_down_weight, 96, 768, d * 96, 0)
    down_piece = jnp.concatenate([down_piece[:, 0:384], down_piece[:, 384:768]], axis=0)
    seg_rows = jnp.pad(segments.astype(BF)[:, None, :], ((0, 0), (0, 15), (0, inputs.shape[-1] - 256)))
    own = send_away(slices(jnp.concatenate([inputs, seg_rows], axis=1)), dp_count, shard_count)
    there = swap_cores(adapter_index_table, dp_count)
    column_ids = jnp.where(
        core == 0,
        jnp.concatenate([adapter_index_table, there], axis=0),
        jnp.concatenate([there, adapter_index_table], axis=0),
    )
    ids = lax.dynamic_index_in_dim(column_ids, z, 0, keepdims=False)

    blocks = jnp.arange(16, dtype=jnp.int32)
    query_block = (8 * core + blocks[0:8])[None, :, None]
    key_block = jnp.where(blocks < 8, 8 * core + blocks, 8 * (1 - core) + blocks - 8)[None, None, :]
    drawn = lax.dynamic_slice_in_dim(random_key_blocks, 8 * core, 8, axis=1)
    allowed = (jnp.abs(query_block - key_block) <= 1) | (query_block < GLOBALS) | (key_block < GLOBALS)
    for n in range(RANDOMS):
        allowed = allowed | (drawn[:, :, n : n + 1] == key_block)
    closed = jnp.pad(jnp.where(allowed, 0.0, -BIG), ((0, 0), (0, 0), (16, 32)))
    closed = closed.reshape(H // 2, 2, 8, 64)
    closed = jnp.concatenate([closed[:, 1], closed[:, 0]], axis=-1)

    qkv_own, meta, up_piece = lax.optimization_barrier((qkv_own, meta, up_piece))
    tokens = own + [swap(part) for part in own]
    qkv_x, qkv_y, qkv_xy = chips(qkv_own, 2, 4, 6)
    qkv_xy, closed, down_piece, ids = lax.optimization_barrier((qkv_xy, closed, down_piece, ids))
    qkv_pieces = spread_over_cores((qkv_own, qkv_x, qkv_y, qkv_xy), dp_count)
    up_own = fetch(after(up_piece, *own))

    def work(*given):
        return project_qkv(
            meta, ids, given[0:4], frozen_query_key_value_weight, given[4:],
            adapter_down_from_width, adapter_up_to_width,
        )

    (q, k, v, masks, hot, x), up_own = lax.optimization_barrier((work(*tokens, *qkv_pieces), up_own))
    up_own = jnp.stack(up_own)
    (mixed, shares), (up_x, up_y, up_there, down_1, down_2) = beside(
        lambda *given: attend(0, 4, *given, closed),
        lambda block, part: (
            *chips(block, 2, 4), swap(block), swap_shards(part, shard_count, 1), swap_shards(part, shard_count, 2)
        ),
        (q, k, v, masks, hot),
        (up_own, down_piece),
    )
    (mixed, shares), (up_a, up_b, up_x_there, up_y_there, down_3) = beside(
        lambda *before: attend(4, H // 2 - 4, q, k, v, masks, hot, closed, *before),
        lambda up_x, up_y, part: (
            *chips(up_x[:, 0:UP_SPLIT], 4),
            *chips(up_y[:, UP_SPLIT:], 2),
            swap(up_x),
            swap(up_y),
            swap_shards(part, shard_count, 3),
        ),
        (mixed, shares),
        (up_x, up_y, down_piece),
    )
    down_own = jnp.stack([down_1, down_2, down_3])
    up_pieces = (up_own, up_there, up_x, up_x_there, up_y, up_y_there, up_a, up_b, swap(up_a), swap(up_b))
    gain1, gain2 = attention_norm_gain, feedforward_norm_gain

    def work(mixed, *pieces):
        return first_half(
            meta, ids, frozen_output_weight, frozen_up_weight, pieces, x, mixed, gain1,
            adapter_down_from_width, adapter_up_to_width, adapter_up_to_hidden,
        )

    (normal, inverse, active, slope), (*down_pieces, cot_a, cot_b) = beside(
        work,
        lambda block, values: (*chips(block, 2, 4, 6), *send_away(slices(values), dp_count, shard_count)),
        (mixed, *up_pieces),
        (after(down_own, up_a, up_b), cotangent),
    )
    down_pieces = spread_over_cores((down_own, *down_pieces), dp_count)
    cots = (cot_a, cot_b)
    results = second_half(
        meta, ids, cots, frozen_output_weight, frozen_up_weight, frozen_down_weight, up_pieces, down_pieces,
        normal, inverse, active, slope, mixed, gain1, gain2,
        adapter_down_from_width, adapter_down_from_hidden, adapter_up_to_width, adapter_up_to_hidden,
    )
    grad_branch = results[2]

    def home(r, part):
        return lax.ppermute(part, ("dp", "shard"), away_pairs(dp_count, shard_count, r))

    def swap_over_shards(*parts):
        return [swap_shards(part, shard_count, step + 1) for step, part in enumerate(parts)]

    (dq, dk, dv, other_sums), (layer_a, layer_b) = beside(
        lambda grad: attend_back(q, k, v, shares, grad, mixed),
        lambda part_a, part_b: (home(0, part_a), home(1, part_b)),
        (results[3],),
        results[0:2],
    )
    grads, rank_grad, first_own, first_other = first_grads(
        meta, ids, x, dq, dk, dv, swap(other_sums), adapter_down_from_width, adapter_up_to_width
    )
    input_parts, (first_other, mid_other) = beside(
        lambda grads: project_back(
            meta, ids, frozen_query_key_value_weight, qkv_pieces, grad_branch, grads, rank_grad,
            adapter_down_from_width,
        ),
        lambda *halves: [swap(half) for half in halves],
        (grads,),
        (first_other, results[5]),
    )
    message, *others = sum_cores(ids, results[4], mid_other, first_own, first_other)
    (layer_out,), moved = beside(
        lambda *parts: (join_parts(meta, parts, BF),),
        swap_over_shards,
        (layer_a, layer_b),
        others,
    )
    messages = jnp.stack([message, *moved])
    _, (part_a, part_b, *moved) = beside(
        lambda: (),
        lambda part_a, part_b, block: (home(0, part_a), home(1, part_b), *chips(block, 2, 4, 6)),
        (),
        (*input_parts, messages),
    )
    messages = jnp.stack([messages, *moved])
    chosen = messages[:, :, 32, 384:390].astype(jnp.int32).reshape(-1)
    in_d, in_f, out_d, out_f = combine(
        chosen, meta, messages, swap(messages), adapter_down_from_width.shape[1], 192, 768
    )
    return (layer_out, join_parts(meta, (part_a, part_b), F32), in_d, in_f, out_d, out_f)


def solution(mesh):
    dp_count, shard_count = mesh.shape["dp"], mesh.shape["shard"]
    paired = dp_count == 8 and shard_count == 4
    return jax.shard_map(
        paired_body if paired else general_body,
        mesh=mesh,
        in_specs=(
            P("dp", "shard", None),
            P("dp", "shard"),
            P(),
            P("dp", None),
            P("shard", None),
            P("shard", None),
            P("shard", None),
            P("shard", None),
            P(),
            P(),
            P(),
            P(),
            P(),
            P(),
            P("dp", "shard", None),
        ),
        out_specs=(
            P("dp", "shard", None),
            P("dp", "shard", None),
            P(None, None, None, "shard"),
            P(None, None, "shard"),
            P(None, None, None, "shard"),
            P(None, None, "shard"),
        ),
        check_vma=False,
    )
```

```python
import functools

import jax
import jax.numpy as jnp
from jax import lax
from jax.experimental import pallas as pl
from jax.experimental.pallas import tpu as pltpu
from jax.sharding import PartitionSpec as P

H = 12
HD = 64
BLOCK = 64
GLOBALS = 2
RANDOMS = 3


EPSILON = 1e-06
NEGATIVE = -1e30


def norm_rows(hidden, gain_vector):
    average = jnp.mean(hidden, axis=-1, keepdims=True)
    centred = hidden - average
    spread = jnp.mean(centred * centred, axis=-1, keepdims=True)
    return centred * lax.rsqrt(spread + EPSILON) * gain_vector


def gelu_exact(values):
    return jax.nn.gelu(values, approximate=False)


def dense_forward(inputs, weight):
    return jnp.einsum("sti,io->sto", inputs, weight, preferred_element_type=jnp.float32)


def dense_backward(grad_low, weight):
    return jnp.einsum("sto,io->sti", grad_low, weight, preferred_element_type=jnp.float32)


def adapt(inputs, down_rows, up_rows):
    rank_part = jnp.einsum(
        "sti,sri->str", inputs, down_rows, preferred_element_type=jnp.float32
    ).astype(jnp.bfloat16)
    return (
        rank_part,
        jnp.einsum("str,sro->sto", rank_part, up_rows, preferred_element_type=jnp.float32),
    )


def adapt_back(inputs, down_rows, up_rows, rank_part, grad_low):
    grad_up = jnp.einsum("str,sto->sro", rank_part, grad_low, preferred_element_type=jnp.float32)
    rank_grad = jnp.einsum(
        "sto,sro->str", grad_low, up_rows, preferred_element_type=jnp.float32
    ).astype(jnp.bfloat16)
    grad_down = jnp.einsum("str,sti->sri", rank_grad, inputs, preferred_element_type=jnp.float32)
    grad_inputs = jnp.einsum(
        "str,sri->sti", rank_grad, down_rows, preferred_element_type=jnp.float32
    )
    return (grad_down, grad_up, grad_inputs)


def table_sum(per_sequence, chosen, table_size):
    matches = (chosen[:, None] == jnp.arange(table_size, dtype=jnp.int32)[None, :]).astype(
        jnp.float32
    )
    return jnp.sum(matches[:, :, None, None] * per_sequence[:, None], axis=0)


def sparse_scores(query_heads, key_picked, permit, scaling):
    scores = (
        jnp.einsum(
            "shbqd,shbkd->shbqk", query_heads, key_picked, preferred_element_type=jnp.float32
        )
        * scaling
    )
    return jnp.where(permit, scores, NEGATIVE)


def global_scores(query_rows, key_rows, seg_query, seg_keys, scaling):
    scores = (
        jnp.einsum("hqd,hkd->hqk", query_rows, key_rows, preferred_element_type=jnp.float32)
        * scaling
    )
    return jnp.where((seg_query[:, None] == seg_keys[None, :])[None], scores, NEGATIVE)


def global_forward(query_rows, key_rows, value_rows, seg_query, seg_keys, scaling):
    scores = global_scores(query_rows, key_rows, seg_query, seg_keys, scaling)
    top_score = jnp.max(scores, axis=-1, keepdims=True)
    weights = jnp.exp(scores - top_score)
    totals = jnp.sum(weights, axis=-1, keepdims=True)
    shares = (weights / totals).astype(jnp.bfloat16)
    attended = jnp.einsum("hqk,hkd->hqd", shares, value_rows, preferred_element_type=jnp.float32)
    return (attended, (top_score + jnp.log(totals))[..., 0])


def global_backward(
    query_rows, key_rows, value_rows, seg_query, seg_keys, grad_rows, log_total, scaling
):
    scores = global_scores(query_rows, key_rows, seg_query, seg_keys, scaling)
    shares = jnp.exp(scores - log_total[..., None])
    share_low = shares.astype(jnp.bfloat16)
    grad_shares = jnp.einsum(
        "hqd,hkd->hqk", grad_rows, value_rows, preferred_element_type=jnp.float32
    )
    centre = jnp.sum(shares * grad_shares, axis=-1, keepdims=True)
    grad_scores = (shares * (grad_shares - centre)).astype(jnp.bfloat16)
    grad_query = (
        jnp.einsum("hqk,hkd->hqd", grad_scores, key_rows, preferred_element_type=jnp.float32)
        * scaling
    )
    grad_keys = (
        jnp.einsum("hqk,hqd->hkd", grad_scores, query_rows, preferred_element_type=jnp.float32)
        * scaling
    )
    grad_values = jnp.einsum(
        "hqk,hqd->hkd", share_low, grad_rows, preferred_element_type=jnp.float32
    )
    return (grad_query, grad_keys, grad_values, centre[..., 0])


def general_body(
    inputs,
    segments,
    random_key_blocks,
    adapter_index_table,
    frozen_query_key_value_weight,
    frozen_output_weight,
    frozen_up_weight,
    frozen_down_weight,
    attention_norm_gain,
    feedforward_norm_gain,
    adapter_down_from_width,
    adapter_down_from_hidden,
    adapter_up_to_width,
    adapter_up_to_hidden,
    cotangent,
):
    seq_count = inputs.shape[0]
    local_tokens = inputs.shape[1]
    width = inputs.shape[2]
    shard_count = lax.axis_size("shard")
    full_length = local_tokens * shard_count
    total_blocks = full_length // BLOCK
    local_blocks = local_tokens // BLOCK
    cand_count = 3 + GLOBALS + RANDOMS
    glob_rows = GLOBALS * BLOCK
    scaling = HD ** (-0.5)

    def select_adapter_table(table, table_column):
        return jnp.take(table, adapter_index_table[:, table_column], axis=0)

    adapter_tables_input = [
        select_adapter_table(adapter_down_from_width[table_column], table_column)
        for table_column in range(5)
    ] + [select_adapter_table(adapter_down_from_hidden, 5)]
    adapter_tables_output = [
        select_adapter_table(adapter_up_to_width[table_column], table_column)
        for table_column in range(4)
    ]
    adapter_tables_output = adapter_tables_output + [
        select_adapter_table(adapter_up_to_hidden, 4),
        select_adapter_table(adapter_up_to_width[4], 5),
    ]
    qkv_full, out_full = (
        lax.all_gather(frozen_query_key_value_weight, "shard", axis=0, tiled=True),
        lax.all_gather(frozen_output_weight, "shard", axis=0, tiled=True),
    )
    main_part = dense_forward(inputs, qkv_full)
    rank_parts = []
    projected = []
    for table_column in range(3):
        rank_part, extra = adapt(
            inputs, adapter_tables_input[table_column], adapter_tables_output[table_column]
        )
        rank_parts.append(rank_part)
        projected.append(
            (main_part[..., table_column * width : (table_column + 1) * width] + extra).astype(
                jnp.bfloat16
            )
        )
    seg_low = segments.astype(jnp.bfloat16)
    key_all, value_all, seg_all = (
        lax.all_gather(projected[1], "shard", axis=1, tiled=True),
        lax.all_gather(projected[2], "shard", axis=1, tiled=True),
        lax.all_gather(seg_low, "shard", axis=1, tiled=True),
    )
    shard_pos = lax.axis_index("shard")
    is_first = shard_pos == 0
    first_block = shard_pos * local_blocks
    block_ids = first_block + jnp.arange(local_blocks, dtype=jnp.int32)
    rand_local = lax.dynamic_slice_in_dim(random_key_blocks, first_block, local_blocks, axis=1)
    window_part = jnp.stack([block_ids - 1, block_ids, block_ids + 1], axis=-1)
    global_ids = jnp.broadcast_to(
        jnp.arange(GLOBALS, dtype=jnp.int32)[None, :], (local_blocks, GLOBALS)
    )
    fixed_part = jnp.concatenate([window_part, global_ids], axis=-1)
    candidates = jnp.concatenate(
        [jnp.broadcast_to(fixed_part[None], (H, local_blocks, 3 + GLOBALS)), rand_local], axis=-1
    )
    candidates = jnp.clip(candidates, 0, total_blocks - 1)
    always_true = jnp.ones((local_blocks,), dtype=bool)
    fixed_valid = jnp.stack(
        [block_ids - 1 >= GLOBALS, always_true, block_ids + 1 < total_blocks]
        + [always_true] * GLOBALS,
        axis=-1,
    )
    valid = jnp.concatenate(
        [
            jnp.broadcast_to(fixed_valid[None], (H, local_blocks, 3 + GLOBALS)),
            jnp.ones((H, local_blocks, RANDOMS), dtype=bool),
        ],
        axis=-1,
    )
    valid_keys = jnp.repeat(valid, BLOCK, axis=-1)
    query_heads = (
        projected[0].reshape(seq_count, local_blocks, BLOCK, H, HD).transpose(0, 3, 1, 2, 4)
    )
    key_source = key_all.reshape(seq_count, total_blocks, BLOCK, H, HD).transpose(0, 3, 1, 2, 4)
    value_source = value_all.reshape(seq_count, total_blocks, BLOCK, H, HD).transpose(0, 3, 1, 2, 4)
    head_index = jnp.arange(H, dtype=jnp.int32)[:, None, None]
    key_picked = key_source[:, head_index, candidates].reshape(
        seq_count, H, local_blocks, cand_count * BLOCK, HD
    )
    value_picked = value_source[:, head_index, candidates].reshape(
        seq_count, H, local_blocks, cand_count * BLOCK, HD
    )
    seg_picked = seg_all.reshape(seq_count, total_blocks, BLOCK)[:, candidates].reshape(
        seq_count, H, local_blocks, cand_count * BLOCK
    )
    seg_local = seg_low.reshape(seq_count, local_blocks, BLOCK)
    permit = valid_keys[None, :, :, None, :] & (
        seg_local[:, None, :, :, None] == seg_picked[:, :, :, None, :]
    )
    scores = sparse_scores(query_heads, key_picked, permit, scaling)
    top_score = jnp.max(scores, axis=-1, keepdims=True)
    weights = jnp.exp(scores - top_score)
    totals = jnp.sum(weights, axis=-1, keepdims=True)
    share_low = (weights / totals).astype(jnp.bfloat16)
    sparse_lse = (top_score + jnp.log(totals))[..., 0]
    sparse_out = jnp.einsum(
        "shbqk,shbkd->shbqd", share_low, value_picked, preferred_element_type=jnp.float32
    )
    key_heads = key_source.reshape(seq_count, H, full_length, HD)
    value_heads = value_source.reshape(seq_count, H, full_length, HD)
    glob_query = query_heads[:, :, :GLOBALS].reshape(seq_count, H, glob_rows, HD)
    glob_seg = seg_low[:, :glob_rows]

    def run_forward(operands):
        return lax.map(
            lambda packet: global_forward(
                packet[0], packet[1], packet[2], packet[3], packet[4], scaling
            ),
            operands,
        )

    def skip_forward(operands):
        return (
            jnp.zeros((seq_count, H, glob_rows, HD), jnp.float32),
            jnp.zeros((seq_count, H, glob_rows), jnp.float32),
        )

    global_out, global_lse = lax.cond(
        is_first, run_forward, skip_forward, (glob_query, key_heads, value_heads, glob_seg, seg_all)
    )
    glob_blocks = global_out.reshape(seq_count, H, GLOBALS, BLOCK, HD)
    head_out = jnp.concatenate(
        [jnp.where(is_first, glob_blocks, sparse_out[:, :, :GLOBALS]), sparse_out[:, :, GLOBALS:]],
        axis=2,
    )
    mixed_low = (
        head_out.transpose(0, 2, 3, 1, 4)
        .reshape(seq_count, local_tokens, width)
        .astype(jnp.bfloat16)
    )
    rank_out, extra_out = adapt(mixed_low, adapter_tables_input[3], adapter_tables_output[3])
    branch = dense_forward(mixed_low, out_full) + extra_out
    first, first_pull = jax.vjp(
        lambda hidden: norm_rows(hidden, attention_norm_gain), inputs.astype(jnp.float32) + branch
    )
    first_low = first.astype(jnp.bfloat16)
    up_full, down_full = (
        lax.all_gather(frozen_up_weight, "shard", axis=0, tiled=True),
        lax.all_gather(frozen_down_weight, "shard", axis=0, tiled=True),
    )
    rank_up, extra_up = adapt(first_low, adapter_tables_input[4], adapter_tables_output[4])
    lifted = dense_forward(first_low, up_full) + extra_up
    activated, gelu_pull = jax.vjp(gelu_exact, lifted)
    active_low = activated.astype(jnp.bfloat16)
    rank_down, extra_down = adapt(active_low, adapter_tables_input[5], adapter_tables_output[5])
    lowered = dense_forward(active_low, down_full) + extra_down
    result, final_pull = jax.vjp(
        lambda hidden: norm_rows(hidden, feedforward_norm_gain), first + lowered
    )
    layer_out = result.astype(jnp.bfloat16)
    up_back, down_back = (
        lax.all_gather(frozen_up_weight, "shard", axis=0, tiled=True),
        lax.all_gather(frozen_down_weight, "shard", axis=0, tiled=True),
    )
    grad_adapt_in = [None] * 6
    grad_adapt_out = [None] * 6
    (grad_sum,) = final_pull(cotangent.astype(jnp.float32))
    grad_lowered = grad_sum.astype(jnp.bfloat16)
    grad_adapt_in[5], grad_adapt_out[5], extra_grad = adapt_back(
        active_low, adapter_tables_input[5], adapter_tables_output[5], rank_down, grad_lowered
    )
    grad_active = dense_backward(grad_lowered, down_back) + extra_grad
    (grad_lifted,) = gelu_pull(grad_active)
    grad_lift_low = grad_lifted.astype(jnp.bfloat16)
    grad_adapt_in[4], grad_adapt_out[4], extra_grad = adapt_back(
        first_low, adapter_tables_input[4], adapter_tables_output[4], rank_up, grad_lift_low
    )
    grad_first = grad_sum + dense_backward(grad_lift_low, up_back) + extra_grad
    (grad_branch,) = first_pull(grad_first)
    grad_branch_low = grad_branch.astype(jnp.bfloat16)
    qkv_back, out_back = (
        lax.all_gather(frozen_query_key_value_weight, "shard", axis=0, tiled=True),
        lax.all_gather(frozen_output_weight, "shard", axis=0, tiled=True),
    )
    grad_adapt_in[3], grad_adapt_out[3], extra_grad = adapt_back(
        mixed_low, adapter_tables_input[3], adapter_tables_output[3], rank_out, grad_branch_low
    )
    grad_mixed = (dense_backward(grad_branch_low, out_back) + extra_grad).astype(jnp.bfloat16)
    grad_heads = grad_mixed.reshape(seq_count, local_blocks, BLOCK, H, HD).transpose(0, 3, 1, 2, 4)
    row_keep = (block_ids >= GLOBALS)[None, None, :, None, None]
    grad_sparse = jnp.where(row_keep, grad_heads, jnp.zeros_like(grad_heads))
    scores = sparse_scores(query_heads, key_picked, permit, scaling)
    shares = jnp.exp(scores - sparse_lse[..., None])
    share_low = shares.astype(jnp.bfloat16)
    grad_shares = jnp.einsum(
        "shbqd,shbkd->shbqk", grad_sparse, value_picked, preferred_element_type=jnp.float32
    )
    centre = jnp.sum(shares * grad_shares, axis=-1, keepdims=True)
    grad_scores = (shares * (grad_shares - centre)).astype(jnp.bfloat16)
    grad_query = (
        jnp.einsum(
            "shbqk,shbkd->shbqd", grad_scores, key_picked, preferred_element_type=jnp.float32
        )
        * scaling
    )
    glob_grad = grad_heads[:, :, :GLOBALS].reshape(seq_count, H, glob_rows, HD)

    def run_backward(operands):
        return lax.map(
            lambda packet: global_backward(
                packet[0], packet[1], packet[2], packet[3], packet[4], packet[5], packet[6], scaling
            ),
            operands,
        )

    def skip_backward(operands):
        return (
            jnp.zeros((seq_count, H, glob_rows, HD), jnp.float32),
            jnp.zeros((seq_count, H, full_length, HD), jnp.float32),
            jnp.zeros((seq_count, H, full_length, HD), jnp.float32),
            jnp.zeros((seq_count, H, glob_rows), jnp.float32),
        )

    glob_dq, glob_dk, glob_dv, glob_centre = lax.cond(
        is_first,
        run_backward,
        skip_backward,
        (glob_query, key_heads, value_heads, glob_seg, seg_all, glob_grad, global_lse),
    )
    grad_query = grad_query.at[:, :, :GLOBALS].add(
        glob_dq.reshape(seq_count, H, GLOBALS, BLOCK, HD)
    )
    grad_key_picked = (
        jnp.einsum(
            "shbqk,shbqd->shbkd", grad_scores, query_heads, preferred_element_type=jnp.float32
        )
        * scaling
    )
    grad_value_picked = jnp.einsum(
        "shbqk,shbqd->shbkd", share_low, grad_sparse, preferred_element_type=jnp.float32
    )
    block_shape = (seq_count, H, local_blocks, cand_count, BLOCK, HD)
    key_grad_blocks = (
        jnp.zeros((seq_count, H, total_blocks, BLOCK, HD), jnp.float32)
        .at[:, head_index, candidates]
        .add(grad_key_picked.reshape(block_shape))
    )
    value_grad_blocks = (
        jnp.zeros((seq_count, H, total_blocks, BLOCK, HD), jnp.float32)
        .at[:, head_index, candidates]
        .add(grad_value_picked.reshape(block_shape))
    )
    key_grad_full = (
        (key_grad_blocks.reshape(seq_count, H, full_length, HD) + glob_dk)
        .transpose(0, 2, 1, 3)
        .reshape(seq_count, full_length, width)
    )
    value_grad_full = (
        (value_grad_blocks.reshape(seq_count, H, full_length, HD) + glob_dv)
        .transpose(0, 2, 1, 3)
        .reshape(seq_count, full_length, width)
    )
    key_grad, value_grad = (
        lax.psum_scatter(
            key_grad_full.astype(jnp.bfloat16), "shard", scatter_dimension=1, tiled=True
        ).astype(jnp.float32),
        lax.psum_scatter(
            value_grad_full.astype(jnp.bfloat16), "shard", scatter_dimension=1, tiled=True
        ).astype(jnp.float32),
    )
    query_grad = grad_query.transpose(0, 2, 3, 1, 4).reshape(seq_count, local_tokens, width)
    grad_proj = [
        query_grad.astype(jnp.bfloat16),
        key_grad.astype(jnp.bfloat16),
        value_grad.astype(jnp.bfloat16),
    ]
    input_grad = grad_branch + dense_backward(jnp.concatenate(grad_proj, axis=-1), qkv_back)
    for table_column in range(3):
        grad_adapt_in[table_column], grad_adapt_out[table_column], extra_grad = adapt_back(
            inputs,
            adapter_tables_input[table_column],
            adapter_tables_output[table_column],
            rank_parts[table_column],
            grad_proj[table_column],
        )
        input_grad = input_grad + extra_grad
    adapter_table_count = adapter_down_from_width.shape[1]
    grad_in_d = jnp.stack(
        [
            table_sum(
                grad_adapt_in[table_column],
                adapter_index_table[:, table_column],
                adapter_table_count,
            )
            for table_column in range(5)
        ],
        axis=0,
    )
    grad_in_f = table_sum(grad_adapt_in[5], adapter_index_table[:, 5], adapter_table_count)
    out_list = [
        table_sum(
            grad_adapt_out[table_column], adapter_index_table[:, table_column], adapter_table_count
        )
        for table_column in range(4)
    ]
    grad_out_d = jnp.stack(
        out_list + [table_sum(grad_adapt_out[5], adapter_index_table[:, 5], adapter_table_count)],
        axis=0,
    )
    grad_out_f = table_sum(grad_adapt_out[4], adapter_index_table[:, 4], adapter_table_count)
    owned = (
        lax.psum_scatter(
            grad_in_d.astype(jnp.bfloat16), "shard", scatter_dimension=3, tiled=True
        ).astype(jnp.float32),
        lax.psum_scatter(
            grad_in_f.astype(jnp.bfloat16), "shard", scatter_dimension=2, tiled=True
        ).astype(jnp.float32),
        lax.psum_scatter(
            grad_out_d.astype(jnp.bfloat16), "shard", scatter_dimension=3, tiled=True
        ).astype(jnp.float32),
        lax.psum_scatter(
            grad_out_f.astype(jnp.bfloat16), "shard", scatter_dimension=2, tiled=True
        ).astype(jnp.float32),
    )
    summed = (
        lax.psum(owned[0].astype(jnp.bfloat16), "dp").astype(jnp.float32),
        lax.psum(owned[1].astype(jnp.bfloat16), "dp").astype(jnp.float32),
        lax.psum(owned[2].astype(jnp.bfloat16), "dp").astype(jnp.float32),
        lax.psum(owned[3].astype(jnp.bfloat16), "dp").astype(jnp.float32),
    )
    return (layer_out, input_grad, summed[0], summed[1], summed[2], summed[3])


BF = jnp.bfloat16
F32 = jnp.float32
NT = (((1,), (1,)), ((), ()))
TN = (((0,), (0,)), ((), ()))
BIG = 1e30
RANK = 16
ANY = pl.ANY
VMEM = pltpu.VMEM
MEBI = 1024 * 1024
SMALL_COST = pl.CostEstimate(flops=1_000_000, bytes_accessed=100_000, transcendentals=0)


def mm(left, right):
    return jnp.dot(left, right, preferred_element_type=F32)


def mm_nt(left, right):
    return lax.dot_general(left, right, NT, preferred_element_type=F32)


def mm_tn(left, right):
    return lax.dot_general(left, right, TN, preferred_element_type=F32)


def whole(shape):
    return pl.BlockSpec(shape, lambda *_: (0,) * len(shape))


def away_pairs(dp_count, shard_count, step):
    pairs = []
    for chip in range(dp_count // 2):
        for k in range(2):
            for z in range(shard_count):
                m = (z & 1) ^ step
                source = (2 * chip + k) * shard_count + z
                target = (2 * chip + (z >> 1)) * shard_count + 2 * k + m
                pairs.append((source, target))
    return pairs


def swap_cores(value, dp_count):
    return lax.ppermute(value, "dp", [(i, i ^ 1) for i in range(dp_count)])


def swap_shards(value, shard_count, step):
    return lax.ppermute(value, "shard", [(i, i ^ step) for i in range(shard_count)])


def spread_over_chips(block, dp_count):
    others = [lax.ppermute(block, "dp", [(i, i ^ o) for i in range(dp_count)]) for o in range(2, dp_count, 2)]
    return [block] + others


def swap_chips(block, dp_count, offset):
    return lax.ppermute(block, "dp", [(i, i ^ offset) for i in range(dp_count)])


def spread_over_cores(blocks, dp_count):
    return [one for block in blocks for one in (block, swap_cores(block, dp_count))]


def spread_in_plane(block, dp_count):
    return spread_over_cores(spread_over_chips(block, dp_count), dp_count)


def join_kernel(meta, part0, part1, out_ref):
    for r, part in enumerate((part0, part1)):
        out_ref[(meta[0] & 1) ^ r] = part[...].astype(out_ref.dtype)


def join_parts(meta, parts, dtype):
    rows, width = parts[0].shape
    return pl.pallas_call(
        join_kernel,
        grid_spec=pltpu.PrefetchScalarGridSpec(
            num_scalar_prefetch=1,
            grid=(1,),
            in_specs=[whole((rows, width))] * 2,
            out_specs=whole((2, rows, width)),
        ),
        out_shape=jax.ShapeDtypeStruct((2, rows, width), dtype),
        compiler_params=pltpu.CompilerParams(vmem_limit_bytes=30 * MEBI),
        cost_estimate=SMALL_COST,
        name="join_parts",
    )(meta, *parts)


def send_away(parts, dp_count, shard_count):
    return [
        lax.ppermute(part, ("dp", "shard"), away_pairs(dp_count, shard_count, r))
        for r, part in enumerate(parts)
    ]


def weight_copies(meta, own_ref, pieces, dest, sems, places):
    z, d = meta[0], meta[1]
    own_rows, columns = own_ref.shape
    copies = [
        pltpu.make_async_copy(
            own_ref, dest.at[pl.ds(pl.multiple_of(z * own_rows, 16), own_rows)], sems.at[0]
        )
    ]
    count = 1
    for o, parts in enumerate(pieces):
        who = d ^ o
        for step in range(3):
            shard = z ^ (step + 1)
            for start, row, column, rows, cols in places(who):
                for piece, first in parts:
                    low, high = max(start, first), min(start + rows, first + piece.shape[1])
                    if low >= high:
                        continue
                    copies.append(
                        pltpu.make_async_copy(
                            piece.at[step, pl.ds(low - first, high - low)],
                            dest.at[
                                pl.ds(pl.multiple_of(shard * own_rows + row + low - start, 16), high - low),
                                pl.ds(pl.multiple_of(column, 128), cols),
                            ],
                            sems.at[count],
                        )
                    )
                    count += 1
    return copies


def one_each(refs):
    return [[(ref, 0)] for ref in refs]


UP_SPLIT = 128


def up_parts(refs):
    return one_each(refs[0:6]) + [[(refs[6], 0), (refs[7], UP_SPLIT)], [(refs[8], 0), (refs[9], UP_SPLIT)]]


def qkv_places(who):
    return [(0, (who >> 1) * 48, (who & 1) * 1152, 48, 1152)]


def out_places(who):
    return [(0, (who >> 1) * 48, (who & 1) * 384, 48, 384)]


def up_places(who):
    return [(48, 0, who * 384, 192, 384)]


def down_places(who):
    return [(0, who * 96, 0, 96, 384), (96, who * 96, 384, 96, 384)]


def token_copies(meta, messages, dest, sems):
    copies = []
    for at, message in enumerate(messages):
        row = 512 * (at >> 1) + 256 * ((meta[0] & 1) ^ (at & 1))
        copies.append(
            pltpu.make_async_copy(
                message.at[pl.ds(0, 256)], dest.at[pl.ds(pl.multiple_of(row, 256), 256)], sems.at[at]
            )
        )
    return copies


def zero_padded(rows, position, count):
    zeros = jnp.zeros_like(rows)
    return jnp.concatenate([rows if i == position else zeros for i in range(count)], axis=0)


def qkv_kernel(meta, ids, *refs):
    messages, w_own, pieces = refs[0:4], refs[4], one_each(refs[5:13])
    ins, outs = refs[13:16], refs[16:19]
    q_ref, k_ref, v_ref, mask_ref, hot_ref, own_ref = refs[19:25]
    xs, segs, weight, wsems, xsems, ssems = refs[25:]
    copies = token_copies(meta, messages, xs, xsems)
    for at, message in enumerate(messages):
        copies.append(
            pltpu.make_async_copy(
                message.at[pl.ds(256, 16), pl.ds(0, 256)],
                segs.at[2 * (at >> 1) + ((meta[0] & 1) ^ (at & 1))],
                ssems.at[at],
            )
        )
    copies += weight_copies(meta, w_own, pieces, weight, wsems, qkv_places)
    for copy in copies:
        copy.start()
    for copy in copies:
        copy.wait()
    lane = lax.broadcasted_iota(jnp.int32, (128, 128), 1)
    lane_of_head = lax.rem(lane, 64)
    as_float = lane_of_head.astype(F32)
    is_segment = lane_of_head < 16
    row_block = lax.broadcasted_iota(jnp.int32, (128, 128), 0) // 64
    for place in range(4):
        row = segs[place].astype(F32)[0:1]
        for half in range(2):
            column = jnp.broadcast_to(row[:, 128 * half : 128 * half + 128], (128, 128)).T
            same = column == as_float
            block_lane = lane_of_head == 16 + 4 * place + 2 * half + row_block
            rows = slice(256 * place + 128 * half, 256 * place + 128 * half + 128)
            mask_ref[rows] = jnp.where(
                is_segment, jnp.where(same, 0.0, -BIG), jnp.where(block_lane, 1.0, 0.0)
            ).astype(BF)
            if place < 2:
                hot_ref[rows] = jnp.where(is_segment & same, 1.0, 0.0).astype(BF)
    own_ref[...] = xs[0:512]
    in_all = jnp.concatenate([ref[0, 0] for ref in ins], axis=0)
    out_all = [zero_padded(ref[0, 0], p, 3) for p, ref in enumerate(outs)]
    targets = (q_ref, k_ref, v_ref)
    for tile in range(4):
        rows = slice(256 * tile, 256 * tile + 256)
        x = xs[rows]
        rank = mm_nt(x, in_all).astype(BF)
        for p in range(0 if tile < 2 else 1, 3):
            value = mm(x, weight[:, 768 * p : 768 * p + 768]) + mm(rank, out_all[p])
            value = value.astype(BF)
            if p == 0:
                value = (value.astype(F32) * HD**-0.5).astype(BF)
            targets[p][rows] = value


def table_spec(p, column, width):
    return pl.BlockSpec((1, 1, RANK, width), lambda i, meta, ids: (p, ids[column], 0, 0))


def hidden_spec(column, width):
    return pl.BlockSpec((1, RANK, width), lambda i, meta, ids: (ids[column], 0, 0))


def any_specs(count):
    return [pl.BlockSpec(memory_space=ANY)] * count


def project_qkv(meta, ids, messages, w_own, pieces, table_in, table_out):
    width = w_own.shape[1] // 3
    return pl.pallas_call(
        qkv_kernel,
        grid_spec=pltpu.PrefetchScalarGridSpec(
            num_scalar_prefetch=2,
            grid=(1,),
            in_specs=any_specs(13)
            + [table_spec(p, p, width) for p in range(3)]
            + [table_spec(p, p, width) for p in range(3)],
            out_specs=[
                whole((512, width)),
                whole((1024, width)),
                whole((1024, width)),
                whole((1024, 128)),
                whole((512, 128)),
                whole((512, width)),
            ],
            scratch_shapes=[
                VMEM((1024, width), BF),
                VMEM((4, 16, 256), BF),
                VMEM((width, 3 * width), BF),
                pltpu.SemaphoreType.DMA((25,)),
                pltpu.SemaphoreType.DMA((4,)),
                pltpu.SemaphoreType.DMA((4,)),
            ],
        ),
        out_shape=[
            jax.ShapeDtypeStruct((512, width), BF),
            jax.ShapeDtypeStruct((1024, width), BF),
            jax.ShapeDtypeStruct((1024, width), BF),
            jax.ShapeDtypeStruct((1024, 128), BF),
            jax.ShapeDtypeStruct((512, 128), BF),
            jax.ShapeDtypeStruct((512, width), BF),
        ],
        compiler_params=pltpu.CompilerParams(vmem_limit_bytes=48 * MEBI),
        cost_estimate=SMALL_COST,
        name="project_qkv",
    )(meta, ids, *messages, w_own, *pieces, *([table_in] * 3), *([table_out] * 3))


def attend_kernel(q_ref, k_ref, v_ref, mask_ref, hot_ref, closed_ref, o_ref, p_ref):
    low = lax.broadcasted_iota(jnp.int32, (512, 128), 1) < 64
    low_keys = lax.broadcasted_iota(jnp.int32, (1024, 128), 1) < 64
    closed = jnp.concatenate(
        [jnp.broadcast_to(closed_ref[0, l : l + 1], (64, 128)) for l in range(8)], axis=0
    )
    extra = (hot_ref[...].astype(F32) + closed).astype(BF)
    q, k, v, masks = q_ref[...], k_ref[...], v_ref[...], mask_ref[...]
    wide = [(jnp.where(low, q, extra), jnp.where(low_keys, k, masks)), (jnp.where(low, extra, q), jnp.where(low_keys, masks, k))]
    size = 512
    units = [(start, head) for start in range(0, 512, size) for head in range(2)]
    raw = lambda unit: mm_nt(wide[unit[1]][0][unit[0] : unit[0] + size], wide[unit[1]][1])
    ahead = raw(units[0])
    mixed = {}
    for n, (start, head) in enumerate(units):
        scores = ahead
        if n + 1 < len(units):
            ahead = raw(units[n + 1])
        weights = jnp.exp(scores - jnp.max(scores, axis=1, keepdims=True))
        shares = (weights * (1.0 / jnp.sum(weights, axis=1, keepdims=True))).astype(BF)
        p_ref[head, start : start + size] = shares
        mixed[head] = mm(shares, v)
        if head == 1:
            o_ref[start : start + size] = jnp.where(low[0:size], mixed[0], mixed[1]).astype(BF)


def attend_more_kernel(q_ref, k_ref, v_ref, mask_ref, hot_ref, closed_ref, mixed, shares, o_ref, p_ref):
    del mixed, shares
    attend_kernel(q_ref, k_ref, v_ref, mask_ref, hot_ref, closed_ref, o_ref, p_ref)


def attend(first, pairs, q, k, v, masks, hot, closed, *before):
    width = q.shape[1]
    half = pl.BlockSpec((512, 128), lambda g: (0, g + first))
    full = pl.BlockSpec((1024, 128), lambda g: (0, g + first))
    return pl.pallas_call(
        attend_more_kernel if before else attend_kernel,
        grid=(pairs,),
        in_specs=[
            half,
            full,
            full,
            whole((1024, 128)),
            whole((512, 128)),
            pl.BlockSpec((1, 8, 128), lambda g: (g + first, 0, 0)),
        ]
        + any_specs(len(before)),
        out_specs=[half, pl.BlockSpec((2, 512, 1024), lambda g: (g + first, 0, 0))],
        out_shape=[
            jax.ShapeDtypeStruct((512, width), BF),
            jax.ShapeDtypeStruct((width // 64, 512, 1024), BF),
        ],
        input_output_aliases={6 + n: n for n in range(len(before))},
        compiler_params=pltpu.CompilerParams(vmem_limit_bytes=56 * MEBI),
        cost_estimate=SMALL_COST,
        name="attend",
    )(q, k, v, masks, hot, closed, *before)


def attend_back_kernel(q_ref, k_ref, v_ref, p_ref, grad_ref, mixed_ref, dq_ref, dk_own, dv_own, other_ref):
    low = lax.broadcasted_iota(jnp.int32, (512, 128), 1) < 64
    q, k, v, grad = q_ref[...], k_ref[...], v_ref[...], grad_ref[...]
    products = grad.astype(F32) * mixed_ref[...].astype(F32)
    q_turned, grad_turned = q.T, grad.T
    zeros, none = jnp.zeros_like(grad), jnp.zeros_like(products)
    dq, dk, dv = [], [], []
    for head in range(2):
        mine = low if head == 0 else jnp.logical_not(low)
        centre = jnp.sum(jnp.where(mine, products, none), axis=1, keepdims=True)
        grad_shares = mm_nt(jnp.where(mine, grad, zeros), v)
        shares = p_ref[head]
        grad_scores = (shares.astype(F32) * (grad_shares - centre)).astype(BF)
        rows = slice(64 * head, 64 * head + 64)
        dq.append(mm(grad_scores, k))
        dk.append(mm(q_turned[rows], grad_scores))
        dv.append(mm(grad_turned[rows], shares))
    dq_ref[...] = (jnp.where(low, dq[0], dq[1]) * HD**-0.5).astype(BF)
    dk = jnp.concatenate(dk, axis=0).T
    dv = jnp.concatenate(dv, axis=0).T
    dk_own[...] = dk[0:512].astype(BF)
    dv_own[...] = dv[0:512].astype(BF)
    other_ref[0] = dk[512:1024].astype(BF)
    other_ref[1] = dv[512:1024].astype(BF)


def attend_back(q, k, v, shares, grad, mixed):
    width = q.shape[1]
    half = pl.BlockSpec((512, 128), lambda g: (0, g))
    full = pl.BlockSpec((1024, 128), lambda g: (0, g))
    return pl.pallas_call(
        attend_back_kernel,
        grid=(width // 128,),
        in_specs=[half, full, full, pl.BlockSpec((2, 512, 1024), lambda g: (g, 0, 0)), half, half],
        out_specs=[half] * 3 + [pl.BlockSpec((2, 512, 128), lambda g: (0, 0, g))],
        out_shape=[
            jax.ShapeDtypeStruct((512, width), BF),
            jax.ShapeDtypeStruct((512, width), BF),
            jax.ShapeDtypeStruct((512, width), BF),
            jax.ShapeDtypeStruct((2, 512, width), BF),
        ],
        compiler_params=pltpu.CompilerParams(vmem_limit_bytes=40 * MEBI),
        cost_estimate=SMALL_COST,
        name="attend_back",
    )(q, k, v, shares, grad, mixed)


def gelu_and_slope(lifted):
    size = jnp.abs(lifted)
    t = 1.0 / (1.0 + 0.23164189 * size)
    poly = t * (
        0.127414796 + t * (-0.142248368 + t * (0.7107068705 + t * (-0.7265760135 + t * 0.5307027145)))
    )
    decay = jnp.exp2(lifted * lifted * -0.7213475204444817)
    tail = poly * decay
    below = jnp.where(lifted < 0.0, tail, 1.0 - tail)
    return jnp.maximum(lifted, 0.0) - size * tail, below + lifted * (decay * 0.3989422804014327)


def norm_parts(hidden):
    average = jnp.mean(hidden, axis=-1, keepdims=True)
    centred = hidden - average
    spread = jnp.mean(centred * centred, axis=-1, keepdims=True)
    inverse = lax.rsqrt(spread + EPSILON)
    return centred * inverse, inverse


def norm_back(grad, gain, normal, inverse):
    scaled = grad * gain
    return inverse * (
        scaled
        - jnp.mean(scaled, axis=-1, keepdims=True)
        - normal * jnp.mean(scaled * normal, axis=-1, keepdims=True)
    )


MID_TILE = 256
MID_PARTS = 4


def first_half_kernel(meta, ids, *refs):
    out_own, up_own, up_pieces = refs[0], refs[1], up_parts(refs[2:12])
    x_ref, mixed_ref, gain1, in3, in4, out3, out4 = refs[12:19]
    normal_ref, inverse_ref, active, slope = refs[19:23]
    w_out, w_up, osems, usems = refs[23:]
    out_copies = weight_copies(meta, out_own, up_pieces, w_out, osems, out_places)
    up_copies = weight_copies(meta, up_own, up_pieces, w_up, usems, up_places)
    is_first = pl.program_id(0) == 0

    @pl.when(is_first)
    def _():
        for copy in out_copies + up_copies:
            copy.start()
        for copy in out_copies:
            copy.wait()

    mixed = mixed_ref[...]
    rank3 = mm_nt(mixed, in3[0, 0]).astype(BF)
    branch = mm(mixed, w_out[...]) + mm(rank3, out3[0, 0])
    normal, inverse = norm_parts(x_ref[...].astype(F32) + branch)
    normal_ref[...] = normal
    inverse_ref[...] = jnp.broadcast_to(inverse, inverse_ref.shape)
    low = (normal * gain1[...][None]).astype(BF)
    rank4 = mm_nt(low, in4[0, 0]).astype(BF)

    @pl.when(is_first)
    def _():
        for copy in up_copies:
            copy.wait()

    part = w_up.shape[1] // MID_PARTS
    columns = [slice(n * part, n * part + part) for n in range(MID_PARTS)]
    lift = lambda cols: mm(low, w_up[:, cols]) + mm(rank4, out4[0, :, cols])
    ahead = lift(columns[0])
    for n, cols in enumerate(columns):
        lifted = ahead
        if n + 1 < MID_PARTS:
            ahead = lift(columns[n + 1])
        value, tangent = gelu_and_slope(lifted)
        active[:, cols] = value.astype(BF)
        slope[:, cols] = tangent.astype(BF)


def first_half(meta, ids, out_own, up_own, up_pieces, x, mixed, gain1, table_in, table_out, table_out_hidden):
    width, hidden = x.shape[1], up_own.shape[1]
    tile = lambda columns: pl.BlockSpec((MID_TILE, columns), lambda i, *_: (i, 0))
    return pl.pallas_call(
        first_half_kernel,
        grid_spec=pltpu.PrefetchScalarGridSpec(
            num_scalar_prefetch=2,
            grid=(512 // MID_TILE,),
            in_specs=any_specs(12)
            + [
                tile(width),
                tile(width),
                whole((width,)),
                table_spec(3, 3, width),
                table_spec(4, 4, width),
                table_spec(3, 3, width),
                hidden_spec(4, hidden),
            ],
            out_specs=[tile(width), tile(128), tile(hidden), tile(hidden)],
            scratch_shapes=[
                VMEM((width, width), BF),
                VMEM((width, hidden), BF),
                pltpu.SemaphoreType.DMA((25,)),
                pltpu.SemaphoreType.DMA((31,)),
            ],
        ),
        out_shape=[
            jax.ShapeDtypeStruct((512, width), F32),
            jax.ShapeDtypeStruct((512, 128), F32),
            jax.ShapeDtypeStruct((512, hidden), BF),
            jax.ShapeDtypeStruct((512, hidden), BF),
        ],
        compiler_params=pltpu.CompilerParams(vmem_limit_bytes=44 * MEBI),
        cost_estimate=SMALL_COST,
        name="first_half",
    )(meta, ids, out_own, up_own, *up_pieces, x, mixed, gain1, table_in, table_in, table_out, table_out_hidden)


def write_halves(meta, gathered, groups, own_half, other_half):
    core = meta[1] & 1
    for r in range(4):
        for half, ref in enumerate((own_half, other_half)):
            rows = [
                gathered[meta[0] ^ r, pl.ds(pl.multiple_of(16 * group + 8 * (core ^ half), 8), 8), :]
                for group in range(groups)
            ]
            ref[r] = jnp.concatenate(rows, axis=0).astype(ref.dtype)


def second_half_kernel(meta, ids, *refs):
    cots, out_own, up_own, down_own = refs[0:2], refs[2], refs[3], refs[4]
    up_pieces, down_pieces = up_parts(refs[5:15]), one_each(refs[15:23])
    normal_ref, inverse_ref, active, slope, mixed_ref = refs[23:28]
    gain1, gain2, in3, in4, in5, out3, out4, out5 = refs[28:36]
    layer_parts, grad_branch_ref, grad_mixed_ref, own_half, other_half = refs[36:38], refs[38], refs[39], refs[40], refs[41]
    (
        cot, w_out, w_up, w_down, layer,
        s_in3, s_in4, s_in5, s_out3, s_out4, s_out5, gathered,
        osems, usems, dsems, xsems,
    ) = refs[42:]
    tile = pl.program_id(0)
    is_first = tile == 0
    near = token_copies(meta, cots, cot, xsems)
    out_copies = weight_copies(meta, out_own, up_pieces, w_out, osems, out_places)
    up_copies = weight_copies(meta, up_own, up_pieces, w_up, usems, up_places)
    down_copies = weight_copies(meta, down_own, down_pieces, w_down, dsems, down_places)

    @pl.when(is_first)
    def _():
        for copy in down_copies + near + up_copies + out_copies:
            copy.start()
        for ref in (s_in3, s_in4, s_in5, s_out3, s_out4, s_out5):
            ref[...] = jnp.zeros_like(ref)
        for copy in down_copies + near:
            copy.wait()

    part = w_up.shape[1] // MID_PARTS
    a_in3, a_in4, a_out3, a_out5 = in3[0, 0], in4[0, 0], out3[0, 0], out5[0, 0]
    rows = pl.ds(pl.multiple_of(tile * MID_TILE, MID_TILE), MID_TILE)
    normal1 = normal_ref[...]
    inverse1 = inverse_ref[:, 0:1]
    first = normal1 * gain1[...][None]
    low1 = first.astype(BF)
    r4 = mm_nt(low1, a_in4).astype(BF)
    r5 = mm_nt(active[...], in5[0]).astype(BF)
    lowered = first + mm(active[...], w_down[...]) + mm(r5, a_out5)
    normal2, inverse2 = norm_parts(lowered)
    layer[rows, :] = (normal2 * gain2[...][None]).astype(BF)
    grad_sum = norm_back(cot[rows, :].astype(F32), gain2[...][None], normal2, inverse2)
    e5 = grad_sum.astype(BF)
    rg5 = mm_nt(e5, a_out5).astype(BF)
    s_out5[...] += mm_tn(r5, e5)

    @pl.when(is_first)
    def _():
        for copy in up_copies + out_copies:
            copy.wait()

    grad_first = grad_sum
    rg4 = jnp.zeros((MID_TILE, RANK), F32)
    for n in range(MID_PARTS):
        cols = slice(n * part, n * part + part)
        grad_active = mm_nt(e5, w_down[cols, :]) + mm(rg5, in5[0, :, cols])
        e4 = (slope[:, cols].astype(F32) * grad_active).astype(BF)
        s_in5[:, cols] += mm_tn(rg5, active[:, cols])
        s_out4[:, cols] += mm_tn(r4, e4)
        grad_first = grad_first + mm_nt(e4, w_up[:, cols])
        rg4 = rg4 + mm_nt(e4, out4[0, :, cols])
    rg4 = rg4.astype(BF)
    s_in4[...] += mm_tn(rg4, low1)
    grad_first = grad_first + mm(rg4, a_in4)
    grad_branch = norm_back(grad_first, gain1[...][None], normal1, inverse1)
    grad_branch_ref[...] = grad_branch
    e3 = grad_branch.astype(BF)
    mixed = mixed_ref[...]
    rank3 = mm_nt(mixed, a_in3).astype(BF)
    rg3 = mm_nt(e3, a_out3).astype(BF)
    s_out3[...] += mm_tn(rank3, e3)
    s_in3[...] += mm_tn(rg3, mixed)
    grad_mixed_ref[...] = (mm_nt(e3, w_out[...]) + mm(rg3, a_in3)).astype(BF)

    @pl.when(tile == 512 // MID_TILE - 1)
    def _():
        wide, narrow = 768, 192
        for owner in range(4):
            start = 0
            for ref, size in (
                (s_in5, wide), (s_out4, wide), (s_in3, narrow), (s_in4, narrow), (s_out3, narrow), (s_out5, narrow),
            ):
                row, column = 16 * (start // 768), start % 768
                gathered[owner, row : row + 16, column : column + size] = ref[:, owner * size : owner * size + size]
                start += size
        for r, ref in enumerate(layer_parts):
            ref[...] = layer[pl.ds(pl.multiple_of(256 * ((meta[0] & 1) ^ r), 256), 256), :]
        write_halves(meta, gathered, 3, own_half, other_half)


def second_half(meta, ids, cots, out_own, up_own, down_own, up_pieces, down_pieces, normal, inverse, active, slope,
                mixed, gain1, gain2, table_in, table_in_hidden, table_out, table_out_hidden):
    width, hidden = normal.shape[1], up_own.shape[1]
    tile = lambda columns: pl.BlockSpec((MID_TILE, columns), lambda i, *_: (i, 0))
    return pl.pallas_call(
        second_half_kernel,
        grid_spec=pltpu.PrefetchScalarGridSpec(
            num_scalar_prefetch=2,
            grid=(512 // MID_TILE,),
            in_specs=any_specs(23)
            + [
                tile(width),
                tile(128),
                tile(hidden),
                tile(hidden),
                tile(width),
                whole((width,)),
                whole((width,)),
                table_spec(3, 3, width),
                table_spec(4, 4, width),
                hidden_spec(5, hidden),
                table_spec(3, 3, width),
                hidden_spec(4, hidden),
                table_spec(4, 5, width),
            ],
            out_specs=[whole((256, width))] * 2 + [tile(width), tile(width)] + [whole((4, 24, width))] * 2,
            scratch_shapes=[
                VMEM((512, width), BF),
                VMEM((width, width), BF),
                VMEM((width, hidden), BF),
                VMEM((hidden, width), BF),
                VMEM((512, width), BF),
                VMEM((RANK, width), F32),
                VMEM((RANK, width), F32),
                VMEM((RANK, hidden), F32),
                VMEM((RANK, width), F32),
                VMEM((RANK, hidden), F32),
                VMEM((RANK, width), F32),
                VMEM((4, 3 * RANK, 768), F32),
                pltpu.SemaphoreType.DMA((25,)),
                pltpu.SemaphoreType.DMA((31,)),
                pltpu.SemaphoreType.DMA((49,)),
                pltpu.SemaphoreType.DMA((2,)),
            ],
        ),
        out_shape=[jax.ShapeDtypeStruct((256, width), BF)] * 2
        + [jax.ShapeDtypeStruct((512, width), F32), jax.ShapeDtypeStruct((512, width), BF)]
        + [jax.ShapeDtypeStruct((4, 24, width), F32), jax.ShapeDtypeStruct((4, 24, width), BF)],
        compiler_params=pltpu.CompilerParams(vmem_limit_bytes=56 * MEBI),
        cost_estimate=SMALL_COST,
        name="second_half",
    )(meta, ids, *cots, out_own, up_own, down_own, *up_pieces, *down_pieces, normal, inverse, active, slope, mixed,
      gain1, gain2, table_in, table_in, table_in_hidden, table_out, table_out_hidden, table_out)


def first_grads_kernel(meta, ids, *refs):
    xs, dq_ref, dk_ref, dv_ref, got_ref = refs[0:5]
    ins, outs = refs[5:8], refs[8:11]
    grads_ref, rank_grad_ref = refs[11:13]
    own_half, other_half = refs[13:15]
    s_in, s_out, gathered = refs[15:]
    in_all = jnp.concatenate([ref[0, 0] for ref in ins], axis=0)
    out_all = jnp.concatenate([zero_padded(ref[0, 0], p, 3) for p, ref in enumerate(outs)], axis=1)
    for tile in range(2):
        rows = slice(256 * tile, 256 * tile + 256)
        grads = jnp.concatenate(
            [dq_ref[rows]]
            + [(ref[rows].astype(F32) + got_ref[n, rows].astype(F32)).astype(BF) for n, ref in enumerate((dk_ref, dv_ref))],
            axis=1,
        )
        grads_ref[rows] = grads
        x = xs[rows]
        rank = mm_nt(x, in_all).astype(BF)
        rank_grad = mm_nt(grads, out_all).astype(BF)
        rank_grad_ref[rows] = rank_grad
        part_in, part_out = mm_tn(rank_grad, x), mm_tn(rank, grads)
        if tile == 0:
            s_in[...] = part_in
            s_out[...] = part_out
        else:
            s_in[...] += part_in
            s_out[...] += part_out
    gathered[...] = jnp.zeros_like(gathered)
    for owner in range(4):
        for p in range(3):
            rows, columns = slice(RANK * p, RANK * p + RANK), slice(192 * owner, 192 * owner + 192)
            gathered[owner, 0:16, 192 * p : 192 * p + 192] = s_in[rows, columns]
            columns = slice(768 * p + 192 * owner, 768 * p + 192 * owner + 192)
            at = (0, 576) if p == 0 else (16, 192 * (p - 1))
            gathered[owner, at[0] : at[0] + 16, at[1] : at[1] + 192] = s_out[rows, columns]
    write_halves(meta, gathered, 2, own_half, other_half)


def first_grads(meta, ids, x, dq, dk, dv, got, table_in, table_out):
    width = x.shape[1]
    return pl.pallas_call(
        first_grads_kernel,
        grid_spec=pltpu.PrefetchScalarGridSpec(
            num_scalar_prefetch=2,
            grid=(1,),
            in_specs=[whole((512, width))] * 4
            + [whole((2, 512, width))]
            + [table_spec(p, p, width) for p in range(3)] * 2,
            out_specs=[whole((512, 3 * width)), whole((512, 3 * RANK))] + [whole((4, 16, width))] * 2,
            scratch_shapes=[
                VMEM((3 * RANK, width), F32),
                VMEM((3 * RANK, 3 * width), F32),
                VMEM((4, 2 * RANK, 768), F32),
            ],
        ),
        out_shape=[jax.ShapeDtypeStruct((512, 3 * width), BF), jax.ShapeDtypeStruct((512, 3 * RANK), BF)]
        + [jax.ShapeDtypeStruct((4, 16, width), F32), jax.ShapeDtypeStruct((4, 16, width), BF)],
        compiler_params=pltpu.CompilerParams(vmem_limit_bytes=30 * MEBI),
        cost_estimate=SMALL_COST,
        name="first_grads",
    )(meta, ids, x, dq, dk, dv, got, *([table_in] * 3), *([table_out] * 3))


def input_grad_kernel(meta, ids, *refs):
    w_own, pieces = refs[0], one_each(refs[1:9])
    branch_ref, grads_ref, rank_grad_ref = refs[9:12]
    ins, parts = refs[12:15], refs[15:17]
    weight, wsems = refs[17:]
    copies = weight_copies(meta, w_own, pieces, weight, wsems, qkv_places)
    for copy in copies:
        copy.start()
    for copy in copies:
        copy.wait()
    in_all = jnp.concatenate([ref[0, 0] for ref in ins], axis=0)
    result = (branch_ref[...] + mm_nt(grads_ref[...], weight[...]) + mm(rank_grad_ref[...], in_all)).astype(BF)
    even = (meta[0] & 1) == 0
    parts[0][...] = jnp.where(even, result[0:256], result[256:512])
    parts[1][...] = jnp.where(even, result[256:512], result[0:256])


def project_back(meta, ids, w_own, pieces, branch, grads, rank_grad, table_in):
    width = branch.shape[1]
    return pl.pallas_call(
        input_grad_kernel,
        grid_spec=pltpu.PrefetchScalarGridSpec(
            num_scalar_prefetch=2,
            grid=(1,),
            in_specs=any_specs(9)
            + [whole((512, width)), whole((512, 3 * width)), whole((512, 3 * RANK))]
            + [table_spec(p, p, width) for p in range(3)],
            out_specs=[whole((256, width))] * 2,
            scratch_shapes=[VMEM((width, 3 * width), BF), pltpu.SemaphoreType.DMA((25,))],
        ),
        out_shape=[jax.ShapeDtypeStruct((256, width), BF)] * 2,
        compiler_params=pltpu.CompilerParams(vmem_limit_bytes=30 * MEBI),
        cost_estimate=SMALL_COST,
        name="project_back",
    )(meta, ids, w_own, *pieces, branch, grads, rank_grad, *([table_in] * 3))


def sum_cores_kernel(ids, mid_own, mid_other, first_own, first_other, *messages):
    row = lax.broadcasted_iota(jnp.int32, (16, 768), 0)
    lane = lax.broadcasted_iota(jnp.int32, (16, 768), 1)
    for r, ref in enumerate(messages):
        mid = mid_own[r] + mid_other[r].astype(F32)
        first = first_own[r] + first_other[r].astype(F32)
        for p in range(6):
            first = jnp.where((row >= 8) & (lane == 384 + p), ids[p].astype(F32), first)
        ref[...] = jnp.concatenate([mid, first], axis=0).astype(BF)


def sum_cores(ids, *halves):
    width = halves[0].shape[-1]
    return pl.pallas_call(
        sum_cores_kernel,
        grid_spec=pltpu.PrefetchScalarGridSpec(
            num_scalar_prefetch=1,
            grid=(1,),
            in_specs=[whole(half.shape) for half in halves],
            out_specs=[whole((40, width))] * 4,
        ),
        out_shape=[jax.ShapeDtypeStruct((40, width), BF)] * 4,
        compiler_params=pltpu.CompilerParams(vmem_limit_bytes=30 * MEBI),
        cost_estimate=SMALL_COST,
        name="sum_cores",
    )(ids, *halves)


def combine_kernel(ids, meta, own, other, in_d, in_f, out_d, out_f):
    for ref in (in_d, in_f, out_d, out_f):
        ref[...] = jnp.zeros_like(ref)
    narrow = in_d.shape[-1]
    for chip in range(4):
        for r in range(4):
            chosen = [ids[(chip * 4 + r) * 6 + p] for p in range(6)]
            for half, messages in enumerate((own, other)):
                ranks = pl.ds(pl.multiple_of(8 * ((meta[1] & 1) ^ half), 8), 8)
                part = messages[chip, r].astype(F32)
                in_f[chosen[5], ranks, :] += part[0:8]
                out_f[chosen[4], ranks, :] += part[8:16]
                for at, (ref, p, which) in enumerate(
                    (
                        (in_d, 3, 3), (in_d, 4, 4), (out_d, 3, 3), (out_d, 4, 5),
                        (in_d, 0, 0), (in_d, 1, 1), (in_d, 2, 2), (out_d, 0, 0),
                        (out_d, 1, 1), (out_d, 2, 2),
                    )
                ):
                    row, column = 16 + 8 * (at // 4), narrow * (at % 4)
                    ref[p, chosen[which], ranks, :] += part[row : row + 8, column : column + narrow]


def combine(ids, meta, own, other, tables, narrow, wide):
    shapes = [(5, tables, RANK, narrow), (tables, RANK, wide)] * 2
    return pl.pallas_call(
        combine_kernel,
        grid_spec=pltpu.PrefetchScalarGridSpec(
            num_scalar_prefetch=2,
            grid=(1,),
            in_specs=[whole(own.shape)] * 2,
            out_specs=[whole(shape) for shape in shapes],
        ),
        out_shape=[jax.ShapeDtypeStruct(shape, F32) for shape in shapes],
        compiler_params=pltpu.CompilerParams(vmem_limit_bytes=30 * MEBI),
        cost_estimate=SMALL_COST,
        name="combine",
    )(ids, meta, own, other)


def after(value, *others):
    return lax.optimization_barrier((value, *others))[0]


def beside(work, transfers, values, moved):
    given = lax.optimization_barrier((tuple(values), tuple(moved)))
    return lax.optimization_barrier((tuple(work(*given[0])), tuple(transfers(*given[1]))))


def paired_body(
    inputs,
    segments,
    random_key_blocks,
    adapter_index_table,
    frozen_query_key_value_weight,
    frozen_output_weight,
    frozen_up_weight,
    frozen_down_weight,
    attention_norm_gain,
    feedforward_norm_gain,
    adapter_down_from_width,
    adapter_down_from_hidden,
    adapter_up_to_width,
    adapter_up_to_hidden,
    cotangent,
):
    dp_count, shard_count = lax.axis_size("dp"), lax.axis_size("shard")
    d, z = lax.axis_index("dp"), lax.axis_index("shard")
    core = d & 1
    meta = jnp.stack([z, d]).astype(jnp.int32)

    def piece(weight, rows, columns, row, column):
        return lax.dynamic_slice(weight, (row, column), (rows, columns))

    def fetch(part):
        return [swap_shards(part, shard_count, step) for step in range(1, shard_count)]

    def slices(values):
        return [lax.dynamic_index_in_dim(values, (z & 1) ^ r, 0, keepdims=False) for r in range(2)]

    def chips(block, *offsets):
        return [swap_chips(block, dp_count, offset) for offset in offsets]

    def swap(block):
        return swap_cores(block, dp_count)

    qkv_own = jnp.stack(fetch(piece(frozen_query_key_value_weight, 48, 1152, (d >> 1) * 48, core * 1152)))
    up_piece = jnp.concatenate(
        [
            piece(frozen_output_weight, 48, 384, (d >> 1) * 48, core * 384),
            piece(frozen_up_weight, 192, 384, 0, d * 384),
        ],
        axis=0,
    )
    down_piece = piece(frozen_down_weight, 96, 768, d * 96, 0)
    down_piece = jnp.concatenate([down_piece[:, 0:384], down_piece[:, 384:768]], axis=0)
    seg_rows = jnp.pad(segments.astype(BF)[:, None, :], ((0, 0), (0, 15), (0, inputs.shape[-1] - 256)))
    own = send_away(slices(jnp.concatenate([inputs, seg_rows], axis=1)), dp_count, shard_count)
    there = swap_cores(adapter_index_table, dp_count)
    column_ids = jnp.where(
        core == 0,
        jnp.concatenate([adapter_index_table, there], axis=0),
        jnp.concatenate([there, adapter_index_table], axis=0),
    )
    ids = lax.dynamic_index_in_dim(column_ids, z, 0, keepdims=False)

    blocks = jnp.arange(16, dtype=jnp.int32)
    query_block = (8 * core + blocks[0:8])[None, :, None]
    key_block = jnp.where(blocks < 8, 8 * core + blocks, 8 * (1 - core) + blocks - 8)[None, None, :]
    drawn = lax.dynamic_slice_in_dim(random_key_blocks, 8 * core, 8, axis=1)
    allowed = (jnp.abs(query_block - key_block) <= 1) | (query_block < GLOBALS) | (key_block < GLOBALS)
    for n in range(RANDOMS):
        allowed = allowed | (drawn[:, :, n : n + 1] == key_block)
    closed = jnp.pad(jnp.where(allowed, 0.0, -BIG), ((0, 0), (0, 0), (16, 32)))
    closed = closed.reshape(H // 2, 2, 8, 64)
    closed = jnp.concatenate([closed[:, 1], closed[:, 0]], axis=-1)

    qkv_own, meta, up_piece = lax.optimization_barrier((qkv_own, meta, up_piece))
    tokens = own + [swap(part) for part in own]
    qkv_x, qkv_y, qkv_xy = chips(qkv_own, 2, 4, 6)
    qkv_xy, closed, down_piece, ids = lax.optimization_barrier((qkv_xy, closed, down_piece, ids))
    qkv_pieces = spread_over_cores((qkv_own, qkv_x, qkv_y, qkv_xy), dp_count)
    up_own = fetch(after(up_piece, *own))

    def work(*given):
        return project_qkv(
            meta, ids, given[0:4], frozen_query_key_value_weight, given[4:],
            adapter_down_from_width, adapter_up_to_width,
        )

    (q, k, v, masks, hot, x), up_own = lax.optimization_barrier((work(*tokens, *qkv_pieces), up_own))
    up_own = jnp.stack(up_own)
    (mixed, shares), (up_x, up_y, up_there, down_1, down_2) = beside(
        lambda *given: attend(0, 4, *given, closed),
        lambda block, part: (
            *chips(block, 2, 4), swap(block), swap_shards(part, shard_count, 1), swap_shards(part, shard_count, 2)
        ),
        (q, k, v, masks, hot),
        (up_own, down_piece),
    )
    (mixed, shares), (up_a, up_b, up_x_there, up_y_there, down_3) = beside(
        lambda *before: attend(4, H // 2 - 4, q, k, v, masks, hot, closed, *before),
        lambda up_x, up_y, part: (
            *chips(up_x[:, 0:UP_SPLIT], 4),
            *chips(up_y[:, UP_SPLIT:], 2),
            swap(up_x),
            swap(up_y),
            swap_shards(part, shard_count, 3),
        ),
        (mixed, shares),
        (up_x, up_y, down_piece),
    )
    down_own = jnp.stack([down_1, down_2, down_3])
    up_pieces = (up_own, up_there, up_x, up_x_there, up_y, up_y_there, up_a, up_b, swap(up_a), swap(up_b))
    gain1, gain2 = attention_norm_gain, feedforward_norm_gain

    def work(mixed, *pieces):
        return first_half(
            meta, ids, frozen_output_weight, frozen_up_weight, pieces, x, mixed, gain1,
            adapter_down_from_width, adapter_up_to_width, adapter_up_to_hidden,
        )

    (normal, inverse, active, slope), (*down_pieces, cot_a, cot_b) = beside(
        work,
        lambda block, values: (*chips(block, 2, 4, 6), *send_away(slices(values), dp_count, shard_count)),
        (mixed, *up_pieces),
        (after(down_own, up_a, up_b), cotangent),
    )
    down_pieces = spread_over_cores((down_own, *down_pieces), dp_count)
    cots = (cot_a, cot_b)
    results = second_half(
        meta, ids, cots, frozen_output_weight, frozen_up_weight, frozen_down_weight, up_pieces, down_pieces,
        normal, inverse, active, slope, mixed, gain1, gain2,
        adapter_down_from_width, adapter_down_from_hidden, adapter_up_to_width, adapter_up_to_hidden,
    )
    grad_branch = results[2]

    def home(r, part):
        return lax.ppermute(part, ("dp", "shard"), away_pairs(dp_count, shard_count, r))

    def swap_over_shards(*parts):
        return [swap_shards(part, shard_count, step + 1) for step, part in enumerate(parts)]

    (dq, dk, dv, other_sums), (layer_a, layer_b) = beside(
        lambda grad: attend_back(q, k, v, shares, grad, mixed),
        lambda part_a, part_b: (home(0, part_a), home(1, part_b)),
        (results[3],),
        results[0:2],
    )
    grads, rank_grad, first_own, first_other = first_grads(
        meta, ids, x, dq, dk, dv, swap(other_sums), adapter_down_from_width, adapter_up_to_width
    )
    input_parts, (first_other, mid_other) = beside(
        lambda grads: project_back(
            meta, ids, frozen_query_key_value_weight, qkv_pieces, grad_branch, grads, rank_grad,
            adapter_down_from_width,
        ),
        lambda *halves: [swap(half) for half in halves],
        (grads,),
        (first_other, results[5]),
    )
    message, *others = sum_cores(ids, results[4], mid_other, first_own, first_other)
    (layer_out,), moved = beside(
        lambda *parts: (join_parts(meta, parts, BF),),
        swap_over_shards,
        (layer_a, layer_b),
        others,
    )
    messages = jnp.stack([message, *moved])
    _, (part_a, part_b, *moved) = beside(
        lambda: (),
        lambda part_a, part_b, block: (home(0, part_a), home(1, part_b), *chips(block, 2, 4, 6)),
        (),
        (*input_parts, messages),
    )
    messages = jnp.stack([messages, *moved])
    chosen = messages[:, :, 32, 384:390].astype(jnp.int32).reshape(-1)
    in_d, in_f, out_d, out_f = combine(
        chosen, meta, messages, swap(messages), adapter_down_from_width.shape[1], 192, 768
    )
    return (layer_out, join_parts(meta, (part_a, part_b), F32), in_d, in_f, out_d, out_f)


def solution(mesh):
    dp_count, shard_count = mesh.shape["dp"], mesh.shape["shard"]
    paired = dp_count == 8 and shard_count == 4
    return jax.shard_map(
        paired_body if paired else general_body,
        mesh=mesh,
        in_specs=(
            P("dp", "shard", None),
            P("dp", "shard"),
            P(),
            P("dp", None),
            P("shard", None),
            P("shard", None),
            P("shard", None),
            P("shard", None),
            P(),
            P(),
            P(),
            P(),
            P(),
            P(),
            P("dp", "shard", None),
        ),
        out_specs=(
            P("dp", "shard", None),
            P("dp", "shard", None),
            P(None, None, None, "shard"),
            P(None, None, "shard"),
            P(None, None, None, "shard"),
            P(None, None, "shard"),
        ),
        check_vma=False,
    )
```
